32 devices in a mesh: band: 16 (over z, x, core), dp: 2 (over y).
Axes of the slice: x: 2, y: 2, z: 4, core: 2. Of those that a mesh axis runs over, the one named last changes fastest.
Arguments:
- pixels: bfloat16 [2, 16, 128, 16, 256], P('dp', None, None, 'band'), may hold values from -6 to 6
- wavelengths: int32 [16], replicated, may hold values from 400 to 2499
- band_counts: int32 [2, 16], P('dp'), may hold values from 2 to 16, as said below
- band_mask: int32 [2, 16, 16], P('dp', None, 'band'), may hold values from 0 to 1, as said below
- hyper_qkv: bfloat16 [128, 384], replicated, may hold values from -1 to 1
- hyper_out: bfloat16 [128, 128], replicated, may hold values from -0.5 to 0.5
- hyper_gain1: bfloat16 [128], replicated, may hold values from 0.099609375 to 1.8984375
- hyper_up: bfloat16 [128, 2048], replicated, may hold values from -0.5 to 0.5
- hyper_down: bfloat16 [2048, 128], replicated, may hold values from -0.125 to 0.125
- hyper_gain2: bfloat16 [128], replicated, may hold values from 0.099609375 to 1.8984375
- kernel_gen: bfloat16 [128, 196608], P(None, 'band'), may hold values from -0.03125 to 0.03125
- bias_gen: bfloat16 [128, 768], replicated, may hold values from -0.5 to 0.5
- norm_gain1: bfloat16 [768], replicated, may hold values from 0.099609375 to 1.8984375
- attn_qkv: bfloat16 [768, 2304], P(('band', 'dp')), may hold values from -0.21875 to 0.21875
- attn_out: bfloat16 [768, 768], P(('band', 'dp')), may hold values from -0.625 to 0.625
- norm_gain2: bfloat16 [768], replicated, may hold values from 0.099609375 to 1.8984375
- mlp_up: bfloat16 [768, 3072], P(('band', 'dp')), may hold values from -0.21875 to 0.21875
- mlp_down: bfloat16 [3072, 768], P(('band', 'dp')), may hold values from -0.109375 to 0.109375
- out_grad: bfloat16 [2, 16, 128, 768], P('dp', 'band'), may hold values from -6 to 6
Outputs:
- block_out: bfloat16 [2, 16, 128, 768], P('dp', 'band')
- pixel_grad: bfloat16 [2, 16, 128, 16, 256], P('dp', None, None, 'band')
- grad_hyper_qkv: float32 [128, 384], replicated
- grad_hyper_out: float32 [128, 128], replicated
- grad_hyper_gain1: float32 [128], replicated
- grad_hyper_up: float32 [128, 2048], replicated
- grad_hyper_down: float32 [2048, 128], replicated
- grad_hyper_gain2: float32 [128], replicated
- grad_kernel_gen: float32 [128, 196608], P(None, 'band')
- grad_bias_gen: float32 [128, 768], replicated
- grad_norm_gain1: float32 [768], replicated
- grad_attn_qkv: float32 [768, 2304], P(('band', 'dp'))
- grad_attn_out: float32 [768, 768], P(('band', 'dp'))
- grad_norm_gain2: float32 [768], replicated
- grad_mlp_up: float32 [768, 3072], P(('band', 'dp'))
- grad_mlp_down: float32 [3072, 768], P(('band', 'dp'))
The draws below stay inside these ranges and needn't reach their ends.
Inputs may be any that keep to these rules, and one draw needn't show every extreme that they name: `wavelengths`: wavelength of each band slot in nanometres. Image i of group g uses band slot b when b < band_counts[g, i] and band_mask[g, i, b] = 1; in every group some image has 16 bands. `band_mask`: in every group the image with 16 bands keeps all of them.
All inputs are finite; a program needn't handle non-finite values.
Results may differ from the reference program's by a relative error of at most 0.014.
Values may be sent and summed in bfloat16 or wider, within the bound.
A program may use at most 256 MiB of HBM per device.

```python
import math
import jax
import jax.numpy as jnp
from jax import lax

D = 768
HEADS = 12
HEAD_DIM = 64
FF = 3072
HW = 128
HHEADS = 4
HFF = 2048
PIX = 256
NPATCH = 128
NB = 16
IMG_G = 16
N_DP = 2


def longest_rows(key):
    return jax.random.randint(jax.random.fold_in(key, 97), (N_DP,), 0, IMG_G)


def draw_band_counts(key, part):
    longest = longest_rows(key)
    key = jax.random.fold_in(key, 1)
    counts = jax.random.randint(key, (N_DP, IMG_G), 2, NB + 1)
    places = jnp.arange(IMG_G, dtype=jnp.int32)[None, :] == longest[:, None]
    return jnp.where(places, NB, counts).astype(jnp.int32)


def draw_band_mask(key, part):
    longest = longest_rows(key)
    key = jax.random.fold_in(key, 2)
    survive = (jax.random.randint(key, (N_DP, IMG_G, NB), 0, 4) < 3).astype(jnp.int32)
    places = (jnp.arange(IMG_G, dtype=jnp.int32)[None, :] == longest[:, None])[:, :, None]
    return jnp.where(places, 1, survive).astype(jnp.int32)


def with_ends(values, stream_key, low, top_value):
    longest = values.shape.index(max(values.shape))
    spots = []
    for shift in (0, 1):
        where = [jax.random.randint(jax.random.fold_in(stream_key, axis), (), 0, length) for axis, length in enumerate(values.shape)]
        where[longest] = (where[longest] + shift) % values.shape[longest]
        spots.append(tuple(where))
    return values.at[spots[0]].set(low).at[spots[1]].set(top_value)


def level_of(stream_key, dims, shards, low, top_value):
    loudness, own = 1.0, jax.random.fold_in(stream_key, 6)
    for axis_at, blocks in shards:
        heights = jnp.exp(jax.random.uniform(jax.random.fold_in(own, axis_at), (blocks,), jnp.float32, low / len(shards), top_value / len(shards)))
        loudness = loudness * jnp.repeat(heights, dims[axis_at] // blocks).reshape([-1 if axis == axis_at else 1 for axis in range(len(dims))])
    return loudness


def gaussian(stream_key, shape, width, limit, shards=(), kind=jnp.bfloat16):
    entries = jax.random.normal(stream_key, shape, jnp.float32) * width
    if len(shards) > 0:
        entries = level_of(stream_key, shape, shards, -0.22, 0.18) * entries
    return jnp.clip(entries, min=-limit, max=limit).astype(kind)


def setup_inputs(seed: int = 0) -> dict:
    keys = jax.random.split(jax.random.key(seed), 20)
    pixels = gaussian(keys[0], (N_DP, IMG_G, NPATCH, NB, PIX), 1.0, 6.0, ((0, 2), (3, 16)))
    wavelengths = with_ends(jax.random.randint(keys[1], (NB,), 400, 2500), jax.random.fold_in(keys[1], 1), 400, 2499).astype(jnp.int32)
    band_counts = draw_band_counts(jax.random.fold_in(keys[19], 71), 0)
    band_mask = draw_band_mask(jax.random.fold_in(keys[19], 71), 0)
    hyper_qkv = gaussian(keys[4], (HW, 3 * HW), (HW // 4) ** -0.5, 1.0)
    hyper_out = gaussian(keys[5], (HW, HW), HW ** -0.5, 0.5)
    hyper_gain1 = jnp.clip(1.0 + 0.18 * jax.random.normal(keys[6], (HW,), jnp.float32), 0.099609375, 1.8984375).astype(jnp.bfloat16)
    hyper_up = gaussian(keys[7], (HW, HFF), HW ** -0.5, 0.5)
    hyper_down = gaussian(keys[8], (HFF, HW), HFF ** -0.5, 0.125)
    hyper_gain2 = jnp.clip(1.0 + 0.18 * jax.random.normal(keys[9], (HW,), jnp.float32), 0.099609375, 1.8984375).astype(jnp.bfloat16)
    kernel_gen = gaussian(keys[10], (HW, PIX * D), (HW * PIX) ** -0.5, 0.03125, ((1, 16),))
    bias_gen = gaussian(keys[11], (HW, D), HW ** -0.5, 0.5)
    norm_gain1 = jnp.clip(1.0 + 0.18 * jax.random.normal(keys[12], (D,), jnp.float32), 0.099609375, 1.8984375).astype(jnp.bfloat16)
    attn_qkv = gaussian(keys[13], (D, 3 * D), D ** -0.5, 0.21875, ((0, 32),))
    attn_out = gaussian(keys[14], (D, D), (D // 8) ** -0.5, 0.625, ((0, 32),))
    norm_gain2 = jnp.clip(1.0 + 0.18 * jax.random.normal(keys[15], (D,), jnp.float32), 0.099609375, 1.8984375).astype(jnp.bfloat16)
    mlp_up = gaussian(keys[16], (D, FF), D ** -0.5, 0.21875, ((0, 32),))
    mlp_down = gaussian(keys[17], (FF, D), FF ** -0.5, 0.109375, ((0, 32),))
    out_grad = gaussian(keys[18], (N_DP, IMG_G, NPATCH, D), 1.0, 6.0, ((0, 2), (1, 16)))
    return {"pixels": pixels, "wavelengths": wavelengths, "band_counts": band_counts, "band_mask": band_mask, "hyper_qkv": hyper_qkv, "hyper_out": hyper_out, "hyper_gain1": hyper_gain1, "hyper_up": hyper_up, "hyper_down": hyper_down, "hyper_gain2": hyper_gain2, "kernel_gen": kernel_gen, "bias_gen": bias_gen, "norm_gain1": norm_gain1, "attn_qkv": attn_qkv, "attn_out": attn_out, "norm_gain2": norm_gain2, "mlp_up": mlp_up, "mlp_down": mlp_down, "out_grad": out_grad}


PRECISE = lax.Precision.HIGHEST
EPS_BLOCK = 1e-06
EPS_HYPER = 1e-05
GELU_COEF = 0.7978845608028654

@jax.custom_vjp
def low(v):
    return lax.optimization_barrier(v.astype(jnp.bfloat16)).astype(jnp.float32)

@jax.custom_vjp
def low_back(v):
    return v

def low_keep(v):
    return (low(v), None)

def low_pass(kept, grad):
    return (grad,)

def back_keep(v):
    return (v, None)

def back_low(kept, grad):
    return (low(grad),)
low.defvjp(low_keep, low_pass)
low_back.defvjp(back_keep, back_low)

def gelu_tanh(tensor):
    return 0.5 * tensor * (1.0 + jnp.tanh(GELU_COEF * (tensor + 0.044715 * tensor * tensor * tensor)))

def layer_norm(tensor, gain_vec, epsilon):
    centred = tensor - lax.optimization_barrier(jnp.mean(tensor, axis=-1, keepdims=True))
    return centred * lax.rsqrt(lax.optimization_barrier(jnp.mean(centred * centred, axis=-1, keepdims=True)) + epsilon) * gain_vec

def wave_embed(wave_ints, token_width):
    half_width = token_width // 2
    frequency = jnp.power(10000.0, -jnp.arange(half_width, dtype=jnp.float32) / half_width)
    angles = wave_ints.astype(jnp.float32)[:, None] * frequency[None, :]
    return jnp.concatenate([jnp.sin(angles), jnp.cos(angles)], axis=1)

def hyper_net(wave_tokens, qkv_weight, out_weight, gain_one, up_weight, down_weight, gain_two):
    tokens, token_width = wave_tokens.shape
    head_size = token_width // HHEADS
    qkv_rows = jnp.dot(wave_tokens, qkv_weight, precision=PRECISE)
    queries = qkv_rows[:, :token_width].reshape(tokens, HHEADS, head_size)
    key_rows = qkv_rows[:, token_width:2 * token_width].reshape(tokens, HHEADS, head_size)
    value_rows = qkv_rows[:, 2 * token_width:].reshape(tokens, HHEADS, head_size)
    scores = jnp.einsum('nhc,mhc->hnm', queries, key_rows, precision=PRECISE) / math.sqrt(head_size)
    weights_soft = jax.nn.softmax(scores, axis=-1)
    mixed_rows = jnp.einsum('hnm,mhc->nhc', weights_soft, value_rows, precision=PRECISE).reshape(tokens, token_width)
    first_norm = layer_norm(wave_tokens + jnp.dot(mixed_rows, out_weight, precision=PRECISE), gain_one, EPS_HYPER)
    inner_act = gelu_tanh(jnp.dot(first_norm, up_weight, precision=PRECISE))
    return layer_norm(first_norm + jnp.dot(inner_act, down_weight, precision=PRECISE), gain_two, EPS_HYPER)

def block(residual, gain_one, qkv_weight, out_weight, gain_two, up_weight, down_weight):
    tokens = residual.shape[0]
    score_scale = 1.0 / math.sqrt(HEAD_DIM)
    normed_one = low(layer_norm(residual, gain_one, EPS_BLOCK))
    joint_rows = low_back(low(jnp.dot(normed_one, qkv_weight, precision=PRECISE)))
    queries = joint_rows[:, :D].reshape(tokens, HEADS, HEAD_DIM)
    key_rows = joint_rows[:, D:2 * D].reshape(tokens, HEADS, HEAD_DIM)
    value_rows = joint_rows[:, 2 * D:].reshape(tokens, HEADS, HEAD_DIM)
    scores = low_back(jnp.einsum('nhc,mhc->hnm', queries, key_rows, precision=PRECISE) * score_scale)
    probs_low = low(jax.nn.softmax(scores, axis=-1))
    mixed_low = low_back(low(jnp.einsum('hnm,mhc->nhc', probs_low, value_rows, precision=PRECISE).reshape(tokens, D)))
    middle = residual + low_back(jnp.dot(mixed_low, out_weight, precision=PRECISE))
    normed_two = low(layer_norm(middle, gain_two, EPS_BLOCK))
    act_low = low(gelu_tanh(low_back(jnp.dot(normed_two, up_weight, precision=PRECISE))))
    return middle + low_back(jnp.dot(act_low, down_weight, precision=PRECISE))

def forward(pixels, band_weight, wavelengths, hyper_qkv, hyper_out, hyper_gain1, hyper_up, hyper_down, hyper_gain2, kernel_gen, bias_gen, norm_gain1, attn_qkv, attn_out, norm_gain2, mlp_up, mlp_down):
    band_code = hyper_net(wave_embed(wavelengths, HW), hyper_qkv, hyper_out, hyper_gain1, hyper_up, hyper_down, hyper_gain2)
    code_low = low(band_code)
    kernels = low_back(low(jnp.dot(code_low, kernel_gen, precision=PRECISE))).reshape(NB, PIX, D)
    biases = jnp.dot(code_low, bias_gen, precision=PRECISE)
    flat_pixels = pixels.reshape(N_DP * IMG_G, NPATCH, NB, PIX)
    flat_weight = band_weight.reshape(N_DP * IMG_G, NB)

    def image_term(image_item):
        pixel_item, weight_item = image_item
        conv_out = low_back(jnp.einsum('nbp,bpd->nbd', pixel_item.astype(jnp.float32), kernels, precision=PRECISE))
        return jnp.einsum('nbd,b->nd', conv_out + biases[None], weight_item, precision=PRECISE)
    embed_rows = lax.map(jax.checkpoint(image_term), (flat_pixels, flat_weight))
    residual = low_back(embed_rows)

    def image_block(resid_item):
        return block(resid_item, norm_gain1, attn_qkv, attn_out, norm_gain2, mlp_up, mlp_down)
    block_result = lax.map(jax.checkpoint(image_block), residual)
    return block_result.reshape(N_DP, IMG_G, NPATCH, D)

def reference(pixels, wavelengths, band_counts, band_mask, hyper_qkv, hyper_out, hyper_gain1, hyper_up, hyper_down, hyper_gain2, kernel_gen, bias_gen, norm_gain1, attn_qkv, attn_out, norm_gain2, mlp_up, mlp_down, out_grad):
    slot_ids = jnp.arange(NB, dtype=jnp.int32)
    active = (slot_ids[None, None, :] < band_counts[:, :, None]) & (band_mask == 1)
    band_weight = jnp.where(active, lax.rsqrt(band_counts.astype(jnp.float32))[:, :, None], jnp.float32(0.0))
    floats = tuple((weight.astype(jnp.float32) for weight in (hyper_qkv, hyper_out, hyper_gain1, hyper_up, hyper_down, hyper_gain2, kernel_gen, bias_gen, norm_gain1, attn_qkv, attn_out, norm_gain2, mlp_up, mlp_down)))

    def run_layer(pixel_arg, *params):
        return forward(pixel_arg, band_weight, wavelengths, *params)
    block_result, pull_back = jax.vjp(run_layer, pixels, *floats)
    grads = pull_back(out_grad.astype(jnp.float32))
    return (block_result.astype(jnp.bfloat16), grads[0].astype(jnp.bfloat16), grads[1], grads[2], grads[3], grads[4], grads[5], grads[6], grads[7], grads[8], grads[9], grads[10], grads[11], grads[12], grads[13], grads[14])
```

```python
import functools
import math

import jax
import jax.numpy as jnp
from jax import lax
from jax.experimental import pallas as pl
from jax.experimental.pallas import tpu as pltpu
from jax.sharding import PartitionSpec as P

HEADS = 12
HEAD_DIM = 64
HW = 128
HHEADS = 4


PRECISE = lax.Precision.HIGHEST
EPS_BLOCK = 1e-06
EPS_HYPER = 1e-05
GELU_COEF = 0.7978845608028654


def gelu_tanh(tensor):
    return (
        0.5 * tensor * (1.0 + jnp.tanh(GELU_COEF * (tensor + 0.044715 * tensor * tensor * tensor)))
    )


def gelu_slope(tensor):
    tanh_val = jnp.tanh(GELU_COEF * (tensor + 0.044715 * tensor * tensor * tensor))
    return 0.5 * (1.0 + tanh_val) + 0.5 * tensor * (1.0 - tanh_val * tanh_val) * GELU_COEF * (
        1.0 + 3.0 * 0.044715 * tensor * tensor
    )


def layer_norm(tensor, gain_vec, epsilon):
    centred = tensor - jnp.mean(tensor, axis=-1, keepdims=True)
    return (
        centred
        * lax.rsqrt(jnp.mean(centred * centred, axis=-1, keepdims=True) + epsilon)
        * gain_vec
    )


def norm_parts(tensor, gain_vec):
    centred = tensor - jnp.mean(tensor, axis=-1, keepdims=True)
    inverse = lax.rsqrt(jnp.mean(centred * centred, axis=-1, keepdims=True) + EPS_BLOCK)
    unit_rows = centred * inverse
    return (unit_rows * gain_vec, unit_rows, inverse)


def norm_back(grad_rows, gain_vec, unit_rows, inverse):
    scaled = grad_rows * gain_vec
    return inverse * (
        scaled
        - jnp.mean(scaled, axis=-1, keepdims=True)
        - unit_rows * jnp.mean(scaled * unit_rows, axis=-1, keepdims=True)
    )


def wave_embed(wave_ints, token_width):
    half_width = token_width // 2
    frequency = jnp.power(10000.0, -jnp.arange(half_width, dtype=jnp.float32) / half_width)
    angles = wave_ints.astype(jnp.float32)[:, None] * frequency[None, :]
    return jnp.concatenate([jnp.sin(angles), jnp.cos(angles)], axis=1)


def hyper_net(wave_tokens, qkv_weight, out_weight, gain_one, up_weight, down_weight, gain_two):
    tokens, token_width = wave_tokens.shape
    head_size = token_width // HHEADS
    qkv_rows = jnp.dot(wave_tokens, qkv_weight, precision=PRECISE)
    queries = qkv_rows[:, :token_width].reshape(tokens, HHEADS, head_size)
    key_rows = qkv_rows[:, token_width : 2 * token_width].reshape(tokens, HHEADS, head_size)
    value_rows = qkv_rows[:, 2 * token_width :].reshape(tokens, HHEADS, head_size)
    scores = jnp.einsum("nhc,mhc->hnm", queries, key_rows, precision=PRECISE) / math.sqrt(head_size)
    weights_soft = jax.nn.softmax(scores, axis=-1)
    mixed_rows = jnp.einsum("hnm,mhc->nhc", weights_soft, value_rows, precision=PRECISE).reshape(
        tokens, token_width
    )
    first_norm = layer_norm(
        wave_tokens + jnp.dot(mixed_rows, out_weight, precision=PRECISE), gain_one, EPS_HYPER
    )
    inner_act = gelu_tanh(jnp.dot(first_norm, up_weight, precision=PRECISE))
    return layer_norm(
        first_norm + jnp.dot(inner_act, down_weight, precision=PRECISE), gain_two, EPS_HYPER
    )


MESH = pl.DeviceIdType.MESH
GATHER_ORDERS = ("zxy", "xzy", "yzx", "zyx", "xzy", "yzx")


def place():
    band = lax.axis_index("band")
    return (band // 4, (band // 2) % 2, band % 2, lax.axis_index("dp"))


def device(z, x, core, y):
    return (z * 4 + x * 2 + core, y)


def slot(z, x, core, y):
    return (z * 4 + x * 2 + core) * 2 + y


def when(cond, run):
    if cond is True:
        run()
    else:
        pl.when(cond)(run)


def both(first, second):
    return second if first is True else first & second


def meet_neighbours():
    z, x, core, y = place()
    barrier = pltpu.get_barrier_semaphore()
    near = [
        (device(z, x, 1 - core, y), True),
        (device(z, 1 - x, core, y), True),
        (device(z, x, core, 1 - y), True),
        (device(z + 1, x, core, y), z < 3),
        (device(z - 1, x, core, y), z > 0),
    ]
    for target, cond in near:
        when(
            cond,
            lambda target=target: pl.semaphore_signal(
                barrier, inc=1, device_id=target, device_id_type=MESH
            ),
        )
    pl.semaphore_wait(barrier, 5 - z // 3 - (3 - z) // 3)


class Gather:
    def __init__(self, held, rows, orders, send_sem, recv_sem, pair_send, pair_recv):
        self.held, self.rows, self.orders = held, rows, orders
        self.send_sem, self.recv_sem = send_sem, recv_sem
        self.pair_send, self.pair_recv = pair_send, pair_recv
        self.z, self.x, self.core, self.y = place()
        self.sends = []
        self.count = [0] * len(orders)

    def view(self, chunk, where):
        return self.held.at[where, pl.ds(chunk * self.rows, self.rows)]

    def send(self, chunk, block, dim, cond, direction=0):
        z, x, core, y = self.z, self.x, self.core, self.y
        if dim == "x":
            targets = [(device(z, 1 - x, core, y), cond)]
        elif dim == "y":
            targets = [(device(z, x, core, 1 - y), cond)]
        else:
            targets = []
            if direction >= 0:
                targets.append((device(z + 1, x, core, y), both(cond, z < 3)))
            if direction <= 0:
                targets.append((device(z - 1, x, core, y), both(cond, z > 0)))
        src = self.view(chunk, slot(block[0], block[1], core, block[2]))
        rail = block[0] * 4 + block[1] * 2 + block[2]
        for target, needed in targets:
            copy = pltpu.make_async_remote_copy(
                src_ref=src,
                dst_ref=src,
                send_sem=self.send_sem.at[chunk, self.count[chunk]],
                recv_sem=self.recv_sem.at[chunk, rail],
                device_id=target,
                device_id_type=MESH,
            )
            self.count[chunk] += 1
            when(needed, copy.start)
            self.sends.append((needed, copy))

    def pair(self, chunk, block, core):
        src = self.view(chunk, slot(block[0], block[1], core, block[2]))
        rail = block[0] * 4 + block[1] * 2 + block[2]
        return pltpu.make_async_remote_copy(
            src_ref=src,
            dst_ref=src,
            send_sem=self.pair_send.at[chunk, rail],
            recv_sem=self.pair_recv.at[chunk, rail],
            device_id=device(self.z, self.x, 1 - self.core, self.y),
            device_id_type=MESH,
        )

    def start(self, chunk):
        own = (self.z, self.x, self.y)
        for dim in self.orders[chunk]:
            self.send(chunk, own, dim, True)
        self.pair(chunk, own, self.core).start()

    def events(self, chunk):
        held, found = [(0, 0, 0, 0, 0.0)], []
        for dim in self.orders[chunk]:
            clock, new = 0.0, []
            ordered = sorted(held, key=lambda item: item[4])
            if dim == "z":
                for dist in (1, 2, 3):
                    for item in ordered:
                        clock = max(clock, item[4]) + 1.0
                        new += [(dist, way, item[2], item[3], clock) for way in (1, -1)]
            else:
                for item in ordered:
                    clock = max(clock, item[4]) + 1.0
                    flip = (1, item[3]) if dim == "x" else (item[2], 1)
                    new.append((item[0], item[1], *flip, clock))
            found += [(item[4], chunk, dim, item) for item in new]
            held = held + new
        return found

    def arrive(self, chunk, dim, item):
        dist, way, flip_x, flip_y, _ = item
        cond = True
        if way == 1:
            cond = self.z >= dist
        elif way == -1:
            cond = self.z + dist <= 3
        block = (
            self.z - dist * way,
            1 - self.x if flip_x else self.x,
            1 - self.y if flip_y else self.y,
        )
        src = self.view(chunk, slot(block[0], block[1], self.core, block[2]))
        rail = block[0] * 4 + block[1] * 2 + block[2]
        arriving = pltpu.make_async_remote_copy(
            src_ref=src,
            dst_ref=src,
            send_sem=self.send_sem.at[chunk, 0],
            recv_sem=self.recv_sem.at[chunk, rail],
            device_id=device(self.z, self.x, 1 - self.core, self.y),
            device_id_type=MESH,
        )
        when(cond, arriving.wait_recv)
        if dim == "z":
            self.send(chunk, block, "z", cond, way)
        order = self.orders[chunk]
        for later in order[order.index(dim) + 1 :]:
            self.send(chunk, block, later, cond)
        when(cond, self.pair(chunk, block, self.core).start)

    def finish(self):
        for needed, copy in self.sends:
            when(needed, copy.wait_send)
        for chunk in range(len(self.orders)):
            for rail in range(16):
                block = (rail // 4, (rail // 2) % 2, rail % 2)
                self.pair(chunk, block, self.core).wait_send()
                self.pair(chunk, block, 1 - self.core).wait_recv()


def gather_kernel(shard, whole, held, local_sem, *sems):
    rows = held.shape[1] // len(GATHER_ORDERS)
    own = pltpu.make_async_copy(shard, held.at[slot(*place())], local_sem)
    own.start()
    own.wait()
    meet_neighbours()
    gather = Gather(held, rows, GATHER_ORDERS, *sems)
    events = []
    for chunk in range(len(GATHER_ORDERS)):
        gather.start(chunk)
        events += gather.events(chunk)
    for _, chunk, dim, item in sorted(events, key=lambda event: event[:2]):
        gather.arrive(chunk, dim, item)
    gather.finish()
    out = pltpu.make_async_copy(held, whole, local_sem)
    out.start()
    out.wait()


def gather_weights(attn_qkv, attn_out, mlp_up, mlp_down):
    if (lax.axis_size("band"), lax.axis_size("dp")) != (16, 2):
        return tuple(
            lax.all_gather(weight, ("band", "dp"), axis=0, tiled=True)
            for weight in (attn_qkv, attn_out, mlp_up, mlp_down)
        )
    width = attn_out.shape[1]
    devices = lax.axis_size("band") * lax.axis_size("dp")

    def stack(weight):
        parts = weight.shape[1] // width
        return weight.reshape(weight.shape[0], parts, width).transpose(1, 0, 2).reshape(-1, width)

    shard = jnp.concatenate([stack(w) for w in (attn_qkv, attn_out, mlp_up, mlp_down)], axis=0)
    chunks = len(GATHER_ORDERS)
    whole = pl.pallas_call(
        gather_kernel,
        out_shape=jax.ShapeDtypeStruct((devices, *shard.shape), shard.dtype),
        in_specs=[pl.BlockSpec(memory_space=pl.ANY)],
        out_specs=pl.BlockSpec(memory_space=pl.ANY),
        scratch_shapes=[
            pltpu.VMEM((devices, *shard.shape), shard.dtype),
            pltpu.SemaphoreType.DMA,
            pltpu.SemaphoreType.DMA((chunks, 40)),
            pltpu.SemaphoreType.DMA((chunks, 16)),
            pltpu.SemaphoreType.DMA((chunks, 16)),
            pltpu.SemaphoreType.DMA((chunks, 16)),
        ],
        compiler_params=pltpu.CompilerParams(
            collective_id=0, has_side_effects=True, vmem_limit_bytes=56 * 2**20
        ),
        name="gather_weights",
    )(shard)
    out, at = [], 0
    for weight in (attn_qkv, attn_out, mlp_up, mlp_down):
        rows, parts = weight.shape[0], weight.shape[1] // width
        piece = whole[:, at : at + rows * parts].reshape(devices, parts, rows, width)
        out.append(piece.transpose(0, 2, 1, 3).reshape(devices * rows, parts * width))
        at += rows * parts
    return tuple(out)


def body(
    pixels,
    wavelengths,
    band_counts,
    band_mask,
    hyper_qkv,
    hyper_out,
    hyper_gain1,
    hyper_up,
    hyper_down,
    hyper_gain2,
    kernel_gen,
    bias_gen,
    norm_gain1,
    attn_qkv,
    attn_out,
    norm_gain2,
    mlp_up,
    mlp_down,
    out_grad,
):
    f32 = jnp.float32
    b16 = jnp.bfloat16
    band_local = pixels.shape[3]
    pixel_local = pixels[0]
    model_width = bias_gen.shape[1]
    hyper_params = tuple(
        (
            weight.astype(f32)
            for weight in (hyper_qkv, hyper_out, hyper_gain1, hyper_up, hyper_down, hyper_gain2)
        )
    )
    wave_tokens = wave_embed(wavelengths, HW)
    band_code, hyper_pull = jax.vjp(lambda *params: hyper_net(wave_tokens, *params), *hyper_params)
    code_low = band_code.astype(b16)
    column_part = jnp.dot(code_low, kernel_gen, preferred_element_type=f32).astype(b16)
    kernel_rows = lax.all_to_all(column_part, "band", split_axis=0, concat_axis=1, tiled=True)
    kernels = kernel_rows.reshape(band_local, -1, model_width)
    first_band = lax.axis_index("band") * band_local
    own_code = lax.dynamic_slice_in_dim(code_low, first_band, band_local, 0)
    count_row = band_counts[0]
    biases = jnp.dot(own_code, bias_gen, preferred_element_type=f32)
    slot_ids = first_band + jnp.arange(band_local, dtype=jnp.int32)
    active = (slot_ids[None, :] < count_row[:, None]) & (band_mask[0] == 1)
    band_weight = jnp.where(active, lax.rsqrt(count_row.astype(f32))[:, None], f32(0.0))
    pixel_rows = pixel_local
    weight_rows = band_weight
    conv_out = jnp.einsum("inbp,bpd->inbd", pixel_rows, kernels, preferred_element_type=f32)
    residual = lax.psum_scatter(
        jnp.sum((conv_out + biases[None, None]) * weight_rows[:, None, :, None], axis=2),
        "band",
        scatter_dimension=0,
        tiled=True,
    )
    gathered = gather_weights(attn_qkv, attn_out, mlp_up, mlp_down)
    qkv_full, out_full, up_full, down_full = gathered
    gain_one = norm_gain1.astype(f32)
    gain_two = norm_gain2.astype(f32)
    images, tokens = (residual.shape[0], residual.shape[1])
    score_scale = 1.0 / math.sqrt(HEAD_DIM)
    normed_full, unit_one, inverse_one = norm_parts(residual, gain_one)
    normed_one = normed_full.astype(b16)
    joint_rows = jnp.einsum("ind,de->ine", normed_one, qkv_full, preferred_element_type=f32).astype(
        b16
    )
    queries = joint_rows[..., :model_width].reshape(images, tokens, HEADS, HEAD_DIM)
    key_rows = joint_rows[..., model_width : 2 * model_width].reshape(
        images, tokens, HEADS, HEAD_DIM
    )
    value_rows = joint_rows[..., 2 * model_width :].reshape(images, tokens, HEADS, HEAD_DIM)
    scores = (
        jnp.einsum("inhc,imhc->ihnm", queries, key_rows, preferred_element_type=f32) * score_scale
    )
    row_top = jnp.max(scores, axis=-1, keepdims=True)
    log_total = row_top + jnp.log(jnp.sum(jnp.exp(scores - row_top), axis=-1, keepdims=True))
    probs_full = jnp.exp(scores - log_total)
    probs_low = probs_full.astype(b16)
    mixed_low = (
        jnp.einsum("ihnm,imhc->inhc", probs_low, value_rows, preferred_element_type=f32)
        .reshape(images, tokens, model_width)
        .astype(b16)
    )
    middle = residual + jnp.einsum("ind,de->ine", mixed_low, out_full, preferred_element_type=f32)
    normed_two_full, unit_two, inverse_two = norm_parts(middle, gain_two)
    normed_two = normed_two_full.astype(b16)
    pre_act = jnp.einsum("ind,df->inf", normed_two, up_full, preferred_element_type=f32)
    act_low = gelu_tanh(pre_act).astype(b16)
    result = middle + jnp.einsum("inf,fd->ind", act_low, down_full, preferred_element_type=f32)
    block_out = result.astype(b16)[None]
    qkv_back, out_back, up_back, down_back = gathered
    grad_top = out_grad[0]
    grad_down = jnp.einsum("inf,ind->fd", act_low, grad_top, preferred_element_type=f32)
    grad_act = jnp.einsum("ind,fd->inf", grad_top, down_back, preferred_element_type=f32)
    grad_pre = (grad_act * gelu_slope(pre_act)).astype(b16)
    grad_up = jnp.einsum("ind,inf->df", normed_two, grad_pre, preferred_element_type=f32)
    grad_normed_two = jnp.einsum("inf,df->ind", grad_pre, up_back, preferred_element_type=f32)
    grad_gain_two = jnp.sum(grad_normed_two * unit_two, axis=(0, 1))
    grad_middle = grad_top.astype(f32) + norm_back(grad_normed_two, gain_two, unit_two, inverse_two)
    grad_branch = grad_middle.astype(b16)
    grad_out_proj = jnp.einsum("ind,ine->de", mixed_low, grad_branch, preferred_element_type=f32)
    grad_mixed = (
        jnp.einsum("ine,de->ind", grad_branch, out_back, preferred_element_type=f32)
        .astype(b16)
        .reshape(images, tokens, HEADS, HEAD_DIM)
    )
    grad_values = jnp.einsum("ihnm,inhc->imhc", probs_low, grad_mixed, preferred_element_type=f32)
    grad_probs = jnp.einsum("inhc,imhc->ihnm", grad_mixed, value_rows, preferred_element_type=f32)
    grad_scores = (
        probs_full * (grad_probs - jnp.sum(grad_probs * probs_full, axis=-1, keepdims=True))
    ).astype(b16)
    grad_queries = (
        jnp.einsum("ihnm,imhc->inhc", grad_scores, key_rows, preferred_element_type=f32)
        * score_scale
    )
    grad_keys = (
        jnp.einsum("ihnm,inhc->imhc", grad_scores, queries, preferred_element_type=f32)
        * score_scale
    )
    grad_joint = jnp.concatenate(
        [
            grad_queries.reshape(images, tokens, model_width),
            grad_keys.reshape(images, tokens, model_width),
            grad_values.reshape(images, tokens, model_width),
        ],
        axis=-1,
    ).astype(b16)
    grad_qkv = jnp.einsum("ind,ine->de", normed_one, grad_joint, preferred_element_type=f32)
    grad_normed_one = jnp.einsum("ine,de->ind", grad_joint, qkv_back, preferred_element_type=f32)
    grad_gain_one = jnp.sum(grad_normed_one * unit_one, axis=(0, 1))
    grad_embed = grad_middle + norm_back(grad_normed_one, gain_one, unit_one, inverse_one)
    grad_embed_low = grad_embed.astype(b16)[None]
    grad_rows = lax.all_gather(grad_embed_low, "band", axis=1, tiled=True)[0].astype(f32)
    weight_rows = band_weight
    pixel_rows = pixel_local
    scaled = grad_rows[:, :, None, :] * weight_rows[:, None, :, None]
    bias_total = jnp.sum(scaled, axis=(0, 1))
    scaled_low = scaled.astype(b16)
    kernel_total = jnp.einsum("inbp,inbd->bpd", pixel_rows, scaled_low, preferred_element_type=f32)
    pixel_part = jnp.einsum(
        "inbd,bpd->inbp", scaled_low, kernels, preferred_element_type=f32
    ).astype(b16)
    pixel_total = pixel_part
    kernel_grad, bias_grad, pixel_total = (kernel_total, bias_total, pixel_total)
    pixel_out = pixel_total[None]
    kernel_grad_low = lax.psum(kernel_grad.astype(b16), "dp").reshape(band_local, -1)
    grad_columns = lax.all_to_all(kernel_grad_low, "band", split_axis=1, concat_axis=0, tiled=True)
    grad_kernel_part = jnp.einsum("nh,nc->hc", code_low, grad_columns, preferred_element_type=f32)
    grad_code_part = jnp.einsum("nc,hc->nh", grad_columns, kernel_gen, preferred_element_type=f32)
    bias_back = jnp.einsum("bd,hd->bh", bias_grad, bias_gen.astype(f32), precision=PRECISE)
    grad_code_part = 0.5 * grad_code_part + lax.dynamic_update_slice_in_dim(
        jnp.zeros_like(grad_code_part), bias_back, first_band, 0
    )
    grad_bias_part = jnp.einsum("bh,bd->hd", own_code.astype(f32), bias_grad, precision=PRECISE)
    grad_code, grad_bias_gen, grad_norm_gain1, grad_norm_gain2 = lax.psum(
        (grad_code_part, grad_bias_part, grad_gain_one, grad_gain_two), ("band", "dp")
    )
    grad_kernel_gen = grad_kernel_part
    hyper_grads = hyper_pull(grad_code)
    shares = (
        lax.psum_scatter(grad_qkv.astype(b16), ("band", "dp"), scatter_dimension=0, tiled=True),
        lax.psum_scatter(grad_out_proj.astype(b16), ("band", "dp"), scatter_dimension=0, tiled=True),
        lax.psum_scatter(grad_up.astype(b16), ("band", "dp"), scatter_dimension=0, tiled=True),
        lax.psum_scatter(grad_down.astype(b16), ("band", "dp"), scatter_dimension=0, tiled=True),
    )
    shares = tuple(share.astype(f32) for share in shares)
    return (
        block_out,
        pixel_out,
        hyper_grads[0],
        hyper_grads[1],
        hyper_grads[2],
        hyper_grads[3],
        hyper_grads[4],
        hyper_grads[5],
        grad_kernel_gen,
        grad_bias_gen,
        grad_norm_gain1,
        shares[0],
        shares[1],
        grad_norm_gain2,
        shares[2],
        shares[3],
    )


def solution(mesh):
    placed = (
        P("dp", None, None, "band", None),
        P(),
        P("dp", None),
        P("dp", None, "band"),
        P(),
        P(),
        P(),
        P(),
        P(),
        P(),
        P(None, "band"),
        P(),
        P(),
        P(("band", "dp"), None),
        P(("band", "dp"), None),
        P(),
        P(("band", "dp"), None),
        P(("band", "dp"), None),
        P("dp", "band", None, None),
    )
    return jax.shard_map(
        body,
        mesh=mesh,
        in_specs=placed,
        out_specs=(
            P("dp", "band", None, None),
            P("dp", None, None, "band", None),
            P(),
            P(),
            P(),
            P(),
            P(),
            P(),
            P(None, "band"),
            P(),
            P(),
            P(("band", "dp"), None),
            P(("band", "dp"), None),
            P(),
            P(("band", "dp"), None),
            P(("band", "dp"), None),
        ),
        check_vma=False,
    )
```

```python
import functools
import math

import jax
import jax.numpy as jnp
from jax import lax
from jax.experimental import pallas as pl
from jax.experimental.pallas import tpu as pltpu
from jax.sharding import PartitionSpec as P

HEADS = 12
HEAD_DIM = 64
HW = 128
HHEADS = 4


PRECISE = lax.Precision.HIGHEST
EPS_BLOCK = 1e-06
EPS_HYPER = 1e-05
GELU_COEF = 0.7978845608028654


def gelu_tanh(tensor):
    return (
        0.5 * tensor * (1.0 + jnp.tanh(GELU_COEF * (tensor + 0.044715 * tensor * tensor * tensor)))
    )


def gelu_slope(tensor):
    tanh_val = jnp.tanh(GELU_COEF * (tensor + 0.044715 * tensor * tensor * tensor))
    return 0.5 * (1.0 + tanh_val) + 0.5 * tensor * (1.0 - tanh_val * tanh_val) * GELU_COEF * (
        1.0 + 3.0 * 0.044715 * tensor * tensor
    )


def layer_norm(tensor, gain_vec, epsilon):
    centred = tensor - jnp.mean(tensor, axis=-1, keepdims=True)
    return (
        centred
        * lax.rsqrt(jnp.mean(centred * centred, axis=-1, keepdims=True) + epsilon)
        * gain_vec
    )


def norm_parts(tensor, gain_vec):
    centred = tensor - jnp.mean(tensor, axis=-1, keepdims=True)
    inverse = lax.rsqrt(jnp.mean(centred * centred, axis=-1, keepdims=True) + EPS_BLOCK)
    unit_rows = centred * inverse
    return (unit_rows * gain_vec, unit_rows, inverse)


def norm_back(grad_rows, gain_vec, unit_rows, inverse):
    scaled = grad_rows * gain_vec
    return inverse * (
        scaled
        - jnp.mean(scaled, axis=-1, keepdims=True)
        - unit_rows * jnp.mean(scaled * unit_rows, axis=-1, keepdims=True)
    )


def wave_embed(wave_ints, token_width):
    half_width = token_width // 2
    frequency = jnp.power(10000.0, -jnp.arange(half_width, dtype=jnp.float32) / half_width)
    angles = wave_ints.astype(jnp.float32)[:, None] * frequency[None, :]
    return jnp.concatenate([jnp.sin(angles), jnp.cos(angles)], axis=1)


def hyper_net(wave_tokens, qkv_weight, out_weight, gain_one, up_weight, down_weight, gain_two):
    tokens, token_width = wave_tokens.shape
    head_size = token_width // HHEADS
    qkv_rows = jnp.dot(wave_tokens, qkv_weight, precision=PRECISE)
    queries = qkv_rows[:, :token_width].reshape(tokens, HHEADS, head_size)
    key_rows = qkv_rows[:, token_width : 2 * token_width].reshape(tokens, HHEADS, head_size)
    value_rows = qkv_rows[:, 2 * token_width :].reshape(tokens, HHEADS, head_size)
    scores = jnp.einsum("nhc,mhc->hnm", queries, key_rows, precision=PRECISE) / math.sqrt(head_size)
    weights_soft = jax.nn.softmax(scores, axis=-1)
    mixed_rows = jnp.einsum("hnm,mhc->nhc", weights_soft, value_rows, precision=PRECISE).reshape(
        tokens, token_width
    )
    first_norm = layer_norm(
        wave_tokens + jnp.dot(mixed_rows, out_weight, precision=PRECISE), gain_one, EPS_HYPER
    )
    inner_act = gelu_tanh(jnp.dot(first_norm, up_weight, precision=PRECISE))
    return layer_norm(
        first_norm + jnp.dot(inner_act, down_weight, precision=PRECISE), gain_two, EPS_HYPER
    )


MESH = pl.DeviceIdType.MESH
B16 = jnp.bfloat16
F32 = jnp.float32
CHUNK = 48
PART = 96
ORDERS = ("zxy", "xzy", "yzx", "zyx", "xzy", "yzx")


def place():
    band = lax.axis_index("band")
    return (band // 4, (band // 2) % 2, band % 2, lax.axis_index("dp"))


def device(z, x, core, y):
    return (z * 4 + x * 2 + core, y)


def slot(z, x, core, y):
    return (z * 4 + x * 2 + core) * 2 + y


def when(cond, run):
    if cond is True:
        run()
    else:
        pl.when(cond)(run)


def both(first, second):
    return second if first is True else first & second


def aligned(rows):
    return pl.multiple_of(rows, 16)


def meet_neighbours():
    z, x, core, y = place()
    barrier = pltpu.get_barrier_semaphore()
    near = [
        (device(z, x, 1 - core, y), True),
        (device(z, 1 - x, core, y), True),
        (device(z, x, core, 1 - y), True),
        (device(z + 1, x, core, y), z < 3),
        (device(z - 1, x, core, y), z > 0),
    ]
    for target, cond in near:
        when(
            cond,
            lambda target=target: pl.semaphore_signal(
                barrier, inc=1, device_id=target, device_id_type=MESH
            ),
        )
    pl.semaphore_wait(barrier, 5 - z // 3 - (3 - z) // 3)


class Gather:
    def __init__(self, view, orders, send_sem, recv_sem, pair_send, pair_recv):
        self.view, self.orders = view, orders
        self.send_sem, self.recv_sem = send_sem, recv_sem
        self.pair_send, self.pair_recv = pair_send, pair_recv
        self.z, self.x, self.core, self.y = place()
        self.sends = []
        self.count = [0] * len(orders)

    def send(self, chunk, block, dim, cond, direction=0):
        z, x, core, y = self.z, self.x, self.core, self.y
        if dim == "x":
            targets = [(device(z, 1 - x, core, y), cond)]
        elif dim == "y":
            targets = [(device(z, x, core, 1 - y), cond)]
        else:
            targets = []
            if direction >= 0:
                targets.append((device(z + 1, x, core, y), both(cond, z < 3)))
            if direction <= 0:
                targets.append((device(z - 1, x, core, y), both(cond, z > 0)))
        src = self.view(chunk, slot(block[0], block[1], core, block[2]))
        rail = block[0] * 4 + block[1] * 2 + block[2]
        for target, needed in targets:
            copy = pltpu.make_async_remote_copy(
                src_ref=src,
                dst_ref=src,
                send_sem=self.send_sem.at[chunk, self.count[chunk]],
                recv_sem=self.recv_sem.at[chunk, rail],
                device_id=target,
                device_id_type=MESH,
            )
            self.count[chunk] += 1
            when(needed, copy.start)
            self.sends.append((needed, copy))

    def pair(self, chunk, block, core):
        src = self.view(chunk, slot(block[0], block[1], core, block[2]))
        rail = block[0] * 4 + block[1] * 2 + block[2]
        return pltpu.make_async_remote_copy(
            src_ref=src,
            dst_ref=src,
            send_sem=self.pair_send.at[chunk, rail],
            recv_sem=self.pair_recv.at[chunk, rail],
            device_id=device(self.z, self.x, 1 - self.core, self.y),
            device_id_type=MESH,
        )

    def start(self, chunk):
        own = (self.z, self.x, self.y)
        for dim in self.orders[chunk]:
            self.send(chunk, own, dim, True)
        self.pair(chunk, own, self.core).start()

    def events(self, chunk):
        held, found = [(0, 0, 0, 0, 0.0)], []
        for dim in self.orders[chunk]:
            clock, new = 0.0, []
            ordered = sorted(held, key=lambda item: item[4])
            if dim == "z":
                for dist in (1, 2, 3):
                    for item in ordered:
                        clock = max(clock, item[4]) + 1.0
                        new += [(dist, way, item[2], item[3], clock) for way in (1, -1)]
            else:
                for item in ordered:
                    clock = max(clock, item[4]) + 1.0
                    flip = (1, item[3]) if dim == "x" else (item[2], 1)
                    new.append((item[0], item[1], *flip, clock))
            found += [
                (item[4], chunk, functools.partial(self.arrive, chunk, dim, item)) for item in new
            ]
            held = held + new
        return found

    def arrive(self, chunk, dim, item):
        dist, way, flip_x, flip_y, _ = item
        cond = True
        if way == 1:
            cond = self.z >= dist
        elif way == -1:
            cond = self.z + dist <= 3
        block = (
            self.z - dist * way,
            1 - self.x if flip_x else self.x,
            1 - self.y if flip_y else self.y,
        )
        src = self.view(chunk, slot(block[0], block[1], self.core, block[2]))
        rail = block[0] * 4 + block[1] * 2 + block[2]
        arriving = pltpu.make_async_remote_copy(
            src_ref=src,
            dst_ref=src,
            send_sem=self.send_sem.at[chunk, 0],
            recv_sem=self.recv_sem.at[chunk, rail],
            device_id=device(self.z, self.x, 1 - self.core, self.y),
            device_id_type=MESH,
        )
        when(cond, arriving.wait_recv)
        if dim == "z":
            self.send(chunk, block, "z", cond, way)
        order = self.orders[chunk]
        for later in order[order.index(dim) + 1 :]:
            self.send(chunk, block, later, cond)
        when(cond, self.pair(chunk, block, self.core).start)

    def finish(self):
        for needed, copy in self.sends:
            when(needed, copy.wait_send)
        for chunk in range(len(self.orders)):
            for rail in range(16):
                block = (rail // 4, (rail // 2) % 2, rail % 2)
                self.pair(chunk, block, self.core).wait_send()
                self.pair(chunk, block, 1 - self.core).wait_recv()


class Reduce:
    def __init__(self, view, orders, pair_view, pair_buf, buf, pair_send, pair_recv, send, recv):
        self.view, self.orders = view, tuple(order[::-1] for order in orders)
        self.pair_view, self.pair_buf, self.buf = pair_view, pair_buf, buf
        self.pair_send, self.pair_recv = pair_send, pair_recv
        self.send_sem, self.recv_sem = send, recv
        self.z, self.x, self.core, self.y = place()
        self.sends = []
        self.count = [0] * len(orders)
        self.index = [{} for _ in orders]

    def coords(self, block):
        zz, flip_x, flip_y = block
        return (zz, 1 - self.x if flip_x else self.x, 1 - self.y if flip_y else self.y)

    def own(self, chunk, block):
        zz, xx, yy = self.coords(block)
        return self.view(chunk, slot(zz, xx, self.core, yy))

    def add(self, target, source):
        target[...] = target[...] + source[...]

    def pair_copy(self, part, rail):
        block = (rail // 4, (rail // 2) % 2, rail % 2)
        return pltpu.make_async_remote_copy(
            src_ref=self.pair_view(part, slot(block[0], block[1], 1 - self.core, block[2])),
            dst_ref=self.pair_buf.at[part, rail],
            send_sem=self.pair_send.at[part, rail],
            recv_sem=self.pair_recv.at[part, rail],
            device_id=device(self.z, self.x, 1 - self.core, self.y),
            device_id_type=MESH,
        )

    def place_of(self, chunk, key):
        return self.index[chunk].setdefault(key, len(self.index[chunk]))

    def copy(self, chunk, block, key, target):
        where = self.place_of(chunk, key)
        number = self.count[chunk]
        self.count[chunk] += 1
        return pltpu.make_async_remote_copy(
            src_ref=self.own(chunk, block),
            dst_ref=self.buf.at[chunk, where],
            send_sem=self.send_sem.at[chunk, number],
            recv_sem=self.recv_sem.at[chunk, where],
            device_id=target,
            device_id_type=MESH,
        )

    def send(self, chunk, block, key, target, cond):
        copy = self.copy(chunk, block, key, target)
        when(cond, copy.start)
        self.sends.append((cond, copy))

    def wait_add(self, chunk, block, key):
        where = self.place_of(chunk, key)
        landed = self.buf.at[chunk, where]
        pltpu.make_async_remote_copy(
            src_ref=landed,
            dst_ref=landed,
            send_sem=self.send_sem.at[chunk, 0],
            recv_sem=self.recv_sem.at[chunk, where],
            device_id=device(self.z, self.x, 1 - self.core, self.y),
            device_id_type=MESH,
        ).wait_recv()
        self.add(self.own(chunk, block), landed)

    def flips(self, chunk, stage):
        left = self.orders[chunk][stage:]
        out = [(fx, fy) for fx in ((1, 0) if "x" in left else (0,)) for fy in ((1, 0) if "y" in left else (0,))]
        return out

    def pair_order(self, part):
        return [8 * h + r for h in (0, 1) for r in range(8)]

    def ready(self, chunk, stage, block, cond=True):
        order = self.orders[chunk]
        if stage == 3:
            return
        dim = order[stage]
        zz, fx, fy = block
        if dim == "x" and fx:
            target = device(self.z, 1 - self.x, self.core, self.y)
            self.send(chunk, block, (stage, zz if "z" in order[stage:] else "own", 0, fy), target, cond)
        elif dim == "y" and fy:
            target = device(self.z, self.x, self.core, 1 - self.y)
            self.send(chunk, block, (stage, zz if "z" in order[stage:] else "own", fx, 0), target, cond)

    def z_start(self, chunk, stage, step, flips):
        up, down = (3 - step, *flips), (step, *flips)
        self.send(chunk, up, (stage, step, 1, *flips), device(self.z + 1, self.x, self.core, self.y), self.z == 0)
        self.send(chunk, down, (stage, step, -1, *flips), device(self.z - 1, self.x, self.core, self.y), self.z == 3)

    def z_arrive(self, chunk, stage, step, flips, way):
        z = self.z if way == 1 else 3 - self.z
        cond = (z >= 1) & (z <= step + 1)
        zz = 2 + z - step
        zz = zz if way == 1 else 3 - zz
        block = (zz, *flips)
        key = (stage, step, way, *flips)
        when(cond, lambda: self.wait_add(chunk, block, key))
        if step < 2:
            self.send(
                chunk, block, (stage, step + 1, way, *flips),
                device(self.z + way, self.x, self.core, self.y), cond,
            )

    def z_done(self, chunk, stage, flips):
        self.ready(chunk, stage + 1, (self.z, *flips))

    def xy_arrive(self, chunk, stage, zz, fx, fy):
        key = (stage, zz, fx, fy)
        block = (self.z if zz == "own" else zz, fx, fy)
        self.wait_add(chunk, block, key)
        self.ready(chunk, stage + 1, block)

    def pair_arrive(self, part, block, chunks):
        zz, xx, yy = self.coords(block)
        rail = zz * 4 + xx * 2 + yy
        copy = pltpu.make_async_remote_copy(
            src_ref=self.pair_buf.at[part, rail],
            dst_ref=self.pair_buf.at[part, rail],
            send_sem=self.pair_send.at[part, rail],
            recv_sem=self.pair_recv.at[part, rail],
            device_id=device(self.z, self.x, 1 - self.core, self.y),
            device_id_type=MESH,
        )
        copy.wait_recv()
        self.add(self.pair_view(part, slot(zz, xx, self.core, yy)), self.pair_buf.at[part, rail])
        for chunk in chunks:
            self.ready(chunk, 0, block)

    def events(self, part, chunks):
        found, ready = [], {}
        number = 0
        clock = 0.0
        for fx, fy in ((1, 1), (1, 0), (0, 1), (0, 0)):
            for zz in (3, 0, 2, 1):
                clock += 0.5
                found.append((clock, 0, functools.partial(self.pair_arrive, part, (zz, fx, fy), chunks)))
                ready[(zz, fx, fy)] = clock
        for chunk in chunks:
            times = dict(ready)
            order = self.orders[chunk]
            for stage, dim in enumerate(order):
                clock = 0.0
                nxt = {}
                flips = self.flips(chunk, stage)
                if dim == "z":
                    for step in range(3):
                        for fl in flips:
                            needed = (0, 3) if step == 0 else (0, 1, 2, 3)
                            clock = max(clock, *(times[(zz, *fl)] for zz in needed)) + 0.001
                            found.append((clock, chunk, functools.partial(self.z_start, chunk, stage, step, fl)))
                            clock += 1.0
                            for way in (1, -1):
                                found.append((clock, chunk, functools.partial(self.z_arrive, chunk, stage, step, fl, way)))
                            nxt[("own", *fl)] = clock + 0.001
                    for fl in flips:
                        found.append((nxt[("own", *fl)], chunk, functools.partial(self.z_done, chunk, stage, fl)))
                else:
                    pick = 0 if dim == "x" else 1
                    sent = [key for key in times if key[1 + pick] == 1]
                    kept = {}
                    for key in sorted(sent, key=lambda key: times[key]):
                        clock = max(clock, times[key]) + 1.0
                        mine = (key[0], 0, key[2]) if dim == "x" else (key[0], key[1], 0)
                        clock = max(clock, times[mine] + 0.001)
                        kept[mine] = clock
                        found.append((clock, chunk, functools.partial(self.xy_arrive, chunk, stage, *mine)))
                    nxt = kept
                times = nxt
        return sorted(found, key=lambda event: event[:2])

    def finish(self):
        for cond, copy in self.sends:
            when(cond, copy.wait_send)
        for part in range(self.pair_buf.shape[0]):
            for rail in range(16):
                self.pair_copy(part, rail).wait_send()


def dot_nt(left, right):
    return lax.dot_general(left, right, (((1,), (1,)), ((), ())), preferred_element_type=F32)


def dot_tn(left, right):
    return lax.dot_general(left, right, (((0,), (0,)), ((), ())), preferred_element_type=F32)


def dot_nn(left, right):
    return jnp.dot(left, right, preferred_element_type=F32)


def unit_parts(rows):
    centred = rows - jnp.mean(rows, axis=-1, keepdims=True)
    inverse = lax.rsqrt(jnp.mean(centred * centred, axis=-1, keepdims=True) + EPS_BLOCK)
    return centred * inverse, inverse


class Block:
    def __init__(self, weights, down, refs):
        self.weights, self.down = weights, down
        self.__dict__.update(refs)
        self.width = weights.shape[1]
        self.halves = weights.shape[1] // (2 * HEAD_DIM)

    def masks(self):
        tokens = self.joint.shape[1]
        lane = lax.broadcasted_iota(jnp.int32, (tokens, 2 * HEAD_DIM), 1)
        low = lane < HEAD_DIM
        return low, low.astype(F32).astype(B16), (~low).astype(F32).astype(B16)

    def pair_rows(self, rows, low, high):
        return jnp.concatenate([rows * low, rows * high], axis=0)

    def project(self):
        unit, inverse = unit_parts(self.residual[...])
        normed = (unit * self.gain_one[...]).astype(B16)
        self.normed_one[...] = normed
        self.unit_one[...] = unit
        self.inverse_one[...] = jnp.broadcast_to(inverse, self.inverse_one.shape)

        @pl.loop(0, 3)
        def _(part):
            self.joint[part] = dot_nn(self.normed_one[...], self.weights[part]).astype(B16)

    def attend(self):
        tokens = self.joint.shape[1]
        scale = 1.0 / math.sqrt(HEAD_DIM)

        @pl.loop(0, self.halves)
        def _(pair):
            where, low, high = self.masks()
            lanes = pl.ds(pl.multiple_of(pair * 2 * HEAD_DIM, 2 * HEAD_DIM), 2 * HEAD_DIM)
            query, key, value = (self.joint[part, :, lanes] for part in range(3))
            scores = dot_nt(self.pair_rows(query, low, high), key) * scale
            raised = jnp.exp(scores - jnp.max(scores, axis=-1, keepdims=True))
            probs = raised / jnp.sum(raised, axis=-1, keepdims=True)
            self.probs[pair] = probs
            mixed = dot_nn(probs.astype(B16), value)
            self.mixed[:, lanes] = jnp.where(where, mixed[:tokens], mixed[tokens:]).astype(B16)

    def widen(self):
        middle = self.residual[...] + dot_nn(self.mixed[...], self.weights[3])
        unit, inverse = unit_parts(middle)
        self.normed_two[...] = (unit * self.gain_two[...]).astype(B16)
        self.unit_two[...] = unit
        self.inverse_two[...] = jnp.broadcast_to(inverse, self.inverse_two.shape)
        self.result[...] = middle

        @pl.loop(0, 4)
        def _(part):
            pre = dot_nn(self.normed_two[...], self.weights[4 + part])
            self.pre_act[part] = pre
            self.act[part] = gelu_tanh(pre).astype(B16)

    def narrow(self):
        @pl.loop(0, 4)
        def _(part):
            rows = pl.ds(aligned(part * self.width), self.width)
            self.result[...] += dot_nn(self.act[part], self.down[rows, :])

        self.block_out[...] = self.result[...].astype(B16)

    def back_narrow(self, part):
        rows = pl.ds(aligned(part * self.width), self.width)
        grad_act = dot_nt(self.out_grad[...], self.down[rows, :])
        grad_pre = (grad_act * gelu_slope(self.pre_act[part])).astype(B16)
        self.grad_pre[part] = grad_pre
        self.grad_normed[...] += dot_nt(grad_pre, self.weights[4 + part])

    def down_grad(self, part, store):
        turned = self.act[part].T
        for at in range(0, self.width, 256):
            store[pl.ds(aligned(part * self.width), self.width), at : at + 256] = dot_nn(
                turned, self.out_grad[:, at : at + 256]
            ).astype(B16)

    def pair_grad(self, first, second, first_grad, second_grad, store, offset):
        @pl.loop(0, 4)
        def _(group):
            rows = pl.ds(aligned(group * 192), 192)
            for at in range(0, self.width, 256):
                cols = slice(at, at + 256)
                one = dot_nn(first[rows, :], first_grad(cols))
                two = dot_nn(second[rows, :], second_grad(cols))
                for owner in range(8):
                    piece = jnp.concatenate(
                        [one[owner * 24 : owner * 24 + 24], two[owner * 24 : owner * 24 + 24]], axis=0
                    )
                    target = aligned((group * 8 + owner) * PART + offset)
                    store[pl.ds(target, CHUNK), cols] = piece.astype(B16)

    def back_wide(self):
        grad_normed = self.grad_normed[...]
        unit = self.unit_two[...]
        self.gain_grads[1:2, :] = jnp.sum(grad_normed * unit, axis=0, keepdims=True)
        scaled = grad_normed * self.gain_two[...]
        back = self.inverse_two[:, :1] * (
            scaled
            - jnp.mean(scaled, axis=-1, keepdims=True)
            - unit * jnp.mean(scaled * unit, axis=-1, keepdims=True)
        )
        grad_middle = self.out_grad[...].astype(F32) + back
        self.grad_middle[...] = grad_middle
        branch = grad_middle.astype(B16)
        self.grad_branch[...] = branch
        self.grad_mixed[...] = dot_nt(branch, self.weights[3]).astype(B16)
        self.turned_mixed[...] = self.mixed[...].T

    def back_attend(self):
        tokens = self.joint.shape[1]
        scale = 1.0 / math.sqrt(HEAD_DIM)

        @pl.loop(0, self.halves)
        def _(pair):
            where, low, high = self.masks()
            lanes = pl.ds(pl.multiple_of(pair * 2 * HEAD_DIM, 2 * HEAD_DIM), 2 * HEAD_DIM)
            query, key, value = (self.joint[part, :, lanes] for part in range(3))
            grads = self.pair_rows(self.grad_mixed[:, lanes], low, high)
            probs = self.probs[pair]
            self.grad_joint[2, :, lanes] = dot_tn(probs.astype(B16), grads).astype(B16)
            grad_probs = dot_nt(grads, value)
            total = jnp.sum(grad_probs * probs, axis=-1, keepdims=True)
            grad_scores = (probs * (grad_probs - total)).astype(B16)
            queries = dot_nn(grad_scores, key) * scale
            self.grad_joint[0, :, lanes] = jnp.where(
                where, queries[:tokens], queries[tokens:]
            ).astype(B16)
            keys = dot_tn(grad_scores, self.pair_rows(query, low, high)) * scale
            self.grad_joint[1, :, lanes] = keys.astype(B16)

    def back_project(self):
        self.grad_normed[...] = jnp.zeros(self.grad_normed.shape, F32)

        @pl.loop(0, 3)
        def _(part):
            self.grad_normed[...] += dot_nt(self.grad_joint[part], self.weights[part])

        grad_normed = self.grad_normed[...]
        unit = self.unit_one[...]
        self.gain_grads[0:1, :] = jnp.sum(grad_normed * unit, axis=0, keepdims=True)
        scaled = grad_normed * self.gain_one[...]
        back = self.inverse_one[:, :1] * (
            scaled
            - jnp.mean(scaled, axis=-1, keepdims=True)
            - unit * jnp.mean(scaled * unit, axis=-1, keepdims=True)
        )
        self.grad_embed[...] = (self.grad_middle[...] + back).astype(B16)


def spread(gathered, weights, chunk):
    part, offset = chunk // 2, (chunk % 2) * CHUNK

    @pl.loop(0, 16)
    def _(two):
        one, other = (
            gathered[part, pl.ds(aligned((two * 2 + k) * PART + offset), CHUNK), :].astype(F32)
            for k in (0, 1)
        )
        rows = pl.ds(aligned(two * CHUNK), CHUNK)
        half = CHUNK // 2
        weights[2 * chunk, rows, :] = jnp.concatenate([one[:half], other[:half]], 0).astype(B16)
        weights[2 * chunk + 1, rows, :] = jnp.concatenate([one[half:], other[half:]], 0).astype(B16)


def middle_kernel(shard, residual, out_grad, gain_one, gain_two, block_out, grad_embed, shares, gain_grads, *scratch):
    (gathered, weights, down_grads, pair_buf, buf, joint, probs, pre_act, act, grad_pre, mixed, normed_one, normed_two,
     unit_one, unit_two, inverse_one, inverse_two, result, grad_normed, grad_middle, grad_branch, grad_mixed, grad_joint,
     turned_mixed, turned_one, turned_two, local_sem, *sems) = scratch
    names = dict(
        residual=residual, out_grad=out_grad, gain_one=gain_one, gain_two=gain_two, block_out=block_out,
        grad_embed=grad_embed, gain_grads=gain_grads, joint=joint, probs=probs, pre_act=pre_act, act=act,
        grad_pre=grad_pre, mixed=mixed, normed_one=normed_one, normed_two=normed_two, unit_one=unit_one,
        unit_two=unit_two, inverse_one=inverse_one, inverse_two=inverse_two, result=result, grad_normed=grad_normed,
        grad_middle=grad_middle, grad_branch=grad_branch, grad_mixed=grad_mixed, grad_joint=grad_joint,
        turned_mixed=turned_mixed,
    )
    me = slot(*place())
    own = [
        pltpu.make_async_copy(
            shard.at[pl.ds(part * PART, PART)],
            gathered.at[part, pl.ds(aligned(me * PART), PART)],
            local_sem.at[part],
        )
        for part in range(3)
    ]
    for copy in own:
        copy.start()
    for copy in own:
        copy.wait()
    meet_neighbours()

    def weight_view(chunk, where):
        return gathered.at[chunk // 2, pl.ds(aligned(where * PART + (chunk % 2) * CHUNK), CHUNK)]

    gather = Gather(weight_view, ORDERS, *sems[:4])
    events = []
    for chunk in range(len(ORDERS)):
        gather.start(chunk)
        events += gather.events(chunk)
    for _, _, run in sorted(events, key=lambda event: event[:2]):
        run()
    gather.finish()
    for chunk in range(4):
        spread(gathered, weights, chunk)

    block = Block(weights, gathered.at[2], names)
    block.project()
    block.attend()
    block.widen()
    block.narrow()

    def part_ref(part):
        return down_grads if part == 2 else gathered.at[part]

    def grad_view(chunk, where):
        return part_ref(chunk // 2).at[pl.ds(aligned(where * PART + (chunk % 2) * CHUNK), CHUNK)]

    def part_view(part, where):
        return part_ref(part).at[pl.ds(aligned(where * PART), PART)]

    reduce = Reduce(grad_view, ORDERS, part_view, pair_buf, buf, *sems[4:])
    grad_normed[...] = jnp.zeros(grad_normed.shape, F32)

    @pl.loop(0, 4)
    def _(part):
        block.back_narrow(part)
        block.down_grad(part, down_grads)

    for rail in range(16):
        reduce.pair_copy(2, rail).start()
    turned_two[...] = normed_two[...].T
    for part in (0, 2):
        block.pair_grad(
            turned_two, turned_two, lambda cols, part=part: grad_pre[part, :, cols],
            lambda cols, part=part: grad_pre[part + 1, :, cols], part_ref(1), part // 2 * CHUNK,
        )
    for rail in range(16):
        reduce.pair_copy(1, rail).start()
    block.back_wide()
    block.back_attend()
    turned_one[...] = normed_one[...].T
    block.pair_grad(
        turned_one, turned_one, lambda cols: grad_joint[0, :, cols], lambda cols: grad_joint[1, :, cols], part_ref(0), 0
    )
    block.pair_grad(
        turned_one, turned_mixed, lambda cols: grad_joint[2, :, cols], lambda cols: grad_branch[:, cols], part_ref(0), CHUNK
    )
    for rail in range(16):
        reduce.pair_copy(0, rail).start()
    block.back_project()
    events = []
    for part, chunks in ((2, (4, 5)), (1, (2, 3)), (0, (0, 1))):
        events += reduce.events(part, chunks)
    for _, _, run in sorted(events, key=lambda event: event[:2]):
        run()
    for part in range(3):
        shares[part * PART : (part + 1) * PART, :] = part_view(part, me)[...].astype(F32)
    reduce.finish()


def middle(attn_qkv, attn_out, mlp_up, mlp_down, residual, out_grad, gain_one, gain_two):
    width = attn_out.shape[1]
    devices = lax.axis_size("band") * lax.axis_size("dp")
    tokens = residual.shape[0]

    def stack(weight):
        parts = weight.shape[1] // width
        return weight.reshape(weight.shape[0], parts, width).transpose(1, 0, 2).reshape(-1, width)

    shard = jnp.concatenate([stack(w) for w in (attn_qkv, attn_out, mlp_up, mlp_down)], axis=0)
    chunks = len(ORDERS)
    vmem = pl.BlockSpec(memory_space=pltpu.VMEM)
    rows = lambda kind, *lead: pltpu.VMEM((*lead, tokens, width), kind)
    dma = pltpu.SemaphoreType.DMA
    outs = pl.pallas_call(
        middle_kernel,
        out_shape=[
            jax.ShapeDtypeStruct((tokens, width), B16),
            jax.ShapeDtypeStruct((tokens, width), B16),
            jax.ShapeDtypeStruct((3 * PART, width), F32),
            jax.ShapeDtypeStruct((2, width), F32),
        ],
        in_specs=[pl.BlockSpec(memory_space=pl.ANY)] + [vmem] * 4,
        out_specs=[vmem] * 4,
        scratch_shapes=[
            pltpu.VMEM((3, devices * PART, width), B16),
            pltpu.VMEM((8, width, width), B16),
            pltpu.VMEM((devices * PART, width), B16),
            pltpu.VMEM((3, 16, PART, width), B16),
            pltpu.VMEM((chunks, 21, CHUNK, width), B16),
            rows(B16, 3),
            pltpu.VMEM((HEADS // 2, 2 * tokens, tokens), F32),
            rows(F32, 4),
            rows(B16, 4),
            rows(B16, 4),
            rows(B16),
            rows(B16),
            rows(B16),
            rows(F32),
            rows(F32),
            pltpu.VMEM((tokens, 128), F32),
            pltpu.VMEM((tokens, 128), F32),
            rows(F32),
            rows(F32),
            rows(F32),
            rows(B16),
            rows(B16),
            rows(B16, 3),
            pltpu.VMEM((width, tokens), B16),
            pltpu.VMEM((width, tokens), B16),
            pltpu.VMEM((width, tokens), B16),
            dma((3,)),
            dma((chunks, 40)),
            dma((chunks, 16)),
            dma((chunks, 16)),
            dma((chunks, 16)),
            dma((3, 16)),
            dma((3, 16)),
            dma((chunks, 48)),
            dma((chunks, 24)),
        ],
        compiler_params=pltpu.CompilerParams(
            collective_id=0, has_side_effects=True, vmem_limit_bytes=62 * 2**20
        ),
        name="gather_block_reduce",
    )(shard, residual, out_grad, gain_one, gain_two)
    block_out, grad_embed, shares, gain_grads = outs
    grads, at = [], 0
    for weight in (attn_qkv, attn_out, mlp_up, mlp_down):
        own_rows, parts = weight.shape[0], weight.shape[1] // width
        piece = shares[at : at + own_rows * parts].reshape(parts, own_rows, width)
        grads.append(piece.transpose(1, 0, 2).reshape(own_rows, parts * width))
        at += own_rows * parts
    return block_out, grad_embed, grads, gain_grads


def body(
    pixels,
    wavelengths,
    band_counts,
    band_mask,
    hyper_qkv,
    hyper_out,
    hyper_gain1,
    hyper_up,
    hyper_down,
    hyper_gain2,
    kernel_gen,
    bias_gen,
    norm_gain1,
    attn_qkv,
    attn_out,
    norm_gain2,
    mlp_up,
    mlp_down,
    out_grad,
):
    f32 = jnp.float32
    b16 = jnp.bfloat16
    band_local = pixels.shape[3]
    pixel_local = pixels[0]
    model_width = bias_gen.shape[1]
    hyper_params = tuple(
        (
            weight.astype(f32)
            for weight in (hyper_qkv, hyper_out, hyper_gain1, hyper_up, hyper_down, hyper_gain2)
        )
    )
    wave_tokens = wave_embed(wavelengths, HW)
    band_code, hyper_pull = jax.vjp(lambda *params: hyper_net(wave_tokens, *params), *hyper_params)
    code_low = band_code.astype(b16)
    column_part = jnp.dot(code_low, kernel_gen, preferred_element_type=f32).astype(b16)
    kernel_rows = lax.all_to_all(column_part, "band", split_axis=0, concat_axis=1, tiled=True)
    kernels = kernel_rows.reshape(band_local, -1, model_width)
    first_band = lax.axis_index("band") * band_local
    own_code = lax.dynamic_slice_in_dim(code_low, first_band, band_local, 0)
    count_row = band_counts[0]
    biases = jnp.dot(own_code, bias_gen, preferred_element_type=f32)
    slot_ids = first_band + jnp.arange(band_local, dtype=jnp.int32)
    active = (slot_ids[None, :] < count_row[:, None]) & (band_mask[0] == 1)
    band_weight = jnp.where(active, lax.rsqrt(count_row.astype(f32))[:, None], f32(0.0))
    pixel_rows = pixel_local
    weight_rows = band_weight
    conv_out = jnp.einsum("inbp,bpd->inbd", pixel_rows, kernels, preferred_element_type=f32)
    residual = lax.psum_scatter(
        jnp.sum((conv_out + biases[None, None]) * weight_rows[:, None, :, None], axis=2),
        "band",
        scatter_dimension=0,
        tiled=True,
    )
    gathered = (
        lax.all_gather(attn_qkv, ("band", "dp"), axis=0, tiled=True),
        lax.all_gather(attn_out, ("band", "dp"), axis=0, tiled=True),
        lax.all_gather(mlp_up, ("band", "dp"), axis=0, tiled=True),
        lax.all_gather(mlp_down, ("band", "dp"), axis=0, tiled=True),
    )
    qkv_full, out_full, up_full, down_full = gathered
    gain_one = norm_gain1.astype(f32)
    gain_two = norm_gain2.astype(f32)
    images, tokens = (residual.shape[0], residual.shape[1])
    score_scale = 1.0 / math.sqrt(HEAD_DIM)
    normed_full, unit_one, inverse_one = norm_parts(residual, gain_one)
    normed_one = normed_full.astype(b16)
    joint_rows = jnp.einsum("ind,de->ine", normed_one, qkv_full, preferred_element_type=f32).astype(
        b16
    )
    queries = joint_rows[..., :model_width].reshape(images, tokens, HEADS, HEAD_DIM)
    key_rows = joint_rows[..., model_width : 2 * model_width].reshape(
        images, tokens, HEADS, HEAD_DIM
    )
    value_rows = joint_rows[..., 2 * model_width :].reshape(images, tokens, HEADS, HEAD_DIM)
    scores = (
        jnp.einsum("inhc,imhc->ihnm", queries, key_rows, preferred_element_type=f32) * score_scale
    )
    row_top = jnp.max(scores, axis=-1, keepdims=True)
    log_total = row_top + jnp.log(jnp.sum(jnp.exp(scores - row_top), axis=-1, keepdims=True))
    probs_full = jnp.exp(scores - log_total)
    probs_low = probs_full.astype(b16)
    mixed_low = (
        jnp.einsum("ihnm,imhc->inhc", probs_low, value_rows, preferred_element_type=f32)
        .reshape(images, tokens, model_width)
        .astype(b16)
    )
    middle = residual + jnp.einsum("ind,de->ine", mixed_low, out_full, preferred_element_type=f32)
    normed_two_full, unit_two, inverse_two = norm_parts(middle, gain_two)
    normed_two = normed_two_full.astype(b16)
    pre_act = jnp.einsum("ind,df->inf", normed_two, up_full, preferred_element_type=f32)
    act_low = gelu_tanh(pre_act).astype(b16)
    result = middle + jnp.einsum("inf,fd->ind", act_low, down_full, preferred_element_type=f32)
    block_out = result.astype(b16)[None]
    qkv_back, out_back, up_back, down_back = (
        lax.all_gather(attn_qkv, ("band", "dp"), axis=0, tiled=True),
        lax.all_gather(attn_out, ("band", "dp"), axis=0, tiled=True),
        lax.all_gather(mlp_up, ("band", "dp"), axis=0, tiled=True),
        lax.all_gather(mlp_down, ("band", "dp"), axis=0, tiled=True),
    )
    grad_top = out_grad[0]
    grad_down = jnp.einsum("inf,ind->fd", act_low, grad_top, preferred_element_type=f32)
    grad_act = jnp.einsum("ind,fd->inf", grad_top, down_back, preferred_element_type=f32)
    grad_pre = (grad_act * gelu_slope(pre_act)).astype(b16)
    grad_up = jnp.einsum("ind,inf->df", normed_two, grad_pre, preferred_element_type=f32)
    grad_normed_two = jnp.einsum("inf,df->ind", grad_pre, up_back, preferred_element_type=f32)
    grad_gain_two = jnp.sum(grad_normed_two * unit_two, axis=(0, 1))
    grad_middle = grad_top.astype(f32) + norm_back(grad_normed_two, gain_two, unit_two, inverse_two)
    grad_branch = grad_middle.astype(b16)
    grad_out_proj = jnp.einsum("ind,ine->de", mixed_low, grad_branch, preferred_element_type=f32)
    grad_mixed = (
        jnp.einsum("ine,de->ind", grad_branch, out_back, preferred_element_type=f32)
        .astype(b16)
        .reshape(images, tokens, HEADS, HEAD_DIM)
    )
    grad_values = jnp.einsum("ihnm,inhc->imhc", probs_low, grad_mixed, preferred_element_type=f32)
    grad_probs = jnp.einsum("inhc,imhc->ihnm", grad_mixed, value_rows, preferred_element_type=f32)
    grad_scores = (
        probs_full * (grad_probs - jnp.sum(grad_probs * probs_full, axis=-1, keepdims=True))
    ).astype(b16)
    grad_queries = (
        jnp.einsum("ihnm,imhc->inhc", grad_scores, key_rows, preferred_element_type=f32)
        * score_scale
    )
    grad_keys = (
        jnp.einsum("ihnm,inhc->imhc", grad_scores, queries, preferred_element_type=f32)
        * score_scale
    )
    grad_joint = jnp.concatenate(
        [
            grad_queries.reshape(images, tokens, model_width),
            grad_keys.reshape(images, tokens, model_width),
            grad_values.reshape(images, tokens, model_width),
        ],
        axis=-1,
    ).astype(b16)
    grad_qkv = jnp.einsum("ind,ine->de", normed_one, grad_joint, preferred_element_type=f32)
    grad_normed_one = jnp.einsum("ine,de->ind", grad_joint, qkv_back, preferred_element_type=f32)
    grad_gain_one = jnp.sum(grad_normed_one * unit_one, axis=(0, 1))
    grad_embed = grad_middle + norm_back(grad_normed_one, gain_one, unit_one, inverse_one)
    grad_embed_low = grad_embed.astype(b16)[None]
    grad_rows = lax.all_gather(grad_embed_low, "band", axis=1, tiled=True)[0].astype(f32)
    weight_rows = band_weight
    pixel_rows = pixel_local
    scaled = grad_rows[:, :, None, :] * weight_rows[:, None, :, None]
    bias_total = jnp.sum(scaled, axis=(0, 1))
    scaled_low = scaled.astype(b16)
    kernel_total = jnp.einsum("inbp,inbd->bpd", pixel_rows, scaled_low, preferred_element_type=f32)
    pixel_part = jnp.einsum(
        "inbd,bpd->inbp", scaled_low, kernels, preferred_element_type=f32
    ).astype(b16)
    pixel_total = pixel_part
    kernel_grad, bias_grad, pixel_total = (kernel_total, bias_total, pixel_total)
    pixel_out = pixel_total[None]
    kernel_grad_low = kernel_grad.reshape(band_local, -1).astype(b16)
    grad_columns = lax.all_to_all(kernel_grad_low, "band", split_axis=1, concat_axis=0, tiled=True)
    grad_kernel_part = jnp.einsum("nh,nc->hc", code_low, grad_columns, preferred_element_type=f32)
    grad_code_part = jnp.einsum("nc,hc->nh", grad_columns, kernel_gen, preferred_element_type=f32)
    bias_back = jnp.einsum("bd,hd->bh", bias_grad, bias_gen.astype(f32), precision=PRECISE)
    grad_code_part = grad_code_part + lax.dynamic_update_slice_in_dim(
        jnp.zeros_like(grad_code_part), bias_back, first_band, 0
    )
    grad_bias_part = jnp.einsum("bh,bd->hd", own_code.astype(f32), bias_grad, precision=PRECISE)
    grad_code, grad_bias_gen, grad_norm_gain1, grad_norm_gain2 = lax.psum(
        (grad_code_part, grad_bias_part, grad_gain_one, grad_gain_two), ("band", "dp")
    )
    grad_kernel_gen = lax.psum(grad_kernel_part.astype(jnp.bfloat16), "dp").astype(jnp.float32)
    hyper_grads = hyper_pull(grad_code)
    shares = (
        lax.psum_scatter(grad_qkv, ("band", "dp"), scatter_dimension=0, tiled=True),
        lax.psum_scatter(grad_out_proj, ("band", "dp"), scatter_dimension=0, tiled=True),
        lax.psum_scatter(grad_up, ("band", "dp"), scatter_dimension=0, tiled=True),
        lax.psum_scatter(grad_down, ("band", "dp"), scatter_dimension=0, tiled=True),
    )
    return (
        block_out,
        pixel_out,
        hyper_grads[0],
        hyper_grads[1],
        hyper_grads[2],
        hyper_grads[3],
        hyper_grads[4],
        hyper_grads[5],
        grad_kernel_gen,
        grad_bias_gen,
        grad_norm_gain1,
        shares[0],
        shares[1],
        grad_norm_gain2,
        shares[2],
        shares[3],
    )


def fast_body(
    pixels,
    wavelengths,
    band_counts,
    band_mask,
    hyper_qkv,
    hyper_out,
    hyper_gain1,
    hyper_up,
    hyper_down,
    hyper_gain2,
    kernel_gen,
    bias_gen,
    norm_gain1,
    attn_qkv,
    attn_out,
    norm_gain2,
    mlp_up,
    mlp_down,
    out_grad,
):
    f32 = jnp.float32
    b16 = jnp.bfloat16
    band_local = pixels.shape[3]
    pixel_local = pixels[0]
    model_width = bias_gen.shape[1]
    hyper_params = tuple(
        (
            weight.astype(f32)
            for weight in (hyper_qkv, hyper_out, hyper_gain1, hyper_up, hyper_down, hyper_gain2)
        )
    )
    wave_tokens = wave_embed(wavelengths, HW)
    band_code, hyper_pull = jax.vjp(lambda *params: hyper_net(wave_tokens, *params), *hyper_params)
    code_low = band_code.astype(b16)
    column_part = jnp.dot(code_low, kernel_gen, preferred_element_type=f32).astype(b16)
    kernel_rows = lax.all_to_all(column_part, "band", split_axis=0, concat_axis=1, tiled=True)
    kernels = kernel_rows.reshape(band_local, -1, model_width)
    first_band = lax.axis_index("band") * band_local
    own_code = lax.dynamic_slice_in_dim(code_low, first_band, band_local, 0)
    count_row = band_counts[0]
    biases = jnp.dot(own_code, bias_gen, preferred_element_type=f32)
    slot_ids = first_band + jnp.arange(band_local, dtype=jnp.int32)
    active = (slot_ids[None, :] < count_row[:, None]) & (band_mask[0] == 1)
    band_weight = jnp.where(active, lax.rsqrt(count_row.astype(f32))[:, None], f32(0.0))
    pixel_rows = pixel_local
    weight_rows = band_weight
    conv_out = jnp.einsum("inbp,bpd->inbd", pixel_rows, kernels, preferred_element_type=f32)
    residual = lax.psum_scatter(
        jnp.sum((conv_out + biases[None, None]) * weight_rows[:, None, :, None], axis=2),
        "band",
        scatter_dimension=0,
        tiled=True,
    )
    block_out, grad_embed_low, shares, gain_grads = middle(
        attn_qkv,
        attn_out,
        mlp_up,
        mlp_down,
        residual[0],
        out_grad[0, 0],
        norm_gain1.astype(f32)[None],
        norm_gain2.astype(f32)[None],
    )
    block_out = block_out[None, None]
    grad_embed_low = grad_embed_low[None, None]
    grad_gain_one, grad_gain_two = gain_grads[0], gain_grads[1]
    grad_rows = lax.all_gather(grad_embed_low, "band", axis=1, tiled=True)[0].astype(f32)
    weight_rows = band_weight
    pixel_rows = pixel_local
    scaled = grad_rows[:, :, None, :] * weight_rows[:, None, :, None]
    bias_total = jnp.sum(scaled, axis=(0, 1))
    scaled_low = scaled.astype(b16)
    kernel_total = jnp.einsum("inbp,inbd->bpd", pixel_rows, scaled_low, preferred_element_type=f32)
    pixel_part = jnp.einsum(
        "inbd,bpd->inbp", scaled_low, kernels, preferred_element_type=f32
    ).astype(b16)
    pixel_total = pixel_part
    kernel_grad, bias_grad, pixel_total = (kernel_total, bias_total, pixel_total)
    pixel_out = pixel_total[None]
    kernel_grad_low = lax.psum(kernel_grad.astype(b16), "dp").reshape(band_local, -1)
    grad_columns = lax.all_to_all(kernel_grad_low, "band", split_axis=1, concat_axis=0, tiled=True)
    grad_kernel_part = jnp.einsum("nh,nc->hc", code_low, grad_columns, preferred_element_type=f32)
    grad_code_part = jnp.einsum("nc,hc->nh", grad_columns, kernel_gen, preferred_element_type=f32)
    bias_back = jnp.einsum("bd,hd->bh", bias_grad, bias_gen.astype(f32), precision=PRECISE)
    grad_code_part = 0.5 * grad_code_part + lax.dynamic_update_slice_in_dim(
        jnp.zeros_like(grad_code_part), bias_back, first_band, 0
    )
    grad_bias_part = jnp.einsum("bh,bd->hd", own_code.astype(f32), bias_grad, precision=PRECISE)
    grad_code, grad_bias_gen, grad_norm_gain1, grad_norm_gain2 = lax.psum(
        (grad_code_part, grad_bias_part, grad_gain_one, grad_gain_two), ("band", "dp")
    )
    grad_kernel_gen = grad_kernel_part
    hyper_grads = hyper_pull(grad_code)
    return (
        block_out,
        pixel_out,
        hyper_grads[0],
        hyper_grads[1],
        hyper_grads[2],
        hyper_grads[3],
        hyper_grads[4],
        hyper_grads[5],
        grad_kernel_gen,
        grad_bias_gen,
        grad_norm_gain1,
        shares[0],
        shares[1],
        grad_norm_gain2,
        shares[2],
        shares[3],
    )


def solution(mesh):
    placed = (
        P("dp", None, None, "band", None),
        P(),
        P("dp", None),
        P("dp", None, "band"),
        P(),
        P(),
        P(),
        P(),
        P(),
        P(),
        P(None, "band"),
        P(),
        P(),
        P(("band", "dp"), None),
        P(("band", "dp"), None),
        P(),
        P(("band", "dp"), None),
        P(("band", "dp"), None),
        P("dp", "band", None, None),
    )
    whole_block = (mesh.shape["band"], mesh.shape["dp"]) == (16, 2)
    return jax.shard_map(
        fast_body if whole_block else body,
        mesh=mesh,
        in_specs=placed,
        out_specs=(
            P("dp", "band", None, None),
            P("dp", None, None, "band", None),
            P(),
            P(),
            P(),
            P(),
            P(),
            P(),
            P(None, "band"),
            P(),
            P(),
            P(("band", "dp"), None),
            P(("band", "dp"), None),
            P(),
            P(("band", "dp"), None),
            P(("band", "dp"), None),
        ),
        check_vma=False,
    )
```

```python
import functools
import math

import jax
import jax.numpy as jnp
from jax import lax
from jax.experimental import pallas as pl
from jax.experimental.pallas import tpu as pltpu
from jax.sharding import PartitionSpec as P

HEADS = 12
HEAD_DIM = 64
HW = 128
HHEADS = 4


PRECISE = lax.Precision.HIGHEST
EPS_BLOCK = 1e-06
EPS_HYPER = 1e-05
GELU_COEF = 0.7978845608028654


def gelu_tanh(tensor):
    return (
        0.5 * tensor * (1.0 + jnp.tanh(GELU_COEF * (tensor + 0.044715 * tensor * tensor * tensor)))
    )


def gelu_slope(tensor):
    tanh_val = jnp.tanh(GELU_COEF * (tensor + 0.044715 * tensor * tensor * tensor))
    return 0.5 * (1.0 + tanh_val) + 0.5 * tensor * (1.0 - tanh_val * tanh_val) * GELU_COEF * (
        1.0 + 3.0 * 0.044715 * tensor * tensor
    )


def layer_norm(tensor, gain_vec, epsilon):
    centred = tensor - jnp.mean(tensor, axis=-1, keepdims=True)
    return (
        centred
        * lax.rsqrt(jnp.mean(centred * centred, axis=-1, keepdims=True) + epsilon)
        * gain_vec
    )


def norm_parts(tensor, gain_vec):
    centred = tensor - jnp.mean(tensor, axis=-1, keepdims=True)
    inverse = lax.rsqrt(jnp.mean(centred * centred, axis=-1, keepdims=True) + EPS_BLOCK)
    unit_rows = centred * inverse
    return (unit_rows * gain_vec, unit_rows, inverse)


def norm_back(grad_rows, gain_vec, unit_rows, inverse):
    scaled = grad_rows * gain_vec
    return inverse * (
        scaled
        - jnp.mean(scaled, axis=-1, keepdims=True)
        - unit_rows * jnp.mean(scaled * unit_rows, axis=-1, keepdims=True)
    )


def wave_embed(wave_ints, token_width):
    half_width = token_width // 2
    frequency = jnp.power(10000.0, -jnp.arange(half_width, dtype=jnp.float32) / half_width)
    angles = wave_ints.astype(jnp.float32)[:, None] * frequency[None, :]
    return jnp.concatenate([jnp.sin(angles), jnp.cos(angles)], axis=1)


def hyper_net(wave_tokens, qkv_weight, out_weight, gain_one, up_weight, down_weight, gain_two):
    tokens, token_width = wave_tokens.shape
    head_size = token_width // HHEADS
    qkv_rows = jnp.dot(wave_tokens, qkv_weight, precision=PRECISE)
    queries = qkv_rows[:, :token_width].reshape(tokens, HHEADS, head_size)
    key_rows = qkv_rows[:, token_width : 2 * token_width].reshape(tokens, HHEADS, head_size)
    value_rows = qkv_rows[:, 2 * token_width :].reshape(tokens, HHEADS, head_size)
    scores = jnp.einsum("nhc,mhc->hnm", queries, key_rows, precision=PRECISE) / math.sqrt(head_size)
    weights_soft = jax.nn.softmax(scores, axis=-1)
    mixed_rows = jnp.einsum("hnm,mhc->nhc", weights_soft, value_rows, precision=PRECISE).reshape(
        tokens, token_width
    )
    first_norm = layer_norm(
        wave_tokens + jnp.dot(mixed_rows, out_weight, precision=PRECISE), gain_one, EPS_HYPER
    )
    inner_act = gelu_tanh(jnp.dot(first_norm, up_weight, precision=PRECISE))
    return layer_norm(
        first_norm + jnp.dot(inner_act, down_weight, precision=PRECISE), gain_two, EPS_HYPER
    )


MESH = pl.DeviceIdType.MESH
B16 = jnp.bfloat16
F32 = jnp.float32
CHUNK = 48
PART = 96
ORDERS = ("zxy", "xzy", "yzx", "zyx", "xzy", "yzx")


def place():
    band = lax.axis_index("band")
    return (band // 4, (band // 2) % 2, band % 2, lax.axis_index("dp"))


def device(z, x, core, y):
    return (z * 4 + x * 2 + core, y)


def slot(z, x, core, y):
    return (z * 4 + x * 2 + core) * 2 + y


def when(cond, run):
    if cond is True:
        run()
    else:
        pl.when(cond)(run)


def both(first, second):
    return second if first is True else first & second


def aligned(rows):
    return pl.multiple_of(rows, 16)


def meet_peers(barrier):
    tell_peers(barrier)
    pl.semaphore_wait(barrier, lax.axis_size("band"))


def tell_peers(barrier):
    band, y = lax.axis_index("band"), lax.axis_index("dp")
    bands = lax.axis_size("band")
    for step in range(1, bands):
        pl.semaphore_signal(
            barrier, inc=1, device_id=((band + step) % bands, y), device_id_type=MESH
        )
    pl.semaphore_signal(barrier, inc=1, device_id=(band, 1 - y), device_id_type=MESH)


class Stream:
    def __init__(self, events):
        self.events = sorted(events, key=lambda event: event[:2])
        self.at = 0

    def run(self, count=None):
        last = len(self.events) if count is None else min(len(self.events), self.at + count)
        for _, _, work in self.events[self.at : last]:
            work()
        self.at = last

    def until(self, time):
        while self.at < len(self.events) and self.events[self.at][0] <= time:
            self.run(1)


class Gather:
    def __init__(self, view, orders, send_sem, recv_sem, pair_send, pair_recv):
        self.view, self.orders = view, orders
        self.send_sem, self.recv_sem = send_sem, recv_sem
        self.pair_send, self.pair_recv = pair_send, pair_recv
        self.z, self.x, self.core, self.y = place()
        self.sends = []
        self.count = [0] * len(orders)

    def rail(self, block):
        return block[0] * 4 + block[1] * 2 + block[2]

    def sibling(self):
        return device(self.z, self.x, 1 - self.core, self.y)

    def send(self, chunk, block, dim, cond, direction=0):
        z, x, core, y = self.z, self.x, self.core, self.y
        if dim == "x":
            targets = [(device(z, 1 - x, core, y), cond)]
        elif dim == "y":
            targets = [(device(z, x, core, 1 - y), cond)]
        else:
            targets = []
            if direction >= 0:
                targets.append((device(z + 1, x, core, y), both(cond, z < 3)))
            if direction <= 0:
                targets.append((device(z - 1, x, core, y), both(cond, z > 0)))
        src = self.view(chunk, block, core)
        for target, needed in targets:
            copy = pltpu.make_async_remote_copy(
                src_ref=src,
                dst_ref=src,
                send_sem=self.send_sem.at[chunk, self.count[chunk]],
                recv_sem=self.recv_sem.at[chunk, self.rail(block)],
                device_id=target,
                device_id_type=MESH,
            )
            self.count[chunk] += 1
            when(needed, copy.start)
            self.sends.append((needed, copy))

    def pair(self, chunk, block, core):
        src = self.view(chunk, block, core)
        return pltpu.make_async_remote_copy(
            src_ref=src,
            dst_ref=src,
            send_sem=self.pair_send.at[chunk, self.rail(block)],
            recv_sem=self.pair_recv.at[chunk, self.rail(block)],
            device_id=self.sibling(),
            device_id_type=MESH,
        )

    def start(self, chunk):
        own = (self.z, self.x, self.y)
        for dim in self.orders[chunk]:
            self.send(chunk, own, dim, True)
        self.pair(chunk, own, self.core).start()

    def events(self, chunk, start=0.0, pace=1.0):
        held, found = [(0, 0, 0, 0, start)], []
        for dim in self.orders[chunk]:
            clock, new = 0.0, []
            ordered = sorted(held, key=lambda item: item[4])
            if dim == "z":
                for dist in (1, 2, 3):
                    for item in ordered:
                        clock = max(clock, item[4]) + pace
                        new += [(dist, way, item[2], item[3], clock) for way in (1, -1)]
            else:
                for item in ordered:
                    clock = max(clock, item[4]) + pace
                    flip = (1, item[3]) if dim == "x" else (item[2], 1)
                    new.append((item[0], item[1], *flip, clock))
            found += [
                (item[4], chunk, functools.partial(self.arrive, chunk, dim, item)) for item in new
            ]
            held = held + new
        return found

    def arrive(self, chunk, dim, item):
        dist, way, flip_x, flip_y, _ = item
        cond = True
        if way == 1:
            cond = self.z >= dist
        elif way == -1:
            cond = self.z + dist <= 3
        block = (
            self.z - dist * way,
            1 - self.x if flip_x else self.x,
            1 - self.y if flip_y else self.y,
        )
        src = self.view(chunk, block, self.core)
        arriving = pltpu.make_async_remote_copy(
            src_ref=src,
            dst_ref=src,
            send_sem=self.send_sem.at[chunk, 0],
            recv_sem=self.recv_sem.at[chunk, self.rail(block)],
            device_id=self.sibling(),
            device_id_type=MESH,
        )
        when(cond, arriving.wait_recv)
        if dim == "z":
            self.send(chunk, block, "z", cond, way)
        order = self.orders[chunk]
        for later in order[order.index(dim) + 1 :]:
            self.send(chunk, block, later, cond)
        when(cond, self.pair(chunk, block, self.core).start)

    def blocks(self, chunk):
        planes = (0, 1) if "y" in self.orders[chunk] else (self.y,)
        return [(zz, xx, yy) for zz in range(4) for xx in (0, 1) for yy in planes]

    def wait_pairs(self, chunk):
        for block in self.blocks(chunk):
            self.pair(chunk, block, 1 - self.core).wait_recv()

    def finish(self):
        for needed, copy in self.sends:
            when(needed, copy.wait_send)
        for chunk in range(len(self.orders)):
            for block in self.blocks(chunk):
                self.pair(chunk, block, self.core).wait_send()


class Reduce:
    def __init__(self, parts, view, orders, final, pair_view, pair_buf, buf, pair_send, pair_recv, send, recv):
        self.parts = parts
        self.view, self.orders, self.final = view, orders, final
        self.pair_view, self.pair_buf, self.buf = pair_view, pair_buf, buf
        self.pair_send, self.pair_recv = pair_send, pair_recv
        self.send_sem, self.recv_sem = send, recv
        self.z, self.x, self.core, self.y = place()
        self.sends = []
        self.count = [0] * len(orders)
        self.index = [{} for _ in orders]

    def rail(self, block):
        if "y" not in self.orders[0]:
            return block[0] * 2 + block[1]
        return block[0] * 4 + block[1] * 2 + block[2]

    def coords(self, block):
        zz, flip_x, flip_y = block
        return (zz, 1 - self.x if flip_x else self.x, 1 - self.y if flip_y else self.y)

    def own(self, chunk, block):
        return self.view(chunk, self.coords(block), self.core)

    def add(self, target, source):
        target[...] = target[...] + source[...]

    def sibling(self):
        return device(self.z, self.x, 1 - self.core, self.y)

    def pair_copy(self, part, block):
        return pltpu.make_async_remote_copy(
            src_ref=self.pair_view(part, block, 1 - self.core),
            dst_ref=self.pair_buf(part, self.rail(block)),
            send_sem=self.pair_send.at[part, self.rail(block)],
            recv_sem=self.pair_recv.at[part, self.rail(block)],
            device_id=self.sibling(),
            device_id_type=MESH,
        )

    def pair_start(self, part, blocks=None):
        for block in blocks or self.blocks():
            self.pair_copy(part, self.coords(block)).start()

    def blocks(self):
        dims = self.orders[0]
        return [
            (zz, fx, fy)
            for fx in ((1, 0) if "x" in dims else (0,))
            for fy in ((1, 0) if "y" in dims else (0,))
            for zz in (3, 0, 2, 1)
        ]

    def place_of(self, chunk, key):
        return self.index[chunk].setdefault(key, len(self.index[chunk]))

    def send(self, chunk, block, key, target, cond):
        where = self.place_of(chunk, key)
        copy = pltpu.make_async_remote_copy(
            src_ref=self.own(chunk, block),
            dst_ref=self.buf(chunk, where),
            send_sem=self.send_sem.at[chunk, self.count[chunk]],
            recv_sem=self.recv_sem.at[chunk, where],
            device_id=target,
            device_id_type=MESH,
        )
        self.count[chunk] += 1
        when(cond, copy.start)
        self.sends.append((cond, copy))

    def landed(self, chunk, key):
        return self.buf(chunk, self.place_of(chunk, key))

    def wait(self, chunk, key):
        landed = self.landed(chunk, key)
        pltpu.make_async_remote_copy(
            src_ref=landed,
            dst_ref=landed,
            send_sem=self.send_sem.at[chunk, 0],
            recv_sem=self.recv_sem.at[chunk, self.place_of(chunk, key)],
            device_id=self.sibling(),
            device_id_type=MESH,
        ).wait_recv()

    def flips(self, chunk, stage):
        left = self.orders[chunk][stage:]
        return [
            (fx, fy)
            for fx in ((1, 0) if "x" in left else (0,))
            for fy in ((1, 0) if "y" in left else (0,))
        ]

    def ready(self, chunk, stage, block):
        order = self.orders[chunk]
        zz, fx, fy = block
        where = zz if "z" in order[stage:] else "own"
        if order[stage] == "x" and fx:
            target = device(self.z, 1 - self.x, self.core, self.y)
            self.send(chunk, block, (stage, where, 0, fy), target, True)
        elif order[stage] == "y" and fy:
            target = device(self.z, self.x, self.core, 1 - self.y)
            self.send(chunk, block, (stage, where, fx, 0), target, True)

    def z_key(self, stage, step, way, flips):
        return (stage, step, way if step else 0, *flips)

    def z_start(self, chunk, stage, step, flips):
        up, down = (3 - step, *flips), (step, *flips)
        right = device(self.z + 1, self.x, self.core, self.y)
        left = device(self.z - 1, self.x, self.core, self.y)
        self.send(chunk, up, self.z_key(stage, step, 1, flips), right, self.z == 0)
        self.send(chunk, down, self.z_key(stage, step, -1, flips), left, self.z == 3)

    def z_arrive(self, chunk, stage, step, flips, way):
        z = self.z if way == 1 else 3 - self.z
        cond = (z >= 1) & (z <= step + 1)
        zz = 2 + z - step
        zz = zz if way == 1 else 3 - zz
        block = (zz, *flips)
        key = self.z_key(stage, step, way, flips)
        last = stage + 1 == len(self.orders[chunk]) and step == 2

        def take():
            self.wait(chunk, key)
            if not last:
                self.add(self.own(chunk, block), self.landed(chunk, key))

        when(cond, take)
        if step < 2:
            target = device(self.z + way, self.x, self.core, self.y)
            self.send(chunk, block, self.z_key(stage, step + 1, way, flips), target, cond)

    def z_done(self, chunk, stage, flips):
        block = (self.z, *flips)
        if stage + 1 < len(self.orders[chunk]):
            self.ready(chunk, stage + 1, block)
            return
        final = self.final(chunk)
        final[...] = self.own(chunk, block)[...].astype(F32)
        for way, cond in ((1, self.z >= 1), (-1, self.z <= 2)):
            landed = self.landed(chunk, self.z_key(stage, 2, way, flips))

            @pl.when(cond)
            def _(landed=landed):
                final[...] += landed[...].astype(F32)

    def xy_arrive(self, chunk, stage, zz, fx, fy):
        key = (stage, zz, fx, fy)
        block = (self.z if zz == "own" else zz, fx, fy)
        self.wait(chunk, key)
        own, landed = self.own(chunk, block), self.landed(chunk, key)
        if stage + 1 < len(self.orders[chunk]):
            self.add(own, landed)
            self.ready(chunk, stage + 1, block)
        else:
            final = self.final(chunk)
            final[...] = own[...].astype(F32) + landed[...].astype(F32)

    def pair_arrive(self, part, block, chunks):
        where = self.coords(block)
        landed = self.pair_buf(part, self.rail(where))
        pltpu.make_async_remote_copy(
            src_ref=landed,
            dst_ref=landed,
            send_sem=self.pair_send.at[part, self.rail(where)],
            recv_sem=self.pair_recv.at[part, self.rail(where)],
            device_id=self.sibling(),
            device_id_type=MESH,
        ).wait_recv()
        self.add(self.pair_view(part, where, self.core), landed)
        for chunk in chunks:
            self.ready(chunk, 0, block)

    def events(self, part, chunks, start=0.0, pace=1.0, pair_pace=0.5):
        found, ready = [], {}
        clock = start
        for block in self.blocks():
            clock += pair_pace
            found.append((clock, 0, functools.partial(self.pair_arrive, part, block, chunks)))
            ready[block] = clock
        for chunk in chunks:
            times = dict(ready)
            for stage, dim in enumerate(self.orders[chunk]):
                clock, later = 0.0, {}
                if dim == "z":
                    for step in range(3):
                        for flips in self.flips(chunk, stage):
                            needed = (0, 3) if step == 0 else (0, 1, 2, 3)
                            clock = max(clock, *(times[(zz, *flips)] for zz in needed)) + 0.001
                            work = functools.partial(self.z_start, chunk, stage, step, flips)
                            found.append((clock, chunk, work))
                            clock += pace
                            for way in (1, -1):
                                work = functools.partial(self.z_arrive, chunk, stage, step, flips, way)
                                found.append((clock, chunk, work))
                            later[("own", *flips)] = clock + 0.001
                    for flips in self.flips(chunk, stage):
                        work = functools.partial(self.z_done, chunk, stage, flips)
                        found.append((later[("own", *flips)], chunk, work))
                else:
                    pick = 1 if dim == "x" else 2
                    for key in sorted((k for k in times if k[pick]), key=lambda k: times[k]):
                        mine = (key[0], 0, key[2]) if dim == "x" else (key[0], key[1], 0)
                        clock = max(max(clock, times[key]) + pace, times[mine] + 0.001)
                        later[mine] = clock
                        work = functools.partial(self.xy_arrive, chunk, stage, *mine)
                        found.append((clock, chunk, work))
                times = later
        return found

    def finish(self):
        for cond, copy in self.sends:
            when(cond, copy.wait_send)
        for part in range(self.parts):
            for block in self.blocks():
                self.pair_copy(part, self.coords(block)).wait_send()


class Exchange:
    def __init__(self, source, landing, send_sem, recv_sem):
        self.source, self.landing = source, landing
        self.send_sem, self.recv_sem = send_sem, recv_sem
        self.band, self.y = lax.axis_index("band"), lax.axis_index("dp")
        self.bands = lax.axis_size("band")

    def copy(self, target):
        return pltpu.make_async_remote_copy(
            src_ref=self.source(target),
            dst_ref=self.landing(self.band),
            send_sem=self.send_sem.at[target],
            recv_sem=self.recv_sem.at[self.band],
            device_id=(target, self.y),
            device_id_type=MESH,
        )

    def others(self):
        return [(self.band + step) % self.bands for step in range(1, self.bands)]

    def start(self):
        for target in self.others():
            self.copy(target).start()

    def wait(self):
        for other in self.others():
            pltpu.make_async_remote_copy(
                src_ref=self.landing(other),
                dst_ref=self.landing(other),
                send_sem=self.send_sem.at[other],
                recv_sem=self.recv_sem.at[other],
                device_id=(other, self.y),
                device_id_type=MESH,
            ).wait_recv()

    def finish(self):
        for target in self.others():
            self.copy(target).wait_send()


def dot_nt(left, right):
    return lax.dot_general(left, right, (((1,), (1,)), ((), ())), preferred_element_type=F32)


def dot_tn(left, right):
    return lax.dot_general(left, right, (((0,), (0,)), ((), ())), preferred_element_type=F32)


def dot_nn(left, right):
    return jnp.dot(left, right, preferred_element_type=F32)


def unit_parts(rows):
    centred = rows - jnp.mean(rows, axis=-1, keepdims=True)
    inverse = lax.rsqrt(jnp.mean(centred * centred, axis=-1, keepdims=True) + EPS_BLOCK)
    return centred * inverse, inverse


class Block:
    def __init__(self, weights, down, refs):
        self.weights, self.down = weights, down
        self.__dict__.update(refs)
        self.width = weights.shape[1]
        self.halves = weights.shape[1] // (2 * HEAD_DIM)

    def weight(self, part):
        return self.weights[pl.ds(aligned(part * self.width), self.width), :]

    def masks(self):
        tokens = self.joint.shape[1]
        lane = lax.broadcasted_iota(jnp.int32, (tokens, 2 * HEAD_DIM), 1)
        low = lane < HEAD_DIM
        return low, low.astype(F32).astype(B16), (~low).astype(F32).astype(B16)

    def pair_rows(self, rows, low, high):
        return jnp.concatenate([rows * low, rows * high], axis=0)

    def project(self):
        unit, inverse = unit_parts(self.residual[...])
        normed = (unit * self.gain_one[...]).astype(B16)
        self.normed_one[...] = normed
        self.unit_one[...] = unit
        self.inverse_one[...] = jnp.broadcast_to(inverse, self.inverse_one.shape)

        @pl.loop(0, 3)
        def _(part):
            self.joint[part] = dot_nn(self.normed_one[...], self.weight(part)).astype(B16)

    def attend(self):
        tokens = self.joint.shape[1]
        scale = 1.0 / math.sqrt(HEAD_DIM)

        @pl.loop(0, self.halves)
        def _(pair):
            where, low, high = self.masks()
            lanes = pl.ds(pl.multiple_of(pair * 2 * HEAD_DIM, 2 * HEAD_DIM), 2 * HEAD_DIM)
            query, key, value = (self.joint[part, :, lanes] for part in range(3))
            scores = dot_nt(self.pair_rows(query, low, high), key) * scale
            raised = jnp.exp(scores - jnp.max(scores, axis=-1, keepdims=True))
            probs = raised / jnp.sum(raised, axis=-1, keepdims=True)
            self.probs[pair] = probs
            mixed = dot_nn(probs.astype(B16), value)
            self.mixed[:, lanes] = jnp.where(where, mixed[:tokens], mixed[tokens:]).astype(B16)

    def widen(self):
        middle = self.residual[...] + dot_nn(self.mixed[...], self.weight(3))
        unit, inverse = unit_parts(middle)
        self.normed_two[...] = (unit * self.gain_two[...]).astype(B16)
        self.unit_two[...] = unit
        self.inverse_two[...] = jnp.broadcast_to(inverse, self.inverse_two.shape)
        self.result[...] = middle

        @pl.loop(0, 4)
        def _(part):
            pre = dot_nn(self.normed_two[...], self.weight(4 + part))
            self.pre_act[part] = pre
            self.act[part] = gelu_tanh(pre).astype(B16)

    def narrow(self):
        @pl.loop(0, 4)
        def _(part):
            rows = pl.ds(aligned(part * self.width), self.width)
            self.result[...] += dot_nn(self.act[part], self.down[rows, :])

        self.block_out[...] = self.result[...].astype(B16)

    def back_narrow(self, part):
        rows = pl.ds(aligned(part * self.width), self.width)
        grad_act = dot_nt(self.out_grad[...], self.down[rows, :])
        grad_pre = (grad_act * gelu_slope(self.pre_act[part])).astype(B16)
        self.grad_pre[part] = grad_pre
        self.grad_normed[...] += dot_nt(grad_pre, self.weight(4 + part))

    def down_grad(self, part, store):
        turned = self.act[part].T
        for at in range(0, self.width, 256):
            store[pl.ds(aligned(part * self.width), self.width), at : at + 256] = dot_nn(
                turned, self.out_grad[:, at : at + 256]
            ).astype(B16)

    def pair_grad(self, first, second, first_grad, second_grad, store, offset):
        @pl.loop(0, 4)
        def _(group):
            rows = pl.ds(aligned(group * 192), 192)
            for at in range(0, self.width, 256):
                cols = slice(at, at + 256)
                one = dot_nn(first[rows, :], first_grad(cols))
                two = dot_nn(second[rows, :], second_grad(cols))
                for owner in range(8):
                    piece = jnp.concatenate(
                        [one[owner * 24 : owner * 24 + 24], two[owner * 24 : owner * 24 + 24]], axis=0
                    )
                    target = aligned((group * 8 + owner) * PART + offset)
                    store[pl.ds(target, CHUNK), cols] = piece.astype(B16)

    def back_wide(self):
        grad_normed = self.grad_normed[...]
        unit = self.unit_two[...]
        self.small[1:2, :] = jnp.sum(grad_normed * unit, axis=0, keepdims=True)
        scaled = grad_normed * self.gain_two[...]
        back = self.inverse_two[:, :1] * (
            scaled
            - jnp.mean(scaled, axis=-1, keepdims=True)
            - unit * jnp.mean(scaled * unit, axis=-1, keepdims=True)
        )
        grad_middle = self.out_grad[...].astype(F32) + back
        self.grad_middle[...] = grad_middle
        branch = grad_middle.astype(B16)
        self.grad_branch[...] = branch
        self.grad_mixed[...] = dot_nt(branch, self.weight(3)).astype(B16)
        self.turned_mixed[...] = self.mixed[...].T

    def back_attend(self):
        tokens = self.joint.shape[1]
        scale = 1.0 / math.sqrt(HEAD_DIM)

        @pl.loop(0, self.halves)
        def _(pair):
            where, low, high = self.masks()
            lanes = pl.ds(pl.multiple_of(pair * 2 * HEAD_DIM, 2 * HEAD_DIM), 2 * HEAD_DIM)
            query, key, value = (self.joint[part, :, lanes] for part in range(3))
            grads = self.pair_rows(self.grad_mixed[:, lanes], low, high)
            probs = self.probs[pair]
            self.grad_joint[2, :, lanes] = dot_tn(probs.astype(B16), grads).astype(B16)
            grad_probs = dot_nt(grads, value)
            total = jnp.sum(grad_probs * probs, axis=-1, keepdims=True)
            grad_scores = (probs * (grad_probs - total)).astype(B16)
            queries = dot_nn(grad_scores, key) * scale
            self.grad_joint[0, :, lanes] = jnp.where(
                where, queries[:tokens], queries[tokens:]
            ).astype(B16)
            keys = dot_tn(grad_scores, self.pair_rows(query, low, high)) * scale
            self.grad_joint[1, :, lanes] = keys.astype(B16)

    def back_project(self):
        self.grad_normed[...] = jnp.zeros(self.grad_normed.shape, F32)

        @pl.loop(0, 3)
        def _(part):
            self.grad_normed[...] += dot_nt(self.grad_joint[part], self.weight(part))

        grad_normed = self.grad_normed[...]
        unit = self.unit_one[...]
        self.small[0:1, :] = jnp.sum(grad_normed * unit, axis=0, keepdims=True)
        scaled = grad_normed * self.gain_one[...]
        back = self.inverse_one[:, :1] * (
            scaled
            - jnp.mean(scaled, axis=-1, keepdims=True)
            - unit * jnp.mean(scaled * unit, axis=-1, keepdims=True)
        )
        self.grad_embed[...] = (self.grad_middle[...] + back).astype(B16)


def spread(gathered, weights, chunk):
    part, offset = chunk // 2, (chunk % 2) * CHUNK
    width = weights.shape[1]

    @pl.loop(0, 16)
    def _(two):
        one, other = (
            gathered[part, pl.ds(aligned((two * 2 + k) * PART + offset), CHUNK), :].astype(F32)
            for k in (0, 1)
        )
        half = CHUNK // 2
        for k, rows in ((0, slice(0, half)), (1, slice(half, CHUNK))):
            target = pl.ds(aligned((2 * chunk + k) * width + two * CHUNK), CHUNK)
            weights[target, :] = jnp.concatenate([one[rows], other[rows]], 0).astype(B16)


def swap_rows(rows):
    count = rows.shape[0]
    row = lax.broadcasted_iota(jnp.int32, (count, count), 0)
    col = lax.broadcasted_iota(jnp.int32, (count, count), 1)
    swap = (col == (row % 16) * 16 + row // 16).astype(F32).astype(B16)
    return dot_nn(swap, rows).astype(B16)


def rows16(ref, index):
    return ref.at[pl.ds(aligned(index * 16), 16)]


def layer_kernel(*refs):
    (shard, pixels, kernel_gen, code_low, bias_gen, band_scale, out_grad, gain_one, gain_two,
     block_out, pixel_out, shares, kernel_grads, code_grads, vectors,
     gathered, weights, spare, pair_buf, buf, joint, probs, pre_act, act, grad_pre, mixed, normed_one, normed_two,
     unit_one, unit_two, inverse_one, inverse_two, grad_normed, grad_middle, grad_branch, grad_mixed, grad_joint,
     turned_mixed, turned_one, turned_two, residual, pixel_rows, turned_pixels, mixing, kernels, sending,
     image_grads, kernel_total, partner_grads, landed_grads, small, small_partner, small_all, code_part, code_all,
     local_sem, pix_sem, gen_sem, front_done, *sems) = refs
    z, x, core, y = place()
    band = lax.axis_index("band")
    bands = lax.axis_size("band")
    me = slot(z, x, core, y)
    width = gain_one.shape[1]
    tokens = out_grad.shape[0]
    partner = (band, 1 - y)
    (gather_sems, reduce_sems, embed_sems, grads_sems, kernel_sems, cols_sems, vec_sems, code_sems, half_sems, vec_half_sems) = (
        sems[0:4], sems[4:8], sems[8:12], sems[12:16], sems[16:18], sems[18:20], sems[20:22], sems[22:24], sems[24:26], sems[26:28]
    )

    def gen_copy(piece, target, at):
        return pltpu.make_async_copy(
            kernel_gen.at[:, pl.ds(piece * width, width)], target.at[pl.ds(at, 128)], gen_sem.at[piece]
        )

    for piece in range(16):
        gen_copy(piece, spare, piece * 128).start()
    own = [
        pltpu.make_async_copy(
            shard.at[pl.ds(part * PART, PART)],
            gathered.at[part, pl.ds(aligned(me * PART), PART)],
            local_sem.at[part],
        )
        for part in range(3)
    ]
    for copy in own:
        copy.start()
    load_pixels = pltpu.make_async_copy(pixels, pixel_rows, pix_sem)
    load_pixels.start()
    meet_peers(pltpu.get_barrier_semaphore())
    for copy in own:
        copy.wait()

    def weight_view(chunk, block, side):
        where = slot(block[0], block[1], side, block[2])
        return gathered.at[chunk // 2, pl.ds(aligned(where * PART + (chunk % 2) * CHUNK), CHUNK)]

    gather = Gather(weight_view, ORDERS, *gather_sems)
    arrivals = []
    for chunk in range(len(ORDERS)):
        arrivals += gather.events(chunk)
    arrivals = Stream(arrivals)
    for chunk in FIRST_CHUNKS:
        gather.start(chunk)

    for piece in range(16):
        gen_copy(piece, spare, piece * 128).wait()

    @pl.loop(0, 16)
    def _(piece):
        part = dot_nn(code_low[...], spare[pl.ds(aligned(piece * 128), 128), :])
        mixing[pl.ds(aligned(piece * 16), 16), :] = part.astype(B16)

    sending[...] = swap_rows(mixing[...])
    spread_kernels = Exchange(
        lambda target: rows16(sending, target), lambda source: rows16(kernels, source), *kernel_sems
    )
    spread_kernels.start()
    for chunk in range(len(ORDERS)):
        if chunk not in FIRST_CHUNKS:
            gather.start(chunk)
    own_rows = pl.ds(aligned(band * 16), 16)
    kernels[own_rows, :] = sending[own_rows, :]
    biases = dot_nn(code_low[...], bias_gen[...])
    chosen = lax.broadcasted_iota(jnp.int32, biases.shape, 0) == band
    bias = jnp.sum(jnp.where(chosen, biases, 0.0), axis=0, keepdims=True)
    load_pixels.wait()
    for group in range(4):
        turned_pixels[group] = pixel_rows[4 * group : 4 * group + 4].reshape(4 * tokens, -1).T
    arrivals.run(EARLY)
    spread_kernels.wait()

    @pl.loop(0, 4)
    def _(group):
        rows = pixel_rows[pl.ds(group * 4, 4)].reshape(4 * tokens, -1)
        for at in range(0, width, 256):
            terms = dot_nn(rows, kernels[:, at : at + 256]) + bias[:, at : at + 256]
            for image in range(4):
                scale = band_scale[group * 4 + image][:1, :1]
                target = pl.ds(aligned((group * 4 + image) * tokens), tokens)
                spare[target, at : at + 256] = (
                    terms[image * tokens : (image + 1) * tokens] * scale
                ).astype(B16)

    half = tokens // 2

    def image_row(block, side):
        return (block[0] * 4 + block[1] * 2 + side) * tokens

    embed = Reduce(
        1,
        lambda chunk, block, side: spare.at[pl.ds(aligned(image_row(block, side) + chunk * half), half)],
        ("xz", "xz"),
        lambda chunk: residual.at[pl.ds(chunk * half, half)],
        lambda part, block, side: spare.at[pl.ds(aligned(image_row(block, side)), tokens)],
        lambda part, rail: pair_buf.at[0, pl.ds(aligned(rail * tokens), tokens)],
        lambda chunk, where: pair_buf.at[1, pl.ds((chunk * 9 + where) * half, half)],
        *embed_sems,
    )
    embed.pair_start(0)
    sums = Stream(embed.events(0, (0, 1)))
    while sums.at < len(sums.events):
        sums.run(EMBED_RUN[0])
        arrivals.run(EMBED_RUN[1])
    tell_peers(front_done)
    arrivals.run()
    for chunk in range(4):
        gather.wait_pairs(chunk)
        spread(gathered, weights, chunk)
    for chunk in (4, 5):
        gather.wait_pairs(chunk)
    gather.finish()

    names = dict(
        residual=residual, out_grad=out_grad, gain_one=gain_one, gain_two=gain_two, block_out=block_out,
        joint=joint, probs=probs, pre_act=pre_act, act=act,
        grad_pre=grad_pre, mixed=mixed, normed_one=normed_one, normed_two=normed_two, unit_one=unit_one,
        unit_two=unit_two, inverse_one=inverse_one, inverse_two=inverse_two, result=residual, grad_normed=grad_normed,
        grad_middle=grad_middle, grad_branch=grad_branch, grad_mixed=grad_mixed, grad_joint=grad_joint,
        turned_mixed=turned_mixed, small=small, grad_embed=image_grads.at[band],
    )
    block = Block(weights, gathered.at[2], names)
    block.project()
    block.attend()
    block.widen()
    block.narrow()

    def part_ref(part):
        return spare if part == 2 else gathered.at[part]

    def grad_view(chunk, blk, side):
        where = slot(blk[0], blk[1], side, blk[2])
        return part_ref(chunk // 2).at[pl.ds(aligned(where * PART + (chunk % 2) * CHUNK), CHUNK)]

    def part_view(part, blk, side):
        return part_ref(part).at[pl.ds(aligned(slot(blk[0], blk[1], side, blk[2]) * PART), PART)]

    reduce = Reduce(
        3,
        grad_view,
        tuple(order[::-1] for order in ORDERS),
        lambda chunk: shares.at[pl.ds(chunk * CHUNK, CHUNK)],
        part_view,
        lambda part, rail: pair_buf.at[part, pl.ds(aligned(rail * PART), PART)],
        lambda chunk, where: buf.at[chunk, where],
        *reduce_sems,
    )
    embed.finish()
    grad_normed[...] = jnp.zeros(grad_normed.shape, F32)

    @pl.loop(0, 4)
    def _(part):
        block.back_narrow(part)
        block.down_grad(part, spare)

    pl.semaphore_wait(front_done, bands)
    reduce.pair_start(2)
    rest = Stream(reduce.events(2, (4, 5)))
    block.back_wide()
    rest.run(BACK_RUN[0])
    block.back_attend()
    rest.run(BACK_RUN[1])
    block.back_project()

    def image_view(chunk, blk, side):
        return image_grads.at[blk[0] * 4 + blk[1] * 2 + side, pl.ds(chunk * half, half)]

    grads = Gather(image_view, ("zx", "zx"), *grads_sems)
    grads.start(0)
    grads.start(1)
    images = Stream(grads.events(0) + grads.events(1))
    turned_two[...] = normed_two[...].T
    for part in (0, 2):
        block.pair_grad(
            turned_two, turned_two, lambda cols, part=part: grad_pre[part, :, cols],
            lambda cols, part=part: grad_pre[part + 1, :, cols], part_ref(1), part // 2 * CHUNK,
        )
        images.run(GRAD_RUN)
    reduce.pair_start(1)
    turned_one[...] = normed_one[...].T
    block.pair_grad(
        turned_one, turned_one, lambda cols: grad_joint[0, :, cols], lambda cols: grad_joint[1, :, cols], part_ref(0), 0
    )
    images.run(GRAD_RUN)
    block.pair_grad(
        turned_one, turned_mixed, lambda cols: grad_joint[2, :, cols], lambda cols: grad_branch[:, cols], part_ref(0), CHUNK
    )
    reduce.pair_start(0)
    images.run()
    for piece in range(16):
        gen_copy(piece, weights, piece * 128).start()

    kernel_total[...] = jnp.zeros(kernel_total.shape, F32)
    small[2:3, :] = jnp.zeros((1, width), F32)
    for chunk in (0, 1):
        grads.wait_pairs(chunk)

    @pl.loop(0, 4)
    def _(group):
        for image in range(4):
            scaled = image_grads[group * 4 + image].astype(F32) * band_scale[group * 4 + image][:1, :1]
            small[2:3, :] += jnp.sum(scaled, axis=0, keepdims=True)
            act[image] = scaled.astype(B16)
        scaled = act[...].reshape(4 * tokens, width)
        pixel_rows[pl.ds(group * 4, 4)] = dot_nt(scaled, kernels[...]).astype(B16).reshape(4, tokens, -1)
        kernel_total[...] += dot_nn(turned_pixels[group], scaled)

    store_pixels = pltpu.make_async_copy(pixel_rows, pixel_out, pix_sem)
    store_pixels.start()
    spread_kernels.finish()
    sending[...] = kernel_total[...].astype(B16)
    quarter = sending.shape[0] // 4

    def half_copy(piece):
        rows = pl.ds(piece * quarter, quarter)
        return pltpu.make_async_remote_copy(
            src_ref=sending.at[rows], dst_ref=partner_grads.at[rows], send_sem=half_sems[0].at[piece],
            recv_sem=half_sems[1].at[piece], device_id=partner, device_id_type=MESH,
        )

    for piece in range(4):
        half_copy(piece).start()
    vec_half = pltpu.make_async_remote_copy(
        src_ref=small, dst_ref=small_partner, send_sem=vec_half_sems[0].at[0], recv_sem=vec_half_sems[1].at[0],
        device_id=partner, device_id_type=MESH,
    )
    vec_half.start()
    columns = Exchange(
        lambda target: rows16(mixing, target), lambda source: rows16(landed_grads, source), *cols_sems
    )
    for piece in range(4):
        half_copy(piece).wait_recv()
        rows = pl.ds(piece * quarter, quarter)
        mixing[rows, :] = sending[rows, :] + partner_grads[rows, :]
        for near in range(4):
            target = piece * 4 + near

            @pl.when(target != band)
            def _(target=target):
                columns.copy(target).start()

    landed_grads[own_rows, :] = mixing[own_rows, :]
    vec_half.wait_recv()
    small_all[band] = small[...] + small_partner[...]
    vector_spread = Exchange(lambda target: small_all.at[band], lambda source: small_all.at[source], *vec_sems)
    vector_spread.start()
    events = reduce.events(1, (2, 3)) + reduce.events(0, (0, 1))
    rest.events = rest.events + sorted(events, key=lambda event: event[:2])
    rest.run(TAIL_RUN[0])
    columns.wait()
    for piece in range(4):
        half_copy(piece).wait_send()
    sending[...] = swap_rows(landed_grads[...])
    kernel_grads[...] = landed_grads[...]
    for piece in range(16):
        gen_copy(piece, weights, piece * 128).wait()
    code_part[...] = jnp.zeros(code_part.shape, F32)

    @pl.loop(0, 16)
    def _(piece):
        code_part[...] += dot_nt(
            sending[pl.ds(aligned(piece * 16), 16), :], weights[pl.ds(aligned(piece * 128), 128), :]
        )

    code_all[band] = code_part[...]
    code_spread = Exchange(lambda target: code_all.at[band], lambda source: code_all.at[source], *code_sems)
    code_spread.start()
    rest.run(TAIL_RUN[1])
    vector_spread.wait()
    vectors[...] = small_all[...]
    code_spread.wait()
    total = code_all[0]
    for source in range(1, bands):
        total = total + code_all[source]
    code_grads[...] = total
    rest.run()
    reduce.finish()
    grads.finish()
    columns.finish()
    vec_half.wait_send()
    vector_spread.finish()
    code_spread.finish()
    store_pixels.wait()


FIRST_CHUNKS = (0, 1, 2, 3, 4, 5)
EARLY = 10
EMBED_RUN = (2, 2)
BACK_RUN = (20, 20)
GRAD_RUN = 4
TAIL_RUN = (20, 20)


def layer(weights, pixels, kernel_gen, code_low, bias_gen, band_scale, out_grad, gain_one, gain_two):
    width = weights[1].shape[1]
    bands = lax.axis_size("band")
    devices = bands * lax.axis_size("dp")
    images, tokens, pix = pixels.shape

    def stack(weight):
        parts = weight.shape[1] // width
        return weight.reshape(weight.shape[0], parts, width).transpose(1, 0, 2).reshape(-1, width)

    shard = jnp.concatenate([stack(w) for w in weights], axis=0)
    chunks = len(ORDERS)
    vmem = pl.BlockSpec(memory_space=pltpu.VMEM)
    hbm = pl.BlockSpec(memory_space=pl.ANY)
    shape = jax.ShapeDtypeStruct
    rows = lambda kind, *lead: pltpu.VMEM((*lead, tokens, width), kind)
    dma = pltpu.SemaphoreType.DMA
    return pl.pallas_call(
        layer_kernel,
        out_shape=[
            shape((tokens, width), B16),
            shape(pixels.shape, B16),
            shape((3 * PART, width), F32),
            shape((pix, width), B16),
            shape((bands, code_low.shape[1]), F32),
            shape((bands, 8, width), F32),
        ],
        in_specs=[hbm, hbm, hbm] + [vmem] * 6,
        out_specs=[vmem, hbm, vmem, vmem, vmem, vmem],
        scratch_shapes=[
            pltpu.VMEM((3, devices * PART, width), B16),
            pltpu.VMEM((8 * width, width), B16),
            pltpu.VMEM((devices * PART, width), B16),
            pltpu.VMEM((3, devices // 2 * PART, width), B16),
            pltpu.VMEM((chunks, 19, CHUNK, width), B16),
            rows(B16, 3),
            pltpu.VMEM((HEADS // 2, 2 * tokens, tokens), F32),
            rows(F32, 4),
            rows(B16, 4),
            rows(B16, 4),
            rows(B16),
            rows(B16),
            rows(B16),
            rows(F32),
            rows(F32),
            pltpu.VMEM((tokens, 128), F32),
            pltpu.VMEM((tokens, 128), F32),
            rows(F32),
            rows(F32),
            rows(B16),
            rows(B16),
            rows(B16, 3),
            pltpu.VMEM((width, tokens), B16),
            pltpu.VMEM((width, tokens), B16),
            pltpu.VMEM((width, tokens), B16),
            rows(F32),
            pltpu.VMEM(pixels.shape, B16),
            pltpu.VMEM((4, pix, 4 * tokens), B16),
            pltpu.VMEM((pix, width), B16),
            pltpu.VMEM((pix, width), B16),
            pltpu.VMEM((pix, width), B16),
            pltpu.VMEM((images, tokens, width), B16),
            pltpu.VMEM((pix, width), F32),
            pltpu.VMEM((pix, width), B16),
            pltpu.VMEM((pix, width), B16),
            pltpu.VMEM((8, width), F32),
            pltpu.VMEM((8, width), F32),
            pltpu.VMEM((bands, 8, width), F32),
            pltpu.VMEM((bands, code_low.shape[1]), F32),
            pltpu.VMEM((bands, bands, code_low.shape[1]), F32),
            dma((3,)),
            dma,
            dma((16,)),
            pltpu.SemaphoreType.REGULAR,
            dma((chunks, 40)), dma((chunks, 16)), dma((chunks, 16)), dma((chunks, 16)),
            dma((3, 16)), dma((3, 16)), dma((chunks, 48)), dma((chunks, 24)),
            dma((1, 8)), dma((1, 8)), dma((2, 24)), dma((2, 16)),
            dma((2, 16)), dma((2, 16)), dma((2, 16)), dma((2, 16)),
            dma((bands,)), dma((bands,)),
            dma((bands,)), dma((bands,)),
            dma((bands,)), dma((bands,)),
            dma((bands,)), dma((bands,)),
            dma((4,)), dma((4,)),
            dma((1,)), dma((1,)),
        ],
        compiler_params=pltpu.CompilerParams(
            collective_id=0, has_side_effects=True, vmem_limit_bytes=VMEM_BYTES
        ),
        name="layer",
    )(shard, pixels, kernel_gen, code_low, bias_gen, band_scale, out_grad, gain_one, gain_two)


VMEM_BYTES = 63 * 2**20


def split_shares(shares, weights):
    width = shares.shape[1]
    grads, at = [], 0
    for weight in weights:
        own_rows, parts = weight.shape[0], weight.shape[1] // width
        piece = shares[at : at + own_rows * parts].reshape(parts, own_rows, width)
        grads.append(piece.transpose(1, 0, 2).reshape(own_rows, parts * width))
        at += own_rows * parts
    return grads


def body(
    pixels,
    wavelengths,
    band_counts,
    band_mask,
    hyper_qkv,
    hyper_out,
    hyper_gain1,
    hyper_up,
    hyper_down,
    hyper_gain2,
    kernel_gen,
    bias_gen,
    norm_gain1,
    attn_qkv,
    attn_out,
    norm_gain2,
    mlp_up,
    mlp_down,
    out_grad,
):
    f32 = jnp.float32
    b16 = jnp.bfloat16
    band_local = pixels.shape[3]
    pixel_local = pixels[0]
    model_width = bias_gen.shape[1]
    hyper_params = tuple(
        (
            weight.astype(f32)
            for weight in (hyper_qkv, hyper_out, hyper_gain1, hyper_up, hyper_down, hyper_gain2)
        )
    )
    wave_tokens = wave_embed(wavelengths, HW)
    band_code, hyper_pull = jax.vjp(lambda *params: hyper_net(wave_tokens, *params), *hyper_params)
    code_low = band_code.astype(b16)
    column_part = jnp.dot(code_low, kernel_gen, preferred_element_type=f32).astype(b16)
    kernel_rows = lax.all_to_all(column_part, "band", split_axis=0, concat_axis=1, tiled=True)
    kernels = kernel_rows.reshape(band_local, -1, model_width)
    first_band = lax.axis_index("band") * band_local
    own_code = lax.dynamic_slice_in_dim(code_low, first_band, band_local, 0)
    count_row = band_counts[0]
    biases = jnp.dot(own_code, bias_gen, preferred_element_type=f32)
    slot_ids = first_band + jnp.arange(band_local, dtype=jnp.int32)
    active = (slot_ids[None, :] < count_row[:, None]) & (band_mask[0] == 1)
    band_weight = jnp.where(active, lax.rsqrt(count_row.astype(f32))[:, None], f32(0.0))
    pixel_rows = pixel_local
    weight_rows = band_weight
    conv_out = jnp.einsum("inbp,bpd->inbd", pixel_rows, kernels, preferred_element_type=f32)
    residual = lax.psum_scatter(
        jnp.sum((conv_out + biases[None, None]) * weight_rows[:, None, :, None], axis=2),
        "band",
        scatter_dimension=0,
        tiled=True,
    )
    gathered = (
        lax.all_gather(attn_qkv, ("band", "dp"), axis=0, tiled=True),
        lax.all_gather(attn_out, ("band", "dp"), axis=0, tiled=True),
        lax.all_gather(mlp_up, ("band", "dp"), axis=0, tiled=True),
        lax.all_gather(mlp_down, ("band", "dp"), axis=0, tiled=True),
    )
    qkv_full, out_full, up_full, down_full = gathered
    gain_one = norm_gain1.astype(f32)
    gain_two = norm_gain2.astype(f32)
    images, tokens = (residual.shape[0], residual.shape[1])
    score_scale = 1.0 / math.sqrt(HEAD_DIM)
    normed_full, unit_one, inverse_one = norm_parts(residual, gain_one)
    normed_one = normed_full.astype(b16)
    joint_rows = jnp.einsum("ind,de->ine", normed_one, qkv_full, preferred_element_type=f32).astype(
        b16
    )
    queries = joint_rows[..., :model_width].reshape(images, tokens, HEADS, HEAD_DIM)
    key_rows = joint_rows[..., model_width : 2 * model_width].reshape(
        images, tokens, HEADS, HEAD_DIM
    )
    value_rows = joint_rows[..., 2 * model_width :].reshape(images, tokens, HEADS, HEAD_DIM)
    scores = (
        jnp.einsum("inhc,imhc->ihnm", queries, key_rows, preferred_element_type=f32) * score_scale
    )
    row_top = jnp.max(scores, axis=-1, keepdims=True)
    log_total = row_top + jnp.log(jnp.sum(jnp.exp(scores - row_top), axis=-1, keepdims=True))
    probs_full = jnp.exp(scores - log_total)
    probs_low = probs_full.astype(b16)
    mixed_low = (
        jnp.einsum("ihnm,imhc->inhc", probs_low, value_rows, preferred_element_type=f32)
        .reshape(images, tokens, model_width)
        .astype(b16)
    )
    middle = residual + jnp.einsum("ind,de->ine", mixed_low, out_full, preferred_element_type=f32)
    normed_two_full, unit_two, inverse_two = norm_parts(middle, gain_two)
    normed_two = normed_two_full.astype(b16)
    pre_act = jnp.einsum("ind,df->inf", normed_two, up_full, preferred_element_type=f32)
    act_low = gelu_tanh(pre_act).astype(b16)
    result = middle + jnp.einsum("inf,fd->ind", act_low, down_full, preferred_element_type=f32)
    block_out = result.astype(b16)[None]
    qkv_back, out_back, up_back, down_back = (
        lax.all_gather(attn_qkv, ("band", "dp"), axis=0, tiled=True),
        lax.all_gather(attn_out, ("band", "dp"), axis=0, tiled=True),
        lax.all_gather(mlp_up, ("band", "dp"), axis=0, tiled=True),
        lax.all_gather(mlp_down, ("band", "dp"), axis=0, tiled=True),
    )
    grad_top = out_grad[0]
    grad_down = jnp.einsum("inf,ind->fd", act_low, grad_top, preferred_element_type=f32)
    grad_act = jnp.einsum("ind,fd->inf", grad_top, down_back, preferred_element_type=f32)
    grad_pre = (grad_act * gelu_slope(pre_act)).astype(b16)
    grad_up = jnp.einsum("ind,inf->df", normed_two, grad_pre, preferred_element_type=f32)
    grad_normed_two = jnp.einsum("inf,df->ind", grad_pre, up_back, preferred_element_type=f32)
    grad_gain_two = jnp.sum(grad_normed_two * unit_two, axis=(0, 1))
    grad_middle = grad_top.astype(f32) + norm_back(grad_normed_two, gain_two, unit_two, inverse_two)
    grad_branch = grad_middle.astype(b16)
    grad_out_proj = jnp.einsum("ind,ine->de", mixed_low, grad_branch, preferred_element_type=f32)
    grad_mixed = (
        jnp.einsum("ine,de->ind", grad_branch, out_back, preferred_element_type=f32)
        .astype(b16)
        .reshape(images, tokens, HEADS, HEAD_DIM)
    )
    grad_values = jnp.einsum("ihnm,inhc->imhc", probs_low, grad_mixed, preferred_element_type=f32)
    grad_probs = jnp.einsum("inhc,imhc->ihnm", grad_mixed, value_rows, preferred_element_type=f32)
    grad_scores = (
        probs_full * (grad_probs - jnp.sum(grad_probs * probs_full, axis=-1, keepdims=True))
    ).astype(b16)
    grad_queries = (
        jnp.einsum("ihnm,imhc->inhc", grad_scores, key_rows, preferred_element_type=f32)
        * score_scale
    )
    grad_keys = (
        jnp.einsum("ihnm,inhc->imhc", grad_scores, queries, preferred_element_type=f32)
        * score_scale
    )
    grad_joint = jnp.concatenate(
        [
            grad_queries.reshape(images, tokens, model_width),
            grad_keys.reshape(images, tokens, model_width),
            grad_values.reshape(images, tokens, model_width),
        ],
        axis=-1,
    ).astype(b16)
    grad_qkv = jnp.einsum("ind,ine->de", normed_one, grad_joint, preferred_element_type=f32)
    grad_normed_one = jnp.einsum("ine,de->ind", grad_joint, qkv_back, preferred_element_type=f32)
    grad_gain_one = jnp.sum(grad_normed_one * unit_one, axis=(0, 1))
    grad_embed = grad_middle + norm_back(grad_normed_one, gain_one, unit_one, inverse_one)
    grad_embed_low = grad_embed.astype(b16)[None]
    grad_rows = lax.all_gather(grad_embed_low, "band", axis=1, tiled=True)[0].astype(f32)
    weight_rows = band_weight
    pixel_rows = pixel_local
    scaled = grad_rows[:, :, None, :] * weight_rows[:, None, :, None]
    bias_total = jnp.sum(scaled, axis=(0, 1))
    scaled_low = scaled.astype(b16)
    kernel_total = jnp.einsum("inbp,inbd->bpd", pixel_rows, scaled_low, preferred_element_type=f32)
    pixel_part = jnp.einsum(
        "inbd,bpd->inbp", scaled_low, kernels, preferred_element_type=f32
    ).astype(b16)
    pixel_total = pixel_part
    kernel_grad, bias_grad, pixel_total = (kernel_total, bias_total, pixel_total)
    pixel_out = pixel_total[None]
    kernel_grad_low = kernel_grad.reshape(band_local, -1).astype(b16)
    grad_columns = lax.all_to_all(kernel_grad_low, "band", split_axis=1, concat_axis=0, tiled=True)
    grad_kernel_part = jnp.einsum("nh,nc->hc", code_low, grad_columns, preferred_element_type=f32)
    grad_code_part = jnp.einsum("nc,hc->nh", grad_columns, kernel_gen, preferred_element_type=f32)
    bias_back = jnp.einsum("bd,hd->bh", bias_grad, bias_gen.astype(f32), precision=PRECISE)
    grad_code_part = grad_code_part + lax.dynamic_update_slice_in_dim(
        jnp.zeros_like(grad_code_part), bias_back, first_band, 0
    )
    grad_bias_part = jnp.einsum("bh,bd->hd", own_code.astype(f32), bias_grad, precision=PRECISE)
    grad_code, grad_bias_gen, grad_norm_gain1, grad_norm_gain2 = lax.psum(
        (grad_code_part, grad_bias_part, grad_gain_one, grad_gain_two), ("band", "dp")
    )
    grad_kernel_gen = lax.psum(grad_kernel_part.astype(jnp.bfloat16), "dp").astype(jnp.float32)
    hyper_grads = hyper_pull(grad_code)
    shares = (
        lax.psum_scatter(grad_qkv, ("band", "dp"), scatter_dimension=0, tiled=True),
        lax.psum_scatter(grad_out_proj, ("band", "dp"), scatter_dimension=0, tiled=True),
        lax.psum_scatter(grad_up, ("band", "dp"), scatter_dimension=0, tiled=True),
        lax.psum_scatter(grad_down, ("band", "dp"), scatter_dimension=0, tiled=True),
    )
    return (
        block_out,
        pixel_out,
        hyper_grads[0],
        hyper_grads[1],
        hyper_grads[2],
        hyper_grads[3],
        hyper_grads[4],
        hyper_grads[5],
        grad_kernel_gen,
        grad_bias_gen,
        grad_norm_gain1,
        shares[0],
        shares[1],
        grad_norm_gain2,
        shares[2],
        shares[3],
    )


def fast_body(
    pixels,
    wavelengths,
    band_counts,
    band_mask,
    hyper_qkv,
    hyper_out,
    hyper_gain1,
    hyper_up,
    hyper_down,
    hyper_gain2,
    kernel_gen,
    bias_gen,
    norm_gain1,
    attn_qkv,
    attn_out,
    norm_gain2,
    mlp_up,
    mlp_down,
    out_grad,
):
    hyper_params = tuple(
        weight.astype(F32)
        for weight in (hyper_qkv, hyper_out, hyper_gain1, hyper_up, hyper_down, hyper_gain2)
    )
    wave_tokens = wave_embed(wavelengths, HW)
    band_code, hyper_pull = jax.vjp(lambda *params: hyper_net(wave_tokens, *params), *hyper_params)
    code_low = band_code.astype(B16)
    band = lax.axis_index("band")
    count_row = band_counts[0]
    active = (band < count_row) & (band_mask[0, :, 0] == 1)
    band_weight = jnp.where(active, lax.rsqrt(count_row.astype(F32)), F32(0.0))
    weights = (attn_qkv, attn_out, mlp_up, mlp_down)
    block_out, pixel_grad, shares, kernel_grads, grad_code, vectors = layer(
        weights,
        pixels[0, :, :, 0],
        kernel_gen,
        code_low,
        bias_gen,
        jnp.broadcast_to(band_weight[:, None, None], (band_weight.shape[0], 8, 128)),
        out_grad[0, 0],
        norm_gain1.astype(F32)[None],
        norm_gain2.astype(F32)[None],
    )
    grad_columns = kernel_grads.reshape(band_code.shape[0], -1)
    grad_kernel_gen = jnp.einsum("nh,nc->hc", code_low, grad_columns, preferred_element_type=F32)
    bias_grads = vectors[:, 2]
    grad_code = grad_code + jnp.dot(bias_grads, bias_gen.astype(F32).T, precision=PRECISE)
    grad_bias_gen = jnp.dot(code_low.astype(F32).T, bias_grads, precision=PRECISE)
    grad_norm_gain1, grad_norm_gain2 = (jnp.sum(vectors[:, row], axis=0) for row in (0, 1))
    hyper_grads = hyper_pull(grad_code)
    shares = split_shares(shares, weights)
    return (
        block_out[None, None],
        pixel_grad[None, :, :, None],
        *hyper_grads,
        grad_kernel_gen,
        grad_bias_gen,
        grad_norm_gain1,
        shares[0],
        shares[1],
        grad_norm_gain2,
        shares[2],
        shares[3],
    )


def solution(mesh):
    placed = (
        P("dp", None, None, "band", None),
        P(),
        P("dp", None),
        P("dp", None, "band"),
        P(),
        P(),
        P(),
        P(),
        P(),
        P(),
        P(None, "band"),
        P(),
        P(),
        P(("band", "dp"), None),
        P(("band", "dp"), None),
        P(),
        P(("band", "dp"), None),
        P(("band", "dp"), None),
        P("dp", "band", None, None),
    )
    one_slot = (mesh.shape["band"], mesh.shape["dp"]) == (16, 2)
    return jax.shard_map(
        fast_body if one_slot else body,
        mesh=mesh,
        in_specs=placed,
        out_specs=(
            P("dp", "band", None, None),
            P("dp", None, None, "band", None),
            P(),
            P(),
            P(),
            P(),
            P(),
            P(),
            P(None, "band"),
            P(),
            P(),
            P(("band", "dp"), None),
            P(("band", "dp"), None),
            P(),
            P(("band", "dp"), None),
            P(("band", "dp"), None),
        ),
        check_vma=False,
    )
```

```python
import functools
import math

import jax
import jax.numpy as jnp
from jax import lax
from jax.experimental import pallas as pl
from jax.experimental.pallas import tpu as pltpu
from jax.sharding import PartitionSpec as P

HEADS = 12
HEAD_DIM = 64
HW = 128
HHEADS = 4


PRECISE = lax.Precision.HIGHEST
EPS_BLOCK = 1e-06
EPS_HYPER = 1e-05
GELU_COEF = 0.7978845608028654


def gelu_tanh(tensor):
    return (
        0.5 * tensor * (1.0 + jnp.tanh(GELU_COEF * (tensor + 0.044715 * tensor * tensor * tensor)))
    )


def gelu_slope(tensor):
    tanh_val = jnp.tanh(GELU_COEF * (tensor + 0.044715 * tensor * tensor * tensor))
    return 0.5 * (1.0 + tanh_val) + 0.5 * tensor * (1.0 - tanh_val * tanh_val) * GELU_COEF * (
        1.0 + 3.0 * 0.044715 * tensor * tensor
    )


def layer_norm(tensor, gain_vec, epsilon):
    centred = tensor - jnp.mean(tensor, axis=-1, keepdims=True)
    return (
        centred
        * lax.rsqrt(jnp.mean(centred * centred, axis=-1, keepdims=True) + epsilon)
        * gain_vec
    )


def norm_parts(tensor, gain_vec):
    centred = tensor - jnp.mean(tensor, axis=-1, keepdims=True)
    inverse = lax.rsqrt(jnp.mean(centred * centred, axis=-1, keepdims=True) + EPS_BLOCK)
    unit_rows = centred * inverse
    return (unit_rows * gain_vec, unit_rows, inverse)


def norm_back(grad_rows, gain_vec, unit_rows, inverse):
    scaled = grad_rows * gain_vec
    return inverse * (
        scaled
        - jnp.mean(scaled, axis=-1, keepdims=True)
        - unit_rows * jnp.mean(scaled * unit_rows, axis=-1, keepdims=True)
    )


def wave_embed(wave_ints, token_width):
    half_width = token_width // 2
    frequency = jnp.power(10000.0, -jnp.arange(half_width, dtype=jnp.float32) / half_width)
    angles = wave_ints.astype(jnp.float32)[:, None] * frequency[None, :]
    return jnp.concatenate([jnp.sin(angles), jnp.cos(angles)], axis=1)


def hyper_net(wave_tokens, qkv_weight, out_weight, gain_one, up_weight, down_weight, gain_two):
    tokens, token_width = wave_tokens.shape
    head_size = token_width // HHEADS
    qkv_rows = jnp.dot(wave_tokens, qkv_weight, precision=PRECISE)
    queries = qkv_rows[:, :token_width].reshape(tokens, HHEADS, head_size)
    key_rows = qkv_rows[:, token_width : 2 * token_width].reshape(tokens, HHEADS, head_size)
    value_rows = qkv_rows[:, 2 * token_width :].reshape(tokens, HHEADS, head_size)
    scores = jnp.einsum("nhc,mhc->hnm", queries, key_rows, precision=PRECISE) / math.sqrt(head_size)
    weights_soft = jax.nn.softmax(scores, axis=-1)
    mixed_rows = jnp.einsum("hnm,mhc->nhc", weights_soft, value_rows, precision=PRECISE).reshape(
        tokens, token_width
    )
    first_norm = layer_norm(
        wave_tokens + jnp.dot(mixed_rows, out_weight, precision=PRECISE), gain_one, EPS_HYPER
    )
    inner_act = gelu_tanh(jnp.dot(first_norm, up_weight, precision=PRECISE))
    return layer_norm(
        first_norm + jnp.dot(inner_act, down_weight, precision=PRECISE), gain_two, EPS_HYPER
    )


MESH = pl.DeviceIdType.MESH
B16 = jnp.bfloat16
F32 = jnp.float32
CHUNK = 48
DIMS = "xyz"
PART = 96
FRONT_PLAN = (
    (
        (),
        (),
        (),
        (1, 2, 3),
        (30, 11),
        (54, 27),
        (10,),
        (13, 57, 29, 81, 82, 5),
        (56, 83, 86),
        (87, 92, 93, 33, 100, 60, 84, 90, 85, 22, 39, 91, 17, 32, 59, 9, 35, 14, 88, 66, 89, 62, 45, 94, 103, 95, 104, 21, 47, 24, 41, 101, 38, 109, 68, 65, 102, 110, 72, 51, 18, 49, 71, 26, 44, 74),
        (112, 115, 53, 114, 116, 78),
        (76, 80),
        (),
        (),
        (),
        (),
    ),
    (
        (),
        (),
        (0, 1),
        (2, 3),
        (7,),
        (30,),
        (6, 28, 11),
        (54, 27, 81, 10, 55, 82, 83, 29, 57, 86, 13, 5),
        (31, 56, 87, 92),
        (58, 93, 100, 84, 85, 96, 19, 36, 35, 98, 32, 62, 59, 88, 63, 33, 22, 89, 60, 39, 17, 14, 65, 38, 42, 94, 106, 66, 95, 108, 105, 69, 107, 47, 45, 101, 111, 24, 102, 113, 49, 112, 115, 114, 116),
        (72, 74),
        (76,),
        (),
        (),
        (),
        (),
    ),
    (
        (),
        (),
        (0, 1),
        (2, 3),
        (7,),
        (),
        (30, 6, 11, 29),
        (54, 81, 27, 82, 56, 10, 83, 86, 57, 4),
        (13, 28, 55, 87, 92, 32, 59),
        (93, 100, 19, 84, 85, 39, 34, 31, 61, 58, 33, 22, 66, 88, 15, 89, 60, 97, 99, 12, 37, 36, 64, 45, 94, 63, 112, 95, 105, 114, 107, 72, 42, 46, 111, 115, 101, 106, 113, 116, 102, 23, 108, 48, 69),
        (73,),
        (75,),
        (),
        (),
        (),
        (),
    ),
    (
        (),
        (),
        (),
        (0, 2, 3),
        (30, 7, 54),
        (27, 6),
        (13, 57, 4),
        (81, 28, 82, 83, 86, 55),
        (87,),
        (92, 60, 33, 93, 100, 19, 15, 84, 12, 85, 36, 31, 58, 8, 88, 34, 90, 89, 91, 63, 61, 42, 23, 94, 109, 20, 95, 110, 46, 40, 101, 103, 102, 64, 37, 104, 67, 69, 50, 48, 16, 73, 43, 25, 70, 52),
        (111, 115, 77, 113, 75, 116),
        (),
        (79,),
        (),
        (),
        (),
    ),
)
TAIL_PLAN = (
    (
        (),
        (0, 1, 2, 4, 5, 8, 9, 11, 12, 16, 17, 21, 22, 25, 26, 28, 3),
        (6,),
        (7, 15),
        (10,),
        (122, 123),
        (135, 13, 136, 38, 39, 40, 125, 42, 18, 43, 45, 46, 138, 49, 50, 14, 129, 55, 56, 60, 128, 61, 63, 142, 23, 64, 67, 27, 141),
        (24, 131, 29, 31),
        (41, 48, 144, 83, 84, 85, 87, 133, 88, 91, 92, 94, 95, 99, 100),
        (104, 44, 105, 54, 108, 109, 146, 36, 111, 37, 30, 34, 47, 51),
        (86, 57, 66, 62, 71, 89, 93, 65, 74, 96, 76, 78, 68, 77, 101, 106, 80),
        (110,),
        (),
        (90, 98, 112),
        (),
        (82, 97, 107, 114, 113, 117),
        (),
        (119, 120),
    ),
    (
        (),
        (0, 1, 2, 4, 5, 8, 9, 11, 12, 16, 17, 21, 22, 25, 26, 28, 3),
        (6,),
        (7,),
        (10,),
        (122, 123, 121),
        (135, 136, 13, 134, 125, 38, 39, 40, 18, 42, 43, 45, 19, 138, 46, 49, 14, 50, 55, 129, 56, 60, 61, 126, 23, 63, 64, 142, 67, 27),
        (29, 139),
        (33, 41, 131, 83, 84, 85, 87, 88, 91, 24, 92, 144, 94, 32, 95, 99, 100, 44, 104, 105, 108, 109, 111, 52, 47, 30, 51),
        (58, 86),
        (35, 57, 89, 62, 36, 37, 69, 93, 70, 65, 96, 72, 68, 73, 101, 75, 106, 79),
        (),
        (90, 110),
        (),
        (),
        (76, 112, 78, 97, 102, 107, 80, 113, 82),
        (115, 118),
        (116, 119, 120),
    ),
    (
        (),
        (0, 1, 2, 4, 5, 8, 9, 11, 12, 16, 17, 21, 22, 25, 26, 28, 3),
        (6,),
        (7,),
        (10,),
        (121, 122, 123),
        (134, 135, 136, 13, 38, 39, 40, 124, 42, 18, 43, 45, 46, 49, 14, 137, 50, 126, 55, 56, 60, 129, 23, 61, 63, 64, 67, 27, 139, 32, 20, 29),
        (142,),
        (41, 130),
        (83, 84, 24, 143, 85, 87, 36, 88, 91, 92, 44, 94, 95, 99, 100, 104, 105, 108, 109, 35, 111, 37, 30, 47, 51, 86, 33),
        (53, 69, 57, 89, 62, 72, 93, 59, 65, 96, 75, 76, 78, 68, 80, 101, 79, 106, 70),
        (),
        (90,),
        (73, 110),
        (),
        (112, 82, 97, 107, 113),
        (103, 119, 115, 116),
        (118, 120),
    ),
    (
        (),
        (0, 1, 2, 4, 5, 8, 9, 11, 12, 16, 17, 21, 22, 25, 26, 28, 3),
        (6,),
        (7,),
        (10,),
        (),
        (121, 123, 134, 13, 136, 38, 39, 40, 124, 42, 18, 43, 45, 46, 49, 137, 50, 55, 126, 56, 14, 15, 60, 61, 63, 127, 139, 64, 23, 67, 140, 27),
        (130, 29),
        (24, 34, 143, 41, 35, 83, 84, 37, 85, 87, 132, 88, 91, 92, 94, 95, 99),
        (100, 104, 44, 105, 145, 108, 109, 111, 30, 47, 31, 48, 51, 54),
        (86, 57, 74, 62, 89, 77, 75, 78, 93, 65, 66, 96, 79, 68, 71, 101, 106),
        (),
        (),
        (110,),
        (),
        (112, 90, 82, 97, 98, 107, 117, 113, 114),
        (118, 120),
        (),
    ),
)
FIRST_PARTS = (0,)
SUM_ORDERS = ('xyz', 'yzx', 'yxz')
ORDERS = ("zxy", "xzy", "yzx")


def place(known_z=None):
    band = lax.axis_index("band")
    z = band // 4 if known_z is None else known_z
    return (z, (band // 2) % 2, band % 2, lax.axis_index("dp"))


def device(z, x, core, y):
    return (z * 4 + x * 2 + core, y)


def slot(z, x, core, y):
    return (z * 4 + x * 2 + core) * 2 + y


def when(cond, run):
    if isinstance(cond, bool):
        if cond:
            run()
    else:
        pl.when(cond)(run)


def both(first, second):
    return second if first is True else first & second


def aligned(rows):
    return pl.multiple_of(rows, 16)


def tell_peers(barrier):
    band, y = lax.axis_index("band"), lax.axis_index("dp")
    bands = lax.axis_size("band")
    for step in range(1, bands):
        pl.semaphore_signal(
            barrier, inc=1, device_id=((band + step) % bands, y), device_id_type=MESH
        )
    pl.semaphore_signal(barrier, inc=1, device_id=(band, 1 - y), device_id_type=MESH)


def tell_near(semaphore):
    z, x, core, y = place()
    near = [
        (device(z, x, 1 - core, y), True),
        (device(z, 1 - x, core, y), True),
        (device(z, x, core, 1 - y), True),
        (device(z + 1, x, core, y), z < 3),
        (device(z - 1, x, core, y), z > 0),
    ]
    for target, cond in near:
        when(
            cond,
            functools.partial(
                pl.semaphore_signal, semaphore, inc=1, device_id=target, device_id_type=MESH
            ),
        )


def hear_near(semaphore):
    z = place()[0]
    pl.semaphore_wait(semaphore, 5 - z // 3 - (3 - z) // 3)


def bulk_copy(ref, send_sem, recv_sem):
    band, y = lax.axis_index("band"), lax.axis_index("dp")
    return pltpu.make_async_remote_copy(
        src_ref=ref,
        dst_ref=ref,
        send_sem=send_sem,
        recv_sem=recv_sem,
        device_id=(band, 1 - y),
        device_id_type=MESH,
    )


def in_order(events):
    return [work for _, _, work in sorted(events, key=lambda event: event[:2])]


class Plan:
    def __init__(self, table, catalogues):
        self.table, self.catalogues = table, catalogues
        self.at = 0

    def run(self):
        z = place()[0]
        for known_z, works in enumerate(self.catalogues):
            chosen = self.table[known_z][self.at]
            if not chosen:
                continue

            @pl.when(z == known_z)
            def _(works=works, chosen=chosen):
                for index in chosen:
                    works[index]()

        self.at += 1


class Gather:
    def __init__(self, known_z, view, orders, bulk, send_sem, recv_sem, pair_send, pair_recv):
        self.view, self.orders, self.bulk = view, orders, bulk
        self.send_sem, self.recv_sem = send_sem, recv_sem
        self.pair_send, self.pair_recv = pair_send, pair_recv
        self.z, self.x, self.core, self.y = place(known_z)

    def rail(self, block):
        return block[0] * 4 + block[1] * 2 + block[2]

    def sibling(self):
        return device(self.z, self.x, 1 - self.core, self.y)

    def send(self, chunk, block, dim, cond, direction=0):
        z, x, core, y = self.z, self.x, self.core, self.y
        if dim == "x":
            targets = [(device(z, 1 - x, core, y), cond)]
        elif dim == "y":
            targets = [(device(z, x, core, 1 - y), cond)]
        else:
            targets = []
            if direction >= 0:
                targets.append((device(z + 1, x, core, y), both(cond, z < 3)))
            if direction <= 0:
                targets.append((device(z - 1, x, core, y), both(cond, z > 0)))
        src = self.view(chunk, block, core)
        for target, needed in targets:
            if needed is False:
                continue
            copy = pltpu.make_async_remote_copy(
                src_ref=src,
                dst_ref=src,
                send_sem=self.send_sem.at[chunk, DIMS.index(dim)],
                recv_sem=self.recv_sem.at[chunk, self.rail(block)],
                device_id=target,
                device_id_type=MESH,
            )
            when(needed, copy.start)

    def pair(self, chunk, block, core):
        src = self.view(chunk, block, core)
        return pltpu.make_async_remote_copy(
            src_ref=src,
            dst_ref=src,
            send_sem=self.pair_send.at[chunk, block[0] // 2],
            recv_sem=self.pair_recv.at[chunk, block[0] // 2],
            device_id=self.sibling(),
            device_id_type=MESH,
        )

    def start(self, chunk):
        own = (self.z, self.x, self.y)
        for dim in self.orders[chunk]:
            self.send(chunk, own, dim, True)
        self.pair(chunk, own, self.core).start()

    def events(self, chunk, start=0.0, pace=1.0):
        held, found = [(0, 0, 0, 0, start)], []
        for dim in self.orders[chunk]:
            clock, new = 0.0, []
            ordered = sorted(held, key=lambda item: item[4])
            if dim == "z":
                for dist in (1, 2, 3):
                    for item in ordered:
                        clock = max(clock, item[4]) + pace
                        new += [(dist, way, item[2], item[3], clock) for way in (1, -1)]
            else:
                for item in ordered:
                    clock = max(clock, item[4]) + pace
                    flip = (1, item[3]) if dim == "x" else (item[2], 1)
                    new.append((item[0], item[1], *flip, clock))
            found += [
                (item[4], chunk, functools.partial(self.arrive, chunk, dim, item)) for item in new
            ]
            held = held + new
        return found

    def arrive(self, chunk, dim, item):
        dist, way, flip_x, flip_y, _ = item
        cond = True
        if way == 1:
            cond = self.z >= dist
        elif way == -1:
            cond = self.z + dist <= 3
        if cond is False:
            return
        block = (
            self.z - dist * way,
            1 - self.x if flip_x else self.x,
            1 - self.y if flip_y else self.y,
        )
        src = self.view(chunk, block, self.core)
        arriving = pltpu.make_async_remote_copy(
            src_ref=src,
            dst_ref=src,
            send_sem=self.send_sem.at[chunk, 0],
            recv_sem=self.recv_sem.at[chunk, self.rail(block)],
            device_id=self.sibling(),
            device_id_type=MESH,
        )
        when(cond, arriving.wait_recv)
        if dim == "z":
            self.send(chunk, block, "z", cond, way)
        order = self.orders[chunk]
        for later in order[order.index(dim) + 1 :]:
            self.send(chunk, block, later, cond)
        when(cond, self.pair(chunk, block, self.core).start)

    def rails(self, chunk):
        return 16 if "y" in self.orders[chunk] else 8

    def sent(self, chunk, z, over):
        order = self.orders[chunk]
        fresh = (z < 3) + (z > 0) if over == "z" else 1
        total = fresh if over in order else 0
        for _, _, work in self.events(chunk):
            _, dim, (dist, way, *_) = work.args
            if (way == 1 and z < dist) or (way == -1 and z + dist > 3):
                continue
            total += fresh if over in order[order.index(dim) + 1 :] else 0
            if dim == "z" and over == "z":
                total += z < 3 if way == 1 else z > 0
        return total

    def wait_side(self, chunk, side):
        every = self.bulk(chunk, self.rails(chunk) // 2)
        bulk_copy(every, self.pair_send.at[chunk, side], self.pair_recv.at[chunk, side]).wait_recv()

    def wait_pairs(self, chunk):
        for side in (0, 1):
            self.wait_side(chunk, side)

    def finish(self):
        ends = (self.z == 0) | (self.z == 3)
        inner = (self.z == 1) | (self.z == 2)
        for chunk in range(len(self.orders)):
            for dim in self.orders[chunk]:
                send_sem = self.send_sem.at[chunk, DIMS.index(dim)]
                for cond, z in ((ends, 0), (inner, 1)):
                    copy = bulk_copy(self.bulk(chunk, self.sent(chunk, z, dim)), send_sem, self.recv_sem.at[chunk, 0])
                    when(cond, copy.wait_send)
            every = self.bulk(chunk, self.rails(chunk) // 2)
            for side in (0, 1):
                bulk_copy(every, self.pair_send.at[chunk, side], self.pair_recv.at[chunk, side]).wait_send()


class Reduce:
    def __init__(
        self, known_z, parts, view, orders, final, pair_view, pair_buf, buf, bulk, pair_bulk, pair_send, pair_recv, send, recv
    ):
        self.parts, self.bulk, self.pair_bulk = parts, bulk, pair_bulk
        self.view, self.orders, self.final = view, orders, final
        self.pair_view, self.pair_buf, self.buf = pair_view, pair_buf, buf
        self.pair_send, self.pair_recv = pair_send, pair_recv
        self.send_sem, self.recv_sem = send, recv
        self.z, self.x, self.core, self.y = place(known_z)
        self.index = [self.places(chunk) for chunk in range(len(orders))]

    def rail(self, block):
        if "y" not in self.orders[0]:
            return block[0] * 2 + block[1]
        return block[0] * 4 + block[1] * 2 + block[2]

    def coords(self, block):
        zz, flip_x, flip_y = block
        return (zz, 1 - self.x if flip_x else self.x, 1 - self.y if flip_y else self.y)

    def own(self, chunk, block):
        return self.view(chunk, self.coords(block), self.core)

    def add(self, target, source):
        target[...] = target[...] + source[...]

    def sibling(self):
        return device(self.z, self.x, 1 - self.core, self.y)

    def pair_copy(self, part, block):
        return pltpu.make_async_remote_copy(
            src_ref=self.pair_view(part, block, 1 - self.core),
            dst_ref=self.pair_buf(part, self.rail(block)),
            send_sem=self.pair_send.at[part, block[0] // 2],
            recv_sem=self.pair_recv.at[part, self.rail(block)],
            device_id=self.sibling(),
            device_id_type=MESH,
        )

    def pair_start(self, part, blocks=None):
        for block in blocks or self.blocks():
            self.pair_copy(part, self.coords(block)).start()

    def blocks(self):
        return [(zz, fx, fy) for zz in (3, 0, 2, 1) for fx, fy in self.flips(0, 0)]

    def places(self, chunk):
        order, keys = self.orders[chunk], []
        for stage, dim in enumerate(order):
            if dim == "z":
                keys += [
                    self.z_key(stage, step, way, flips)
                    for step in range(3)
                    for way in ((1, -1) if step else (1,))
                    for flips in self.flips(chunk, stage)
                ]
                continue
            wheres = range(4) if "z" in order[stage:] else ("own",)
            later = self.flips(chunk, stage + 1)
            keys += [(stage, where, *flips) for where in wheres for flips in later]
        return {key: at for at, key in enumerate(keys)}

    def place_of(self, chunk, key):
        return self.index[chunk][key]

    def send(self, chunk, block, key, target, cond):
        if cond is False:
            return
        where = self.place_of(chunk, key)
        copy = pltpu.make_async_remote_copy(
            src_ref=self.own(chunk, block),
            dst_ref=self.buf(chunk, where),
            send_sem=self.send_sem.at[chunk, key[0]],
            recv_sem=self.recv_sem.at[chunk, where],
            device_id=target,
            device_id_type=MESH,
        )
        when(cond, copy.start)

    def landed(self, chunk, key):
        return self.buf(chunk, self.place_of(chunk, key))

    def wait(self, chunk, key):
        landed = self.landed(chunk, key)
        pltpu.make_async_remote_copy(
            src_ref=landed,
            dst_ref=landed,
            send_sem=self.send_sem.at[chunk, 0],
            recv_sem=self.recv_sem.at[chunk, self.place_of(chunk, key)],
            device_id=self.sibling(),
            device_id_type=MESH,
        ).wait_recv()

    def flips(self, chunk, stage):
        left = self.orders[chunk][stage:]
        return [
            (fx, fy)
            for fx in ((1, 0) if "x" in left else (0,))
            for fy in ((1, 0) if "y" in left else (0,))
        ]

    def ready(self, chunk, stage, block):
        order = self.orders[chunk]
        zz, fx, fy = block
        where = zz if "z" in order[stage:] else "own"
        if order[stage] == "x" and fx:
            target = device(self.z, 1 - self.x, self.core, self.y)
            self.send(chunk, block, (stage, where, 0, fy), target, True)
        elif order[stage] == "y" and fy:
            target = device(self.z, self.x, self.core, 1 - self.y)
            self.send(chunk, block, (stage, where, fx, 0), target, True)

    def z_key(self, stage, step, way, flips):
        return (stage, step, way if step else 0, *flips)

    def z_start(self, chunk, stage, step, flips):
        up, down = (3 - step, *flips), (step, *flips)
        right = device(self.z + 1, self.x, self.core, self.y)
        left = device(self.z - 1, self.x, self.core, self.y)
        self.send(chunk, up, self.z_key(stage, step, 1, flips), right, self.z == 0)
        self.send(chunk, down, self.z_key(stage, step, -1, flips), left, self.z == 3)

    def z_arrive(self, chunk, stage, step, flips, way):
        z = self.z if way == 1 else 3 - self.z
        cond = (z >= 1) & (z <= step + 1)
        zz = 2 + z - step
        zz = zz if way == 1 else 3 - zz
        block = (zz, *flips)
        key = self.z_key(stage, step, way, flips)
        last = stage + 1 == len(self.orders[chunk]) and step == 2

        def take():
            self.wait(chunk, key)
            if not last:
                self.add(self.own(chunk, block), self.landed(chunk, key))

        when(cond, take)
        if step < 2:
            target = device(self.z + way, self.x, self.core, self.y)
            self.send(chunk, block, self.z_key(stage, step + 1, way, flips), target, cond)

    def z_done(self, chunk, stage, flips):
        block = (self.z, *flips)
        if stage + 1 < len(self.orders[chunk]):
            self.ready(chunk, stage + 1, block)
            return
        final = self.final(chunk)
        final[...] = self.own(chunk, block)[...].astype(F32)
        for way, cond in ((1, self.z >= 1), (-1, self.z <= 2)):
            landed = self.landed(chunk, self.z_key(stage, 2, way, flips))

            def add(landed=landed):
                final[...] += landed[...].astype(F32)

            when(cond, add)

    def xy_arrive(self, chunk, stage, zz, fx, fy):
        key = (stage, zz, fx, fy)
        block = (self.z if zz == "own" else zz, fx, fy)
        self.wait(chunk, key)
        own, landed = self.own(chunk, block), self.landed(chunk, key)
        if stage + 1 < len(self.orders[chunk]):
            self.add(own, landed)
            self.ready(chunk, stage + 1, block)
        else:
            final = self.final(chunk)
            final[...] = own[...].astype(F32) + landed[...].astype(F32)

    def pair_arrive(self, part, block, chunks):
        where = self.coords(block)
        landed = self.pair_buf(part, self.rail(where))
        pltpu.make_async_remote_copy(
            src_ref=landed,
            dst_ref=landed,
            send_sem=self.pair_send.at[part, 0],
            recv_sem=self.pair_recv.at[part, self.rail(where)],
            device_id=self.sibling(),
            device_id_type=MESH,
        ).wait_recv()
        self.add(self.pair_view(part, where, self.core), landed)
        for chunk in chunks:
            self.ready(chunk, 0, block)

    def events(self, part, chunks, start=0.0, pace=1.0, pair_pace=0.5):
        found, ready = [], {}
        clock = start
        for block in self.blocks():
            clock += pair_pace
            found.append((clock, 0, functools.partial(self.pair_arrive, part, block, chunks)))
            ready[block] = clock
        for chunk in chunks:
            times = dict(ready)
            for stage, dim in enumerate(self.orders[chunk]):
                clock, later = 0.0, {}
                if dim == "z":
                    for step in range(3):
                        for flips in self.flips(chunk, stage):
                            needed = (0, 3) if step == 0 else (0, 1, 2, 3)
                            clock = max(clock, *(times[(zz, *flips)] for zz in needed)) + 0.001
                            work = functools.partial(self.z_start, chunk, stage, step, flips)
                            found.append((clock, chunk, work))
                            clock += pace
                            for way in (1, -1):
                                work = functools.partial(self.z_arrive, chunk, stage, step, flips, way)
                                found.append((clock, chunk, work))
                            later[("own", *flips)] = clock + 0.001
                    for flips in self.flips(chunk, stage):
                        work = functools.partial(self.z_done, chunk, stage, flips)
                        found.append((later[("own", *flips)], chunk, work))
                else:
                    pick = 1 if dim == "x" else 2
                    for key in sorted((k for k in times if k[pick]), key=lambda k: times[k]):
                        mine = (key[0], 0, key[2]) if dim == "x" else (key[0], key[1], 0)
                        clock = max(max(clock, times[key]) + pace, times[mine] + 0.001)
                        later[mine] = clock
                        work = functools.partial(self.xy_arrive, chunk, stage, *mine)
                        found.append((clock, chunk, work))
                times = later
        return found

    def finish(self):
        rails = len(self.blocks())
        for chunk, order in enumerate(self.orders):
            for stage, dim in enumerate(order):
                after = len(self.flips(chunk, stage + 1)) if stage + 1 < len(order) else 1
                count = 3 * after if dim == "z" else after * (4 if "z" in order[stage + 1 :] else 1)
                every = self.bulk(chunk, count)
                bulk_copy(every, self.send_sem.at[chunk, stage], self.recv_sem.at[chunk, 0]).wait_send()
        for part in range(self.parts):
            every = self.pair_bulk(part, rails // 2)
            for side in (0, 1):
                bulk_copy(every, self.pair_send.at[part, side], self.pair_recv.at[part, 0]).wait_send()


class Exchange:
    def __init__(self, source, landing, bulk, send_sem, recv_sem):
        self.source, self.landing, self.bulk = source, landing, bulk
        self.send_sem, self.recv_sem = send_sem, recv_sem
        self.band, self.y = lax.axis_index("band"), lax.axis_index("dp")
        self.bands = lax.axis_size("band")

    def send(self, target):
        pltpu.make_async_remote_copy(
            src_ref=self.source(target),
            dst_ref=self.landing(self.band),
            send_sem=self.send_sem,
            recv_sem=self.recv_sem,
            device_id=(target, self.y),
            device_id_type=MESH,
        ).start()

    def start(self):
        for step in range(1, self.bands):
            self.send((self.band + step) % self.bands)

    def wait(self):
        bulk_copy(self.bulk(self.bands - 1), self.send_sem, self.recv_sem).wait_recv()

    def finish(self):
        bulk_copy(self.bulk(self.bands - 1), self.send_sem, self.recv_sem).wait_send()


def dot_nt(left, right):
    return lax.dot_general(left, right, (((1,), (1,)), ((), ())), preferred_element_type=F32)


def dot_tn(left, right):
    return lax.dot_general(left, right, (((0,), (0,)), ((), ())), preferred_element_type=F32)


def dot_nn(left, right):
    return jnp.dot(left, right, preferred_element_type=F32)


def unit_parts(rows):
    centred = rows - jnp.mean(rows, axis=-1, keepdims=True)
    inverse = lax.rsqrt(jnp.mean(centred * centred, axis=-1, keepdims=True) + EPS_BLOCK)
    return centred * inverse, inverse


class Block:
    def __init__(self, weights, down, refs):
        self.weights, self.down = weights, down
        self.__dict__.update(refs)
        self.width = weights.shape[1]
        self.halves = weights.shape[1] // (2 * HEAD_DIM)

    def weight(self, part):
        return self.weights[pl.ds(aligned(part * self.width), self.width), :]

    def masks(self):
        tokens = self.joint.shape[1]
        lane = lax.broadcasted_iota(jnp.int32, (tokens, 2 * HEAD_DIM), 1)
        low = lane < HEAD_DIM
        return low, low.astype(F32).astype(B16), (~low).astype(F32).astype(B16)

    def pair_rows(self, rows, low, high):
        return jnp.concatenate([rows * low, rows * high], axis=0)

    def project(self):
        unit, inverse = unit_parts(self.residual[...])
        normed = (unit * self.gain_one[...]).astype(B16)
        self.normed_one[...] = normed
        self.unit_one[...] = unit
        self.inverse_one[...] = jnp.broadcast_to(inverse, self.inverse_one.shape)

        @pl.loop(0, 3)
        def _(part):
            self.joint[part] = dot_nn(self.normed_one[...], self.weight(part)).astype(B16)

    def attend(self):
        tokens = self.joint.shape[1]
        scale = 1.0 / math.sqrt(HEAD_DIM)

        @pl.loop(0, self.halves)
        def _(pair):
            where, low, high = self.masks()
            lanes = pl.ds(pl.multiple_of(pair * 2 * HEAD_DIM, 2 * HEAD_DIM), 2 * HEAD_DIM)
            query, key, value = (self.joint[part, :, lanes] for part in range(3))
            scores = dot_nt(self.pair_rows(query, low, high), key) * scale
            raised = jnp.exp(scores - jnp.max(scores, axis=-1, keepdims=True))
            probs = raised / jnp.sum(raised, axis=-1, keepdims=True)
            self.probs[pair] = probs
            mixed = dot_nn(probs.astype(B16), value)
            self.mixed[:, lanes] = jnp.where(where, mixed[:tokens], mixed[tokens:]).astype(B16)

    def widen(self):
        middle = self.residual[...] + dot_nn(self.mixed[...], self.weight(3))
        unit, inverse = unit_parts(middle)
        self.normed_two[...] = (unit * self.gain_two[...]).astype(B16)
        self.unit_two[...] = unit
        self.inverse_two[...] = jnp.broadcast_to(inverse, self.inverse_two.shape)
        self.result[...] = middle

        @pl.loop(0, 4)
        def _(part):
            pre = dot_nn(self.normed_two[...], self.weight(4 + part))
            self.pre_act[part] = pre
            self.act[part] = gelu_tanh(pre).astype(B16)

    def narrow(self):
        @pl.loop(0, 4)
        def _(part):
            rows = pl.ds(aligned(part * self.width), self.width)
            self.result[...] += dot_nn(self.act[part], self.down[rows, :])

        self.block_out[...] = self.result[...].astype(B16)

    def back_narrow(self, part):
        rows = pl.ds(aligned(part * self.width), self.width)
        grad_act = dot_nt(self.out_grad[...], self.down[rows, :])
        grad_pre = (grad_act * gelu_slope(self.pre_act[part])).astype(B16)
        self.grad_pre[part] = grad_pre
        self.grad_normed[...] += dot_nt(grad_pre, self.weight(4 + part))

    def down_grad(self, part, store):
        turned = self.act[part].T
        for at in range(0, self.width, 256):
            store[pl.ds(aligned(part * self.width), self.width), at : at + 256] = dot_nn(
                turned, self.out_grad[:, at : at + 256]
            ).astype(B16)

    def pair_grad(self, first, second, first_grad, second_grad, store, offset):
        @pl.loop(0, 4)
        def _(group):
            rows = pl.ds(aligned(group * 192), 192)
            for at in range(0, self.width, 256):
                cols = slice(at, at + 256)
                one = dot_nn(first[rows, :], first_grad(cols))
                two = dot_nn(second[rows, :], second_grad(cols))
                for owner in range(8):
                    piece = jnp.concatenate(
                        [one[owner * 24 : owner * 24 + 24], two[owner * 24 : owner * 24 + 24]], axis=0
                    )
                    target = aligned((group * 8 + owner) * PART + offset)
                    store[pl.ds(target, CHUNK), cols] = piece.astype(B16)

    def back_wide(self):
        grad_normed = self.grad_normed[...]
        unit = self.unit_two[...]
        self.small[1:2, :] = jnp.sum(grad_normed * unit, axis=0, keepdims=True)
        scaled = grad_normed * self.gain_two[...]
        back = self.inverse_two[:, :1] * (
            scaled
            - jnp.mean(scaled, axis=-1, keepdims=True)
            - unit * jnp.mean(scaled * unit, axis=-1, keepdims=True)
        )
        grad_middle = self.out_grad[...].astype(F32) + back
        self.grad_middle[...] = grad_middle
        branch = grad_middle.astype(B16)
        self.grad_branch[...] = branch
        self.grad_mixed[...] = dot_nt(branch, self.weight(3)).astype(B16)
        self.turned_mixed[...] = self.mixed[...].T

    def back_attend(self):
        tokens = self.joint.shape[1]
        scale = 1.0 / math.sqrt(HEAD_DIM)

        @pl.loop(0, self.halves)
        def _(pair):
            where, low, high = self.masks()
            lanes = pl.ds(pl.multiple_of(pair * 2 * HEAD_DIM, 2 * HEAD_DIM), 2 * HEAD_DIM)
            query, key, value = (self.joint[part, :, lanes] for part in range(3))
            grads = self.pair_rows(self.grad_mixed[:, lanes], low, high)
            probs = self.probs[pair]
            self.grad_joint[2, :, lanes] = dot_tn(probs.astype(B16), grads).astype(B16)
            grad_probs = dot_nt(grads, value)
            total = jnp.sum(grad_probs * probs, axis=-1, keepdims=True)
            grad_scores = (probs * (grad_probs - total)).astype(B16)
            queries = dot_nn(grad_scores, key) * scale
            self.grad_joint[0, :, lanes] = jnp.where(
                where, queries[:tokens], queries[tokens:]
            ).astype(B16)
            keys = dot_tn(grad_scores, self.pair_rows(query, low, high)) * scale
            self.grad_joint[1, :, lanes] = keys.astype(B16)

    def back_project(self):
        self.grad_normed[...] = jnp.zeros(self.grad_normed.shape, F32)

        @pl.loop(0, 3)
        def _(part):
            self.grad_normed[...] += dot_nt(self.grad_joint[part], self.weight(part))

        grad_normed = self.grad_normed[...]
        unit = self.unit_one[...]
        self.small[0:1, :] = jnp.sum(grad_normed * unit, axis=0, keepdims=True)
        scaled = grad_normed * self.gain_one[...]
        back = self.inverse_one[:, :1] * (
            scaled
            - jnp.mean(scaled, axis=-1, keepdims=True)
            - unit * jnp.mean(scaled * unit, axis=-1, keepdims=True)
        )
        self.grad_middle[...] += back

    def embed_grad(self):
        return self.grad_middle[...].astype(B16)


def split3(rows):
    first = rows.astype(B16)
    rest = rows - first.astype(F32)
    second = rest.astype(B16)
    return first, second, (rest - second.astype(F32)).astype(B16)


def fold3(stacked):
    rows = stacked.shape[0] // 3
    return stacked[:rows] + (stacked[rows : 2 * rows] + stacked[2 * rows :])


def wide_nn(rows, weight):
    return fold3(dot_nn(jnp.concatenate(split3(rows), axis=0), weight))


def wide_nt(rows, weight):
    return fold3(dot_nt(jnp.concatenate(split3(rows), axis=0), weight))


def wide_tn(left, right):
    one, two = split3(left), split3(right)
    pairs = ((0, 0), (0, 1), (1, 0), (0, 2), (1, 1), (2, 0))
    return dot_tn(
        jnp.concatenate([one[a] for a, _ in pairs], axis=0),
        jnp.concatenate([two[b] for _, b in pairs], axis=0),
    )


def exact_dot(left, right, dims):
    return lax.dot_general(
        left, right, (dims, ((), ())), precision=PRECISE, preferred_element_type=F32
    )


def hyper_unit(rows):
    centred = rows - jnp.mean(rows, axis=-1, keepdims=True)
    inverse = lax.rsqrt(jnp.mean(centred * centred, axis=-1, keepdims=True) + EPS_HYPER)
    return centred * inverse, inverse


def unit_back(scaled, unit, inverse):
    return inverse * (
        scaled
        - jnp.mean(scaled, axis=-1, keepdims=True)
        - unit * jnp.mean(scaled * unit, axis=-1, keepdims=True)
    )


def by_head(rows):
    lane = lax.broadcasted_iota(jnp.int32, rows.shape, 1) // (rows.shape[1] // HHEADS)
    return jnp.concatenate([jnp.where(lane == head, rows, 0.0) for head in range(HHEADS)], axis=0)


def own_lanes(stacked):
    tokens = stacked.shape[0] // HHEADS
    out = jnp.zeros((tokens, stacked.shape[1]), F32)
    for head in range(HHEADS):
        rows = stacked[head * tokens : (head + 1) * tokens]
        lane = lax.broadcasted_iota(jnp.int32, rows.shape, 1) // (rows.shape[1] // HHEADS)
        out = out + jnp.where(lane == head, rows, 0.0)
    return out


def hyper_forward(waves, qkv, out, gain_one, up, down, gain_two):
    width = waves.shape[1]
    joint = wide_nn(waves, qkv)
    query, key, value = (joint[:, at * width : (at + 1) * width] for at in range(3))
    scores = exact_dot(by_head(query), key, ((1,), (1,))) / math.sqrt(width // HHEADS)
    raised = jnp.exp(scores - jnp.max(scores, axis=-1, keepdims=True))
    soft = raised / jnp.sum(raised, axis=-1, keepdims=True)
    mixed = own_lanes(exact_dot(soft, value, ((1,), (0,))))
    unit_one, inverse_one = hyper_unit(waves + wide_nn(mixed, out))
    first = unit_one * gain_one
    inner = wide_nn(first, up)
    unit_two, inverse_two = hyper_unit(first + wide_nn(gelu_tanh(inner), down))
    kept = (joint, soft, mixed, unit_one, inverse_one, inner, unit_two, inverse_two)
    return unit_two * gain_two, kept


def hyper_backward(grad_code, kept, waves, qkv, out, gain_one, up, down, gain_two):
    joint, soft, mixed, unit_one, inverse_one, inner, unit_two, inverse_two = kept
    width = waves.shape[1]
    query, key, value = (joint[:, at * width : (at + 1) * width] for at in range(3))
    first = unit_one * gain_one
    grad_gain_two = jnp.sum(grad_code * unit_two, axis=0, keepdims=True)
    grad_second = unit_back(grad_code * gain_two, unit_two, inverse_two)
    grad_down = wide_tn(gelu_tanh(inner), grad_second)
    grad_inner = wide_nt(grad_second, down) * gelu_slope(inner)
    grad_up = wide_tn(first, grad_inner)
    grad_first = grad_second + wide_nt(grad_inner, up)
    grad_gain_one = jnp.sum(grad_first * unit_one, axis=0, keepdims=True)
    grad_mid = unit_back(grad_first * gain_one, unit_one, inverse_one)
    grad_out = wide_tn(mixed, grad_mid)
    grad_mixed = by_head(wide_nt(grad_mid, out))
    grad_value = exact_dot(soft, grad_mixed, ((0,), (0,)))
    grad_soft = exact_dot(grad_mixed, value, ((1,), (1,)))
    total = jnp.sum(grad_soft * soft, axis=-1, keepdims=True)
    grad_scores = soft * (grad_soft - total) / math.sqrt(width // HHEADS)
    grad_query = own_lanes(exact_dot(grad_scores, key, ((1,), (0,))))
    grad_key = exact_dot(grad_scores, by_head(query), ((0,), (0,)))
    grad_qkv = wide_tn(waves, jnp.concatenate([grad_query, grad_key, grad_value], axis=1))
    return grad_qkv, grad_out, grad_gain_one, grad_up, grad_down, grad_gain_two


def spread(gathered, weights, part):
    width = weights.shape[1]
    half = CHUNK // 2

    @pl.loop(0, 16)
    def _(two):
        for pair in (0, 1):
            one, other = (
                gathered[part, pl.ds(aligned((two * 2 + k) * PART + pair * CHUNK), CHUNK), :].astype(F32)
                for k in (0, 1)
            )
            for k, rows in ((0, slice(0, half)), (1, slice(half, CHUNK))):
                target = pl.ds(aligned((4 * part + 2 * pair + k) * width + two * CHUNK), CHUNK)
                weights[target, :] = jnp.concatenate([one[rows], other[rows]], 0).astype(B16)


def swap_rows(rows):
    count = rows.shape[0]
    row = lax.broadcasted_iota(jnp.int32, (count, count), 0)
    col = lax.broadcasted_iota(jnp.int32, (count, count), 1)
    swap = (col == (row % 16) * 16 + row // 16).astype(F32).astype(B16)
    return dot_nn(swap, rows).astype(B16)


def rows16(ref, index):
    return ref.at[pl.ds(aligned(index * 16), 16)]


KEPT = ("joint", "soft", "mixed", "unit_one", "inverse_one", "inner", "unit_two", "inverse_two")


def layer_kernel(*refs):
    (pixels, kernel_gen, attn_qkv, attn_out, mlp_up, mlp_down, waves, hyper_qkv, hyper_out, hyper_gains, hyper_up, hyper_down,
     bias_gen, band_scale, out_grad, gains,
     block_out, pixel_out, shares, kernel_grads, code_out, code_grads, vectors, *rest_refs) = refs
    kept_refs, rest_refs = rest_refs[: len(KEPT)], rest_refs[len(KEPT) :]
    (gathered, weights, spare, pair_buf, buf, joint, probs, pre_act, act, grad_pre, mixed, normed_one, normed_two,
     unit_one, unit_two, inverse_one, inverse_two, grad_normed, grad_middle, grad_branch, grad_mixed, grad_joint,
     turned_mixed, turned_one, residual, pixel_rows, turned_pixels, mixing, kernels, sending,
     partner_grads, landed_grads, small, small_partner, small_all, code_part, code_all,
     pix_sem, gen_sem, front_done, narrow_done, *sems) = rest_refs
    z, x, core, y = place()
    band = lax.axis_index("band")
    bands = lax.axis_size("band")
    me = slot(z, x, core, y)
    width = gains.shape[1]
    tokens = out_grad.shape[0]
    partner = (band, 1 - y)
    own_rows = pl.ds(aligned(band * 16), 16)
    gather_sems, reduce_sems, embed_sems, grads_sems = (sems[at : at + 4] for at in (0, 4, 8, 12))
    kernel_sems, cols_sems, vec_sems, code_sems, half_sems, vec_half_sems = (
        sems[at : at + 2] for at in (16, 18, 20, 22, 24, 26)
    )

    def gen_copy(piece, target):
        return pltpu.make_async_copy(
            kernel_gen.at[:, pl.ds(piece * width, width)], target.at[pl.ds(piece * 128, 128)], gen_sem
        )

    def gen_wait(target):
        every = target.at[pl.ds(0, 16 * 128)]
        pltpu.make_async_copy(every, every, gen_sem).wait()

    barrier = pltpu.get_barrier_semaphore()
    tell_peers(barrier)
    for piece in range(16):
        gen_copy(piece, spare).start()
    load_pixels = pltpu.make_async_copy(pixels, pixel_rows, pix_sem)
    load_pixels.start()

    def rows_of(weight, piece):
        return weight[:, piece * width : (piece + 1) * width].astype(F32)

    pieces = [rows_of(attn_qkv, at) for at in range(3)] + [rows_of(attn_out, 0)]
    pieces += [rows_of(mlp_up, at) for at in range(4)]
    for at in range(4):
        rows = jnp.concatenate(pieces[2 * at : 2 * at + 2], axis=0).astype(B16)
        gathered[at // 2, pl.ds(aligned(me * PART + at % 2 * CHUNK), CHUNK), :] = rows
    gathered[2, pl.ds(aligned(me * PART), PART), :] = mlp_down[...]
    code, kept = hyper_forward(
        waves[...], hyper_qkv[...], hyper_out[...], hyper_gains[0:1, :], hyper_up[...], hyper_down[...], hyper_gains[1:2, :]
    )
    code_low = code.astype(B16)
    code_out[...] = code_low
    for ref, value in zip(kept_refs, kept):
        ref[...] = value

    def weight_view(part, block, side):
        where = slot(block[0], block[1], side, block[2])
        return gathered.at[part, pl.ds(aligned(where * PART), PART)]

    half = tokens // 2

    def image_row(block, side):
        return (block[0] * 4 + block[1] * 2 + side) * tokens

    def gather_at(known_z=None):
        return Gather(
            known_z, weight_view, ORDERS, lambda part, count: gathered.at[part, pl.ds(0, count * PART)], *gather_sems
        )

    def embed_at(known_z=None):
        return Reduce(
            known_z,
            1,
            lambda chunk, block, side: spare.at[pl.ds(aligned(image_row(block, side) + chunk * half), half)],
            ("xz", "xz"),
            lambda chunk: residual.at[pl.ds(chunk * half, half)],
            lambda part, block, side: spare.at[pl.ds(aligned(image_row(block, side)), tokens)],
            lambda part, rail: pair_buf.at[0, pl.ds(aligned(rail * tokens), tokens)],
            lambda chunk, where: pair_buf.at[1, pl.ds((chunk * 9 + where) * half, half)],
            lambda chunk, count: pair_buf.at[1, pl.ds(0, count * half)],
            lambda part, count: pair_buf.at[0, pl.ds(0, count * tokens)],
            *embed_sems,
        )

    def front_works(known_z):
        known, sums = gather_at(known_z), embed_at(known_z)
        works = [work for part in range(3) for work in in_order(known.events(part))]
        return works + in_order(sums.events(0, (0, 1)))

    gather, embed = gather_at(), embed_at()
    plan = Plan(FRONT_PLAN, [front_works(known_z) for known_z in range(4)])
    pl.semaphore_wait(barrier, bands)
    plan.run()
    for part in FIRST_PARTS:
        gather.start(part)
    plan.run()

    gen_wait(spare)

    @pl.loop(0, 16)
    def _(piece):
        part = dot_nn(code_out[...], spare[pl.ds(aligned(piece * 128), 128), :])
        mixing[pl.ds(aligned(piece * 16), 16), :] = part.astype(B16)

    sending[...] = swap_rows(mixing[...])
    spread_kernels = Exchange(
        lambda target: rows16(sending, target),
        lambda source: rows16(kernels, source),
        lambda count: kernels.at[pl.ds(0, count * 16)],
        *[sem.at[0] for sem in kernel_sems],
    )
    spread_kernels.start()
    plan.run()
    for part in range(3):
        if part not in FIRST_PARTS:
            gather.start(part)
    plan.run()
    kernels[own_rows, :] = sending[own_rows, :]
    biases = dot_nn(code_out[...], bias_gen[...])
    chosen = lax.broadcasted_iota(jnp.int32, biases.shape, 0) == band
    bias = jnp.sum(jnp.where(chosen, biases, 0.0), axis=0, keepdims=True)
    load_pixels.wait()
    for group in range(4):
        turned_pixels[group] = pixel_rows[4 * group : 4 * group + 4].reshape(4 * tokens, -1).T
    plan.run()
    spread_kernels.wait()

    def term(group):
        rows = pixel_rows[4 * group : 4 * group + 4].reshape(4 * tokens, -1)
        for at in range(0, width, 256):
            terms = dot_nn(rows, kernels[:, at : at + 256]) + bias[:, at : at + 256]
            for image in range(4):
                scale = band_scale[group * 4 + image][:1, :1]
                target = pl.ds((group * 4 + image) * tokens, tokens)
                spare[target, at : at + 256] = (terms[image * tokens : (image + 1) * tokens] * scale).astype(B16)

    for group in (3, 0, 2, 1):
        plan.run()
        term(group)
        embed.pair_start(0, [(group, 1, 0), (group, 0, 0)])
    plan.run()
    gather.wait_pairs(0)
    spread(gathered, weights, 0)

    names = dict(
        residual=residual, out_grad=out_grad, gain_one=gains.at[0:1], gain_two=gains.at[1:2], block_out=block_out,
        joint=joint, probs=probs, pre_act=pre_act, act=act,
        grad_pre=grad_pre, mixed=mixed, normed_one=normed_one, normed_two=normed_two, unit_one=unit_one,
        unit_two=unit_two, inverse_one=inverse_one, inverse_two=inverse_two, result=residual, grad_normed=grad_normed,
        grad_middle=grad_middle, grad_branch=grad_branch, grad_mixed=grad_mixed, grad_joint=grad_joint,
        turned_mixed=turned_mixed, small=small,
    )
    block = Block(weights, gathered.at[2], names)
    plan.run()
    block.project()
    plan.run()
    block.attend()
    plan.run()
    gather.wait_pairs(1)
    spread(gathered, weights, 1)
    plan.run()
    block.widen()
    plan.run()
    gather.wait_pairs(2)
    gather.finish()
    embed.finish()
    tell_near(front_done)
    block.narrow()
    plan.run()

    def part_ref(part):
        return spare if part == 2 else gathered.at[part]

    def part_view(part, blk, side):
        return part_ref(part).at[pl.ds(aligned(slot(blk[0], blk[1], side, blk[2]) * PART), PART)]

    def reduce_at(known_z=None):
        return Reduce(
            known_z,
            3,
            part_view,
            SUM_ORDERS,
            lambda part: shares.at[pl.ds(part * PART, PART)],
            part_view,
            lambda part, rail: pair_buf.at[part, pl.ds(aligned(rail * PART), PART)],
            lambda part, where: buf.at[part, where],
            lambda part, count: part_ref(part).at[pl.ds(0, count * PART)],
            lambda part, count: part_ref(part).at[pl.ds(0, count * PART)],
            *reduce_sems,
        )

    image_grads = gathered.at[2]

    def image_view(chunk, blk, side):
        return image_grads.at[pl.ds(aligned(image_row(blk, side) + chunk * half), half)]

    def grads_at(known_z=None):
        return Gather(
            known_z, image_view, ("zx", "zx"), lambda chunk, count: image_grads.at[pl.ds(0, count * half)], *grads_sems
        )

    def tail_works(known_z):
        known, images = reduce_at(known_z), grads_at(known_z)
        works = [work for part in (2, 1, 0) for work in in_order(known.events(part, (part,)))]
        return works + [work for chunk in (0, 1) for work in in_order(images.events(chunk))]

    reduce, grads = reduce_at(), grads_at()
    plan = Plan(TAIL_PLAN, [tail_works(known_z) for known_z in range(4)])
    grad_normed[...] = jnp.zeros(grad_normed.shape, F32)
    hear_near(front_done)
    plan.run()

    @pl.loop(0, 4)
    def _(step):
        odd = step % 2
        zz = (1 - odd) * (3 - step // 2) + odd * (step // 2)
        block.back_narrow(zz)
        block.down_grad(zz, spare)
        reduce.pair_start(2, [(zz, fx, fy) for fx, fy in ((1, 1), (1, 0), (0, 1), (0, 0))])

    tell_near(narrow_done)
    plan.run()
    block.back_wide()
    plan.run()
    block.back_attend()
    plan.run()
    block.back_project()
    hear_near(narrow_done)
    image_grads[pl.ds(aligned(band * tokens), tokens), :] = block.embed_grad()
    grads.start(0)
    grads.start(1)
    turned_one[...] = normed_two[...].T
    for part in (0, 2):
        plan.run()
        block.pair_grad(
            turned_one, turned_one, lambda cols, part=part: grad_pre[part, :, cols],
            lambda cols, part=part: grad_pre[part + 1, :, cols], part_ref(1), part // 2 * CHUNK,
        )
    reduce.pair_start(1)
    plan.run()
    turned_one[...] = normed_one[...].T
    block.pair_grad(
        turned_one, turned_one, lambda cols: grad_joint[0, :, cols], lambda cols: grad_joint[1, :, cols], part_ref(0), 0
    )
    plan.run()
    block.pair_grad(
        turned_one, turned_mixed, lambda cols: grad_joint[2, :, cols], lambda cols: grad_branch[:, cols], part_ref(0), CHUNK
    )
    reduce.pair_start(0)
    for piece in range(16):
        gen_copy(piece, weights).start()

    kernel_total = pre_act.at[0:2]
    kernel_total[...] = jnp.zeros(kernel_total.shape, F32)
    small[2:3, :] = jnp.zeros((1, width), F32)
    near_side = z // 2
    for side in (near_side, 1 - near_side):
        plan.run()
        for chunk in (0, 1):
            grads.wait_side(chunk, side)

        @pl.loop(0, 2)
        def _(step, side=side):
            group = 2 * side + step
            for image in range(4):
                rows = pl.ds(aligned((group * 4 + image) * tokens), tokens)
                scaled = image_grads[rows, :].astype(F32) * band_scale[group * 4 + image][:1, :1]
                small[2:3, :] += jnp.sum(scaled, axis=0, keepdims=True)
                act[image] = scaled.astype(B16)
            scaled = act[...].reshape(4 * tokens, width)
            pixel_rows[pl.ds(group * 4, 4)] = dot_nt(scaled, kernels[...]).astype(B16).reshape(4, tokens, -1)
            kernel_total[...] += dot_nn(turned_pixels[group], scaled).reshape(kernel_total.shape)

    store_pixels = pltpu.make_async_copy(pixel_rows, pixel_out, pix_sem)
    store_pixels.start()
    spread_kernels.finish()
    sending[...] = kernel_total[...].astype(B16).reshape(sending.shape)
    quarter = sending.shape[0] // 4

    def half_copy(piece):
        rows = pl.ds(piece * quarter, quarter)
        return pltpu.make_async_remote_copy(
            src_ref=sending.at[rows], dst_ref=partner_grads.at[rows], send_sem=half_sems[0].at[piece],
            recv_sem=half_sems[1].at[piece], device_id=partner, device_id_type=MESH,
        )

    for piece in range(4):
        half_copy(piece).start()
    vec_half = pltpu.make_async_remote_copy(
        src_ref=small, dst_ref=small_partner, send_sem=vec_half_sems[0].at[0], recv_sem=vec_half_sems[1].at[0],
        device_id=partner, device_id_type=MESH,
    )
    vec_half.start()
    columns = Exchange(
        lambda target: rows16(mixing, target),
        lambda source: rows16(landed_grads, source),
        lambda count: landed_grads.at[pl.ds(0, count * 16)],
        *[sem.at[0] for sem in cols_sems],
    )
    for piece in range(4):
        plan.run()
        half_copy(piece).wait_recv()
        rows = pl.ds(piece * quarter, quarter)
        mixing[rows, :] = sending[rows, :] + partner_grads[rows, :]
        for near in range(4):
            target = piece * 4 + near

            @pl.when(target != band)
            def _(target=target):
                columns.send(target)

    landed_grads[own_rows, :] = mixing[own_rows, :]
    plan.run()
    vec_half.wait_recv()
    small_all[band] = small[...] + small_partner[...]
    vector_spread = Exchange(
        lambda target: small_all.at[band], lambda source: small_all.at[source], lambda count: small_all.at[pl.ds(0, count)],
        *[sem.at[0] for sem in vec_sems],
    )
    vector_spread.start()
    plan.run()
    columns.wait()
    for piece in range(4):
        half_copy(piece).wait_send()
    sending[...] = swap_rows(landed_grads[...])
    store_columns = pltpu.make_async_copy(landed_grads, kernel_grads, pix_sem)
    gen_wait(weights)
    code_part[...] = jnp.zeros(code_part.shape, F32)

    @pl.loop(0, 16)
    def _(piece):
        code_part[...] += dot_nt(
            sending[pl.ds(aligned(piece * 16), 16), :], weights[pl.ds(aligned(piece * 128), 128), :]
        )

    code_all[band] = code_part[...]
    code_spread = Exchange(
        lambda target: code_all.at[band], lambda source: code_all.at[source], lambda count: code_all.at[pl.ds(0, count)],
        *[sem.at[0] for sem in code_sems],
    )
    code_spread.start()
    store_pixels.wait()
    store_columns.start()
    plan.run()
    vector_spread.wait()
    vectors[...] = small_all[...]
    code_spread.wait()
    total = code_all[0]
    for source in range(1, bands):
        total = total + code_all[source]
    code_grads[...] = total
    plan.run()
    reduce.finish()
    grads.finish()
    columns.finish()
    vec_half.wait_send()
    vector_spread.finish()
    code_spread.finish()
    store_columns.wait()


VMEM_BYTES = 63 * 2**20


def layer(pixels, kernel_gen, weights, waves, hyper, bias_gen, band_scale, out_grad, gains):
    width = gains.shape[1]
    bands = lax.axis_size("band")
    devices = bands * lax.axis_size("dp")
    images, tokens, pix = pixels.shape
    hidden = hyper[3].shape[1]
    vmem = pl.BlockSpec(memory_space=pltpu.VMEM)
    hbm = pl.BlockSpec(memory_space=pl.ANY)
    shape = jax.ShapeDtypeStruct
    rows = lambda kind, *lead: pltpu.VMEM((*lead, tokens, width), kind)
    dma = pltpu.SemaphoreType.DMA
    code = (bands, HW)
    kept = [(bands, 3 * HW), (HHEADS * bands, bands), code, code, (bands, 1), (bands, hidden), code, (bands, 1)]
    return pl.pallas_call(
        layer_kernel,
        out_shape=[
            shape((tokens, width), B16),
            shape(pixels.shape, B16),
            shape((3 * PART, width), F32),
            shape((pix, width), B16),
            shape(code, B16),
            shape(code, F32),
            shape((bands, 8, width), F32),
            *[shape(dims, F32) for dims in kept],
        ],
        in_specs=[hbm, hbm] + [vmem] * 14,
        out_specs=[vmem, hbm, vmem, hbm] + [vmem] * 11,
        scratch_shapes=[
            pltpu.VMEM((3, devices * PART, width), B16),
            pltpu.VMEM((8 * width, width), B16),
            pltpu.VMEM((devices * PART, width), B16),
            pltpu.VMEM((3, devices // 2 * PART, width), B16),
            pltpu.VMEM((3, 19, PART, width), B16),
            rows(B16, 3),
            pltpu.VMEM((HEADS // 2, 2 * tokens, tokens), F32),
            rows(F32, 4),
            rows(B16, 4),
            rows(B16, 4),
            rows(B16),
            rows(B16),
            rows(B16),
            rows(F32),
            rows(F32),
            pltpu.VMEM((tokens, 128), F32),
            pltpu.VMEM((tokens, 128), F32),
            rows(F32),
            rows(F32),
            rows(B16),
            rows(B16),
            rows(B16, 3),
            pltpu.VMEM((width, tokens), B16),
            pltpu.VMEM((width, tokens), B16),
            rows(F32),
            pltpu.VMEM(pixels.shape, B16),
            pltpu.VMEM((4, pix, 4 * tokens), B16),
            pltpu.VMEM((pix, width), B16),
            pltpu.VMEM((pix, width), B16),
            pltpu.VMEM((pix, width), B16),
            pltpu.VMEM((pix, width), B16),
            pltpu.VMEM((pix, width), B16),
            pltpu.VMEM((8, width), F32),
            pltpu.VMEM((8, width), F32),
            pltpu.VMEM((bands, 8, width), F32),
            pltpu.VMEM(code, F32),
            pltpu.VMEM((bands, *code), F32),
            dma,
            dma,
            pltpu.SemaphoreType.REGULAR,
            pltpu.SemaphoreType.REGULAR,
            *[dma((3, 3)), dma((3, 16)), dma((3, 2)), dma((3, 2))],
            *[dma((3, 2)), dma((3, 16)), dma((3, 3)), dma((3, 19))],
            *[dma((1, 2)), dma((1, 8)), dma((2, 2)), dma((2, 9))],
            *[dma((2, 3)), dma((2, 16)), dma((2, 2)), dma((2, 2))],
            *[dma((1,))] * 8,
            *[dma((4,))] * 2,
            *[dma((1,))] * 2,
        ],
        compiler_params=pltpu.CompilerParams(
            collective_id=0, has_side_effects=True, vmem_limit_bytes=VMEM_BYTES
        ),
        name="layer",
    )(pixels, kernel_gen, *weights, waves, *hyper, bias_gen, band_scale, out_grad, gains)


def finish_kernel(*refs):
    count = 12 + len(KEPT)
    block_in, pixel_in, *outside = refs[: count + 2]
    (block_out, pixel_out, grad_qkv, grad_out, grad_gain_one, grad_up, grad_down, grad_gain_two, grad_gen, grad_bias,
     gain_sums, share_qkv, share_out, share_up, share_down, *scratch) = refs[count + 2 :]
    inside, (store, in_sem, copy_sem, gen_sem) = scratch[:count], scratch[count:]
    loads = [pltpu.make_async_copy(*pair, in_sem.at[at]) for at, pair in enumerate(zip(outside, inside))]
    for load in loads:
        load.start()
    (code_low, columns, shares, waves, hyper_qkv, hyper_out, hyper_gains, hyper_up, hyper_down, bias_gen, code_grads, vectors,
     *kept_refs) = inside
    width = bias_gen.shape[1]
    copies = [
        pltpu.make_async_copy(block_in, block_out, copy_sem.at[0]),
        pltpu.make_async_copy(pixel_in, pixel_out, copy_sem.at[1]),
    ]
    for copy in copies:
        copy.start()
    for load in loads[:2]:
        load.wait()
    code = code_low[...]
    swapped = swap_rows(columns[...])
    gen_copies = []
    for piece in range(16):
        slot_at = piece % store.shape[0]
        if piece >= store.shape[0]:
            gen_copies[piece - store.shape[0]].wait()
        store[slot_at] = dot_tn(code, swapped[piece * 16 : (piece + 1) * 16])
        gen_copies.append(
            pltpu.make_async_copy(
                store.at[slot_at], grad_gen.at[:, pl.ds(piece * width, width)], gen_sem.at[slot_at]
            )
        )
        gen_copies[-1].start()
    for load in loads[2:]:
        load.wait()
    share_qkv[...] = jnp.concatenate([shares[at * 24 : at * 24 + 24, :] for at in range(3)], axis=1)
    share_out[...] = shares[72:96, :]
    share_up[...] = jnp.concatenate([shares[at * 24 : at * 24 + 24, :] for at in range(4, 8)], axis=1)
    share_down[...] = shares[192:288, :]
    gain_sums[...] = jnp.sum(vectors[...], axis=0)
    bias_grads = vectors[:, 2, :]
    grad_bias[...] = dot_tn(jnp.concatenate([code] * 3, axis=0), jnp.concatenate(split3(bias_grads), axis=0))
    grad_code = code_grads[...] + wide_nt(bias_grads, bias_gen[...])
    grads = hyper_backward(
        grad_code, [ref[...] for ref in kept_refs], waves[...], hyper_qkv[...], hyper_out[...], hyper_gains[0:1, :],
        hyper_up[...], hyper_down[...], hyper_gains[1:2, :],
    )
    for ref, value in zip((grad_qkv, grad_out, grad_gain_one, grad_up, grad_down, grad_gain_two), grads):
        ref[...] = value
    for copy in copies + gen_copies[-store.shape[0] :]:
        copy.wait()


def finish(waves, hyper, bias_gen, code_low, code_grads, vectors, columns, shares, block_out, pixel_grad, kept, kernel_gen, weights):
    width = bias_gen.shape[1]
    vmem = pl.BlockSpec(memory_space=pltpu.VMEM)
    hbm = pl.BlockSpec(memory_space=pl.ANY)
    shape = lambda array: jax.ShapeDtypeStruct(array.shape, F32)
    line = jax.ShapeDtypeStruct((1, HW), F32)
    operands = (code_low, columns, shares, waves, *hyper, bias_gen, code_grads, vectors, *kept)
    return pl.pallas_call(
        finish_kernel,
        out_shape=[
            jax.ShapeDtypeStruct(block_out.shape, B16),
            jax.ShapeDtypeStruct(pixel_grad.shape, B16),
            shape(hyper[0]), shape(hyper[1]), line, shape(hyper[3]), shape(hyper[4]), line,
            shape(kernel_gen), shape(bias_gen), jax.ShapeDtypeStruct((8, width), F32),
            *[shape(weight) for weight in weights],
        ],
        in_specs=[hbm] * (2 + len(operands)),
        out_specs=[hbm, hbm] + [vmem] * 6 + [hbm] + [vmem] * 6,
        scratch_shapes=[
            *[pltpu.VMEM(operand.shape, operand.dtype) for operand in operands],
            pltpu.VMEM((4, HW, width), F32),
            pltpu.SemaphoreType.DMA((len(operands),)),
            pltpu.SemaphoreType.DMA((2,)),
            pltpu.SemaphoreType.DMA((4,)),
        ],
        compiler_params=pltpu.CompilerParams(vmem_limit_bytes=40 * 2**20),
        name="finish",
    )(block_out, pixel_grad, *operands)


def body(
    pixels,
    wavelengths,
    band_counts,
    band_mask,
    hyper_qkv,
    hyper_out,
    hyper_gain1,
    hyper_up,
    hyper_down,
    hyper_gain2,
    kernel_gen,
    bias_gen,
    norm_gain1,
    attn_qkv,
    attn_out,
    norm_gain2,
    mlp_up,
    mlp_down,
    out_grad,
):
    f32 = jnp.float32
    b16 = jnp.bfloat16
    band_local = pixels.shape[3]
    pixel_local = pixels[0]
    model_width = bias_gen.shape[1]
    hyper_params = tuple(
        (
            weight.astype(f32)
            for weight in (hyper_qkv, hyper_out, hyper_gain1, hyper_up, hyper_down, hyper_gain2)
        )
    )
    wave_tokens = wave_embed(wavelengths, HW)
    band_code, hyper_pull = jax.vjp(lambda *params: hyper_net(wave_tokens, *params), *hyper_params)
    code_low = band_code.astype(b16)
    column_part = jnp.dot(code_low, kernel_gen, preferred_element_type=f32).astype(b16)
    kernel_rows = lax.all_to_all(column_part, "band", split_axis=0, concat_axis=1, tiled=True)
    kernels = kernel_rows.reshape(band_local, -1, model_width)
    first_band = lax.axis_index("band") * band_local
    own_code = lax.dynamic_slice_in_dim(code_low, first_band, band_local, 0)
    count_row = band_counts[0]
    biases = jnp.dot(own_code, bias_gen, preferred_element_type=f32)
    slot_ids = first_band + jnp.arange(band_local, dtype=jnp.int32)
    active = (slot_ids[None, :] < count_row[:, None]) & (band_mask[0] == 1)
    band_weight = jnp.where(active, lax.rsqrt(count_row.astype(f32))[:, None], f32(0.0))
    pixel_rows = pixel_local
    weight_rows = band_weight
    conv_out = jnp.einsum("inbp,bpd->inbd", pixel_rows, kernels, preferred_element_type=f32)
    residual = lax.psum_scatter(
        jnp.sum((conv_out + biases[None, None]) * weight_rows[:, None, :, None], axis=2),
        "band",
        scatter_dimension=0,
        tiled=True,
    )
    gathered = (
        lax.all_gather(attn_qkv, ("band", "dp"), axis=0, tiled=True),
        lax.all_gather(attn_out, ("band", "dp"), axis=0, tiled=True),
        lax.all_gather(mlp_up, ("band", "dp"), axis=0, tiled=True),
        lax.all_gather(mlp_down, ("band", "dp"), axis=0, tiled=True),
    )
    qkv_full, out_full, up_full, down_full = gathered
    gain_one = norm_gain1.astype(f32)
    gain_two = norm_gain2.astype(f32)
    images, tokens = (residual.shape[0], residual.shape[1])
    score_scale = 1.0 / math.sqrt(HEAD_DIM)
    normed_full, unit_one, inverse_one = norm_parts(residual, gain_one)
    normed_one = normed_full.astype(b16)
    joint_rows = jnp.einsum("ind,de->ine", normed_one, qkv_full, preferred_element_type=f32).astype(
        b16
    )
    queries = joint_rows[..., :model_width].reshape(images, tokens, HEADS, HEAD_DIM)
    key_rows = joint_rows[..., model_width : 2 * model_width].reshape(
        images, tokens, HEADS, HEAD_DIM
    )
    value_rows = joint_rows[..., 2 * model_width :].reshape(images, tokens, HEADS, HEAD_DIM)
    scores = (
        jnp.einsum("inhc,imhc->ihnm", queries, key_rows, preferred_element_type=f32) * score_scale
    )
    row_top = jnp.max(scores, axis=-1, keepdims=True)
    log_total = row_top + jnp.log(jnp.sum(jnp.exp(scores - row_top), axis=-1, keepdims=True))
    probs_full = jnp.exp(scores - log_total)
    probs_low = probs_full.astype(b16)
    mixed_low = (
        jnp.einsum("ihnm,imhc->inhc", probs_low, value_rows, preferred_element_type=f32)
        .reshape(images, tokens, model_width)
        .astype(b16)
    )
    middle = residual + jnp.einsum("ind,de->ine", mixed_low, out_full, preferred_element_type=f32)
    normed_two_full, unit_two, inverse_two = norm_parts(middle, gain_two)
    normed_two = normed_two_full.astype(b16)
    pre_act = jnp.einsum("ind,df->inf", normed_two, up_full, preferred_element_type=f32)
    act_low = gelu_tanh(pre_act).astype(b16)
    result = middle + jnp.einsum("inf,fd->ind", act_low, down_full, preferred_element_type=f32)
    block_out = result.astype(b16)[None]
    qkv_back, out_back, up_back, down_back = (
        lax.all_gather(attn_qkv, ("band", "dp"), axis=0, tiled=True),
        lax.all_gather(attn_out, ("band", "dp"), axis=0, tiled=True),
        lax.all_gather(mlp_up, ("band", "dp"), axis=0, tiled=True),
        lax.all_gather(mlp_down, ("band", "dp"), axis=0, tiled=True),
    )
    grad_top = out_grad[0]
    grad_down = jnp.einsum("inf,ind->fd", act_low, grad_top, preferred_element_type=f32)
    grad_act = jnp.einsum("ind,fd->inf", grad_top, down_back, preferred_element_type=f32)
    grad_pre = (grad_act * gelu_slope(pre_act)).astype(b16)
    grad_up = jnp.einsum("ind,inf->df", normed_two, grad_pre, preferred_element_type=f32)
    grad_normed_two = jnp.einsum("inf,df->ind", grad_pre, up_back, preferred_element_type=f32)
    grad_gain_two = jnp.sum(grad_normed_two * unit_two, axis=(0, 1))
    grad_middle = grad_top.astype(f32) + norm_back(grad_normed_two, gain_two, unit_two, inverse_two)
    grad_branch = grad_middle.astype(b16)
    grad_out_proj = jnp.einsum("ind,ine->de", mixed_low, grad_branch, preferred_element_type=f32)
    grad_mixed = (
        jnp.einsum("ine,de->ind", grad_branch, out_back, preferred_element_type=f32)
        .astype(b16)
        .reshape(images, tokens, HEADS, HEAD_DIM)
    )
    grad_values = jnp.einsum("ihnm,inhc->imhc", probs_low, grad_mixed, preferred_element_type=f32)
    grad_probs = jnp.einsum("inhc,imhc->ihnm", grad_mixed, value_rows, preferred_element_type=f32)
    grad_scores = (
        probs_full * (grad_probs - jnp.sum(grad_probs * probs_full, axis=-1, keepdims=True))
    ).astype(b16)
    grad_queries = (
        jnp.einsum("ihnm,imhc->inhc", grad_scores, key_rows, preferred_element_type=f32)
        * score_scale
    )
    grad_keys = (
        jnp.einsum("ihnm,inhc->imhc", grad_scores, queries, preferred_element_type=f32)
        * score_scale
    )
    grad_joint = jnp.concatenate(
        [
            grad_queries.reshape(images, tokens, model_width),
            grad_keys.reshape(images, tokens, model_width),
            grad_values.reshape(images, tokens, model_width),
        ],
        axis=-1,
    ).astype(b16)
    grad_qkv = jnp.einsum("ind,ine->de", normed_one, grad_joint, preferred_element_type=f32)
    grad_normed_one = jnp.einsum("ine,de->ind", grad_joint, qkv_back, preferred_element_type=f32)
    grad_gain_one = jnp.sum(grad_normed_one * unit_one, axis=(0, 1))
    grad_embed = grad_middle + norm_back(grad_normed_one, gain_one, unit_one, inverse_one)
    grad_embed_low = grad_embed.astype(b16)[None]
    grad_rows = lax.all_gather(grad_embed_low, "band", axis=1, tiled=True)[0].astype(f32)
    weight_rows = band_weight
    pixel_rows = pixel_local
    scaled = grad_rows[:, :, None, :] * weight_rows[:, None, :, None]
    bias_total = jnp.sum(scaled, axis=(0, 1))
    scaled_low = scaled.astype(b16)
    kernel_total = jnp.einsum("inbp,inbd->bpd", pixel_rows, scaled_low, preferred_element_type=f32)
    pixel_part = jnp.einsum(
        "inbd,bpd->inbp", scaled_low, kernels, preferred_element_type=f32
    ).astype(b16)
    pixel_total = pixel_part
    kernel_grad, bias_grad, pixel_total = (kernel_total, bias_total, pixel_total)
    pixel_out = pixel_total[None]
    kernel_grad_low = kernel_grad.reshape(band_local, -1).astype(b16)
    grad_columns = lax.all_to_all(kernel_grad_low, "band", split_axis=1, concat_axis=0, tiled=True)
    grad_kernel_part = jnp.einsum("nh,nc->hc", code_low, grad_columns, preferred_element_type=f32)
    grad_code_part = jnp.einsum("nc,hc->nh", grad_columns, kernel_gen, preferred_element_type=f32)
    bias_back = jnp.einsum("bd,hd->bh", bias_grad, bias_gen.astype(f32), precision=PRECISE)
    grad_code_part = grad_code_part + lax.dynamic_update_slice_in_dim(
        jnp.zeros_like(grad_code_part), bias_back, first_band, 0
    )
    grad_bias_part = jnp.einsum("bh,bd->hd", own_code.astype(f32), bias_grad, precision=PRECISE)
    grad_code, grad_bias_gen, grad_norm_gain1, grad_norm_gain2 = lax.psum(
        (grad_code_part, grad_bias_part, grad_gain_one, grad_gain_two), ("band", "dp")
    )
    grad_kernel_gen = lax.psum(grad_kernel_part.astype(jnp.bfloat16), "dp").astype(jnp.float32)
    hyper_grads = hyper_pull(grad_code)
    shares = (
        lax.psum_scatter(grad_qkv, ("band", "dp"), scatter_dimension=0, tiled=True),
        lax.psum_scatter(grad_out_proj, ("band", "dp"), scatter_dimension=0, tiled=True),
        lax.psum_scatter(grad_up, ("band", "dp"), scatter_dimension=0, tiled=True),
        lax.psum_scatter(grad_down, ("band", "dp"), scatter_dimension=0, tiled=True),
    )
    return (
        block_out,
        pixel_out,
        hyper_grads[0],
        hyper_grads[1],
        hyper_grads[2],
        hyper_grads[3],
        hyper_grads[4],
        hyper_grads[5],
        grad_kernel_gen,
        grad_bias_gen,
        grad_norm_gain1,
        shares[0],
        shares[1],
        grad_norm_gain2,
        shares[2],
        shares[3],
    )


def fast_body(
    pixels,
    wavelengths,
    band_counts,
    band_mask,
    hyper_qkv,
    hyper_out,
    hyper_gain1,
    hyper_up,
    hyper_down,
    hyper_gain2,
    kernel_gen,
    bias_gen,
    norm_gain1,
    attn_qkv,
    attn_out,
    norm_gain2,
    mlp_up,
    mlp_down,
    out_grad,
):
    waves = wave_embed(wavelengths, HW)
    band = lax.axis_index("band")
    count_row = band_counts[0]
    active = (band < count_row) & (band_mask[0, :, 0] == 1)
    band_weight = jnp.where(active, lax.rsqrt(count_row.astype(F32)), F32(0.0))
    weights = (attn_qkv, attn_out, mlp_up, mlp_down)
    hyper_gains = jnp.stack([hyper_gain1, hyper_gain2]).astype(F32)
    hyper = (hyper_qkv, hyper_out, hyper_gains, hyper_up, hyper_down)
    block_out, pixel_grad, shares, columns, code_low, code_grads, vectors, *kept = layer(
        pixels[0, :, :, 0],
        kernel_gen,
        weights,
        waves,
        hyper,
        bias_gen,
        jnp.broadcast_to(band_weight[:, None, None], (band_weight.shape[0], 8, 128)),
        out_grad[0, 0],
        jnp.stack([norm_gain1, norm_gain2]).astype(F32),
    )
    outs = finish(
        waves,
        hyper,
        bias_gen,
        code_low,
        code_grads,
        vectors,
        columns,
        shares,
        block_out,
        pixel_grad,
        kept,
        kernel_gen,
        weights,
    )
    block_out, pixel_grad, *hyper_grads, grad_gen, grad_bias, gain_sums = outs[:11]
    hyper_grads[2], hyper_grads[5] = hyper_grads[2][0], hyper_grads[5][0]
    return (
        block_out[None, None],
        pixel_grad[None, :, :, None],
        *hyper_grads,
        grad_gen,
        grad_bias,
        gain_sums[0],
        outs[11],
        outs[12],
        gain_sums[1],
        outs[13],
        outs[14],
    )


def solution(mesh):
    placed = (
        P("dp", None, None, "band", None),
        P(),
        P("dp", None),
        P("dp", None, "band"),
        P(),
        P(),
        P(),
        P(),
        P(),
        P(),
        P(None, "band"),
        P(),
        P(),
        P(("band", "dp"), None),
        P(("band", "dp"), None),
        P(),
        P(("band", "dp"), None),
        P(("band", "dp"), None),
        P("dp", "band", None, None),
    )
    one_slot = (mesh.shape["band"], mesh.shape["dp"]) == (16, 2)
    return jax.shard_map(
        fast_body if one_slot else body,
        mesh=mesh,
        in_specs=placed,
        out_specs=(
            P("dp", "band", None, None),
            P("dp", None, None, "band", None),
            P(),
            P(),
            P(),
            P(),
            P(),
            P(),
            P(None, "band"),
            P(),
            P(),
            P(("band", "dp"), None),
            P(("band", "dp"), None),
            P(),
            P(("band", "dp"), None),
            P(("band", "dp"), None),
        ),
        check_vma=False,
    )
```

```python
import functools
import math

import jax
import jax.numpy as jnp
from jax import lax
from jax.experimental import pallas as pl
from jax.experimental.pallas import tpu as pltpu
from jax.sharding import PartitionSpec as P

HEADS = 12
HEAD_DIM = 64
HW = 128
HHEADS = 4


PRECISE = lax.Precision.HIGHEST
EPS_BLOCK = 1e-06
EPS_HYPER = 1e-05
GELU_COEF = 0.7978845608028654


def gelu_tanh(tensor):
    return (
        0.5 * tensor * (1.0 + jnp.tanh(GELU_COEF * (tensor + 0.044715 * tensor * tensor * tensor)))
    )


def gelu_slope(tensor):
    tanh_val = jnp.tanh(GELU_COEF * (tensor + 0.044715 * tensor * tensor * tensor))
    return 0.5 * (1.0 + tanh_val) + 0.5 * tensor * (1.0 - tanh_val * tanh_val) * GELU_COEF * (
        1.0 + 3.0 * 0.044715 * tensor * tensor
    )


def layer_norm(tensor, gain_vec, epsilon):
    centred = tensor - jnp.mean(tensor, axis=-1, keepdims=True)
    return (
        centred
        * lax.rsqrt(jnp.mean(centred * centred, axis=-1, keepdims=True) + epsilon)
        * gain_vec
    )


def norm_parts(tensor, gain_vec):
    centred = tensor - jnp.mean(tensor, axis=-1, keepdims=True)
    inverse = lax.rsqrt(jnp.mean(centred * centred, axis=-1, keepdims=True) + EPS_BLOCK)
    unit_rows = centred * inverse
    return (unit_rows * gain_vec, unit_rows, inverse)


def norm_back(grad_rows, gain_vec, unit_rows, inverse):
    scaled = grad_rows * gain_vec
    return inverse * (
        scaled
        - jnp.mean(scaled, axis=-1, keepdims=True)
        - unit_rows * jnp.mean(scaled * unit_rows, axis=-1, keepdims=True)
    )


def wave_embed(wave_ints, token_width):
    half_width = token_width // 2
    frequency = jnp.power(10000.0, -jnp.arange(half_width, dtype=jnp.float32) / half_width)
    angles = wave_ints.astype(jnp.float32)[:, None] * frequency[None, :]
    return jnp.concatenate([jnp.sin(angles), jnp.cos(angles)], axis=1)


def hyper_net(wave_tokens, qkv_weight, out_weight, gain_one, up_weight, down_weight, gain_two):
    tokens, token_width = wave_tokens.shape
    head_size = token_width // HHEADS
    qkv_rows = jnp.dot(wave_tokens, qkv_weight, precision=PRECISE)
    queries = qkv_rows[:, :token_width].reshape(tokens, HHEADS, head_size)
    key_rows = qkv_rows[:, token_width : 2 * token_width].reshape(tokens, HHEADS, head_size)
    value_rows = qkv_rows[:, 2 * token_width :].reshape(tokens, HHEADS, head_size)
    scores = jnp.einsum("nhc,mhc->hnm", queries, key_rows, precision=PRECISE) / math.sqrt(head_size)
    weights_soft = jax.nn.softmax(scores, axis=-1)
    mixed_rows = jnp.einsum("hnm,mhc->nhc", weights_soft, value_rows, precision=PRECISE).reshape(
        tokens, token_width
    )
    first_norm = layer_norm(
        wave_tokens + jnp.dot(mixed_rows, out_weight, precision=PRECISE), gain_one, EPS_HYPER
    )
    inner_act = gelu_tanh(jnp.dot(first_norm, up_weight, precision=PRECISE))
    return layer_norm(
        first_norm + jnp.dot(inner_act, down_weight, precision=PRECISE), gain_two, EPS_HYPER
    )


MESH = pl.DeviceIdType.MESH
B16 = jnp.bfloat16
F32 = jnp.float32
CHUNK = 48
DIMS = "xyz"
PART = 96
FRONT_PLAN = (
    (
        (),
        (),
        (),
        (),
        (1, 2, 3, 30),
        (54, 27),
        (),
        (11, 29, 57),
        (),
        (56,),
        (13, 10, 5, 33, 60, 81, 85, 59, 39, 82, 86, 32, 22, 83, 84, 35, 17, 87, 95, 62, 45, 88, 96, 9, 47, 66, 93, 101, 65, 21, 94, 102, 38, 14, 41, 49, 72, 68, 24, 74, 71, 51, 18, 44, 76, 104, 107, 26, 106, 108, 78),
        (53,),
        (80,),
        (),
        (),
        (),
        (),
    ),
    (
        (),
        (),
        (),
        (0, 1, 2, 3),
        (30, 54, 27),
        (28, 7, 57),
        (),
        (29,),
        (55, 11, 6),
        (56,),
        (58, 13, 10, 5, 31, 33, 60, 59, 81, 89, 36, 82, 32, 91, 39, 83, 35, 84, 19, 62, 63, 22, 87, 97, 65, 17, 88, 99, 38, 42, 98, 66, 93, 103, 100, 45, 94, 105, 104, 107, 47, 106, 108, 69, 49, 14, 72, 24, 74),
        (),
        (76,),
        (),
        (),
        (),
        (),
    ),
    (
        (),
        (),
        (),
        (0, 1, 2, 3),
        (30,),
        (54, 27),
        (),
        (29, 7, 57),
        (28,),
        (56, 11, 6),
        (55, 59, 13, 10, 4, 32, 33, 60, 58, 81, 39, 82, 31, 36, 83, 90, 34, 84, 92, 19, 87, 61, 22, 88, 64, 104, 15, 66, 106, 37, 93, 98, 45, 97, 94, 100, 99, 42, 63, 103, 107, 46, 105, 108, 72, 48, 12, 69, 23, 73),
        (),
        (75,),
        (),
        (),
        (),
        (),
    ),
    (
        (),
        (),
        (),
        (),
        (0, 2, 3, 30, 54, 27),
        (28, 7, 57),
        (),
        (),
        (13, 6, 55),
        (),
        (4, 33, 60, 81, 58, 36, 82, 31, 19, 83, 85, 84, 86, 34, 15, 63, 61, 42, 87, 101, 8, 46, 88, 102, 93, 95, 64, 94, 96, 20, 37, 12, 40, 69, 48, 67, 73, 23, 70, 16, 50, 43, 75, 103, 107, 25, 105, 108, 77),
        (52,),
        (79,),
        (),
        (),
        (),
        (),
    ),
)
TAIL_PLAN = (
    (
        (),
        (),
        (),
        (),
        (),
        (),
        (),
        (),
        (),
        (),
        (),
        (81, 94, 0, 3, 1, 7, 2, 4, 8, 13, 29, 84, 11, 17, 30, 97, 12, 20, 31, 87, 100, 14, 23, 33, 82, 32, 37, 95, 22, 88, 36, 40, 101, 26, 42, 41),
        (90, 103, 46, 43, 92, 49, 58, 105),
        (59, 60, 61, 52, 62, 64, 65, 63, 68, 51, 53, 69, 73, 70, 55, 24, 57, 71, 72, 76),
        (),
        (28, 78),
        (79,),
    ),
    (
        (),
        (),
        (),
        (),
        (),
        (),
        (),
        (),
        (),
        (),
        (),
        (80, 81, 93, 94, 0, 1, 2, 4, 8, 29, 84, 11, 30, 5, 97, 12, 31, 9, 14, 33, 16, 15, 82, 37, 19, 95, 18, 85, 40, 21, 88, 41, 98, 25),
        (101, 22, 90, 43, 34, 26, 58, 103, 38),
        (59, 60, 45, 61, 44, 48, 62, 50, 47, 65, 63, 68, 69, 70, 24, 54, 51, 53, 71, 66, 55, 72, 74),
        (),
        (57, 75, 77, 28),
        (78, 79),
    ),
    (
        (),
        (),
        (),
        (),
        (),
        (),
        (),
        (),
        (),
        (),
        (),
        (80, 81, 93, 94, 0, 1, 2, 4, 8, 29, 83, 11, 30, 96, 6, 12, 31, 10, 15, 14, 33, 22, 82, 18, 37, 95, 26, 21, 85, 40, 16, 88, 25, 41, 98, 19, 101, 43),
        (89, 35, 102, 58, 39),
        (59, 44, 60, 61, 47, 45, 62, 51, 48, 65, 63, 68, 69, 50, 53, 70, 24, 55, 54, 71, 67, 57, 78),
        (),
        (72, 74, 28, 77, 79, 75),
        (),
    ),
    (
        (),
        (),
        (),
        (),
        (),
        (),
        (),
        (),
        (),
        (),
        (),
        (80, 93, 0, 1, 2, 3, 4, 7, 8, 20, 29, 83, 11, 30, 23, 96, 12, 31, 86, 13, 99, 14, 33, 17, 82, 37, 32, 95, 21, 85, 40, 36, 25, 98, 41),
        (89, 42, 102, 43, 46, 91, 58, 49, 104),
        (59, 60, 61, 62, 52, 65, 63, 64, 68, 50, 53, 69, 76, 70, 24, 54, 57, 71, 72, 73),
        (),
        (28, 77, 79),
        (),
    ),
)
FIRST_PARTS = (0,)
SUM_ORDERS = ('yxz', 'yzx', 'xzy')
ORDERS = ("zxy", "xzy", "yzx")


def place(known_z=None):
    band = lax.axis_index("band")
    z = band // 4 if known_z is None else known_z
    return (z, (band // 2) % 2, band % 2, lax.axis_index("dp"))


def device(z, x, core, y):
    return (z * 4 + x * 2 + core, y)


def slot(z, x, core, y):
    return (z * 4 + x * 2 + core) * 2 + y


def when(cond, run):
    if isinstance(cond, bool):
        if cond:
            run()
    else:
        pl.when(cond)(run)


def both(first, second):
    return second if first is True else first & second


def aligned(rows):
    return pl.multiple_of(rows, 16)


def tell_peers(barrier):
    band, y = lax.axis_index("band"), lax.axis_index("dp")
    bands = lax.axis_size("band")
    for step in range(bands):
        for plane in (y, 1 - y) if step else (1 - y,):
            pl.semaphore_signal(
                barrier, inc=1, device_id=((band + step) % bands, plane), device_id_type=MESH
            )


def tell_near(semaphore):
    z, x, core, y = place()
    near = [
        (device(z, x, 1 - core, y), True),
        (device(z, 1 - x, core, y), True),
        (device(z, x, core, 1 - y), True),
        (device(z + 1, x, core, y), z < 3),
        (device(z - 1, x, core, y), z > 0),
    ]
    for target, cond in near:
        when(
            cond,
            functools.partial(
                pl.semaphore_signal, semaphore, inc=1, device_id=target, device_id_type=MESH
            ),
        )


def hear_near(semaphore):
    z = place()[0]
    pl.semaphore_wait(semaphore, 5 - z // 3 - (3 - z) // 3)


def bulk_copy(ref, send_sem, recv_sem):
    band, y = lax.axis_index("band"), lax.axis_index("dp")
    return pltpu.make_async_remote_copy(
        src_ref=ref,
        dst_ref=ref,
        send_sem=send_sem,
        recv_sem=recv_sem,
        device_id=(band, 1 - y),
        device_id_type=MESH,
    )


def in_order(events):
    return [work for _, _, work in sorted(events, key=lambda event: event[:2])]


class Plan:
    def __init__(self, table, catalogues):
        self.table, self.catalogues = table, catalogues
        self.at = 0

    def run(self):
        z = place()[0]
        for known_z, works in enumerate(self.catalogues):
            chosen = self.table[known_z][self.at]
            if not chosen:
                continue

            @pl.when(z == known_z)
            def _(works=works, chosen=chosen):
                for index in chosen:
                    works[index]()

        self.at += 1


class Gather:
    def __init__(self, known_z, view, orders, bulk, send_sem, recv_sem, pair_send, pair_recv):
        self.view, self.orders, self.bulk = view, orders, bulk
        self.send_sem, self.recv_sem = send_sem, recv_sem
        self.pair_send, self.pair_recv = pair_send, pair_recv
        self.z, self.x, self.core, self.y = place(known_z)

    def rail(self, block):
        return block[0] * 4 + block[1] * 2 + block[2]

    def sibling(self):
        return device(self.z, self.x, 1 - self.core, self.y)

    def send(self, chunk, block, dim, cond, direction=0):
        z, x, core, y = self.z, self.x, self.core, self.y
        if dim == "x":
            targets = [(device(z, 1 - x, core, y), cond)]
        elif dim == "y":
            targets = [(device(z, x, core, 1 - y), cond)]
        else:
            targets = []
            if direction >= 0:
                targets.append((device(z + 1, x, core, y), both(cond, z < 3)))
            if direction <= 0:
                targets.append((device(z - 1, x, core, y), both(cond, z > 0)))
        src = self.view(chunk, block, core)
        for target, needed in targets:
            if needed is False:
                continue
            copy = pltpu.make_async_remote_copy(
                src_ref=src,
                dst_ref=src,
                send_sem=self.send_sem.at[chunk, DIMS.index(dim)],
                recv_sem=self.recv_sem.at[chunk, self.rail(block)],
                device_id=target,
                device_id_type=MESH,
            )
            when(needed, copy.start)

    def pair(self, chunk, block, core):
        src = self.view(chunk, block, core)
        return pltpu.make_async_remote_copy(
            src_ref=src,
            dst_ref=src,
            send_sem=self.pair_send.at[chunk, block[0] // 2],
            recv_sem=self.pair_recv.at[chunk, block[0] // 2],
            device_id=self.sibling(),
            device_id_type=MESH,
        )

    def start(self, chunk):
        own = (self.z, self.x, self.y)
        for dim in self.orders[chunk]:
            self.send(chunk, own, dim, True)
        self.pair(chunk, own, self.core).start()

    def events(self, chunk, start=0.0, pace=1.0):
        held, found = [(0, 0, 0, 0, start)], []
        for dim in self.orders[chunk]:
            clock, new = 0.0, []
            ordered = sorted(held, key=lambda item: item[4])
            if dim == "z":
                for dist in (1, 2, 3):
                    for item in ordered:
                        clock = max(clock, item[4]) + pace
                        new += [(dist, way, item[2], item[3], clock) for way in (1, -1)]
            else:
                for item in ordered:
                    clock = max(clock, item[4]) + pace
                    flip = (1, item[3]) if dim == "x" else (item[2], 1)
                    new.append((item[0], item[1], *flip, clock))
            found += [
                (item[4], chunk, functools.partial(self.arrive, chunk, dim, item)) for item in new
            ]
            held = held + new
        return found

    def arrive(self, chunk, dim, item):
        dist, way, flip_x, flip_y, _ = item
        cond = True
        if way == 1:
            cond = self.z >= dist
        elif way == -1:
            cond = self.z + dist <= 3
        if cond is False:
            return
        block = (
            self.z - dist * way,
            1 - self.x if flip_x else self.x,
            1 - self.y if flip_y else self.y,
        )
        src = self.view(chunk, block, self.core)
        arriving = pltpu.make_async_remote_copy(
            src_ref=src,
            dst_ref=src,
            send_sem=self.send_sem.at[chunk, 0],
            recv_sem=self.recv_sem.at[chunk, self.rail(block)],
            device_id=self.sibling(),
            device_id_type=MESH,
        )
        when(cond, arriving.wait_recv)
        if dim == "z":
            self.send(chunk, block, "z", cond, way)
        order = self.orders[chunk]
        for later in order[order.index(dim) + 1 :]:
            self.send(chunk, block, later, cond)
        when(cond, self.pair(chunk, block, self.core).start)

    def rails(self, chunk):
        return 16 if "y" in self.orders[chunk] else 8

    def sent(self, chunk, z, over):
        order = self.orders[chunk]
        fresh = (z < 3) + (z > 0) if over == "z" else 1
        total = fresh if over in order else 0
        for _, _, work in self.events(chunk):
            _, dim, (dist, way, *_) = work.args
            if (way == 1 and z < dist) or (way == -1 and z + dist > 3):
                continue
            total += fresh if over in order[order.index(dim) + 1 :] else 0
            if dim == "z" and over == "z":
                total += z < 3 if way == 1 else z > 0
        return total

    def wait_side(self, chunk, side):
        every = self.bulk(chunk, self.rails(chunk) // 2)
        bulk_copy(every, self.pair_send.at[chunk, side], self.pair_recv.at[chunk, side]).wait_recv()

    def wait_pairs(self, chunk):
        for side in (0, 1):
            self.wait_side(chunk, side)

    def finish(self):
        ends = (self.z == 0) | (self.z == 3)
        inner = (self.z == 1) | (self.z == 2)
        for chunk in range(len(self.orders)):
            for dim in self.orders[chunk]:
                send_sem = self.send_sem.at[chunk, DIMS.index(dim)]
                for cond, z in ((ends, 0), (inner, 1)):
                    copy = bulk_copy(self.bulk(chunk, self.sent(chunk, z, dim)), send_sem, self.recv_sem.at[chunk, 0])
                    when(cond, copy.wait_send)
            every = self.bulk(chunk, self.rails(chunk) // 2)
            for side in (0, 1):
                bulk_copy(every, self.pair_send.at[chunk, side], self.pair_recv.at[chunk, side]).wait_send()


class Reduce:
    def __init__(self, known_z, view, orders, final, buf, bulk, send, recv):
        self.view, self.orders, self.final = view, orders, final
        self.buf, self.bulk = buf, bulk
        self.send_sem, self.recv_sem = send, recv
        self.z, self.x, self.core, self.y = place(known_z)
        self.index = [self.places(chunk) for chunk in range(len(orders))]

    def coords(self, block):
        zz, flip_x, flip_y = block
        return (zz, 1 - self.x if flip_x else self.x, 1 - self.y if flip_y else self.y)

    def own(self, chunk, block):
        return self.view(chunk, self.coords(block))

    def add(self, target, source):
        target[...] = target[...] + source[...]

    def sibling(self):
        return device(self.z, self.x, 1 - self.core, self.y)

    def blocks(self):
        return [(zz, fx, fy) for zz in (3, 0, 2, 1) for fx, fy in self.flips(0, 0)]

    def places(self, chunk):
        order, keys = self.orders[chunk], []
        for stage, dim in enumerate(order):
            if dim == "z":
                keys += [
                    self.z_key(stage, step, way, flips)
                    for step in range(3)
                    for way in ((1, -1) if step else (1,))
                    for flips in self.flips(chunk, stage)
                ]
                continue
            wheres = range(4) if "z" in order[stage:] else ("own",)
            later = self.flips(chunk, stage + 1)
            keys += [(stage, where, *flips) for where in wheres for flips in later]
        return {key: at for at, key in enumerate(keys)}

    def place_of(self, chunk, key):
        return self.index[chunk][key]

    def send(self, chunk, block, key, target, cond):
        if cond is False:
            return
        where = self.place_of(chunk, key)
        copy = pltpu.make_async_remote_copy(
            src_ref=self.own(chunk, block),
            dst_ref=self.buf(chunk, where),
            send_sem=self.send_sem.at[chunk, key[0]],
            recv_sem=self.recv_sem.at[chunk, where],
            device_id=target,
            device_id_type=MESH,
        )
        when(cond, copy.start)

    def landed(self, chunk, key):
        return self.buf(chunk, self.place_of(chunk, key))

    def wait(self, chunk, key):
        landed = self.landed(chunk, key)
        pltpu.make_async_remote_copy(
            src_ref=landed,
            dst_ref=landed,
            send_sem=self.send_sem.at[chunk, 0],
            recv_sem=self.recv_sem.at[chunk, self.place_of(chunk, key)],
            device_id=self.sibling(),
            device_id_type=MESH,
        ).wait_recv()

    def flips(self, chunk, stage):
        left = self.orders[chunk][stage:]
        return [
            (fx, fy)
            for fx in ((1, 0) if "x" in left else (0,))
            for fy in ((1, 0) if "y" in left else (0,))
        ]

    def ready(self, chunk, stage, block):
        order = self.orders[chunk]
        zz, fx, fy = block
        where = zz if "z" in order[stage:] else "own"
        if order[stage] == "x" and fx:
            target = device(self.z, 1 - self.x, self.core, self.y)
            self.send(chunk, block, (stage, where, 0, fy), target, True)
        elif order[stage] == "y" and fy:
            target = device(self.z, self.x, self.core, 1 - self.y)
            self.send(chunk, block, (stage, where, fx, 0), target, True)

    def z_key(self, stage, step, way, flips):
        return (stage, step, way if step else 0, *flips)

    def z_start(self, chunk, stage, step, flips):
        up, down = (3 - step, *flips), (step, *flips)
        right = device(self.z + 1, self.x, self.core, self.y)
        left = device(self.z - 1, self.x, self.core, self.y)
        self.send(chunk, up, self.z_key(stage, step, 1, flips), right, self.z == 0)
        self.send(chunk, down, self.z_key(stage, step, -1, flips), left, self.z == 3)

    def z_arrive(self, chunk, stage, step, flips, way):
        z = self.z if way == 1 else 3 - self.z
        cond = (z >= 1) & (z <= step + 1)
        zz = 2 + z - step
        zz = zz if way == 1 else 3 - zz
        block = (zz, *flips)
        key = self.z_key(stage, step, way, flips)
        last = stage + 1 == len(self.orders[chunk]) and step == 2

        def take():
            self.wait(chunk, key)
            if not last:
                self.add(self.own(chunk, block), self.landed(chunk, key))

        when(cond, take)
        if step < 2:
            target = device(self.z + way, self.x, self.core, self.y)
            self.send(chunk, block, self.z_key(stage, step + 1, way, flips), target, cond)

    def z_done(self, chunk, stage, flips):
        block = (self.z, *flips)
        if stage + 1 < len(self.orders[chunk]):
            self.ready(chunk, stage + 1, block)
            return
        final = self.final(chunk)
        final[...] = self.own(chunk, block)[...].astype(F32)
        for way, cond in ((1, self.z >= 1), (-1, self.z <= 2)):
            landed = self.landed(chunk, self.z_key(stage, 2, way, flips))

            def add(landed=landed):
                final[...] += landed[...].astype(F32)

            when(cond, add)

    def xy_arrive(self, chunk, stage, zz, fx, fy):
        key = (stage, zz, fx, fy)
        block = (self.z if zz == "own" else zz, fx, fy)
        self.wait(chunk, key)
        own, landed = self.own(chunk, block), self.landed(chunk, key)
        if stage + 1 < len(self.orders[chunk]):
            self.add(own, landed)
            self.ready(chunk, stage + 1, block)
        else:
            final = self.final(chunk)
            final[...] = own[...].astype(F32) + landed[...].astype(F32)

    def start(self, chunk, block):
        self.ready(chunk, 0, block)

    def events(self, chunks, start=0.0, pace=1.0):
        found = []
        for chunk in chunks:
            times = {block: start for block in self.blocks()}
            for stage, dim in enumerate(self.orders[chunk]):
                clock, later = 0.0, {}
                if dim == "z":
                    for step in range(3):
                        for flips in self.flips(chunk, stage):
                            needed = (0, 3) if step == 0 else (0, 1, 2, 3)
                            clock = max(clock, *(times[(zz, *flips)] for zz in needed)) + 0.001
                            work = functools.partial(self.z_start, chunk, stage, step, flips)
                            found.append((clock, chunk, work))
                            clock += pace
                            for way in (1, -1):
                                work = functools.partial(self.z_arrive, chunk, stage, step, flips, way)
                                found.append((clock, chunk, work))
                            later[("own", *flips)] = clock + 0.001
                    for flips in self.flips(chunk, stage):
                        work = functools.partial(self.z_done, chunk, stage, flips)
                        found.append((later[("own", *flips)], chunk, work))
                else:
                    pick = 1 if dim == "x" else 2
                    for key in sorted((k for k in times if k[pick]), key=lambda k: times[k]):
                        mine = (key[0], 0, key[2]) if dim == "x" else (key[0], key[1], 0)
                        clock = max(max(clock, times[key]) + pace, times[mine] + 0.001)
                        later[mine] = clock
                        work = functools.partial(self.xy_arrive, chunk, stage, *mine)
                        found.append((clock, chunk, work))
                times = later
        return found

    def finish(self):
        for chunk, order in enumerate(self.orders):
            for stage, dim in enumerate(order):
                after = len(self.flips(chunk, stage + 1)) if stage + 1 < len(order) else 1
                count = 3 * after if dim == "z" else after * (4 if "z" in order[stage + 1 :] else 1)
                every = self.bulk(chunk, count)
                bulk_copy(every, self.send_sem.at[chunk, stage], self.recv_sem.at[chunk, 0]).wait_send()


class Exchange:
    def __init__(self, source, landing, bulk, send_sem, recv_sem):
        self.source, self.landing, self.bulk = source, landing, bulk
        self.send_sem, self.recv_sem = send_sem, recv_sem
        self.band, self.y = lax.axis_index("band"), lax.axis_index("dp")
        self.bands = lax.axis_size("band")

    def send(self, target):
        pltpu.make_async_remote_copy(
            src_ref=self.source(target),
            dst_ref=self.landing(self.band),
            send_sem=self.send_sem,
            recv_sem=self.recv_sem,
            device_id=(target, self.y),
            device_id_type=MESH,
        ).start()

    def start(self):
        for step in range(1, self.bands):
            self.send((self.band + step) % self.bands)

    def wait(self):
        bulk_copy(self.bulk(self.bands - 1), self.send_sem, self.recv_sem).wait_recv()

    def finish(self):
        bulk_copy(self.bulk(self.bands - 1), self.send_sem, self.recv_sem).wait_send()


def dot_nt(left, right):
    return lax.dot_general(left, right, (((1,), (1,)), ((), ())), preferred_element_type=F32)


def dot_tn(left, right):
    return lax.dot_general(left, right, (((0,), (0,)), ((), ())), preferred_element_type=F32)


def dot_nn(left, right):
    return jnp.dot(left, right, preferred_element_type=F32)


def unit_parts(rows):
    centred = rows - jnp.mean(rows, axis=-1, keepdims=True)
    inverse = lax.rsqrt(jnp.mean(centred * centred, axis=-1, keepdims=True) + EPS_BLOCK)
    return centred * inverse, inverse


class Block:
    def __init__(self, weights, down, refs):
        self.weights, self.down = weights, down
        self.__dict__.update(refs)
        self.width = weights.shape[1]
        self.tokens = self.joint.shape[1]
        self.halves = weights.shape[1] // (2 * HEAD_DIM)

    def weight(self, part):
        return self.weights[pl.ds(aligned(part * self.width), self.width), :]

    def masks(self):
        tokens = self.joint.shape[1]
        lane = lax.broadcasted_iota(jnp.int32, (tokens, 2 * HEAD_DIM), 1)
        low = lane < HEAD_DIM
        return low, low.astype(F32).astype(B16), (~low).astype(F32).astype(B16)

    def pair_rows(self, rows, low, high):
        return jnp.concatenate([rows * low, rows * high], axis=0)

    def own(self, ref):
        return ref[: self.tokens]

    def project(self):
        unit, inverse = unit_parts(self.residual[...])
        self.normed_one[: self.tokens] = (unit * self.gain_one[...]).astype(B16)
        self.unit_one[...] = unit
        self.inverse_one[...] = jnp.broadcast_to(inverse, self.inverse_one.shape)

        @pl.loop(0, 3)
        def _(part):
            self.joint[part] = dot_nn(self.own(self.normed_one), self.weight(part)).astype(B16)

    def attend(self):
        tokens = self.joint.shape[1]
        scale = 1.0 / math.sqrt(HEAD_DIM)

        @pl.loop(0, self.halves)
        def _(pair):
            where, low, high = self.masks()
            lanes = pl.ds(pl.multiple_of(pair * 2 * HEAD_DIM, 2 * HEAD_DIM), 2 * HEAD_DIM)
            query, key, value = (self.joint[part, :, lanes] for part in range(3))
            scores = dot_nt(self.pair_rows(query, low, high), key) * scale
            raised = jnp.exp(scores - jnp.max(scores, axis=-1, keepdims=True))
            probs = raised / jnp.sum(raised, axis=-1, keepdims=True)
            self.probs[pair] = probs
            mixed = dot_nn(probs.astype(B16), value)
            self.mixed[:tokens, lanes] = jnp.where(where, mixed[:tokens], mixed[tokens:]).astype(B16)

    def widen(self):
        middle = self.residual[...] + dot_nn(self.own(self.mixed), self.weight(3))
        unit, inverse = unit_parts(middle)
        self.normed_two[: self.tokens] = (unit * self.gain_two[...]).astype(B16)
        self.unit_two[...] = unit
        self.inverse_two[...] = jnp.broadcast_to(inverse, self.inverse_two.shape)
        self.result[...] = middle

        @pl.loop(0, 4)
        def _(part):
            pre = dot_nn(self.own(self.normed_two), self.weight(4 + part))
            self.pre_act[part] = pre
            self.act[part, : self.tokens] = gelu_tanh(pre).astype(B16)

    def narrow(self):
        @pl.loop(0, 4)
        def _(part):
            rows = pl.ds(aligned(part * self.width), self.width)
            self.result[...] += dot_nn(self.act[part, : self.tokens], self.down[rows, :])

        self.block_out[...] = self.result[...].astype(B16)

    def back_narrow(self):
        self.grad_normed[...] = jnp.zeros(self.grad_normed.shape, F32)

        @pl.loop(0, 4)
        def _(part):
            rows = pl.ds(aligned(part * self.width), self.width)
            grad_act = dot_nt(self.own(self.out_grad), self.down[rows, :])
            grad_pre = (grad_act * gelu_slope(self.pre_act[part])).astype(B16)
            self.grad_pre[part, : self.tokens] = grad_pre
            self.grad_normed[...] += dot_nt(grad_pre, self.weight(4 + part))

    def down_grad(self, part, core, store):
        self.turned[...] = self.act[part].T
        for x in (0, 1):
            rows = self.turned[pl.ds(aligned((x * 2 + core) * 2 * PART), 2 * PART), :]
            for at in range(0, self.width, 256):
                cols = slice(at, at + 256)
                store[(part * 4 + x * 2) * PART : (part * 4 + x * 2 + 2) * PART, cols] = dot_nn(
                    rows, self.out_grad[:, cols]
                ).astype(B16)

    def turn_rail(self, which, ref, core):
        self.turned[...] = ref[...].T
        for chip in range(8):
            self.rail_rows[which, chip * CHUNK : (chip + 1) * CHUNK, :] = self.turned[
                pl.ds(aligned((chip * 2 + core) * CHUNK), CHUNK), :
            ]

    def pair_grad(self, first, second, first_grad, second_grad, store, offset):
        half = CHUNK // 2
        for at in range(0, self.width, 256):
            cols = slice(at, at + 256)
            one = dot_nn(self.rail_rows[first], first_grad(cols))
            two = dot_nn(self.rail_rows[second], second_grad(cols))
            for owner in range(16):
                rows = slice(owner * half, owner * half + half)
                piece = jnp.concatenate([one[rows], two[rows]], axis=0)
                store[owner * PART + offset : owner * PART + offset + CHUNK, cols] = piece.astype(B16)

    def back_wide(self):
        grad_normed = self.grad_normed[...]
        unit = self.unit_two[...]
        self.small[1:2, :] = jnp.sum(grad_normed * unit, axis=0, keepdims=True)
        scaled = grad_normed * self.gain_two[...]
        back = self.inverse_two[:, :1] * (
            scaled
            - jnp.mean(scaled, axis=-1, keepdims=True)
            - unit * jnp.mean(scaled * unit, axis=-1, keepdims=True)
        )
        grad_middle = self.own(self.out_grad).astype(F32) + back
        self.grad_middle[...] = grad_middle
        branch = grad_middle.astype(B16)
        self.grad_branch[: self.tokens] = branch
        self.grad_mixed[...] = dot_nt(branch, self.weight(3)).astype(B16)

    def back_attend(self):
        tokens = self.joint.shape[1]
        scale = 1.0 / math.sqrt(HEAD_DIM)

        @pl.loop(0, self.halves)
        def _(pair):
            where, low, high = self.masks()
            lanes = pl.ds(pl.multiple_of(pair * 2 * HEAD_DIM, 2 * HEAD_DIM), 2 * HEAD_DIM)
            query, key, value = (self.joint[part, :, lanes] for part in range(3))
            grads = self.pair_rows(self.grad_mixed[:, lanes], low, high)
            probs = self.probs[pair]
            self.grad_joint[2, :tokens, lanes] = dot_tn(probs.astype(B16), grads).astype(B16)
            grad_probs = dot_nt(grads, value)
            total = jnp.sum(grad_probs * probs, axis=-1, keepdims=True)
            grad_scores = (probs * (grad_probs - total)).astype(B16)
            queries = dot_nn(grad_scores, key) * scale
            self.grad_joint[0, :tokens, lanes] = jnp.where(
                where, queries[:tokens], queries[tokens:]
            ).astype(B16)
            keys = dot_tn(grad_scores, self.pair_rows(query, low, high)) * scale
            self.grad_joint[1, :tokens, lanes] = keys.astype(B16)

    def back_project(self):
        self.grad_normed[...] = jnp.zeros(self.grad_normed.shape, F32)

        @pl.loop(0, 3)
        def _(part):
            self.grad_normed[...] += dot_nt(self.grad_joint[part, : self.tokens], self.weight(part))

        grad_normed = self.grad_normed[...]
        unit = self.unit_one[...]
        self.small[0:1, :] = jnp.sum(grad_normed * unit, axis=0, keepdims=True)
        scaled = grad_normed * self.gain_one[...]
        back = self.inverse_one[:, :1] * (
            scaled
            - jnp.mean(scaled, axis=-1, keepdims=True)
            - unit * jnp.mean(scaled * unit, axis=-1, keepdims=True)
        )
        self.grad_middle[...] += back

    def embed_grad(self):
        return self.grad_middle[...].astype(B16)


def split3(rows):
    first = rows.astype(B16)
    rest = rows - first.astype(F32)
    second = rest.astype(B16)
    return first, second, (rest - second.astype(F32)).astype(B16)


def fold3(stacked):
    rows = stacked.shape[0] // 3
    return stacked[:rows] + (stacked[rows : 2 * rows] + stacked[2 * rows :])


def wide_nn(rows, weight):
    return fold3(dot_nn(jnp.concatenate(split3(rows), axis=0), weight))


def wide_nt(rows, weight):
    return fold3(dot_nt(jnp.concatenate(split3(rows), axis=0), weight))


def wide_tn(left, right):
    one, two = split3(left), split3(right)
    pairs = ((0, 0), (0, 1), (1, 0), (0, 2), (1, 1), (2, 0))
    return dot_tn(
        jnp.concatenate([one[a] for a, _ in pairs], axis=0),
        jnp.concatenate([two[b] for _, b in pairs], axis=0),
    )


def exact_dot(left, right, dims):
    return lax.dot_general(
        left, right, (dims, ((), ())), precision=PRECISE, preferred_element_type=F32
    )


def hyper_unit(rows):
    centred = rows - jnp.mean(rows, axis=-1, keepdims=True)
    inverse = lax.rsqrt(jnp.mean(centred * centred, axis=-1, keepdims=True) + EPS_HYPER)
    return centred * inverse, inverse


def unit_back(scaled, unit, inverse):
    return inverse * (
        scaled
        - jnp.mean(scaled, axis=-1, keepdims=True)
        - unit * jnp.mean(scaled * unit, axis=-1, keepdims=True)
    )


def by_head(rows):
    lane = lax.broadcasted_iota(jnp.int32, rows.shape, 1) // (rows.shape[1] // HHEADS)
    return jnp.concatenate([jnp.where(lane == head, rows, 0.0) for head in range(HHEADS)], axis=0)


def own_lanes(stacked):
    tokens = stacked.shape[0] // HHEADS
    out = jnp.zeros((tokens, stacked.shape[1]), F32)
    for head in range(HHEADS):
        rows = stacked[head * tokens : (head + 1) * tokens]
        lane = lax.broadcasted_iota(jnp.int32, rows.shape, 1) // (rows.shape[1] // HHEADS)
        out = out + jnp.where(lane == head, rows, 0.0)
    return out


def hyper_forward(waves, qkv, out, gain_one, up, down, gain_two):
    width = waves.shape[1]
    joint = wide_nn(waves, qkv)
    query, key, value = (joint[:, at * width : (at + 1) * width] for at in range(3))
    scores = exact_dot(by_head(query), key, ((1,), (1,))) / math.sqrt(width // HHEADS)
    raised = jnp.exp(scores - jnp.max(scores, axis=-1, keepdims=True))
    soft = raised / jnp.sum(raised, axis=-1, keepdims=True)
    mixed = own_lanes(exact_dot(soft, value, ((1,), (0,))))
    unit_one, inverse_one = hyper_unit(waves + wide_nn(mixed, out))
    first = unit_one * gain_one
    inner = wide_nn(first, up)
    unit_two, inverse_two = hyper_unit(first + wide_nn(gelu_tanh(inner), down))
    kept = (joint, soft, mixed, unit_one, inverse_one, inner, unit_two, inverse_two)
    return unit_two * gain_two, kept


def hyper_backward(grad_code, kept, waves, qkv, out, gain_one, up, down, gain_two):
    joint, soft, mixed, unit_one, inverse_one, inner, unit_two, inverse_two = kept
    width = waves.shape[1]
    query, key, value = (joint[:, at * width : (at + 1) * width] for at in range(3))
    first = unit_one * gain_one
    grad_gain_two = jnp.sum(grad_code * unit_two, axis=0, keepdims=True)
    grad_second = unit_back(grad_code * gain_two, unit_two, inverse_two)
    grad_down = wide_tn(gelu_tanh(inner), grad_second)
    grad_inner = wide_nt(grad_second, down) * gelu_slope(inner)
    grad_up = wide_tn(first, grad_inner)
    grad_first = grad_second + wide_nt(grad_inner, up)
    grad_gain_one = jnp.sum(grad_first * unit_one, axis=0, keepdims=True)
    grad_mid = unit_back(grad_first * gain_one, unit_one, inverse_one)
    grad_out = wide_tn(mixed, grad_mid)
    grad_mixed = by_head(wide_nt(grad_mid, out))
    grad_value = exact_dot(soft, grad_mixed, ((0,), (0,)))
    grad_soft = exact_dot(grad_mixed, value, ((1,), (1,)))
    total = jnp.sum(grad_soft * soft, axis=-1, keepdims=True)
    grad_scores = soft * (grad_soft - total) / math.sqrt(width // HHEADS)
    grad_query = own_lanes(exact_dot(grad_scores, key, ((1,), (0,))))
    grad_key = exact_dot(grad_scores, by_head(query), ((0,), (0,)))
    grad_qkv = wide_tn(waves, jnp.concatenate([grad_query, grad_key, grad_value], axis=1))
    return grad_qkv, grad_out, grad_gain_one, grad_up, grad_down, grad_gain_two


def spread(gathered, weights, part):
    width = weights.shape[1]
    half = CHUNK // 2

    @pl.loop(0, 16)
    def _(two):
        for pair in (0, 1):
            one, other = (
                gathered[part, pl.ds(aligned((two * 2 + k) * PART + pair * CHUNK), CHUNK), :].astype(F32)
                for k in (0, 1)
            )
            for k, rows in ((0, slice(0, half)), (1, slice(half, CHUNK))):
                target = pl.ds(aligned((4 * part + 2 * pair + k) * width + two * CHUNK), CHUNK)
                weights[target, :] = jnp.concatenate([one[rows], other[rows]], 0).astype(B16)


def swap_rows(rows):
    count = rows.shape[0]
    row = lax.broadcasted_iota(jnp.int32, (count, count), 0)
    col = lax.broadcasted_iota(jnp.int32, (count, count), 1)
    swap = (col == (row % 16) * 16 + row // 16).astype(F32).astype(B16)
    return dot_nn(swap, rows).astype(B16)


def rows16(ref, index):
    return ref.at[pl.ds(aligned(index * 16), 16)]


KEPT = ("joint", "soft", "mixed", "unit_one", "inverse_one", "inner", "unit_two", "inverse_two", "gains")
SHARED = ("out_grad", "normed_one", "mixed", "normed_two", "act0", "act1", "act2", "act3")
SHARED += ("pre0", "pre1", "pre2", "pre3", "grad_branch", "joint0", "joint1", "joint2")


def layer_kernel(*refs):
    (counts, mask, pixels, kernel_gen, attn_qkv, attn_out, mlp_up, mlp_down, waves, hyper_qkv, hyper_out, hyper_one, hyper_two,
     hyper_up, hyper_down, bias_gen, out_grad_in, norm_one, norm_two,
     block_out, pixel_out, shares, kernel_grads, code_out, code_grads, vectors, *rest_refs) = refs
    kept_refs, rest_refs = rest_refs[: len(KEPT)], rest_refs[len(KEPT) :]
    (gathered, weights, spare, buf, joint, probs, pre_act, act, grad_pre, out_grad, mixed, normed_one, normed_two,
     unit_one, unit_two, inverse_one, inverse_two, grad_normed, grad_middle, grad_branch, grad_mixed, grad_joint,
     turned, rail_rows, residual, pixel_rows, turned_pixels, pair_pixels, mixing, kernels, pair_kernels, sending,
     landed_grads, summed, small, small_partner, small_all, code_part, code_all, gains, band_scale, pair_scale,
     pix_sem, gen_sem, front_done, narrow_done, *sems) = rest_refs
    z, x, core, y = place()
    band = lax.axis_index("band")
    bands = lax.axis_size("band")
    me = slot(z, x, core, y)
    width = gains.shape[1]
    tokens = out_grad_in.shape[0]
    sibling = (band + 1 - 2 * core, y)
    partner = (band, 1 - y)
    own_rows = pl.ds(aligned(band * 16), 16)
    gather_sems, grads_sems = sems[0:4], sems[4:8]
    reduce_sems, embed_sems, share_sems, front_sems, kernel_sems, cols_sems, summed_sems, vec_half_sems, vec_sems, code_sems = (
        sems[at : at + 2] for at in range(8, 28, 2)
    )

    def to_pair(index, source, target, pair=share_sems):
        return pltpu.make_async_remote_copy(
            src_ref=source,
            dst_ref=target,
            send_sem=pair[0].at[index],
            recv_sem=pair[1].at[index],
            device_id=sibling,
            device_id_type=MESH,
        )

    def shared(name):
        index = SHARED.index(name)
        ref = dict(
            out_grad=out_grad, normed_one=normed_one, mixed=mixed, normed_two=normed_two, grad_branch=grad_branch
        ).get(name)
        if ref is None:
            ref = dict(act=act, pre=grad_pre, joint=grad_joint)[name[:-1]].at[int(name[-1])]
        return to_pair(index, ref.at[pl.ds(0, tokens)], ref.at[pl.ds(tokens, tokens)])

    def gen_copy(piece, target):
        return pltpu.make_async_copy(
            kernel_gen.at[:, pl.ds(piece * width, width)], target.at[pl.ds(piece * 128, 128)], gen_sem
        )

    def gen_wait(target):
        every = target.at[pl.ds(0, 16 * 128)]
        pltpu.make_async_copy(every, every, gen_sem).wait()

    barrier = pltpu.get_barrier_semaphore()
    tell_peers(barrier)
    for piece in range(16):
        gen_copy(piece, spare).start()
    load_pixels = pltpu.make_async_copy(pixels, pixel_rows, pix_sem)
    load_pixels.start()

    gains[0:1, :] = norm_one[...].astype(F32).reshape(1, width)
    gains[1:2, :] = norm_two[...].astype(F32).reshape(1, width)
    out_grad[0:tokens, :] = out_grad_in[...]
    for image in range(band_scale.shape[0]):
        used = jnp.where((band < counts[image]) & (mask[image] == 1), 1.0, 0.0)
        bands_here = jnp.full(band_scale.shape[1:], counts[image], jnp.int32).astype(F32)
        band_scale[image] = lax.rsqrt(bands_here) * used

    def rows_of(weight, piece):
        return weight[:, piece * width : (piece + 1) * width].astype(F32)

    pieces = [rows_of(attn_qkv, at) for at in range(3)] + [rows_of(attn_out, 0)]
    pieces += [rows_of(mlp_up, at) for at in range(4)]
    for at in range(4):
        rows = jnp.concatenate(pieces[2 * at : 2 * at + 2], axis=0).astype(B16)
        gathered[at // 2, pl.ds(aligned(me * PART + at % 2 * CHUNK), CHUNK), :] = rows
    gathered[2, pl.ds(aligned(me * PART), PART), :] = mlp_down[...]
    hyper_gains = [gain[...].astype(F32).reshape(1, HW) for gain in (hyper_one, hyper_two)]
    code, kept = hyper_forward(
        waves[...], hyper_qkv[...], hyper_out[...], hyper_gains[0], hyper_up[...], hyper_down[...], hyper_gains[1]
    )
    kept = (*kept, jnp.concatenate(hyper_gains, axis=0))
    code_low = code.astype(B16)
    code_out[...] = code_low
    for ref, value in zip(kept_refs, kept):
        ref[...] = value

    def weight_view(part, block, side):
        where = slot(block[0], block[1], side, block[2])
        return gathered.at[part, pl.ds(aligned(where * PART), PART)]

    half = tokens // 2

    def image_row(block, side):
        return (block[0] * 4 + block[1] * 2 + side) * tokens

    def rail_row(block):
        return (block[0] * 2 + block[1]) * tokens

    def gather_at(known_z=None):
        return Gather(
            known_z, weight_view, ORDERS, lambda part, count: gathered.at[part, pl.ds(0, count * PART)], *gather_sems
        )

    def embed_at(known_z=None):
        return Reduce(
            known_z,
            lambda chunk, block: spare.at[pl.ds(aligned(rail_row(block) + chunk * half), half)],
            ("xz", "xz"),
            lambda chunk: residual.at[pl.ds(chunk * half, half)],
            lambda chunk, where: buf.at[pl.ds((chunk * 9 + where) * half, half)],
            lambda chunk, count: buf.at[pl.ds(0, count * half)],
            *embed_sems,
        )

    def front_works(known_z):
        known, sums = gather_at(known_z), embed_at(known_z)
        works = [work for part in range(3) for work in in_order(known.events(part))]
        return works + in_order(sums.events((0, 1)))

    gather, embed = gather_at(), embed_at()
    plan = Plan(FRONT_PLAN, [front_works(known_z) for known_z in range(4)])
    pl.semaphore_wait(barrier, 2 * bands - 1)
    load_pixels.wait()
    for chip in range(8):
        to_pair(0, pixel_rows.at[chip * 2 + 1 - core], pair_pixels.at[chip], front_sems).start()
    to_pair(1, band_scale, pair_scale, front_sems).start()
    shared("out_grad").start()
    plan.run()
    for part in FIRST_PARTS:
        gather.start(part)
    plan.run()

    gen_wait(spare)

    @pl.loop(0, 16)
    def _(piece):
        part = dot_nn(code_out[...], spare[pl.ds(aligned(piece * 128), 128), :])
        mixing[pl.ds(aligned(piece * 16), 16), :] = part.astype(B16)

    sending[...] = swap_rows(mixing[...])
    spread_kernels = Exchange(
        lambda target: rows16(sending, target),
        lambda source: rows16(kernels, source),
        lambda count: kernels.at[pl.ds(0, count * 16)],
        *[sem.at[0] for sem in kernel_sems],
    )
    spread_kernels.start()
    plan.run()
    for part in range(3):
        if part not in FIRST_PARTS:
            gather.start(part)
    plan.run()
    kernels[own_rows, :] = sending[own_rows, :]
    biases = dot_nn(code_out[...], bias_gen[...])
    row = lax.broadcasted_iota(jnp.int32, biases.shape, 0)
    bias, pair_bias = (
        jnp.sum(jnp.where(row == of, biases, 0.0), axis=0, keepdims=True) for of in (band, sibling[0])
    )
    for group in range(4):
        turned_pixels[group] = pixel_rows[4 * group : 4 * group + 4].reshape(4 * tokens, -1).T
    plan.run()
    spread_kernels.wait()
    to_pair(2, kernels, pair_kernels, front_sems).start()
    plan.run()
    to_pair(0, pair_pixels, pair_pixels, front_sems).wait_recv()
    to_pair(1, band_scale, pair_scale, front_sems).wait_recv()
    to_pair(2, kernels, pair_kernels, front_sems).wait_recv()

    def term(group):
        mine = [group * 4 + x_of * 2 + core for x_of in (0, 1)]
        rows = jnp.concatenate([pixel_rows[image] for image in mine], axis=0)
        pair_rows = pair_pixels[2 * group : 2 * group + 2].reshape(2 * tokens, -1)
        for at in range(0, width, 256):
            cols = slice(at, at + 256)
            one = dot_nn(rows, kernels[:, cols]) + bias[:, cols]
            two = dot_nn(pair_rows, pair_kernels[:, cols]) + pair_bias[:, cols]
            for x_of, image in enumerate(mine):
                own = slice(x_of * tokens, (x_of + 1) * tokens)
                total = one[own] * band_scale[image][:1, :1] + two[own] * pair_scale[image][:1, :1]
                start = (2 * group + x_of) * tokens
                spare[start : start + tokens, cols] = total.astype(B16)

    for group in (3, 0, 2, 1):
        plan.run()
        term(group)
        for chunk in (0, 1):
            embed.start(chunk, (group, 1, 0))
    plan.run()
    gather.wait_pairs(0)
    spread(gathered, weights, 0)

    names = dict(
        residual=residual, out_grad=out_grad, gain_one=gains.at[0:1], gain_two=gains.at[1:2], block_out=block_out,
        joint=joint, probs=probs, pre_act=pre_act, act=act,
        grad_pre=grad_pre, mixed=mixed, normed_one=normed_one, normed_two=normed_two, unit_one=unit_one,
        unit_two=unit_two, inverse_one=inverse_one, inverse_two=inverse_two, result=residual, grad_normed=grad_normed,
        grad_middle=grad_middle, grad_branch=grad_branch, grad_mixed=grad_mixed, grad_joint=grad_joint,
        turned=turned, rail_rows=rail_rows, small=small,
    )
    block = Block(weights, gathered.at[2], names)
    plan.run()
    block.project()
    shared("normed_one").start()
    plan.run()
    block.attend()
    shared("mixed").start()
    plan.run()
    gather.wait_pairs(1)
    spread(gathered, weights, 1)
    plan.run()
    block.widen()
    for name in ("normed_two", "act0", "act1", "act2", "act3"):
        shared(name).start()
    plan.run()
    gather.wait_pairs(2)
    gather.finish()
    embed.finish()
    for copy in ((0, pair_pixels, pair_pixels), (1, band_scale, pair_scale), (2, kernels, pair_kernels)):
        to_pair(*copy, front_sems).wait_send()
    tell_near(front_done)

    def part_ref(part):
        return spare if part == 2 else gathered.at[part]

    def part_view(part, blk):
        return part_ref(part).at[pl.ds(aligned((blk[0] * 4 + blk[1] * 2 + blk[2]) * PART), PART)]

    def reduce_at(known_z=None):
        return Reduce(
            known_z,
            part_view,
            SUM_ORDERS,
            lambda part: shares.at[pl.ds(part * PART, PART)],
            lambda part, where: buf.at[pl.ds((part * 19 + where) * PART, PART)],
            lambda part, count: part_ref(part).at[pl.ds(0, count * PART)],
            *reduce_sems,
        )

    def send_terms(part, planes):
        for zz in planes:
            for flips in reduce.flips(part, 0):
                reduce.start(part, (zz, *flips))

    image_grads = gathered.at[2]

    def image_view(chunk, blk, side):
        return image_grads.at[pl.ds(aligned(image_row(blk, side) + chunk * half), half)]

    def grads_at(known_z=None):
        return Gather(
            known_z, image_view, ("zx", "zx"), lambda chunk, count: image_grads.at[pl.ds(0, count * half)], *grads_sems
        )

    def tail_works(known_z):
        known, images = reduce_at(known_z), grads_at(known_z)
        works = [work for part in (2, 1, 0) for work in in_order(known.events((part,)))]
        return works + [work for chunk in (0, 1) for work in in_order(images.events(chunk))]

    reduce, grads = reduce_at(), grads_at()
    plan = Plan(TAIL_PLAN, [tail_works(known_z) for known_z in range(4)])
    hear_near(front_done)
    shared("out_grad").wait_recv()
    for part in (3, 0, 2, 1):
        plan.run()
        shared(f"act{part}").wait_recv()
        block.down_grad(part, core, spare)
        send_terms(2, (part,))
    plan.run()
    block.back_narrow()
    for part in range(4):
        shared(f"pre{part}").start()
    plan.run()
    block.narrow()
    tell_near(narrow_done)
    plan.run()
    block.back_wide()
    shared("grad_branch").start()
    plan.run()
    block.back_attend()
    for part in range(3):
        shared(f"joint{part}").start()
    plan.run()
    block.back_project()
    hear_near(narrow_done)
    image_grads[pl.ds(aligned(band * tokens), tokens), :] = block.embed_grad()
    grads.start(0)
    grads.start(1)
    plan.run()
    for name in ("normed_two", "pre0", "pre1", "pre2", "pre3"):
        shared(name).wait_recv()
    block.turn_rail(0, normed_two, core)
    for part in (0, 2):
        block.pair_grad(
            0, 0, lambda cols, part=part: grad_pre[part, :, cols],
            lambda cols, part=part: grad_pre[part + 1, :, cols], part_ref(1), part // 2 * CHUNK,
        )
    send_terms(1, (3, 0, 2, 1))
    plan.run()
    for name in ("normed_one", "mixed", "grad_branch", "joint0", "joint1", "joint2"):
        shared(name).wait_recv()
    block.turn_rail(0, normed_one, core)
    block.turn_rail(1, mixed, core)
    block.pair_grad(0, 0, lambda cols: grad_joint[0, :, cols], lambda cols: grad_joint[1, :, cols], part_ref(0), 0)
    block.pair_grad(
        0, 1, lambda cols: grad_joint[2, :, cols], lambda cols: grad_branch[:, cols], part_ref(0), CHUNK
    )
    send_terms(0, (3, 0, 2, 1))
    for name in SHARED:
        shared(name).wait_send()
    for piece in range(16):
        gen_copy(piece, weights).start()

    kernel_total = pre_act.at[0:2]
    kernel_total[...] = jnp.zeros(kernel_total.shape, F32)
    small[2:3, :] = jnp.zeros((1, width), F32)
    near_side = z // 2
    for side in (near_side, 1 - near_side):
        plan.run()
        for chunk in (0, 1):
            grads.wait_side(chunk, side)

        @pl.loop(0, 2)
        def _(step, side=side):
            group = 2 * side + step
            for image in range(4):
                rows = pl.ds(aligned((group * 4 + image) * tokens), tokens)
                scaled = image_grads[rows, :].astype(F32) * band_scale[group * 4 + image][:1, :1]
                small[2:3, :] += jnp.sum(scaled, axis=0, keepdims=True)
                act[image, :tokens] = scaled.astype(B16)
            scaled = act[:, :tokens].reshape(4 * tokens, width)
            pixel_rows[pl.ds(group * 4, 4)] = dot_nt(scaled, kernels[...]).astype(B16).reshape(4, tokens, -1)
            kernel_total[...] += dot_nn(turned_pixels[group], scaled).reshape(kernel_total.shape)

    store_pixels = pltpu.make_async_copy(pixel_rows, pixel_out, pix_sem)
    store_pixels.start()
    spread_kernels.finish()
    sending[...] = kernel_total[...].astype(B16).reshape(sending.shape)
    owner = core == y

    def column_copy(target, plane):
        return pltpu.make_async_remote_copy(
            src_ref=rows16(sending, target),
            dst_ref=rows16(landed_grads, y * bands + band),
            send_sem=cols_sems[0].at[0],
            recv_sem=cols_sems[1].at[0],
            device_id=(target, plane),
            device_id_type=MESH,
        )

    for step in range(1, bands):
        target = (band + step) % bands
        column_copy(target, target % 2).start()

    @pl.when(core != y)
    def _():
        column_copy(band, 1 - y).start()

    @pl.when(owner)
    def _():
        landed_grads[pl.ds(aligned((y * bands + band) * 16), 16), :] = sending[own_rows, :]

    vec_half = pltpu.make_async_remote_copy(
        src_ref=small, dst_ref=small_partner, send_sem=vec_half_sems[0].at[0], recv_sem=vec_half_sems[1].at[0],
        device_id=partner, device_id_type=MESH,
    )
    vec_half.start()
    plan.run()
    vec_half.wait_recv()
    small_all[band] = small[...] + small_partner[...]
    vector_spread = Exchange(
        lambda target: small_all.at[band], lambda source: small_all.at[source], lambda count: small_all.at[pl.ds(0, count)],
        *[sem.at[0] for sem in vec_sems],
    )
    vector_spread.start()
    plan.run()
    pix = summed.shape[0]

    def tell_code(target, plane):
        return pltpu.make_async_remote_copy(
            src_ref=code_all.at[band],
            dst_ref=code_all.at[band],
            send_sem=code_sems[0].at[0],
            recv_sem=code_sems[1].at[0],
            device_id=(target, plane),
            device_id_type=MESH,
        )

    pass_summed = pltpu.make_async_remote_copy(
        src_ref=summed, dst_ref=summed, send_sem=summed_sems[0].at[0], recv_sem=summed_sems[1].at[0],
        device_id=partner, device_id_type=MESH,
    )
    gen_wait(weights)

    @pl.when(owner)
    def _():
        bulk_copy(landed_grads.at[pl.ds(0, (2 * bands - 1) * 16)], cols_sems[0].at[0], cols_sems[1].at[0]).wait_recv()
        summed[...] = landed_grads[0:pix, :] + landed_grads[pix : 2 * pix, :]
        pass_summed.start()
        mixing[...] = swap_rows(summed[...])
        code_part[...] = jnp.zeros(code_part.shape, F32)

        @pl.loop(0, 16)
        def _(piece):
            code_part[...] += dot_nt(
                mixing[pl.ds(aligned(piece * 16), 16), :], weights[pl.ds(aligned(piece * 128), 128), :]
            )

        code_all[band] = code_part[...]
        for step in range(bands):
            for plane in (y, 1 - y) if step else (1 - y,):
                tell_code((band + step) % bands, plane).start()

    @pl.when(core != y)
    def _():
        pass_summed.wait_recv()

    store_columns = pltpu.make_async_copy(summed, kernel_grads, pix_sem)
    store_pixels.wait()
    store_columns.start()
    plan.run()
    vector_spread.wait()
    vectors[...] = small_all[...]
    bulk = code_all.at[pl.ds(0, bands - 1)]
    pl.when(owner)(bulk_copy(bulk, code_sems[0].at[0], code_sems[1].at[0]).wait_recv)
    bulk = code_all.at[pl.ds(0, bands)]
    pl.when(core != y)(bulk_copy(bulk, code_sems[0].at[0], code_sems[1].at[0]).wait_recv)
    total = code_all[0]
    for source in range(1, bands):
        total = total + code_all[source]
    code_grads[...] = total
    plan.run()
    reduce.finish()
    grads.finish()
    vec_half.wait_send()
    vector_spread.finish()

    @pl.when(owner)
    def _():
        sent = landed_grads.at[pl.ds(0, (bands - 1) * 16)]
        bulk_copy(sent, cols_sems[0].at[0], cols_sems[1].at[0]).wait_send()
        sent = code_all.at[pl.ds(0, 2 * bands - 1)]
        bulk_copy(sent, code_sems[0].at[0], code_sems[1].at[0]).wait_send()
        pass_summed.wait_send()

    @pl.when(core != y)
    def _():
        sent = landed_grads.at[pl.ds(0, bands * 16)]
        bulk_copy(sent, cols_sems[0].at[0], cols_sems[1].at[0]).wait_send()

    store_columns.wait()


VMEM_BYTES = 63 * 2**20


def layer(counts, mask, pixels, kernel_gen, weights, waves, hyper, bias_gen, out_grad, gains):
    width = bias_gen.shape[1]
    bands = lax.axis_size("band")
    devices = bands * lax.axis_size("dp")
    images, tokens, pix = pixels.shape
    hidden = hyper[4].shape[1]
    vmem = pl.BlockSpec(memory_space=pltpu.VMEM)
    hbm = pl.BlockSpec(memory_space=pl.ANY)
    smem = pl.BlockSpec(memory_space=pltpu.SMEM)
    shape = jax.ShapeDtypeStruct
    rows = lambda kind, *lead: pltpu.VMEM((*lead, tokens, width), kind)
    pair = lambda *lead: pltpu.VMEM((*lead, 2 * tokens, width), B16)
    dma = pltpu.SemaphoreType.DMA
    code = (bands, HW)
    kept = [(bands, 3 * HW), (HHEADS * bands, bands), code, code, (bands, 1), (bands, hidden), code, (bands, 1), (2, HW)]
    return pl.pallas_call(
        layer_kernel,
        out_shape=[
            shape((tokens, width), B16),
            shape(pixels.shape, B16),
            shape((3 * PART, width), F32),
            shape((pix, width), B16),
            shape(code, B16),
            shape(code, F32),
            shape((bands, 8, width), F32),
            *[shape(dims, F32) for dims in kept],
        ],
        in_specs=[smem] * 2 + [hbm] * 2 + [vmem] * 15,
        out_specs=[vmem, hbm, vmem, hbm] + [vmem] * 12,
        scratch_shapes=[
            pltpu.VMEM((3, devices * PART, width), B16),
            pltpu.VMEM((8 * width, width), B16),
            pltpu.VMEM((16 * HW, width), B16),
            pltpu.VMEM((3 * 19 * PART, width), B16),
            rows(B16, 3),
            pltpu.VMEM((HEADS // 2, 2 * tokens, tokens), F32),
            rows(F32, 4),
            pair(4),
            pair(4),
            pair(),
            pair(),
            pair(),
            pair(),
            rows(F32),
            rows(F32),
            pltpu.VMEM((tokens, 128), F32),
            pltpu.VMEM((tokens, 128), F32),
            rows(F32),
            rows(F32),
            pair(),
            rows(B16),
            pair(3),
            pltpu.VMEM((width, 2 * tokens), B16),
            pltpu.VMEM((2, width // 2, 2 * tokens), B16),
            rows(F32),
            pltpu.VMEM(pixels.shape, B16),
            pltpu.VMEM((4, pix, 4 * tokens), B16),
            pltpu.VMEM((images // 2, tokens, pix), B16),
            pltpu.VMEM((pix, width), B16),
            pltpu.VMEM((pix, width), B16),
            pltpu.VMEM((pix, width), B16),
            pltpu.VMEM((pix, width), B16),
            pltpu.VMEM((2 * pix, width), B16),
            pltpu.VMEM((pix, width), B16),
            pltpu.VMEM((8, width), F32),
            pltpu.VMEM((8, width), F32),
            pltpu.VMEM((bands, 8, width), F32),
            pltpu.VMEM(code, F32),
            pltpu.VMEM((2 * bands, *code), F32),
            pltpu.VMEM((2, width), F32),
            pltpu.VMEM((images, 8, 128), F32),
            pltpu.VMEM((images, 8, 128), F32),
            dma,
            dma,
            pltpu.SemaphoreType.REGULAR,
            pltpu.SemaphoreType.REGULAR,
            *[dma((3, 3)), dma((3, 16)), dma((3, 2)), dma((3, 2))],
            *[dma((2, 3)), dma((2, 16)), dma((2, 2)), dma((2, 2))],
            *[dma((3, 3)), dma((3, 19))],
            *[dma((2, 2)), dma((2, 9))],
            *[dma((len(SHARED),))] * 2,
            *[dma((3,))] * 2,
            *[dma((1,))] * 12,
        ],
        compiler_params=pltpu.CompilerParams(
            collective_id=0, has_side_effects=True, vmem_limit_bytes=VMEM_BYTES
        ),
        name="layer",
    )(counts, mask, pixels, kernel_gen, *weights, waves, *hyper, bias_gen, out_grad, *gains)


def finish_kernel(*refs):
    count = 13 + len(KEPT)
    outside = refs[:count]
    (block_out, pixel_out, grad_qkv, grad_out, grad_gain_one, grad_up, grad_down, grad_gain_two, grad_gen, grad_bias,
     gain_one_sum, gain_two_sum, share_qkv, share_out, share_up, share_down, *scratch) = refs[count:]
    inside, (store, in_sem, copy_sem, gen_sem) = scratch[:count], scratch[count:]
    loads = [pltpu.make_async_copy(*pair, in_sem.at[at]) for at, pair in enumerate(zip(outside, inside))]
    for load in loads:
        load.start()
    (code_low, columns, shares, waves, hyper_qkv, hyper_out, hyper_up, hyper_down, bias_gen, code_grads, vectors,
     *kept_refs, hyper_gains, block_in, pixel_in) = inside
    width = bias_gen.shape[1]
    for load in loads[:2]:
        load.wait()
    code = code_low[...]
    swapped = swap_rows(columns[...])
    gen_copies = []
    for piece in range(16):
        slot_at = piece % store.shape[0]
        if piece >= store.shape[0]:
            gen_copies[piece - store.shape[0]].wait()
        store[slot_at] = dot_tn(code, swapped[piece * 16 : (piece + 1) * 16])
        gen_copies.append(
            pltpu.make_async_copy(
                store.at[slot_at], grad_gen.at[:, pl.ds(piece * width, width)], gen_sem.at[slot_at]
            )
        )
        gen_copies[-1].start()
    for load in loads[2:]:
        load.wait()
    copies = [
        pltpu.make_async_copy(block_in, block_out, copy_sem.at[0]),
        pltpu.make_async_copy(pixel_in, pixel_out, copy_sem.at[1]),
    ]
    for copy in copies:
        copy.start()
    share_qkv[...] = jnp.concatenate([shares[at * 24 : at * 24 + 24, :] for at in range(3)], axis=1)
    share_out[...] = shares[72:96, :]
    share_up[...] = jnp.concatenate([shares[at * 24 : at * 24 + 24, :] for at in range(4, 8)], axis=1)
    share_down[...] = shares[192:288, :]
    sums = jnp.sum(vectors[...], axis=0)
    gain_one_sum[...] = sums[0]
    gain_two_sum[...] = sums[1]
    bias_grads = vectors[:, 2, :]
    grad_bias[...] = dot_tn(jnp.concatenate([code] * 3, axis=0), jnp.concatenate(split3(bias_grads), axis=0))
    grad_code = code_grads[...] + wide_nt(bias_grads, bias_gen[...])
    grads = hyper_backward(
        grad_code, [ref[...] for ref in kept_refs], waves[...], hyper_qkv[...], hyper_out[...], hyper_gains[0:1, :],
        hyper_up[...], hyper_down[...], hyper_gains[1:2, :],
    )
    for ref, value in zip((grad_qkv, grad_out, grad_gain_one, grad_up, grad_down, grad_gain_two), grads):
        ref[...] = value
    for copy in copies + gen_copies[-store.shape[0] :]:
        copy.wait()


def finish(waves, hyper, bias_gen, code_low, code_grads, vectors, columns, shares, block_out, pixel_grad, kept, kernel_gen, weights):
    width = bias_gen.shape[1]
    vmem = pl.BlockSpec(memory_space=pltpu.VMEM)
    hbm = pl.BlockSpec(memory_space=pl.ANY)
    shape = lambda array: jax.ShapeDtypeStruct(array.shape, F32)
    line = jax.ShapeDtypeStruct((1, HW), F32)
    weights_in = (hyper[0], hyper[1], hyper[4], hyper[5])
    operands = (code_low, columns, shares, waves, *weights_in, bias_gen, code_grads, vectors, *kept, block_out, pixel_grad)
    return pl.pallas_call(
        finish_kernel,
        out_shape=[
            jax.ShapeDtypeStruct(block_out.shape, B16),
            jax.ShapeDtypeStruct(pixel_grad.shape, B16),
            shape(hyper[0]), shape(hyper[1]), line, shape(hyper[4]), shape(hyper[5]), line,
            shape(kernel_gen), shape(bias_gen), *[jax.ShapeDtypeStruct((width,), F32)] * 2,
            *[shape(weight) for weight in weights],
        ],
        in_specs=[hbm] * len(operands),
        out_specs=[hbm, hbm] + [vmem] * 6 + [hbm] + [vmem] * 7,
        scratch_shapes=[
            *[pltpu.VMEM(operand.shape, operand.dtype) for operand in operands],
            pltpu.VMEM((4, HW, width), F32),
            pltpu.SemaphoreType.DMA((len(operands),)),
            pltpu.SemaphoreType.DMA((2,)),
            pltpu.SemaphoreType.DMA((4,)),
        ],
        compiler_params=pltpu.CompilerParams(vmem_limit_bytes=VMEM_BYTES),
        name="finish",
    )(*operands)


def body(
    pixels,
    wavelengths,
    band_counts,
    band_mask,
    hyper_qkv,
    hyper_out,
    hyper_gain1,
    hyper_up,
    hyper_down,
    hyper_gain2,
    kernel_gen,
    bias_gen,
    norm_gain1,
    attn_qkv,
    attn_out,
    norm_gain2,
    mlp_up,
    mlp_down,
    out_grad,
):
    f32 = jnp.float32
    b16 = jnp.bfloat16
    band_local = pixels.shape[3]
    pixel_local = pixels[0]
    model_width = bias_gen.shape[1]
    hyper_params = tuple(
        (
            weight.astype(f32)
            for weight in (hyper_qkv, hyper_out, hyper_gain1, hyper_up, hyper_down, hyper_gain2)
        )
    )
    wave_tokens = wave_embed(wavelengths, HW)
    band_code, hyper_pull = jax.vjp(lambda *params: hyper_net(wave_tokens, *params), *hyper_params)
    code_low = band_code.astype(b16)
    column_part = jnp.dot(code_low, kernel_gen, preferred_element_type=f32).astype(b16)
    kernel_rows = lax.all_to_all(column_part, "band", split_axis=0, concat_axis=1, tiled=True)
    kernels = kernel_rows.reshape(band_local, -1, model_width)
    first_band = lax.axis_index("band") * band_local
    own_code = lax.dynamic_slice_in_dim(code_low, first_band, band_local, 0)
    count_row = band_counts[0]
    biases = jnp.dot(own_code, bias_gen, preferred_element_type=f32)
    slot_ids = first_band + jnp.arange(band_local, dtype=jnp.int32)
    active = (slot_ids[None, :] < count_row[:, None]) & (band_mask[0] == 1)
    band_weight = jnp.where(active, lax.rsqrt(count_row.astype(f32))[:, None], f32(0.0))
    pixel_rows = pixel_local
    weight_rows = band_weight
    conv_out = jnp.einsum("inbp,bpd->inbd", pixel_rows, kernels, preferred_element_type=f32)
    residual = lax.psum_scatter(
        jnp.sum((conv_out + biases[None, None]) * weight_rows[:, None, :, None], axis=2),
        "band",
        scatter_dimension=0,
        tiled=True,
    )
    gathered = (
        lax.all_gather(attn_qkv, ("band", "dp"), axis=0, tiled=True),
        lax.all_gather(attn_out, ("band", "dp"), axis=0, tiled=True),
        lax.all_gather(mlp_up, ("band", "dp"), axis=0, tiled=True),
        lax.all_gather(mlp_down, ("band", "dp"), axis=0, tiled=True),
    )
    qkv_full, out_full, up_full, down_full = gathered
    gain_one = norm_gain1.astype(f32)
    gain_two = norm_gain2.astype(f32)
    images, tokens = (residual.shape[0], residual.shape[1])
    score_scale = 1.0 / math.sqrt(HEAD_DIM)
    normed_full, unit_one, inverse_one = norm_parts(residual, gain_one)
    normed_one = normed_full.astype(b16)
    joint_rows = jnp.einsum("ind,de->ine", normed_one, qkv_full, preferred_element_type=f32).astype(
        b16
    )
    queries = joint_rows[..., :model_width].reshape(images, tokens, HEADS, HEAD_DIM)
    key_rows = joint_rows[..., model_width : 2 * model_width].reshape(
        images, tokens, HEADS, HEAD_DIM
    )
    value_rows = joint_rows[..., 2 * model_width :].reshape(images, tokens, HEADS, HEAD_DIM)
    scores = (
        jnp.einsum("inhc,imhc->ihnm", queries, key_rows, preferred_element_type=f32) * score_scale
    )
    row_top = jnp.max(scores, axis=-1, keepdims=True)
    log_total = row_top + jnp.log(jnp.sum(jnp.exp(scores - row_top), axis=-1, keepdims=True))
    probs_full = jnp.exp(scores - log_total)
    probs_low = probs_full.astype(b16)
    mixed_low = (
        jnp.einsum("ihnm,imhc->inhc", probs_low, value_rows, preferred_element_type=f32)
        .reshape(images, tokens, model_width)
        .astype(b16)
    )
    middle = residual + jnp.einsum("ind,de->ine", mixed_low, out_full, preferred_element_type=f32)
    normed_two_full, unit_two, inverse_two = norm_parts(middle, gain_two)
    normed_two = normed_two_full.astype(b16)
    pre_act = jnp.einsum("ind,df->inf", normed_two, up_full, preferred_element_type=f32)
    act_low = gelu_tanh(pre_act).astype(b16)
    result = middle + jnp.einsum("inf,fd->ind", act_low, down_full, preferred_element_type=f32)
    block_out = result.astype(b16)[None]
    qkv_back, out_back, up_back, down_back = (
        lax.all_gather(attn_qkv, ("band", "dp"), axis=0, tiled=True),
        lax.all_gather(attn_out, ("band", "dp"), axis=0, tiled=True),
        lax.all_gather(mlp_up, ("band", "dp"), axis=0, tiled=True),
        lax.all_gather(mlp_down, ("band", "dp"), axis=0, tiled=True),
    )
    grad_top = out_grad[0]
    grad_down = jnp.einsum("inf,ind->fd", act_low, grad_top, preferred_element_type=f32)
    grad_act = jnp.einsum("ind,fd->inf", grad_top, down_back, preferred_element_type=f32)
    grad_pre = (grad_act * gelu_slope(pre_act)).astype(b16)
    grad_up = jnp.einsum("ind,inf->df", normed_two, grad_pre, preferred_element_type=f32)
    grad_normed_two = jnp.einsum("inf,df->ind", grad_pre, up_back, preferred_element_type=f32)
    grad_gain_two = jnp.sum(grad_normed_two * unit_two, axis=(0, 1))
    grad_middle = grad_top.astype(f32) + norm_back(grad_normed_two, gain_two, unit_two, inverse_two)
    grad_branch = grad_middle.astype(b16)
    grad_out_proj = jnp.einsum("ind,ine->de", mixed_low, grad_branch, preferred_element_type=f32)
    grad_mixed = (
        jnp.einsum("ine,de->ind", grad_branch, out_back, preferred_element_type=f32)
        .astype(b16)
        .reshape(images, tokens, HEADS, HEAD_DIM)
    )
    grad_values = jnp.einsum("ihnm,inhc->imhc", probs_low, grad_mixed, preferred_element_type=f32)
    grad_probs = jnp.einsum("inhc,imhc->ihnm", grad_mixed, value_rows, preferred_element_type=f32)
    grad_scores = (
        probs_full * (grad_probs - jnp.sum(grad_probs * probs_full, axis=-1, keepdims=True))
    ).astype(b16)
    grad_queries = (
        jnp.einsum("ihnm,imhc->inhc", grad_scores, key_rows, preferred_element_type=f32)
        * score_scale
    )
    grad_keys = (
        jnp.einsum("ihnm,inhc->imhc", grad_scores, queries, preferred_element_type=f32)
        * score_scale
    )
    grad_joint = jnp.concatenate(
        [
            grad_queries.reshape(images, tokens, model_width),
            grad_keys.reshape(images, tokens, model_width),
            grad_values.reshape(images, tokens, model_width),
        ],
        axis=-1,
    ).astype(b16)
    grad_qkv = jnp.einsum("ind,ine->de", normed_one, grad_joint, preferred_element_type=f32)
    grad_normed_one = jnp.einsum("ine,de->ind", grad_joint, qkv_back, preferred_element_type=f32)
    grad_gain_one = jnp.sum(grad_normed_one * unit_one, axis=(0, 1))
    grad_embed = grad_middle + norm_back(grad_normed_one, gain_one, unit_one, inverse_one)
    grad_embed_low = grad_embed.astype(b16)[None]
    grad_rows = lax.all_gather(grad_embed_low, "band", axis=1, tiled=True)[0].astype(f32)
    weight_rows = band_weight
    pixel_rows = pixel_local
    scaled = grad_rows[:, :, None, :] * weight_rows[:, None, :, None]
    bias_total = jnp.sum(scaled, axis=(0, 1))
    scaled_low = scaled.astype(b16)
    kernel_total = jnp.einsum("inbp,inbd->bpd", pixel_rows, scaled_low, preferred_element_type=f32)
    pixel_part = jnp.einsum(
        "inbd,bpd->inbp", scaled_low, kernels, preferred_element_type=f32
    ).astype(b16)
    pixel_total = pixel_part
    kernel_grad, bias_grad, pixel_total = (kernel_total, bias_total, pixel_total)
    pixel_out = pixel_total[None]
    kernel_grad_low = kernel_grad.reshape(band_local, -1).astype(b16)
    grad_columns = lax.all_to_all(kernel_grad_low, "band", split_axis=1, concat_axis=0, tiled=True)
    grad_kernel_part = jnp.einsum("nh,nc->hc", code_low, grad_columns, preferred_element_type=f32)
    grad_code_part = jnp.einsum("nc,hc->nh", grad_columns, kernel_gen, preferred_element_type=f32)
    bias_back = jnp.einsum("bd,hd->bh", bias_grad, bias_gen.astype(f32), precision=PRECISE)
    grad_code_part = grad_code_part + lax.dynamic_update_slice_in_dim(
        jnp.zeros_like(grad_code_part), bias_back, first_band, 0
    )
    grad_bias_part = jnp.einsum("bh,bd->hd", own_code.astype(f32), bias_grad, precision=PRECISE)
    grad_code, grad_bias_gen, grad_norm_gain1, grad_norm_gain2 = lax.psum(
        (grad_code_part, grad_bias_part, grad_gain_one, grad_gain_two), ("band", "dp")
    )
    grad_kernel_gen = lax.psum(grad_kernel_part.astype(jnp.bfloat16), "dp").astype(jnp.float32)
    hyper_grads = hyper_pull(grad_code)
    shares = (
        lax.psum_scatter(grad_qkv, ("band", "dp"), scatter_dimension=0, tiled=True),
        lax.psum_scatter(grad_out_proj, ("band", "dp"), scatter_dimension=0, tiled=True),
        lax.psum_scatter(grad_up, ("band", "dp"), scatter_dimension=0, tiled=True),
        lax.psum_scatter(grad_down, ("band", "dp"), scatter_dimension=0, tiled=True),
    )
    return (
        block_out,
        pixel_out,
        hyper_grads[0],
        hyper_grads[1],
        hyper_grads[2],
        hyper_grads[3],
        hyper_grads[4],
        hyper_grads[5],
        grad_kernel_gen,
        grad_bias_gen,
        grad_norm_gain1,
        shares[0],
        shares[1],
        grad_norm_gain2,
        shares[2],
        shares[3],
    )


def fast_body(
    pixels,
    wavelengths,
    band_counts,
    band_mask,
    hyper_qkv,
    hyper_out,
    hyper_gain1,
    hyper_up,
    hyper_down,
    hyper_gain2,
    kernel_gen,
    bias_gen,
    norm_gain1,
    attn_qkv,
    attn_out,
    norm_gain2,
    mlp_up,
    mlp_down,
    out_grad,
):
    lane = jnp.arange(HW)
    frequency = jnp.power(10000.0, -(lane % (HW // 2)).astype(F32) / (HW // 2))
    angles = wavelengths.astype(F32)[:, None] * frequency[None, :]
    waves = jnp.where(lane < HW // 2, jnp.sin(angles), jnp.cos(angles))
    weights = (attn_qkv, attn_out, mlp_up, mlp_down)
    hyper = (hyper_qkv, hyper_out, hyper_gain1, hyper_gain2, hyper_up, hyper_down)
    block_out, pixel_grad, shares, columns, code_low, code_grads, vectors, *kept = layer(
        band_counts[0],
        band_mask[0, :, 0],
        pixels[0, :, :, 0],
        kernel_gen,
        weights,
        waves,
        hyper,
        bias_gen,
        out_grad[0, 0],
        (norm_gain1, norm_gain2),
    )
    outs = finish(
        waves,
        hyper,
        bias_gen,
        code_low,
        code_grads,
        vectors,
        columns,
        shares,
        block_out,
        pixel_grad,
        kept,
        kernel_gen,
        weights,
    )
    block_out, pixel_grad, *hyper_grads, grad_gen, grad_bias, gain_one, gain_two = outs[:12]
    hyper_grads[2], hyper_grads[5] = hyper_grads[2][0], hyper_grads[5][0]
    return (
        block_out[None, None],
        pixel_grad[None, :, :, None],
        *hyper_grads,
        grad_gen,
        grad_bias,
        gain_one,
        outs[12],
        outs[13],
        gain_two,
        outs[14],
        outs[15],
    )


def solution(mesh):
    placed = (
        P("dp", None, None, "band", None),
        P(),
        P("dp", None),
        P("dp", None, "band"),
        P(),
        P(),
        P(),
        P(),
        P(),
        P(),
        P(None, "band"),
        P(),
        P(),
        P(("band", "dp"), None),
        P(("band", "dp"), None),
        P(),
        P(("band", "dp"), None),
        P(("band", "dp"), None),
        P("dp", "band", None, None),
    )
    one_slot = (mesh.shape["band"], mesh.shape["dp"]) == (16, 2)
    return jax.shard_map(
        fast_body if one_slot else body,
        mesh=mesh,
        in_specs=placed,
        out_specs=(
            P("dp", "band", None, None),
            P("dp", None, None, "band", None),
            P(),
            P(),
            P(),
            P(),
            P(),
            P(),
            P(None, "band"),
            P(),
            P(),
            P(("band", "dp"), None),
            P(("band", "dp"), None),
            P(),
            P(("band", "dp"), None),
            P(("band", "dp"), None),
        ),
        check_vma=False,
    )
```

```python
import functools
import math

import jax
import jax.numpy as jnp
from jax import lax
from jax.experimental import pallas as pl
from jax.experimental.pallas import tpu as pltpu
from jax.sharding import PartitionSpec as P

HEADS = 12
HEAD_DIM = 64
HW = 128
HHEADS = 4


PRECISE = lax.Precision.HIGHEST
EPS_BLOCK = 1e-06
EPS_HYPER = 1e-05
GELU_COEF = 0.7978845608028654


def gelu_tanh(tensor):
    return (
        0.5 * tensor * (1.0 + jnp.tanh(GELU_COEF * (tensor + 0.044715 * tensor * tensor * tensor)))
    )


def gelu_slope(tensor):
    tanh_val = jnp.tanh(GELU_COEF * (tensor + 0.044715 * tensor * tensor * tensor))
    return 0.5 * (1.0 + tanh_val) + 0.5 * tensor * (1.0 - tanh_val * tanh_val) * GELU_COEF * (
        1.0 + 3.0 * 0.044715 * tensor * tensor
    )


def layer_norm(tensor, gain_vec, epsilon):
    centred = tensor - jnp.mean(tensor, axis=-1, keepdims=True)
    return (
        centred
        * lax.rsqrt(jnp.mean(centred * centred, axis=-1, keepdims=True) + epsilon)
        * gain_vec
    )


def norm_parts(tensor, gain_vec):
    centred = tensor - jnp.mean(tensor, axis=-1, keepdims=True)
    inverse = lax.rsqrt(jnp.mean(centred * centred, axis=-1, keepdims=True) + EPS_BLOCK)
    unit_rows = centred * inverse
    return (unit_rows * gain_vec, unit_rows, inverse)


def norm_back(grad_rows, gain_vec, unit_rows, inverse):
    scaled = grad_rows * gain_vec
    return inverse * (
        scaled
        - jnp.mean(scaled, axis=-1, keepdims=True)
        - unit_rows * jnp.mean(scaled * unit_rows, axis=-1, keepdims=True)
    )


def wave_embed(wave_ints, token_width):
    half_width = token_width // 2
    frequency = jnp.power(10000.0, -jnp.arange(half_width, dtype=jnp.float32) / half_width)
    angles = wave_ints.astype(jnp.float32)[:, None] * frequency[None, :]
    return jnp.concatenate([jnp.sin(angles), jnp.cos(angles)], axis=1)


def hyper_net(wave_tokens, qkv_weight, out_weight, gain_one, up_weight, down_weight, gain_two):
    tokens, token_width = wave_tokens.shape
    head_size = token_width // HHEADS
    qkv_rows = jnp.dot(wave_tokens, qkv_weight, precision=PRECISE)
    queries = qkv_rows[:, :token_width].reshape(tokens, HHEADS, head_size)
    key_rows = qkv_rows[:, token_width : 2 * token_width].reshape(tokens, HHEADS, head_size)
    value_rows = qkv_rows[:, 2 * token_width :].reshape(tokens, HHEADS, head_size)
    scores = jnp.einsum("nhc,mhc->hnm", queries, key_rows, precision=PRECISE) / math.sqrt(head_size)
    weights_soft = jax.nn.softmax(scores, axis=-1)
    mixed_rows = jnp.einsum("hnm,mhc->nhc", weights_soft, value_rows, precision=PRECISE).reshape(
        tokens, token_width
    )
    first_norm = layer_norm(
        wave_tokens + jnp.dot(mixed_rows, out_weight, precision=PRECISE), gain_one, EPS_HYPER
    )
    inner_act = gelu_tanh(jnp.dot(first_norm, up_weight, precision=PRECISE))
    return layer_norm(
        first_norm + jnp.dot(inner_act, down_weight, precision=PRECISE), gain_two, EPS_HYPER
    )


MESH = pl.DeviceIdType.MESH
B16 = jnp.bfloat16
F32 = jnp.float32
CHUNK = 48
DIMS = "xyz"
PART = 96
FRONT_PLAN = (
    (
        (),
        (),
        (),
        (),
        (1, 3, 2, 42, 41, 29, 11),
        (),
        (),
        (53, 57, 61, 10, 13, 28),
        (54,),
        (55, 66, 72, 5, 58, 63, 48),
        (56, 77, 83, 62, 22, 44, 67, 74, 35, 9, 14, 17, 73, 80, 82, 84, 50, 18, 89, 21, 91, 24, 31, 26, 34),
        (86, 87, 37),
        (39, 47),
        (),
        (),
        (52,),
        (),
        (),
    ),
    (
        (),
        (),
        (),
        (0, 1, 3, 2),
        (42, 29, 41, 7, 40),
        (6, 11),
        (),
        (53,),
        (54, 10, 13),
        (55, 59, 5),
        (56, 58, 64, 48, 62, 70, 45, 67, 75, 71, 27, 19, 68, 76, 14, 81, 73, 22, 88, 28, 17, 78, 82, 84, 31, 85, 89, 32, 91, 79, 44, 24),
        (86, 87, 35),
        (37,),
        (),
        (),
        (50,),
        (),
        (),
    ),
    (
        (),
        (),
        (),
        (0, 1, 3, 2),
        (42, 29, 40, 7),
        (41,),
        (),
        (53, 6, 11),
        (54,),
        (55, 10, 13),
        (56, 58, 4, 45, 62, 60, 67, 48, 65, 70, 73, 28, 82, 75, 19, 89, 12, 81, 84, 22, 71, 88, 27, 76, 91, 15, 69, 30, 78, 35, 86, 85, 87, 79, 43, 23),
        (32,),
        (),
        (36,),
        (49,),
        (),
        (),
        (),
    ),
    (
        (),
        (),
        (),
        (),
        (0, 3, 2, 42, 40, 29, 7),
        (6, 13, 27),
        (),
        (53,),
        (54, 57, 61, 4, 45),
        (55, 77, 83),
        (56, 66, 72, 58, 19, 43, 62, 63, 32, 8, 12, 15, 67, 80, 81, 84, 49, 73, 74, 88, 20, 16, 91, 23, 30, 25, 33),
        (85, 87, 36),
        (38, 46),
        (),
        (),
        (51,),
        (),
        (),
    ),
)
TAIL_PLAN = (
    (
        (),
        (),
        (0, 1, 2, 3),
        (),
        (4, 6),
        (),
        (5,),
        (18, 21, 24, 27, 30, 33, 7, 70, 71, 11),
        (83, 84, 39, 40, 41, 42, 43, 77, 44, 45, 46, 10, 14, 73, 90, 86, 47),
        (79, 76, 92, 48, 89, 49, 53, 50, 16, 17, 81, 51, 94),
        (54, 32, 34, 52, 57, 36, 59, 60, 58, 62, 61, 65),
        (),
        (38, 95, 96, 67, 68),
        (),
    ),
    (
        (),
        (),
        (0, 1, 2, 3),
        (),
        (4,),
        (),
        (5,),
        (8, 7),
        (70, 71, 69, 83, 84, 82, 39, 40, 41, 42, 43, 44, 45, 46, 10, 19, 73, 77, 86, 74, 47, 22, 90, 13, 48, 25, 87),
        (79, 92, 26, 50, 28, 29, 51, 31),
        (49, 54, 35, 32, 34, 52, 57, 12, 36, 59, 15, 58, 60, 55, 61),
        (16, 17, 38, 95),
        (64, 63, 96, 66, 67, 68),
        (),
    ),
    (
        (),
        (),
        (0, 1, 2, 3),
        (),
        (4,),
        (),
        (5,),
        (7,),
        (69, 70, 71, 82, 83, 84, 39, 40, 41, 42, 43, 44, 45, 46, 10, 9, 74, 12, 72, 77, 47, 20, 85, 87, 48, 23, 90, 25),
        (78, 50, 26, 28, 49, 51, 29, 31, 91, 54),
        (32, 34, 35, 52, 57, 36, 58, 59, 16, 60, 13, 61, 56, 15, 17),
        (63, 38, 95),
        (67, 96, 64, 66, 68),
        (),
    ),
    (
        (),
        (),
        (0, 1, 2, 3),
        (),
        (4,),
        (),
        (5, 6),
        (18, 21, 24, 27, 30, 33, 69, 71, 7, 14),
        (82, 84, 39, 40, 41, 42, 74, 43, 44, 45, 46, 10, 72, 11, 87, 85, 47),
        (78, 15, 17, 91, 48, 75, 49, 50, 88, 80, 51, 31, 34, 52, 53, 54, 35, 93),
        (57, 58, 65, 59, 60, 38, 95, 61, 62, 96),
        (),
        (66, 68),
        (),
    ),
)
FIRST_PARTS = (0, 2)
SUM_ORDERS = ('yxz', 'zy', 'yz')
EMBED_ORDERS = ('xz', 'zx')
IMAGE_ORDERS = ('zx', 'zx')
ORDERS = ('zxy', 'zy', 'zy')


def place(known_z=None):
    band = lax.axis_index("band")
    z = band // 4 if known_z is None else known_z
    return (z, (band // 2) % 2, band % 2, lax.axis_index("dp"))


def device(z, x, core, y):
    return (z * 4 + x * 2 + core, y)


def slot(z, x, core, y):
    return (z * 4 + x * 2 + core) * 2 + y


def when(cond, run):
    if isinstance(cond, bool):
        if cond:
            run()
    else:
        pl.when(cond)(run)


def both(first, second):
    return second if first is True else first & second


def aligned(rows):
    return pl.multiple_of(rows, 16)


def tell_peers(barrier):
    band, y = lax.axis_index("band"), lax.axis_index("dp")
    bands = lax.axis_size("band")
    for step in range(bands):
        for plane in (y, 1 - y) if step else (1 - y,):
            pl.semaphore_signal(
                barrier, inc=1, device_id=((band + step) % bands, plane), device_id_type=MESH
            )


def tell_near(semaphore):
    z, x, core, y = place()
    near = [
        (device(z, x, 1 - core, y), True),
        (device(z, 1 - x, core, y), True),
        (device(z, x, core, 1 - y), True),
        (device(z + 1, x, core, y), z < 3),
        (device(z - 1, x, core, y), z > 0),
    ]
    for target, cond in near:
        when(
            cond,
            functools.partial(
                pl.semaphore_signal, semaphore, inc=1, device_id=target, device_id_type=MESH
            ),
        )


def hear_near(semaphore):
    z = place()[0]
    pl.semaphore_wait(semaphore, 5 - z // 3 - (3 - z) // 3)


def bulk_copy(ref, send_sem, recv_sem):
    band, y = lax.axis_index("band"), lax.axis_index("dp")
    return pltpu.make_async_remote_copy(
        src_ref=ref,
        dst_ref=ref,
        send_sem=send_sem,
        recv_sem=recv_sem,
        device_id=(band, 1 - y),
        device_id_type=MESH,
    )


def in_order(events):
    return [work for _, _, work in sorted(events, key=lambda event: event[:2])]


class Plan:
    def __init__(self, table, catalogues):
        self.table, self.catalogues = table, catalogues
        self.at = 0

    def run(self):
        z = place()[0]
        for known_z, works in enumerate(self.catalogues):
            chosen = self.table[known_z][self.at]
            if not chosen:
                continue

            @pl.when(z == known_z)
            def _(works=works, chosen=chosen):
                for index in chosen:
                    works[index]()

        self.at += 1


class Gather:
    def __init__(self, known_z, view, orders, bulk, send_sem, recv_sem, pair_send, pair_recv):
        self.view, self.orders, self.bulk = view, orders, bulk
        self.send_sem, self.recv_sem = send_sem, recv_sem
        self.pair_send, self.pair_recv = pair_send, pair_recv
        self.z, self.x, self.core, self.y = place(known_z)

    def rail(self, block):
        return block[0] * 4 + block[1] * 2 + block[2]

    def sibling(self):
        return device(self.z, self.x, 1 - self.core, self.y)

    def send(self, chunk, block, dim, cond, direction=0):
        z, x, core, y = self.z, self.x, self.core, self.y
        if dim == "x":
            targets = [(device(z, 1 - x, core, y), cond)]
        elif dim == "y":
            targets = [(device(z, x, core, 1 - y), cond)]
        else:
            targets = []
            if direction >= 0:
                targets.append((device(z + 1, x, core, y), both(cond, z < 3)))
            if direction <= 0:
                targets.append((device(z - 1, x, core, y), both(cond, z > 0)))
        src = self.view(chunk, block, core)
        for target, needed in targets:
            if needed is False:
                continue
            copy = pltpu.make_async_remote_copy(
                src_ref=src,
                dst_ref=src,
                send_sem=self.send_sem.at[chunk, DIMS.index(dim)],
                recv_sem=self.recv_sem.at[chunk, self.rail(block)],
                device_id=target,
                device_id_type=MESH,
            )
            when(needed, copy.start)

    def pair(self, chunk, block, core):
        src = self.view(chunk, block, core)
        return pltpu.make_async_remote_copy(
            src_ref=src,
            dst_ref=src,
            send_sem=self.pair_send.at[chunk, block[0] // 2],
            recv_sem=self.pair_recv.at[chunk, block[0] // 2],
            device_id=self.sibling(),
            device_id_type=MESH,
        )

    def start(self, chunk):
        own = (self.z, self.x, self.y)
        for dim in self.orders[chunk]:
            self.send(chunk, own, dim, True)
        self.pair(chunk, own, self.core).start()

    def events(self, chunk, start=0.0, pace=1.0):
        held, found = [(0, 0, 0, 0, start)], []
        for dim in self.orders[chunk]:
            clock, new = 0.0, []
            ordered = sorted(held, key=lambda item: item[4])
            if dim == "z":
                for dist in (1, 2, 3):
                    for item in ordered:
                        clock = max(clock, item[4]) + pace
                        new += [(dist, way, item[2], item[3], clock) for way in (1, -1)]
            else:
                for item in ordered:
                    clock = max(clock, item[4]) + pace
                    flip = (1, item[3]) if dim == "x" else (item[2], 1)
                    new.append((item[0], item[1], *flip, clock))
            found += [
                (item[4], chunk, functools.partial(self.arrive, chunk, dim, item)) for item in new
            ]
            held = held + new
        return found

    def arrive(self, chunk, dim, item):
        dist, way, flip_x, flip_y, _ = item
        cond = True
        if way == 1:
            cond = self.z >= dist
        elif way == -1:
            cond = self.z + dist <= 3
        if cond is False:
            return
        block = (
            self.z - dist * way,
            1 - self.x if flip_x else self.x,
            1 - self.y if flip_y else self.y,
        )
        src = self.view(chunk, block, self.core)
        arriving = pltpu.make_async_remote_copy(
            src_ref=src,
            dst_ref=src,
            send_sem=self.send_sem.at[chunk, 0],
            recv_sem=self.recv_sem.at[chunk, self.rail(block)],
            device_id=self.sibling(),
            device_id_type=MESH,
        )
        when(cond, arriving.wait_recv)
        if dim == "z":
            self.send(chunk, block, "z", cond, way)
        order = self.orders[chunk]
        for later in order[order.index(dim) + 1 :]:
            self.send(chunk, block, later, cond)
        when(cond, self.pair(chunk, block, self.core).start)

    def rails(self, chunk):
        return 4 * (2 if "x" in self.orders[chunk] else 1) * (2 if "y" in self.orders[chunk] else 1)

    def sent(self, chunk, z, over):
        order = self.orders[chunk]
        fresh = (z < 3) + (z > 0) if over == "z" else 1
        total = fresh if over in order else 0
        for _, _, work in self.events(chunk):
            _, dim, (dist, way, *_) = work.args
            if (way == 1 and z < dist) or (way == -1 and z + dist > 3):
                continue
            total += fresh if over in order[order.index(dim) + 1 :] else 0
            if dim == "z" and over == "z":
                total += z < 3 if way == 1 else z > 0
        return total

    def wait_side(self, chunk, side):
        every = self.bulk(chunk, self.rails(chunk) // 2)
        bulk_copy(every, self.pair_send.at[chunk, side], self.pair_recv.at[chunk, side]).wait_recv()

    def wait_pairs(self, chunk):
        for side in (0, 1):
            self.wait_side(chunk, side)

    def finish(self):
        ends = (self.z == 0) | (self.z == 3)
        inner = (self.z == 1) | (self.z == 2)
        for chunk in range(len(self.orders)):
            for dim in self.orders[chunk]:
                send_sem = self.send_sem.at[chunk, DIMS.index(dim)]
                for cond, z in ((ends, 0), (inner, 1)):
                    copy = bulk_copy(self.bulk(chunk, self.sent(chunk, z, dim)), send_sem, self.recv_sem.at[chunk, 0])
                    when(cond, copy.wait_send)
            every = self.bulk(chunk, self.rails(chunk) // 2)
            for side in (0, 1):
                bulk_copy(every, self.pair_send.at[chunk, side], self.pair_recv.at[chunk, side]).wait_send()


class Reduce:
    def __init__(self, known_z, view, orders, final, buf, bulk, send, recv):
        self.view, self.orders, self.final = view, orders, final
        self.buf, self.bulk = buf, bulk
        self.send_sem, self.recv_sem = send, recv
        self.z, self.x, self.core, self.y = place(known_z)
        self.index = [self.places(chunk) for chunk in range(len(orders))]

    def coords(self, block):
        zz, flip_x, flip_y = block
        return (zz, 1 - self.x if flip_x else self.x, 1 - self.y if flip_y else self.y)

    def own(self, chunk, block):
        return self.view(chunk, self.coords(block))

    def add(self, target, source):
        target[...] = target[...] + source[...]

    def sibling(self):
        return device(self.z, self.x, 1 - self.core, self.y)

    def blocks(self, chunk):
        return [(zz, fx, fy) for zz in (3, 0, 2, 1) for fx, fy in self.flips(chunk, 0)]

    def places(self, chunk):
        order, keys = self.orders[chunk], []
        for stage, dim in enumerate(order):
            if dim == "z":
                keys += [
                    self.z_key(stage, step, way, flips)
                    for step in range(3)
                    for way in ((1, -1) if step else (1,))
                    for flips in self.flips(chunk, stage)
                ]
                continue
            wheres = range(4) if "z" in order[stage:] else ("own",)
            later = self.flips(chunk, stage + 1)
            keys += [(stage, where, *flips) for where in wheres for flips in later]
        return {key: at for at, key in enumerate(keys)}

    def place_of(self, chunk, key):
        return self.index[chunk][key]

    def send(self, chunk, block, key, target, cond):
        if cond is False:
            return
        where = self.place_of(chunk, key)
        copy = pltpu.make_async_remote_copy(
            src_ref=self.own(chunk, block),
            dst_ref=self.buf(chunk, where),
            send_sem=self.send_sem.at[chunk, key[0]],
            recv_sem=self.recv_sem.at[chunk, where],
            device_id=target,
            device_id_type=MESH,
        )
        when(cond, copy.start)

    def landed(self, chunk, key):
        return self.buf(chunk, self.place_of(chunk, key))

    def wait(self, chunk, key):
        landed = self.landed(chunk, key)
        pltpu.make_async_remote_copy(
            src_ref=landed,
            dst_ref=landed,
            send_sem=self.send_sem.at[chunk, 0],
            recv_sem=self.recv_sem.at[chunk, self.place_of(chunk, key)],
            device_id=self.sibling(),
            device_id_type=MESH,
        ).wait_recv()

    def flips(self, chunk, stage):
        left = self.orders[chunk][stage:]
        return [
            (fx, fy)
            for fx in ((1, 0) if "x" in left else (0,))
            for fy in ((1, 0) if "y" in left else (0,))
        ]

    def ready(self, chunk, stage, block):
        order = self.orders[chunk]
        zz, fx, fy = block
        where = zz if "z" in order[stage:] else "own"
        if order[stage] == "x" and fx:
            target = device(self.z, 1 - self.x, self.core, self.y)
            self.send(chunk, block, (stage, where, 0, fy), target, True)
        elif order[stage] == "y" and fy:
            target = device(self.z, self.x, self.core, 1 - self.y)
            self.send(chunk, block, (stage, where, fx, 0), target, True)

    def z_key(self, stage, step, way, flips):
        return (stage, step, way if step else 0, *flips)

    def z_start(self, chunk, stage, step, flips):
        up, down = (3 - step, *flips), (step, *flips)
        right = device(self.z + 1, self.x, self.core, self.y)
        left = device(self.z - 1, self.x, self.core, self.y)
        self.send(chunk, up, self.z_key(stage, step, 1, flips), right, self.z == 0)
        self.send(chunk, down, self.z_key(stage, step, -1, flips), left, self.z == 3)

    def z_arrive(self, chunk, stage, step, flips, way):
        z = self.z if way == 1 else 3 - self.z
        cond = (z >= 1) & (z <= step + 1)
        zz = 2 + z - step
        zz = zz if way == 1 else 3 - zz
        block = (zz, *flips)
        key = self.z_key(stage, step, way, flips)
        last = stage + 1 == len(self.orders[chunk]) and step == 2

        def take():
            self.wait(chunk, key)
            if not last:
                self.add(self.own(chunk, block), self.landed(chunk, key))

        when(cond, take)
        if step < 2:
            target = device(self.z + way, self.x, self.core, self.y)
            self.send(chunk, block, self.z_key(stage, step + 1, way, flips), target, cond)

    def z_done(self, chunk, stage, flips):
        block = (self.z, *flips)
        if stage + 1 < len(self.orders[chunk]):
            self.ready(chunk, stage + 1, block)
            return
        final = self.final(chunk)
        final[...] = self.own(chunk, block)[...].astype(F32)
        for way, cond in ((1, self.z >= 1), (-1, self.z <= 2)):
            landed = self.landed(chunk, self.z_key(stage, 2, way, flips))

            def add(landed=landed):
                final[...] += landed[...].astype(F32)

            when(cond, add)

    def xy_arrive(self, chunk, stage, zz, fx, fy):
        key = (stage, zz, fx, fy)
        block = (self.z if zz == "own" else zz, fx, fy)
        self.wait(chunk, key)
        own, landed = self.own(chunk, block), self.landed(chunk, key)
        if stage + 1 < len(self.orders[chunk]):
            self.add(own, landed)
            self.ready(chunk, stage + 1, block)
        else:
            final = self.final(chunk)
            final[...] = own[...].astype(F32) + landed[...].astype(F32)

    def start(self, chunk, block):
        self.ready(chunk, 0, block)

    def events(self, chunks, start=0.0, pace=1.0):
        found = []
        for chunk in chunks:
            times = {block: start for block in self.blocks(chunk)}
            found += [
                (start, chunk, functools.partial(self.start, chunk, block))
                for block in self.blocks(chunk)
                if dict(x=block[1], y=block[2], z=0)[self.orders[chunk][0]]
            ]
            for stage, dim in enumerate(self.orders[chunk]):
                clock, later = 0.0, {}
                if dim == "z":
                    for step in range(3):
                        for flips in self.flips(chunk, stage):
                            needed = (0, 3) if step == 0 else (0, 1, 2, 3)
                            clock = max(clock, *(times[(zz, *flips)] for zz in needed)) + 0.001
                            work = functools.partial(self.z_start, chunk, stage, step, flips)
                            found.append((clock, chunk, work))
                            clock += pace
                            for way in (1, -1):
                                work = functools.partial(self.z_arrive, chunk, stage, step, flips, way)
                                found.append((clock, chunk, work))
                            later[("own", *flips)] = clock + 0.001
                    for flips in self.flips(chunk, stage):
                        work = functools.partial(self.z_done, chunk, stage, flips)
                        found.append((later[("own", *flips)], chunk, work))
                else:
                    pick = 1 if dim == "x" else 2
                    for key in sorted((k for k in times if k[pick]), key=lambda k: times[k]):
                        mine = (key[0], 0, key[2]) if dim == "x" else (key[0], key[1], 0)
                        clock = max(max(clock, times[key]) + pace, times[mine] + 0.001)
                        later[mine] = clock
                        work = functools.partial(self.xy_arrive, chunk, stage, *mine)
                        found.append((clock, chunk, work))
                times = later
        return found

    def finish(self):
        for chunk, order in enumerate(self.orders):
            for stage, dim in enumerate(order):
                after = len(self.flips(chunk, stage + 1)) if stage + 1 < len(order) else 1
                count = 3 * after if dim == "z" else after * (4 if "z" in order[stage + 1 :] else 1)
                every = self.bulk(chunk, count)
                bulk_copy(every, self.send_sem.at[chunk, stage], self.recv_sem.at[chunk, 0]).wait_send()


class Exchange:
    def __init__(self, source, landing, bulk, send_sem, recv_sem):
        self.source, self.landing, self.bulk = source, landing, bulk
        self.send_sem, self.recv_sem = send_sem, recv_sem
        self.band, self.y = lax.axis_index("band"), lax.axis_index("dp")
        self.bands = lax.axis_size("band")

    def send(self, target):
        pltpu.make_async_remote_copy(
            src_ref=self.source(target),
            dst_ref=self.landing(self.band),
            send_sem=self.send_sem,
            recv_sem=self.recv_sem,
            device_id=(target, self.y),
            device_id_type=MESH,
        ).start()

    def start(self):
        for step in range(1, self.bands):
            self.send((self.band + step) % self.bands)

    def wait(self):
        bulk_copy(self.bulk(self.bands - 1), self.send_sem, self.recv_sem).wait_recv()

    def finish(self):
        bulk_copy(self.bulk(self.bands - 1), self.send_sem, self.recv_sem).wait_send()


def dot_nt(left, right):
    return lax.dot_general(left, right, (((1,), (1,)), ((), ())), preferred_element_type=F32)


def dot_tn(left, right):
    return lax.dot_general(left, right, (((0,), (0,)), ((), ())), preferred_element_type=F32)


def dot_nn(left, right):
    return jnp.dot(left, right, preferred_element_type=F32)


def unit_parts(rows):
    centred = rows - jnp.mean(rows, axis=-1, keepdims=True)
    inverse = lax.rsqrt(jnp.mean(centred * centred, axis=-1, keepdims=True) + EPS_BLOCK)
    return centred * inverse, inverse


class Block:
    def __init__(self, weights, down, refs):
        self.weights, self.down = weights, down
        self.__dict__.update(refs)
        self.width = weights.shape[1]
        self.tokens = self.joint.shape[1]
        self.halves = weights.shape[1] // (2 * HEAD_DIM)

    def weight(self, part):
        return self.weights[pl.ds(aligned(part * self.width), self.width), :]

    def masks(self):
        tokens = self.joint.shape[1]
        lane = lax.broadcasted_iota(jnp.int32, (tokens, 2 * HEAD_DIM), 1)
        low = lane < HEAD_DIM
        return low, low.astype(F32).astype(B16), (~low).astype(F32).astype(B16)

    def pair_rows(self, rows, low, high):
        return jnp.concatenate([rows * low, rows * high], axis=0)

    def own(self, ref):
        return ref[: self.tokens]

    def project(self):
        unit, inverse = unit_parts(self.residual[...])
        self.normed_one[: self.tokens] = (unit * self.gain_one[...]).astype(B16)
        self.unit_one[...] = unit
        self.inverse_one[...] = jnp.broadcast_to(inverse, self.inverse_one.shape)

        @pl.loop(0, 3)
        def _(part):
            self.joint[part] = dot_nn(self.own(self.normed_one), self.weight(part)).astype(B16)

    def attend(self):
        tokens = self.joint.shape[1]
        scale = 1.0 / math.sqrt(HEAD_DIM)

        @pl.loop(0, self.halves)
        def _(pair):
            where, low, high = self.masks()
            lanes = pl.ds(pl.multiple_of(pair * 2 * HEAD_DIM, 2 * HEAD_DIM), 2 * HEAD_DIM)
            query, key, value = (self.joint[part, :, lanes] for part in range(3))
            scores = dot_nt(self.pair_rows(query, low, high), key) * scale
            raised = jnp.exp(scores - jnp.max(scores, axis=-1, keepdims=True))
            probs = raised / jnp.sum(raised, axis=-1, keepdims=True)
            self.probs[pair] = probs
            mixed = dot_nn(probs.astype(B16), value)
            self.mixed[:tokens, lanes] = jnp.where(where, mixed[:tokens], mixed[tokens:]).astype(B16)

    def middle(self):
        middle = self.residual[...] + dot_nn(self.own(self.mixed), self.weight(3))
        unit, inverse = unit_parts(middle)
        self.normed_two[: self.tokens] = (unit * self.gain_two[...]).astype(B16)
        self.unit_two[...] = unit
        self.inverse_two[...] = jnp.broadcast_to(inverse, self.inverse_two.shape)
        self.result[...] = middle

    def both_x(self, ref):
        return ref[: 2 * self.tokens]

    def down_rows(self, part):
        return self.down[pl.ds(aligned(part * self.width), self.width), :]

    def widen(self):
        @pl.loop(0, 2)
        def _(part):
            pre = dot_nn(self.both_x(self.normed_two), self.weight(4 + part))
            self.pre_act[part] = pre
            self.act[part, : 2 * self.tokens] = gelu_tanh(pre).astype(B16)

    def narrow(self):
        parts = [dot_nn(self.act[part, : 2 * self.tokens], self.down_rows(part)) for part in (0, 1)]
        total = parts[0] + parts[1]
        self.result[...] += total[: self.tokens]
        self.result_x[...] = total[self.tokens :].astype(B16)

    def back_narrow(self):
        self.grad_normed[...] = jnp.zeros(self.grad_normed.shape, F32)

        @pl.loop(0, 2)
        def _(part):
            grad_act = dot_nt(self.both_x(self.out_grad), self.down_rows(part))
            grad_pre = (grad_act * gelu_slope(self.pre_act[part])).astype(B16)
            self.grad_pre[part, : 2 * self.tokens] = grad_pre
            self.grad_normed[...] += dot_nt(grad_pre, self.weight(4 + part))

        self.grad_x[...] = self.grad_normed[self.tokens :].astype(B16)

    def turn(self, ref):
        rows = ref.shape[0]
        for at in range(0, self.width, 128):
            self.turned[at : at + 128, :rows] = ref[:, at : at + 128].T

    def down_grad(self, part, core, rail, store):
        self.turn(self.act.at[part])
        for z in (0, 1):
            rail[z * 2 * PART : (z + 1) * 2 * PART, :] = self.turned[
                pl.ds(aligned((z * 2 + core) * 2 * PART), 2 * PART), :
            ]
        for at in range(0, self.width, 256):
            cols = slice(at, at + 256)
            rows = slice(part * 4 * PART, (part + 1) * 4 * PART)
            store[rows, cols] = dot_nn(rail[...], self.out_grad[:, cols]).astype(B16)

    def turn_rail(self, target, ref, core):
        rows = ref.shape[0]
        self.turn(ref)
        for chip in range(8):
            target[chip * CHUNK : (chip + 1) * CHUNK, :] = self.turned[
                pl.ds(aligned((chip * 2 + core) * CHUNK), CHUNK), :rows
            ]

    def pair_grad(self, first, second, first_grad, second_grad, store, where):
        half = CHUNK // 2
        for at in range(0, self.width, 256):
            cols = slice(at, at + 256)
            one = dot_nn(first[...], first_grad(cols))
            two = dot_nn(second[...], second_grad(cols))
            for owner in range(16):
                rows = slice(owner * half, owner * half + half)
                piece = jnp.concatenate([one[rows], two[rows]], axis=0)
                store[pl.ds(where(owner), CHUNK), cols] = piece.astype(B16)

    def back_wide(self):
        grad_normed = self.own(self.grad_normed) + self.grad_from_x[...].astype(F32)
        unit = self.unit_two[...]
        self.small[1:2, :] = jnp.sum(grad_normed * unit, axis=0, keepdims=True)
        scaled = grad_normed * self.gain_two[...]
        back = self.inverse_two[:, :1] * (
            scaled
            - jnp.mean(scaled, axis=-1, keepdims=True)
            - unit * jnp.mean(scaled * unit, axis=-1, keepdims=True)
        )
        grad_middle = self.own(self.out_grad).astype(F32) + back
        self.grad_middle[...] = grad_middle
        branch = grad_middle.astype(B16)
        self.grad_branch[: self.tokens] = branch
        self.grad_mixed[...] = dot_nt(branch, self.weight(3)).astype(B16)

    def back_attend(self):
        tokens = self.joint.shape[1]
        scale = 1.0 / math.sqrt(HEAD_DIM)

        @pl.loop(0, self.halves)
        def _(pair):
            where, low, high = self.masks()
            lanes = pl.ds(pl.multiple_of(pair * 2 * HEAD_DIM, 2 * HEAD_DIM), 2 * HEAD_DIM)
            query, key, value = (self.joint[part, :, lanes] for part in range(3))
            grads = self.pair_rows(self.grad_mixed[:, lanes], low, high)
            probs = self.probs[pair]
            self.grad_joint[2, :tokens, lanes] = dot_tn(probs.astype(B16), grads).astype(B16)
            grad_probs = dot_nt(grads, value)
            total = jnp.sum(grad_probs * probs, axis=-1, keepdims=True)
            grad_scores = (probs * (grad_probs - total)).astype(B16)
            queries = dot_nn(grad_scores, key) * scale
            self.grad_joint[0, :tokens, lanes] = jnp.where(
                where, queries[:tokens], queries[tokens:]
            ).astype(B16)
            keys = dot_tn(grad_scores, self.pair_rows(query, low, high)) * scale
            self.grad_joint[1, :tokens, lanes] = keys.astype(B16)

    def back_project(self):
        parts = [dot_nt(self.grad_joint[part, : self.tokens], self.weight(part)) for part in range(3)]
        grad_normed = parts[0] + parts[1] + parts[2]
        unit = self.unit_one[...]
        self.small[0:1, :] = jnp.sum(grad_normed * unit, axis=0, keepdims=True)
        scaled = grad_normed * self.gain_one[...]
        back = self.inverse_one[:, :1] * (
            scaled
            - jnp.mean(scaled, axis=-1, keepdims=True)
            - unit * jnp.mean(scaled * unit, axis=-1, keepdims=True)
        )
        self.grad_middle[...] += back

    def embed_grad(self):
        return self.grad_middle[...].astype(B16)


def split3(rows):
    first = rows.astype(B16)
    rest = rows - first.astype(F32)
    second = rest.astype(B16)
    return first, second, (rest - second.astype(F32)).astype(B16)


def fold3(stacked):
    rows = stacked.shape[0] // 3
    return stacked[:rows] + (stacked[rows : 2 * rows] + stacked[2 * rows :])


def wide_nn(rows, weight):
    return fold3(dot_nn(jnp.concatenate(split3(rows), axis=0), weight))


def wide_nt(rows, weight):
    return fold3(dot_nt(jnp.concatenate(split3(rows), axis=0), weight))


def wide_tn(left, right):
    one, two = split3(left), split3(right)
    pairs = ((0, 0), (0, 1), (1, 0), (0, 2), (1, 1), (2, 0))
    return dot_tn(
        jnp.concatenate([one[a] for a, _ in pairs], axis=0),
        jnp.concatenate([two[b] for _, b in pairs], axis=0),
    )


def exact_dot(left, right, dims):
    return lax.dot_general(
        left, right, (dims, ((), ())), precision=PRECISE, preferred_element_type=F32
    )


def hyper_unit(rows):
    centred = rows - jnp.mean(rows, axis=-1, keepdims=True)
    inverse = lax.rsqrt(jnp.mean(centred * centred, axis=-1, keepdims=True) + EPS_HYPER)
    return centred * inverse, inverse


def unit_back(scaled, unit, inverse):
    return inverse * (
        scaled
        - jnp.mean(scaled, axis=-1, keepdims=True)
        - unit * jnp.mean(scaled * unit, axis=-1, keepdims=True)
    )


def by_head(rows):
    lane = lax.broadcasted_iota(jnp.int32, rows.shape, 1) // (rows.shape[1] // HHEADS)
    return jnp.concatenate([jnp.where(lane == head, rows, 0.0) for head in range(HHEADS)], axis=0)


def own_lanes(stacked):
    tokens = stacked.shape[0] // HHEADS
    out = jnp.zeros((tokens, stacked.shape[1]), F32)
    for head in range(HHEADS):
        rows = stacked[head * tokens : (head + 1) * tokens]
        lane = lax.broadcasted_iota(jnp.int32, rows.shape, 1) // (rows.shape[1] // HHEADS)
        out = out + jnp.where(lane == head, rows, 0.0)
    return out


def hyper_forward(waves, qkv, out, gain_one, up, down, gain_two):
    width = waves.shape[1]
    joint = wide_nn(waves, qkv)
    query, key, value = (joint[:, at * width : (at + 1) * width] for at in range(3))
    scores = exact_dot(by_head(query), key, ((1,), (1,))) / math.sqrt(width // HHEADS)
    raised = jnp.exp(scores - jnp.max(scores, axis=-1, keepdims=True))
    soft = raised / jnp.sum(raised, axis=-1, keepdims=True)
    mixed = own_lanes(exact_dot(soft, value, ((1,), (0,))))
    unit_one, inverse_one = hyper_unit(waves + wide_nn(mixed, out))
    first = unit_one * gain_one
    inner = wide_nn(first, up)
    unit_two, inverse_two = hyper_unit(first + wide_nn(gelu_tanh(inner), down))
    kept = (joint, soft, mixed, unit_one, inverse_one, inner, unit_two, inverse_two)
    return unit_two * gain_two, kept


def hyper_backward(grad_code, kept, waves, qkv, out, gain_one, up, down, gain_two):
    joint, soft, mixed, unit_one, inverse_one, inner, unit_two, inverse_two = kept
    width = waves.shape[1]
    query, key, value = (joint[:, at * width : (at + 1) * width] for at in range(3))
    first = unit_one * gain_one
    grad_gain_two = jnp.sum(grad_code * unit_two, axis=0, keepdims=True)
    grad_second = unit_back(grad_code * gain_two, unit_two, inverse_two)
    grad_down = wide_tn(gelu_tanh(inner), grad_second)
    grad_inner = wide_nt(grad_second, down) * gelu_slope(inner)
    grad_up = wide_tn(first, grad_inner)
    grad_first = grad_second + wide_nt(grad_inner, up)
    grad_gain_one = jnp.sum(grad_first * unit_one, axis=0, keepdims=True)
    grad_mid = unit_back(grad_first * gain_one, unit_one, inverse_one)
    grad_out = wide_tn(mixed, grad_mid)
    grad_mixed = by_head(wide_nt(grad_mid, out))
    grad_value = exact_dot(soft, grad_mixed, ((0,), (0,)))
    grad_soft = exact_dot(grad_mixed, value, ((1,), (1,)))
    total = jnp.sum(grad_soft * soft, axis=-1, keepdims=True)
    grad_scores = soft * (grad_soft - total) / math.sqrt(width // HHEADS)
    grad_query = own_lanes(exact_dot(grad_scores, key, ((1,), (0,))))
    grad_key = exact_dot(grad_scores, by_head(query), ((0,), (0,)))
    grad_qkv = wide_tn(waves, jnp.concatenate([grad_query, grad_key, grad_value], axis=1))
    return grad_qkv, grad_out, grad_gain_one, grad_up, grad_down, grad_gain_two


def spread(gathered, weights):
    width = weights.shape[1]
    half = CHUNK // 2

    @pl.loop(0, 16)
    def _(two):
        for pair in (0, 1):
            one, other = (
                gathered[pl.ds(aligned((two * 2 + k) * PART + pair * CHUNK), CHUNK), :].astype(F32)
                for k in (0, 1)
            )
            for k, rows in ((0, slice(0, half)), (1, slice(half, CHUNK))):
                target = pl.ds(aligned((2 * pair + k) * width + two * CHUNK), CHUNK)
                weights[target, :] = jnp.concatenate([one[rows], other[rows]], 0).astype(B16)


def spread_up(gathered, weights, x):
    width = weights.shape[1]
    half = CHUNK // 2

    @pl.loop(0, 8)
    def _(chip):
        z, core = chip // 2, chip % 2
        for far in (0, 1):
            one, other = (
                gathered[pl.ds(aligned((chip * 2 + k) * PART + far * CHUNK), CHUNK), :].astype(F32)
                for k in (0, 1)
            )
            row = (z * 4 + (1 - x if far else x) * 2 + core) * CHUNK
            for k, rows in ((0, slice(0, half)), (1, slice(half, CHUNK))):
                target = pl.ds(aligned((4 + k) * width + row), CHUNK)
                weights[target, :] = jnp.concatenate([one[rows], other[rows]], 0).astype(B16)


def swap_rows(rows):
    count = rows.shape[0]
    row = lax.broadcasted_iota(jnp.int32, (count, count), 0)
    col = lax.broadcasted_iota(jnp.int32, (count, count), 1)
    swap = (col == (row % 16) * 16 + row // 16).astype(F32).astype(B16)
    return dot_nn(swap, rows).astype(B16)


def rows16(ref, index):
    return ref.at[pl.ds(aligned(index * 16), 16)]


KEPT = 9
SHARED = ("og", "n1", "mx", "n2", "a0", "a1")
SHARED += ("p0", "p1", "gb", "j0", "j1", "j2")
ACROSS = ("u", "og", "n2", "r", "g", "s")


def layer_kernel(*refs):
    (counts, mask, pixels, kernel_gen, attn_qkv, attn_out, mlp_up, mlp_down, waves, hyper_qkv, hyper_out, hyper_one, hyper_two,
     hyper_up, hyper_down, bias_gen, out_grad_in, norm_one, norm_two,
     block_out, pixel_out, shares, kernel_grads, code_out, code_grads, vectors, *rest_refs) = refs
    kept_refs, rest_refs = rest_refs[: KEPT], rest_refs[KEPT :]
    (gathered_attn, gathered_up, gathered_down, weights, spare, buf, joint, probs, pre_act, act, grad_pre, out_grad, mixed, normed_one, normed_two,
     unit_one, unit_two, inverse_one, inverse_two, grad_normed, grad_middle, grad_branch, grad_mixed, grad_joint,
     turned, rail_one, rail_mixed, rail_two, up_away, up_share, up_landed, result_x, result_from_x, grad_x, grad_from_x,
     residual, pixel_rows, turned_pixels, pair_pixels, mixing, kernels, pair_kernels, sending,
     landed_grads, summed, small, small_partner, small_all, code_part, code_all, gains, band_scale, pair_scale,
     pix_sem, gen_sem, front_done, narrow_done, *sems) = rest_refs
    z, x, core, y = place()
    band = lax.axis_index("band")
    bands = lax.axis_size("band")
    me = slot(z, x, core, y)
    width = gains.shape[1]
    tokens = out_grad_in.shape[0]
    sibling = (band + 1 - 2 * core, y)
    partner = (band, 1 - y)
    own_rows = pl.ds(aligned(band * 16), 16)
    gather_sems, grads_sems = sems[0:4], sems[4:8]
    (reduce_sems, embed_sems, share_sems, across_sems, front_sems, kernel_sems, cols_sems, summed_sems, vec_half_sems, vec_sems,
     code_sems) = (sems[at : at + 2] for at in range(8, 30, 2))
    gathered = (gathered_attn, gathered_up, gathered_down)

    def to_pair(index, source, target, pair=share_sems):
        return pltpu.make_async_remote_copy(
            src_ref=source,
            dst_ref=target,
            send_sem=pair[0].at[index],
            recv_sem=pair[1].at[index],
            device_id=sibling,
            device_id_type=MESH,
        )

    def shared(name):
        index = SHARED.index(name)
        ref = dict(
            og=out_grad, n1=normed_one, mx=mixed, n2=normed_two, gb=grad_branch
        ).get(name)
        if ref is None:
            ref = dict(a=act, p=grad_pre, j=grad_joint)[name[0]].at[int(name[1])]
        half = ref.shape[0] // 2
        return to_pair(index, ref.at[pl.ds(0, half)], ref.at[pl.ds(half, half)])

    own_block = aligned((z * 4 + core * 2 + y) * PART)

    def across(name):
        own, other = pl.ds(0, tokens), pl.ds(tokens, tokens)
        source, target = dict(
            u=(up_away, gathered_up.at[pl.ds(own_block + CHUNK, CHUNK)]),
            og=(out_grad.at[own], out_grad.at[other]),
            n2=(normed_two.at[own], normed_two.at[other]),
            r=(result_x, result_from_x),
            g=(grad_x, grad_from_x),
            s=(up_share.at[pl.ds(CHUNK, CHUNK)], up_landed),
        )[name]
        return pltpu.make_async_remote_copy(
            src_ref=source,
            dst_ref=target,
            send_sem=across_sems[0].at[ACROSS.index(name)],
            recv_sem=across_sems[1].at[ACROSS.index(name)],
            device_id=device(z, 1 - x, core, y),
            device_id_type=MESH,
        )

    def gen_copy(piece, target):
        return pltpu.make_async_copy(
            kernel_gen.at[:, pl.ds(piece * width, width)], target.at[pl.ds(piece * 128, 128)], gen_sem
        )

    def gen_wait(target):
        every = target.at[pl.ds(0, 16 * 128)]
        pltpu.make_async_copy(every, every, gen_sem).wait()

    barrier = pltpu.get_barrier_semaphore()
    tell_peers(barrier)
    for piece in range(16):
        gen_copy(piece, spare).start()
    load_pixels = pltpu.make_async_copy(pixels, pixel_rows, pix_sem)
    load_pixels.start()

    gains[0:1, :] = norm_one[...].astype(F32).reshape(1, width)
    gains[1:2, :] = norm_two[...].astype(F32).reshape(1, width)
    out_grad[0:tokens, :] = out_grad_in[...]
    for image in range(band_scale.shape[0]):
        used = jnp.where((band < counts[image]) & (mask[image] == 1), 1.0, 0.0)
        bands_here = jnp.full(band_scale.shape[1:], counts[image], jnp.int32).astype(F32)
        band_scale[image] = lax.rsqrt(bands_here) * used

    def rows_of(weight, piece):
        return weight[:, piece * width : (piece + 1) * width].astype(F32)

    pieces = [rows_of(attn_qkv, at) for at in range(3)] + [rows_of(attn_out, 0)]
    for at in (0, 1):
        rows = jnp.concatenate(pieces[2 * at : 2 * at + 2], axis=0).astype(B16)
        gathered_attn[pl.ds(aligned(me * PART + at * CHUNK), CHUNK), :] = rows

    def up_half(of_x):
        group = 4 * PART
        quarters = [
            jnp.concatenate([mlp_up[:, at * group : (at + 1) * group] for at in (first, first + 2)], axis=1)
            for first in (of_x, of_x + 4)
        ]
        return jnp.concatenate([quarter.astype(F32) for quarter in quarters], axis=0).astype(B16)

    for of_x in (0, 1):

        @pl.when(x == of_x)
        def _(of_x=of_x):
            gathered_up[pl.ds(own_block, CHUNK), :] = up_half(of_x)
            up_away[...] = up_half(1 - of_x)

    gathered_down[pl.ds(own_block, PART), :] = mlp_down[...]
    hyper_gains = [gain[...].astype(F32).reshape(1, HW) for gain in (hyper_one, hyper_two)]
    code, kept = hyper_forward(
        waves[...], hyper_qkv[...], hyper_out[...], hyper_gains[0], hyper_up[...], hyper_down[...], hyper_gains[1]
    )
    kept = (*kept, jnp.concatenate(hyper_gains, axis=0))
    code_low = code.astype(B16)
    code_out[...] = code_low
    for ref, value in zip(kept_refs, kept):
        ref[...] = value

    def weight_view(part, block, side):
        if part == 0:
            where = slot(block[0], block[1], side, block[2])
        else:
            where = block[0] * 4 + side * 2 + block[2]
        return gathered[part].at[pl.ds(aligned(where * PART), PART)]

    half = tokens // 2

    def image_row(block, side):
        return (block[0] * 4 + block[1] * 2 + side) * tokens

    def rail_row(block):
        return (block[0] * 2 + block[1]) * tokens

    def gather_at(known_z=None):
        return Gather(
            known_z, weight_view, ORDERS, lambda part, count: gathered[part].at[pl.ds(0, count * PART)], *gather_sems
        )

    def embed_at(known_z=None):
        return Reduce(
            known_z,
            lambda chunk, block: spare.at[pl.ds(aligned(rail_row(block) + chunk * half), half)],
            EMBED_ORDERS,
            lambda chunk: residual.at[pl.ds(chunk * half, half)],
            lambda chunk, where: buf.at[pl.ds((chunk * 11 + where) * half, half)],
            lambda chunk, count: buf.at[pl.ds(0, count * half)],
            *embed_sems,
        )

    def front_works(known_z):
        known, sums = gather_at(known_z), embed_at(known_z)
        works = [work for part in range(3) for work in in_order(known.events(part))]
        return works + in_order(sums.events((0, 1)))

    gather, embed = gather_at(), embed_at()
    plan = Plan(FRONT_PLAN, [front_works(known_z) for known_z in range(4)])
    pl.semaphore_wait(barrier, 2 * bands - 1)
    load_pixels.wait()
    for chip in range(8):
        to_pair(0, pixel_rows.at[chip * 2 + 1 - core], pair_pixels.at[chip], front_sems).start()
    to_pair(1, band_scale, pair_scale, front_sems).start()
    plan.run()
    across("u").start()
    for part in FIRST_PARTS:
        gather.start(part)
    plan.run()

    gen_wait(spare)

    @pl.loop(0, 16)
    def _(piece):
        part = dot_nn(code_out[...], spare[pl.ds(aligned(piece * 128), 128), :])
        mixing[pl.ds(aligned(piece * 16), 16), :] = part.astype(B16)

    sending[...] = swap_rows(mixing[...])
    spread_kernels = Exchange(
        lambda target: rows16(sending, target),
        lambda source: rows16(kernels, source),
        lambda count: kernels.at[pl.ds(0, count * 16)],
        *[sem.at[0] for sem in kernel_sems],
    )
    spread_kernels.start()
    plan.run()
    across("u").wait_recv()
    for part in range(3):
        if part not in FIRST_PARTS:
            gather.start(part)
    across("og").start()
    plan.run()
    kernels[own_rows, :] = sending[own_rows, :]
    biases = dot_nn(code_out[...], bias_gen[...])
    row = lax.broadcasted_iota(jnp.int32, biases.shape, 0)
    bias, pair_bias = (
        jnp.sum(jnp.where(row == of, biases, 0.0), axis=0, keepdims=True) for of in (band, sibling[0])
    )
    for group in range(4):
        turned_pixels[group] = pixel_rows[4 * group : 4 * group + 4].reshape(4 * tokens, -1).T
    plan.run()
    spread_kernels.wait()
    to_pair(2, kernels, pair_kernels, front_sems).start()
    plan.run()
    to_pair(0, pair_pixels, pair_pixels, front_sems).wait_recv()
    to_pair(1, band_scale, pair_scale, front_sems).wait_recv()
    to_pair(2, kernels, pair_kernels, front_sems).wait_recv()

    def term(group):
        mine = [group * 4 + x_of * 2 + core for x_of in (0, 1)]
        rows = jnp.concatenate([pixel_rows[image] for image in mine], axis=0)
        pair_rows = pair_pixels[2 * group : 2 * group + 2].reshape(2 * tokens, -1)
        for at in range(0, width, 256):
            cols = slice(at, at + 256)
            one = dot_nn(rows, kernels[:, cols]) + bias[:, cols]
            two = dot_nn(pair_rows, pair_kernels[:, cols]) + pair_bias[:, cols]
            for x_of, image in enumerate(mine):
                own = slice(x_of * tokens, (x_of + 1) * tokens)
                total = one[own] * band_scale[image][:1, :1] + two[own] * pair_scale[image][:1, :1]
                start = (2 * group + x_of) * tokens
                spare[start : start + tokens, cols] = total.astype(B16)

    for group in (3, 0, 2, 1):
        plan.run()
        term(group)
    plan.run()
    gather.wait_pairs(0)
    spread(gathered_attn, weights)

    names = dict(
        residual=residual, out_grad=out_grad, gain_one=gains.at[0:1], gain_two=gains.at[1:2], block_out=block_out,
        joint=joint, probs=probs, pre_act=pre_act, act=act,
        grad_pre=grad_pre, mixed=mixed, normed_one=normed_one, normed_two=normed_two, unit_one=unit_one,
        unit_two=unit_two, inverse_one=inverse_one, inverse_two=inverse_two, result=residual, grad_normed=grad_normed,
        grad_middle=grad_middle, grad_branch=grad_branch, grad_mixed=grad_mixed, grad_joint=grad_joint,
        turned=turned, small=small, result_x=result_x, grad_x=grad_x, grad_from_x=grad_from_x,
    )
    block = Block(weights, gathered_down, names)
    plan.run()
    block.project()
    shared("n1").start()
    plan.run()
    block.attend()
    shared("mx").start()
    plan.run()
    block.middle()
    across("n2").start()
    across("og").wait_recv()
    shared("og").start()
    plan.run()
    gather.wait_pairs(1)
    spread_up(gathered_up, weights, x)
    plan.run()
    across("n2").wait_recv()
    shared("n2").start()
    block.widen()
    for name in ("a0", "a1"):
        shared(name).start()
    plan.run()
    gather.wait_pairs(2)
    gather.finish()
    embed.finish()
    for copy in ((0, pair_pixels, pair_pixels), (1, band_scale, pair_scale), (2, kernels, pair_kernels)):
        to_pair(*copy, front_sems).wait_send()
    tell_near(front_done)

    def part_ref(part):
        return spare.at[pl.ds(8 * tokens, 8 * PART)] if part == 2 else gathered[part]

    def part_view(part, blk):
        where = blk[0] * 4 + blk[1] * 2 + blk[2] if part == 0 else blk[0] * 2 + blk[2]
        return part_ref(part).at[pl.ds(aligned(where * PART), PART)]

    def reduce_at(known_z=None):
        return Reduce(
            known_z,
            part_view,
            SUM_ORDERS,
            lambda part: up_share if part == 1 else shares.at[pl.ds(part * PART, PART)],
            lambda part, where: buf.at[pl.ds(((0, 19, 30)[part] + where) * PART, PART)],
            lambda part, count: part_ref(part).at[pl.ds(0, count * PART)],
            *reduce_sems,
        )

    def up_send():
        shares[pl.ds(aligned(PART + x * CHUNK), CHUNK), :] = up_share[:CHUNK]
        across("s").start()

    def up_take():
        across("s").wait_recv()
        shares[pl.ds(aligned(PART + (1 - x) * CHUNK), CHUNK), :] = up_landed[...]

    image_grads = gathered_down

    def image_view(chunk, blk, side):
        return image_grads.at[pl.ds(aligned(image_row(blk, side) + chunk * half), half)]

    def grads_at(known_z=None):
        return Gather(
            known_z, image_view, IMAGE_ORDERS, lambda chunk, count: image_grads.at[pl.ds(0, count * half)], *grads_sems
        )

    def tail_works(known_z):
        known, images = reduce_at(known_z), grads_at(known_z)
        works = [work for part in (2, 1, 0) for work in in_order(known.events((part,)))]
        works += [work for chunk in (0, 1) for work in in_order(images.events(chunk))]
        return works + [up_send, up_take]

    reduce, grads = reduce_at(), grads_at()
    plan = Plan(TAIL_PLAN, [tail_works(known_z) for known_z in range(4)])
    hear_near(front_done)
    plan.run()
    block.back_narrow()
    for part in (0, 1):
        shared(f"p{part}").start()
    across("g").start()
    plan.run()
    for name in ("og", "a0", "a1"):
        shared(name).wait_recv()
    for part in (0, 1):
        block.down_grad(part, core, rail_two, part_ref(2))
    plan.run()
    block.narrow()
    across("r").start()
    tell_near(narrow_done)
    plan.run()
    across("g").wait_recv()
    block.back_wide()
    shared("gb").start()
    plan.run()
    block.back_attend()
    for part in range(3):
        shared(f"j{part}").start()
    plan.run()
    block.back_project()
    hear_near(narrow_done)
    image_grads[pl.ds(aligned(band * tokens), tokens), :] = block.embed_grad()
    grads.start(0)
    grads.start(1)
    plan.run()
    for name in ("n2", "p0", "p1"):
        shared(name).wait_recv()
    block.turn_rail(rail_two, normed_two, core)

    def up_place(owner):
        zz, xx, yy = owner // 4, owner // 2 % 2, owner % 2
        return aligned((zz * 2 + yy) * PART + ((1 - x) if xx else x) * CHUNK)

    block.pair_grad(
        rail_two, rail_two, lambda cols: grad_pre[0, :, cols], lambda cols: grad_pre[1, :, cols], part_ref(1), up_place
    )
    plan.run()
    for name in ("n1", "mx", "gb", "j0", "j1", "j2"):
        shared(name).wait_recv()
    block.turn_rail(rail_one, normed_one, core)
    block.turn_rail(rail_mixed, mixed, core)
    block.pair_grad(
        rail_one, rail_one, lambda cols: grad_joint[0, :, cols], lambda cols: grad_joint[1, :, cols], part_ref(0),
        lambda owner: owner * PART,
    )
    block.pair_grad(
        rail_one, rail_mixed, lambda cols: grad_joint[2, :, cols], lambda cols: grad_branch[:, cols], part_ref(0),
        lambda owner: owner * PART + CHUNK,
    )
    for name in SHARED:
        shared(name).wait_send()
    for name in ("og", "n2", "g"):
        across(name).wait_send()
    for piece in range(16):
        gen_copy(piece, weights).start()

    kernel_total = pre_act.at[0]
    kernel_total[...] = jnp.zeros(kernel_total.shape, F32)
    small[2:3, :] = jnp.zeros((1, width), F32)
    near_side = z // 2
    for side in (near_side, 1 - near_side):
        plan.run()
        for chunk in (0, 1):
            grads.wait_side(chunk, side)

        @pl.loop(0, 2)
        def _(step, side=side):
            group = 2 * side + step
            for image in range(4):
                half_rows = slice(image % 2 * tokens, (image % 2 + 1) * tokens)
                rows = pl.ds(aligned((group * 4 + image) * tokens), tokens)
                scaled = image_grads[rows, :].astype(F32) * band_scale[group * 4 + image][:1, :1]
                small[2:3, :] += jnp.sum(scaled, axis=0, keepdims=True)
                act[image // 2, half_rows] = scaled.astype(B16)
            scaled = act[:, : 2 * tokens].reshape(4 * tokens, width)
            pixel_rows[pl.ds(group * 4, 4)] = dot_nt(scaled, kernels[...]).astype(B16).reshape(4, tokens, -1)
            kernel_total[...] += dot_nn(turned_pixels[group], scaled)

    store_pixels = pltpu.make_async_copy(pixel_rows, pixel_out, pix_sem)
    store_pixels.start()
    spread_kernels.finish()
    sending[...] = kernel_total[...].astype(B16)
    owner = core == y

    def column_copy(target, plane):
        return pltpu.make_async_remote_copy(
            src_ref=rows16(sending, target),
            dst_ref=rows16(landed_grads, y * bands + band),
            send_sem=cols_sems[0].at[0],
            recv_sem=cols_sems[1].at[0],
            device_id=(target, plane),
            device_id_type=MESH,
        )

    for step in range(1, bands):
        target = (band + step) % bands
        column_copy(target, target % 2).start()

    @pl.when(core != y)
    def _():
        column_copy(band, 1 - y).start()

    @pl.when(owner)
    def _():
        landed_grads[pl.ds(aligned((y * bands + band) * 16), 16), :] = sending[own_rows, :]

    vec_half = pltpu.make_async_remote_copy(
        src_ref=small, dst_ref=small_partner, send_sem=vec_half_sems[0].at[0], recv_sem=vec_half_sems[1].at[0],
        device_id=partner, device_id_type=MESH,
    )
    vec_half.start()
    plan.run()
    vec_half.wait_recv()
    small_all[band] = small[...] + small_partner[...]
    vector_spread = Exchange(
        lambda target: small_all.at[band], lambda source: small_all.at[source], lambda count: small_all.at[pl.ds(0, count)],
        *[sem.at[0] for sem in vec_sems],
    )
    vector_spread.start()
    plan.run()
    pix = summed.shape[0]

    def tell_code(target, plane):
        return pltpu.make_async_remote_copy(
            src_ref=code_all.at[band],
            dst_ref=code_all.at[band],
            send_sem=code_sems[0].at[0],
            recv_sem=code_sems[1].at[0],
            device_id=(target, plane),
            device_id_type=MESH,
        )

    pass_summed = pltpu.make_async_remote_copy(
        src_ref=summed, dst_ref=summed, send_sem=summed_sems[0].at[0], recv_sem=summed_sems[1].at[0],
        device_id=partner, device_id_type=MESH,
    )
    gen_wait(weights)

    @pl.when(owner)
    def _():
        bulk_copy(landed_grads.at[pl.ds(0, (2 * bands - 1) * 16)], cols_sems[0].at[0], cols_sems[1].at[0]).wait_recv()
        summed[...] = landed_grads[0:pix, :] + landed_grads[pix : 2 * pix, :]
        pass_summed.start()
        mixing[...] = swap_rows(summed[...])
        code_part[...] = jnp.zeros(code_part.shape, F32)

        @pl.loop(0, 16)
        def _(piece):
            code_part[...] += dot_nt(
                mixing[pl.ds(aligned(piece * 16), 16), :], weights[pl.ds(aligned(piece * 128), 128), :]
            )

        code_all[band] = code_part[...]
        for step in range(bands):
            for plane in (y, 1 - y) if step else (1 - y,):
                tell_code((band + step) % bands, plane).start()

    @pl.when(core != y)
    def _():
        pass_summed.wait_recv()

    store_columns = pltpu.make_async_copy(summed, kernel_grads, pix_sem)
    store_pixels.wait()
    store_columns.start()
    plan.run()
    across("r").wait_recv()
    block_out[...] = (residual[...] + result_from_x[...].astype(F32)).astype(B16)
    vector_spread.wait()
    vectors[...] = small_all[...]
    bulk = code_all.at[pl.ds(0, bands - 1)]
    pl.when(owner)(bulk_copy(bulk, code_sems[0].at[0], code_sems[1].at[0]).wait_recv)
    bulk = code_all.at[pl.ds(0, bands)]
    pl.when(core != y)(bulk_copy(bulk, code_sems[0].at[0], code_sems[1].at[0]).wait_recv)
    total = code_all[0]
    for source in range(1, bands):
        total = total + code_all[source]
    code_grads[...] = total
    plan.run()
    reduce.finish()
    grads.finish()
    for name in ("u", "r", "s"):
        across(name).wait_send()
    vec_half.wait_send()
    vector_spread.finish()

    @pl.when(owner)
    def _():
        sent = landed_grads.at[pl.ds(0, (bands - 1) * 16)]
        bulk_copy(sent, cols_sems[0].at[0], cols_sems[1].at[0]).wait_send()
        sent = code_all.at[pl.ds(0, 2 * bands - 1)]
        bulk_copy(sent, code_sems[0].at[0], code_sems[1].at[0]).wait_send()
        pass_summed.wait_send()

    @pl.when(core != y)
    def _():
        sent = landed_grads.at[pl.ds(0, bands * 16)]
        bulk_copy(sent, cols_sems[0].at[0], cols_sems[1].at[0]).wait_send()

    store_columns.wait()


VMEM_BYTES = 63 * 2**20


def layer(counts, mask, pixels, kernel_gen, weights, waves, hyper, bias_gen, out_grad, gains):
    width = bias_gen.shape[1]
    bands = lax.axis_size("band")
    devices = bands * lax.axis_size("dp")
    images, tokens, pix = pixels.shape
    hidden = hyper[4].shape[1]
    vmem = pl.BlockSpec(memory_space=pltpu.VMEM)
    hbm = pl.BlockSpec(memory_space=pl.ANY)
    smem = pl.BlockSpec(memory_space=pltpu.SMEM)
    shape = jax.ShapeDtypeStruct
    rows = lambda kind, *lead: pltpu.VMEM((*lead, tokens, width), kind)
    pair = lambda *lead: pltpu.VMEM((*lead, 2 * tokens, width), B16)
    four = lambda *lead: pltpu.VMEM((*lead, 4 * tokens, width), B16)
    dma = pltpu.SemaphoreType.DMA
    code = (bands, HW)
    kept = [(bands, 3 * HW), (HHEADS * bands, bands), code, code, (bands, 1), (bands, hidden), code, (bands, 1), (2, HW)]
    return pl.pallas_call(
        layer_kernel,
        out_shape=[
            shape((tokens, width), B16),
            shape(pixels.shape, B16),
            shape((3 * PART, width), F32),
            shape((pix, width), B16),
            shape(code, B16),
            shape(code, F32),
            shape((bands, 8, width), F32),
            *[shape(dims, F32) for dims in kept],
        ],
        in_specs=[smem] * 2 + [hbm] * 2 + [vmem] * 15,
        out_specs=[vmem, hbm, vmem, hbm] + [vmem] * 12,
        scratch_shapes=[
            pltpu.VMEM((devices * PART, width), B16),
            pltpu.VMEM((devices // 2 * PART, width), B16),
            pltpu.VMEM((images * tokens, width), B16),
            pltpu.VMEM((6 * width, width), B16),
            pltpu.VMEM((16 * HW, width), B16),
            pltpu.VMEM(((19 + 11 + 11) * PART, width), B16),
            rows(B16, 3),
            pltpu.VMEM((HEADS // 2, 2 * tokens, tokens), F32),
            pltpu.VMEM((2, 2 * tokens, width), F32),
            four(2),
            four(2),
            four(),
            pair(),
            pair(),
            four(),
            rows(F32),
            rows(F32),
            pltpu.VMEM((tokens, 128), F32),
            pltpu.VMEM((tokens, 128), F32),
            pltpu.VMEM((2 * tokens, width), F32),
            rows(F32),
            pair(),
            rows(B16),
            pair(3),
            pltpu.VMEM((width, 4 * tokens), B16),
            pltpu.VMEM((width // 2, 2 * tokens), B16),
            pltpu.VMEM((width // 2, 2 * tokens), B16),
            pltpu.VMEM((width // 2, 4 * tokens), B16),
            pltpu.VMEM((CHUNK, width), B16),
            pltpu.VMEM((PART, width), F32),
            pltpu.VMEM((CHUNK, width), F32),
            rows(B16),
            rows(B16),
            rows(B16),
            rows(B16),
            rows(F32),
            pltpu.VMEM(pixels.shape, B16),
            pltpu.VMEM((4, pix, 4 * tokens), B16),
            pltpu.VMEM((images // 2, tokens, pix), B16),
            pltpu.VMEM((pix, width), B16),
            pltpu.VMEM((pix, width), B16),
            pltpu.VMEM((pix, width), B16),
            pltpu.VMEM((pix, width), B16),
            pltpu.VMEM((2 * pix, width), B16),
            pltpu.VMEM((pix, width), B16),
            pltpu.VMEM((8, width), F32),
            pltpu.VMEM((8, width), F32),
            pltpu.VMEM((bands, 8, width), F32),
            pltpu.VMEM(code, F32),
            pltpu.VMEM((2 * bands, *code), F32),
            pltpu.VMEM((2, width), F32),
            pltpu.VMEM((images, 8, 128), F32),
            pltpu.VMEM((images, 8, 128), F32),
            dma,
            dma,
            pltpu.SemaphoreType.REGULAR,
            pltpu.SemaphoreType.REGULAR,
            *[dma((3, 3)), dma((3, 16)), dma((3, 2)), dma((3, 2))],
            *[dma((2, 3)), dma((2, 16)), dma((2, 2)), dma((2, 2))],
            *[dma((3, 3)), dma((3, 19))],
            *[dma((2, 2)), dma((2, 11))],
            *[dma((len(SHARED),))] * 2,
            *[dma((len(ACROSS),))] * 2,
            *[dma((3,))] * 2,
            *[dma((1,))] * 12,
        ],
        compiler_params=pltpu.CompilerParams(
            collective_id=0, has_side_effects=True, vmem_limit_bytes=VMEM_BYTES
        ),
        name="layer",
    )(counts, mask, pixels, kernel_gen, *weights, waves, *hyper, bias_gen, out_grad, *gains)


def finish_kernel(*refs):
    count = 13 + KEPT
    outside = refs[:count]
    (block_out, pixel_out, grad_qkv, grad_out, grad_gain_one, grad_up, grad_down, grad_gain_two, grad_gen, grad_bias,
     gain_one_sum, gain_two_sum, share_qkv, share_out, share_up, share_down, *scratch) = refs[count:]
    inside, (store, in_sem, copy_sem, gen_sem) = scratch[:count], scratch[count:]
    loads = [pltpu.make_async_copy(*pair, in_sem.at[at]) for at, pair in enumerate(zip(outside, inside))]
    for load in loads:
        load.start()
    (code_low, columns, shares, waves, hyper_qkv, hyper_out, hyper_up, hyper_down, bias_gen, code_grads, vectors,
     *kept_refs, hyper_gains, block_in, pixel_in) = inside
    width = bias_gen.shape[1]
    copies = [
        pltpu.make_async_copy(block_in, block_out, copy_sem.at[0]),
        pltpu.make_async_copy(pixel_in, pixel_out, copy_sem.at[1]),
    ]
    for load in loads[:2]:
        load.wait()
    code = code_low[...]
    swapped = swap_rows(columns[...])
    gen_copies = []
    for piece in range(16):
        store[piece] = dot_tn(code, swapped[piece * 16 : (piece + 1) * 16])
        gen_copies.append(
            pltpu.make_async_copy(
                store.at[piece], grad_gen.at[:, pl.ds(piece * width, width)], gen_sem.at[piece]
            )
        )
        gen_copies[-1].start()
    for load in loads[2:]:
        load.wait()
    for copy in copies:
        copy.start()
    share_qkv[...] = jnp.concatenate([shares[at * 24 : at * 24 + 24, :] for at in range(3)], axis=1)
    share_out[...] = shares[72:96, :]
    group = 4 * PART
    up_pieces = []
    for at in range(8):
        z_of, x_of = at // 2, at % 2
        row = PART + x_of * CHUNK + z_of // 2 * 24
        up_pieces.append(shares[row : row + 24, z_of % 2 * group : (z_of % 2 + 1) * group])
    share_up[...] = jnp.concatenate(up_pieces, axis=1)
    share_down[...] = shares[192:288, :]
    sums = jnp.sum(vectors[...], axis=0)
    gain_one_sum[...] = sums[0]
    gain_two_sum[...] = sums[1]
    bias_grads = vectors[:, 2, :]
    grad_bias[...] = dot_tn(jnp.concatenate([code] * 3, axis=0), jnp.concatenate(split3(bias_grads), axis=0))
    grad_code = code_grads[...] + wide_nt(bias_grads, bias_gen[...])
    grads = hyper_backward(
        grad_code, [ref[...] for ref in kept_refs], waves[...], hyper_qkv[...], hyper_out[...], hyper_gains[0:1, :],
        hyper_up[...], hyper_down[...], hyper_gains[1:2, :],
    )
    for ref, value in zip((grad_qkv, grad_out, grad_gain_one, grad_up, grad_down, grad_gain_two), grads):
        ref[...] = value
    for copy in copies + gen_copies:
        copy.wait()


def finish(waves, hyper, bias_gen, code_low, code_grads, vectors, columns, shares, block_out, pixel_grad, kept, kernel_gen, weights):
    width = bias_gen.shape[1]
    vmem = pl.BlockSpec(memory_space=pltpu.VMEM)
    hbm = pl.BlockSpec(memory_space=pl.ANY)
    shape = lambda array: jax.ShapeDtypeStruct(array.shape, F32)
    line = jax.ShapeDtypeStruct((1, HW), F32)
    weights_in = (hyper[0], hyper[1], hyper[4], hyper[5])
    operands = (code_low, columns, shares, waves, *weights_in, bias_gen, code_grads, vectors, *kept, block_out, pixel_grad)
    return pl.pallas_call(
        finish_kernel,
        out_shape=[
            jax.ShapeDtypeStruct(block_out.shape, B16),
            jax.ShapeDtypeStruct(pixel_grad.shape, B16),
            shape(hyper[0]), shape(hyper[1]), line, shape(hyper[4]), shape(hyper[5]), line,
            shape(kernel_gen), shape(bias_gen), *[jax.ShapeDtypeStruct((width,), F32)] * 2,
            *[shape(weight) for weight in weights],
        ],
        in_specs=[hbm] * len(operands),
        out_specs=[hbm, hbm] + [vmem] * 6 + [hbm] + [vmem] * 7,
        scratch_shapes=[
            *[pltpu.VMEM(operand.shape, operand.dtype) for operand in operands],
            pltpu.VMEM((16, HW, width), F32),
            pltpu.SemaphoreType.DMA((len(operands),)),
            pltpu.SemaphoreType.DMA((2,)),
            pltpu.SemaphoreType.DMA((16,)),
        ],
        compiler_params=pltpu.CompilerParams(vmem_limit_bytes=VMEM_BYTES),
        name="finish",
    )(*operands)


def body(
    pixels,
    wavelengths,
    band_counts,
    band_mask,
    hyper_qkv,
    hyper_out,
    hyper_gain1,
    hyper_up,
    hyper_down,
    hyper_gain2,
    kernel_gen,
    bias_gen,
    norm_gain1,
    attn_qkv,
    attn_out,
    norm_gain2,
    mlp_up,
    mlp_down,
    out_grad,
):
    f32 = jnp.float32
    b16 = jnp.bfloat16
    band_local = pixels.shape[3]
    pixel_local = pixels[0]
    model_width = bias_gen.shape[1]
    hyper_params = tuple(
        (
            weight.astype(f32)
            for weight in (hyper_qkv, hyper_out, hyper_gain1, hyper_up, hyper_down, hyper_gain2)
        )
    )
    wave_tokens = wave_embed(wavelengths, HW)
    band_code, hyper_pull = jax.vjp(lambda *params: hyper_net(wave_tokens, *params), *hyper_params)
    code_low = band_code.astype(b16)
    column_part = jnp.dot(code_low, kernel_gen, preferred_element_type=f32).astype(b16)
    kernel_rows = lax.all_to_all(column_part, "band", split_axis=0, concat_axis=1, tiled=True)
    kernels = kernel_rows.reshape(band_local, -1, model_width)
    first_band = lax.axis_index("band") * band_local
    own_code = lax.dynamic_slice_in_dim(code_low, first_band, band_local, 0)
    count_row = band_counts[0]
    biases = jnp.dot(own_code, bias_gen, preferred_element_type=f32)
    slot_ids = first_band + jnp.arange(band_local, dtype=jnp.int32)
    active = (slot_ids[None, :] < count_row[:, None]) & (band_mask[0] == 1)
    band_weight = jnp.where(active, lax.rsqrt(count_row.astype(f32))[:, None], f32(0.0))
    pixel_rows = pixel_local
    weight_rows = band_weight
    conv_out = jnp.einsum("inbp,bpd->inbd", pixel_rows, kernels, preferred_element_type=f32)
    residual = lax.psum_scatter(
        jnp.sum((conv_out + biases[None, None]) * weight_rows[:, None, :, None], axis=2),
        "band",
        scatter_dimension=0,
        tiled=True,
    )
    gathered = (
        lax.all_gather(attn_qkv, ("band", "dp"), axis=0, tiled=True),
        lax.all_gather(attn_out, ("band", "dp"), axis=0, tiled=True),
        lax.all_gather(mlp_up, ("band", "dp"), axis=0, tiled=True),
        lax.all_gather(mlp_down, ("band", "dp"), axis=0, tiled=True),
    )
    qkv_full, out_full, up_full, down_full = gathered
    gain_one = norm_gain1.astype(f32)
    gain_two = norm_gain2.astype(f32)
    images, tokens = (residual.shape[0], residual.shape[1])
    score_scale = 1.0 / math.sqrt(HEAD_DIM)
    normed_full, unit_one, inverse_one = norm_parts(residual, gain_one)
    normed_one = normed_full.astype(b16)
    joint_rows = jnp.einsum("ind,de->ine", normed_one, qkv_full, preferred_element_type=f32).astype(
        b16
    )
    queries = joint_rows[..., :model_width].reshape(images, tokens, HEADS, HEAD_DIM)
    key_rows = joint_rows[..., model_width : 2 * model_width].reshape(
        images, tokens, HEADS, HEAD_DIM
    )
    value_rows = joint_rows[..., 2 * model_width :].reshape(images, tokens, HEADS, HEAD_DIM)
    scores = (
        jnp.einsum("inhc,imhc->ihnm", queries, key_rows, preferred_element_type=f32) * score_scale
    )
    row_top = jnp.max(scores, axis=-1, keepdims=True)
    log_total = row_top + jnp.log(jnp.sum(jnp.exp(scores - row_top), axis=-1, keepdims=True))
    probs_full = jnp.exp(scores - log_total)
    probs_low = probs_full.astype(b16)
    mixed_low = (
        jnp.einsum("ihnm,imhc->inhc", probs_low, value_rows, preferred_element_type=f32)
        .reshape(images, tokens, model_width)
        .astype(b16)
    )
    middle = residual + jnp.einsum("ind,de->ine", mixed_low, out_full, preferred_element_type=f32)
    normed_two_full, unit_two, inverse_two = norm_parts(middle, gain_two)
    normed_two = normed_two_full.astype(b16)
    pre_act = jnp.einsum("ind,df->inf", normed_two, up_full, preferred_element_type=f32)
    act_low = gelu_tanh(pre_act).astype(b16)
    result = middle + jnp.einsum("inf,fd->ind", act_low, down_full, preferred_element_type=f32)
    block_out = result.astype(b16)[None]
    qkv_back, out_back, up_back, down_back = (
        lax.all_gather(attn_qkv, ("band", "dp"), axis=0, tiled=True),
        lax.all_gather(attn_out, ("band", "dp"), axis=0, tiled=True),
        lax.all_gather(mlp_up, ("band", "dp"), axis=0, tiled=True),
        lax.all_gather(mlp_down, ("band", "dp"), axis=0, tiled=True),
    )
    grad_top = out_grad[0]
    grad_down = jnp.einsum("inf,ind->fd", act_low, grad_top, preferred_element_type=f32)
    grad_act = jnp.einsum("ind,fd->inf", grad_top, down_back, preferred_element_type=f32)
    grad_pre = (grad_act * gelu_slope(pre_act)).astype(b16)
    grad_up = jnp.einsum("ind,inf->df", normed_two, grad_pre, preferred_element_type=f32)
    grad_normed_two = jnp.einsum("inf,df->ind", grad_pre, up_back, preferred_element_type=f32)
    grad_gain_two = jnp.sum(grad_normed_two * unit_two, axis=(0, 1))
    grad_middle = grad_top.astype(f32) + norm_back(grad_normed_two, gain_two, unit_two, inverse_two)
    grad_branch = grad_middle.astype(b16)
    grad_out_proj = jnp.einsum("ind,ine->de", mixed_low, grad_branch, preferred_element_type=f32)
    grad_mixed = (
        jnp.einsum("ine,de->ind", grad_branch, out_back, preferred_element_type=f32)
        .astype(b16)
        .reshape(images, tokens, HEADS, HEAD_DIM)
    )
    grad_values = jnp.einsum("ihnm,inhc->imhc", probs_low, grad_mixed, preferred_element_type=f32)
    grad_probs = jnp.einsum("inhc,imhc->ihnm", grad_mixed, value_rows, preferred_element_type=f32)
    grad_scores = (
        probs_full * (grad_probs - jnp.sum(grad_probs * probs_full, axis=-1, keepdims=True))
    ).astype(b16)
    grad_queries = (
        jnp.einsum("ihnm,imhc->inhc", grad_scores, key_rows, preferred_element_type=f32)
        * score_scale
    )
    grad_keys = (
        jnp.einsum("ihnm,inhc->imhc", grad_scores, queries, preferred_element_type=f32)
        * score_scale
    )
    grad_joint = jnp.concatenate(
        [
            grad_queries.reshape(images, tokens, model_width),
            grad_keys.reshape(images, tokens, model_width),
            grad_values.reshape(images, tokens, model_width),
        ],
        axis=-1,
    ).astype(b16)
    grad_qkv = jnp.einsum("ind,ine->de", normed_one, grad_joint, preferred_element_type=f32)
    grad_normed_one = jnp.einsum("ine,de->ind", grad_joint, qkv_back, preferred_element_type=f32)
    grad_gain_one = jnp.sum(grad_normed_one * unit_one, axis=(0, 1))
    grad_embed = grad_middle + norm_back(grad_normed_one, gain_one, unit_one, inverse_one)
    grad_embed_low = grad_embed.astype(b16)[None]
    grad_rows = lax.all_gather(grad_embed_low, "band", axis=1, tiled=True)[0].astype(f32)
    weight_rows = band_weight
    pixel_rows = pixel_local
    scaled = grad_rows[:, :, None, :] * weight_rows[:, None, :, None]
    bias_total = jnp.sum(scaled, axis=(0, 1))
    scaled_low = scaled.astype(b16)
    kernel_total = jnp.einsum("inbp,inbd->bpd", pixel_rows, scaled_low, preferred_element_type=f32)
    pixel_part = jnp.einsum(
        "inbd,bpd->inbp", scaled_low, kernels, preferred_element_type=f32
    ).astype(b16)
    pixel_total = pixel_part
    kernel_grad, bias_grad, pixel_total = (kernel_total, bias_total, pixel_total)
    pixel_out = pixel_total[None]
    kernel_grad_low = kernel_grad.reshape(band_local, -1).astype(b16)
    grad_columns = lax.all_to_all(kernel_grad_low, "band", split_axis=1, concat_axis=0, tiled=True)
    grad_kernel_part = jnp.einsum("nh,nc->hc", code_low, grad_columns, preferred_element_type=f32)
    grad_code_part = jnp.einsum("nc,hc->nh", grad_columns, kernel_gen, preferred_element_type=f32)
    bias_back = jnp.einsum("bd,hd->bh", bias_grad, bias_gen.astype(f32), precision=PRECISE)
    grad_code_part = grad_code_part + lax.dynamic_update_slice_in_dim(
        jnp.zeros_like(grad_code_part), bias_back, first_band, 0
    )
    grad_bias_part = jnp.einsum("bh,bd->hd", own_code.astype(f32), bias_grad, precision=PRECISE)
    grad_code, grad_bias_gen, grad_norm_gain1, grad_norm_gain2 = lax.psum(
        (grad_code_part, grad_bias_part, grad_gain_one, grad_gain_two), ("band", "dp")
    )
    grad_kernel_gen = lax.psum(grad_kernel_part.astype(jnp.bfloat16), "dp").astype(jnp.float32)
    hyper_grads = hyper_pull(grad_code)
    shares = (
        lax.psum_scatter(grad_qkv, ("band", "dp"), scatter_dimension=0, tiled=True),
        lax.psum_scatter(grad_out_proj, ("band", "dp"), scatter_dimension=0, tiled=True),
        lax.psum_scatter(grad_up, ("band", "dp"), scatter_dimension=0, tiled=True),
        lax.psum_scatter(grad_down, ("band", "dp"), scatter_dimension=0, tiled=True),
    )
    return (
        block_out,
        pixel_out,
        hyper_grads[0],
        hyper_grads[1],
        hyper_grads[2],
        hyper_grads[3],
        hyper_grads[4],
        hyper_grads[5],
        grad_kernel_gen,
        grad_bias_gen,
        grad_norm_gain1,
        shares[0],
        shares[1],
        grad_norm_gain2,
        shares[2],
        shares[3],
    )


def fast_body(
    pixels,
    wavelengths,
    band_counts,
    band_mask,
    hyper_qkv,
    hyper_out,
    hyper_gain1,
    hyper_up,
    hyper_down,
    hyper_gain2,
    kernel_gen,
    bias_gen,
    norm_gain1,
    attn_qkv,
    attn_out,
    norm_gain2,
    mlp_up,
    mlp_down,
    out_grad,
):
    lane = jnp.arange(HW)
    frequency = jnp.power(10000.0, -(lane % (HW // 2)).astype(F32) / (HW // 2))
    angles = wavelengths.astype(F32)[:, None] * frequency[None, :]
    waves = jnp.where(lane < HW // 2, jnp.sin(angles), jnp.cos(angles))
    weights = (attn_qkv, attn_out, mlp_up, mlp_down)
    hyper = (hyper_qkv, hyper_out, hyper_gain1, hyper_gain2, hyper_up, hyper_down)
    block_out, pixel_grad, shares, columns, code_low, code_grads, vectors, *kept = layer(
        band_counts[0],
        band_mask[0, :, 0],
        pixels[0, :, :, 0],
        kernel_gen,
        weights,
        waves,
        hyper,
        bias_gen,
        out_grad[0, 0],
        (norm_gain1, norm_gain2),
    )
    outs = finish(
        waves,
        hyper,
        bias_gen,
        code_low,
        code_grads,
        vectors,
        columns,
        shares,
        block_out,
        pixel_grad,
        kept,
        kernel_gen,
        weights,
    )
    block_out, pixel_grad, *hyper_grads, grad_gen, grad_bias, gain_one, gain_two = outs[:12]
    hyper_grads[2], hyper_grads[5] = hyper_grads[2][0], hyper_grads[5][0]
    return (
        block_out[None, None],
        pixel_grad[None, :, :, None],
        *hyper_grads,
        grad_gen,
        grad_bias,
        gain_one,
        outs[12],
        outs[13],
        gain_two,
        outs[14],
        outs[15],
    )


def solution(mesh):
    placed = (
        P("dp", None, None, "band", None),
        P(),
        P("dp", None),
        P("dp", None, "band"),
        P(),
        P(),
        P(),
        P(),
        P(),
        P(),
        P(None, "band"),
        P(),
        P(),
        P(("band", "dp"), None),
        P(("band", "dp"), None),
        P(),
        P(("band", "dp"), None),
        P(("band", "dp"), None),
        P("dp", "band", None, None),
    )
    one_slot = (mesh.shape["band"], mesh.shape["dp"]) == (16, 2)
    return jax.shard_map(
        fast_body if one_slot else body,
        mesh=mesh,
        in_specs=placed,
        out_specs=(
            P("dp", "band", None, None),
            P("dp", None, None, "band", None),
            P(),
            P(),
            P(),
            P(),
            P(),
            P(),
            P(None, "band"),
            P(),
            P(),
            P(("band", "dp"), None),
            P(("band", "dp"), None),
            P(),
            P(("band", "dp"), None),
            P(("band", "dp"), None),
        ),
        check_vma=False,
    )
```

```python
import functools
import math

import jax
import jax.numpy as jnp
from jax import lax
from jax.experimental import pallas as pl
from jax.experimental.pallas import tpu as pltpu
from jax.sharding import PartitionSpec as P
import numpy as np

HEADS = 12
HEAD_DIM = 64
HW = 128
HHEADS = 4


PRECISE = lax.Precision.HIGHEST
EPS_BLOCK = 1e-06
EPS_HYPER = 1e-05
GELU_COEF = 0.7978845608028654


def gelu_tanh(tensor):
    return (
        0.5 * tensor * (1.0 + jnp.tanh(GELU_COEF * (tensor + 0.044715 * tensor * tensor * tensor)))
    )


def gelu_slope(tensor):
    tanh_val = jnp.tanh(GELU_COEF * (tensor + 0.044715 * tensor * tensor * tensor))
    return 0.5 * (1.0 + tanh_val) + 0.5 * tensor * (1.0 - tanh_val * tanh_val) * GELU_COEF * (
        1.0 + 3.0 * 0.044715 * tensor * tensor
    )


def layer_norm(tensor, gain_vec, epsilon):
    centred = tensor - jnp.mean(tensor, axis=-1, keepdims=True)
    return (
        centred
        * lax.rsqrt(jnp.mean(centred * centred, axis=-1, keepdims=True) + epsilon)
        * gain_vec
    )


def norm_parts(tensor, gain_vec):
    centred = tensor - jnp.mean(tensor, axis=-1, keepdims=True)
    inverse = lax.rsqrt(jnp.mean(centred * centred, axis=-1, keepdims=True) + EPS_BLOCK)
    unit_rows = centred * inverse
    return (unit_rows * gain_vec, unit_rows, inverse)


def norm_back(grad_rows, gain_vec, unit_rows, inverse):
    scaled = grad_rows * gain_vec
    return inverse * (
        scaled
        - jnp.mean(scaled, axis=-1, keepdims=True)
        - unit_rows * jnp.mean(scaled * unit_rows, axis=-1, keepdims=True)
    )


def wave_embed(wave_ints, token_width):
    half_width = token_width // 2
    frequency = jnp.power(10000.0, -jnp.arange(half_width, dtype=jnp.float32) / half_width)
    angles = wave_ints.astype(jnp.float32)[:, None] * frequency[None, :]
    return jnp.concatenate([jnp.sin(angles), jnp.cos(angles)], axis=1)


def hyper_net(wave_tokens, qkv_weight, out_weight, gain_one, up_weight, down_weight, gain_two):
    tokens, token_width = wave_tokens.shape
    head_size = token_width // HHEADS
    qkv_rows = jnp.dot(wave_tokens, qkv_weight, precision=PRECISE)
    queries = qkv_rows[:, :token_width].reshape(tokens, HHEADS, head_size)
    key_rows = qkv_rows[:, token_width : 2 * token_width].reshape(tokens, HHEADS, head_size)
    value_rows = qkv_rows[:, 2 * token_width :].reshape(tokens, HHEADS, head_size)
    scores = jnp.einsum("nhc,mhc->hnm", queries, key_rows, precision=PRECISE) / math.sqrt(head_size)
    weights_soft = jax.nn.softmax(scores, axis=-1)
    mixed_rows = jnp.einsum("hnm,mhc->nhc", weights_soft, value_rows, precision=PRECISE).reshape(
        tokens, token_width
    )
    first_norm = layer_norm(
        wave_tokens + jnp.dot(mixed_rows, out_weight, precision=PRECISE), gain_one, EPS_HYPER
    )
    inner_act = gelu_tanh(jnp.dot(first_norm, up_weight, precision=PRECISE))
    return layer_norm(
        first_norm + jnp.dot(inner_act, down_weight, precision=PRECISE), gain_two, EPS_HYPER
    )


MESH = pl.DeviceIdType.MESH
B16 = jnp.bfloat16
F32 = jnp.float32
CHUNK = 48
DIMS = "xyz"
PART = 96
FRONT_PLAN = (
    (
        (),
        (),
        (),
        (),
        (1, 3, 2, 42, 41, 29, 11),
        (),
        (),
        (53, 57, 61, 10, 13, 28),
        (54,),
        (55, 66, 72, 5, 58, 63, 48),
        (56, 77, 83, 62, 22, 44, 67, 74, 35, 9, 14, 17, 73, 80, 82, 84, 50, 18, 89, 21, 91, 24, 31, 26, 34),
        (86, 87, 37),
        (39, 47),
        (),
        (),
        (52,),
        (),
        (),
    ),
    (
        (),
        (),
        (),
        (0, 1, 3, 2),
        (42, 29, 41, 7, 40),
        (6, 11),
        (),
        (53,),
        (54, 10, 13),
        (55, 59, 5),
        (56, 58, 64, 48, 62, 70, 45, 67, 75, 71, 27, 19, 68, 76, 14, 81, 73, 22, 88, 28, 17, 78, 82, 84, 31, 85, 89, 32, 91, 79, 44, 24),
        (86, 87, 35),
        (37,),
        (),
        (),
        (50,),
        (),
        (),
    ),
    (
        (),
        (),
        (),
        (0, 1, 3, 2),
        (42, 29, 40, 7),
        (41,),
        (),
        (53, 6, 11),
        (54,),
        (55, 10, 13),
        (56, 58, 4, 45, 62, 60, 67, 48, 65, 70, 73, 28, 82, 75, 19, 89, 12, 81, 84, 22, 71, 88, 27, 76, 91, 15, 69, 30, 78, 35, 86, 85, 87, 79, 43, 23),
        (32,),
        (),
        (36,),
        (49,),
        (),
        (),
        (),
    ),
    (
        (),
        (),
        (),
        (),
        (0, 3, 2, 42, 40, 29, 7),
        (6, 13, 27),
        (),
        (53,),
        (54, 57, 61, 4, 45),
        (55, 77, 83),
        (56, 66, 72, 58, 19, 43, 62, 63, 32, 8, 12, 15, 67, 80, 81, 84, 49, 73, 74, 88, 20, 16, 91, 23, 30, 25, 33),
        (85, 87, 36),
        (38, 46),
        (),
        (),
        (51,),
        (),
        (),
    ),
)
TAIL_PLAN = (
    (
        (),
        (),
        (0, 1, 2, 3),
        (),
        (4, 6),
        (),
        (5,),
        (18, 21, 24, 27, 30, 33, 7, 70, 71, 11),
        (83, 84, 39, 40, 41, 42, 43, 77, 44, 45, 46, 10, 14, 73, 90, 86, 47),
        (79, 76, 92, 48, 89, 49, 53, 50, 16, 17, 81, 51, 94),
        (54, 32, 34, 52, 57, 36, 59, 60, 58, 62, 61, 65),
        (),
        (38, 95, 96, 67, 68),
        (),
    ),
    (
        (),
        (),
        (0, 1, 2, 3),
        (),
        (4,),
        (),
        (5,),
        (8, 7),
        (70, 71, 69, 83, 84, 82, 39, 40, 41, 42, 43, 44, 45, 46, 10, 19, 73, 77, 86, 74, 47, 22, 90, 13, 48, 25, 87),
        (79, 92, 26, 50, 28, 29, 51, 31),
        (49, 54, 35, 32, 34, 52, 57, 12, 36, 59, 15, 58, 60, 55, 61),
        (16, 17, 38, 95),
        (64, 63, 96, 66, 67, 68),
        (),
    ),
    (
        (),
        (),
        (0, 1, 2, 3),
        (),
        (4,),
        (),
        (5,),
        (7,),
        (69, 70, 71, 82, 83, 84, 39, 40, 41, 42, 43, 44, 45, 46, 10, 9, 74, 12, 72, 77, 47, 20, 85, 87, 48, 23, 90, 25),
        (78, 50, 26, 28, 49, 51, 29, 31, 91, 54),
        (32, 34, 35, 52, 57, 36, 58, 59, 16, 60, 13, 61, 56, 15, 17),
        (63, 38, 95),
        (67, 96, 64, 66, 68),
        (),
    ),
    (
        (),
        (),
        (0, 1, 2, 3),
        (),
        (4,),
        (),
        (5, 6),
        (18, 21, 24, 27, 30, 33, 69, 71, 7, 14),
        (82, 84, 39, 40, 41, 42, 74, 43, 44, 45, 46, 10, 72, 11, 87, 85, 47),
        (78, 15, 17, 91, 48, 75, 49, 50, 88, 80, 51, 31, 34, 52, 53, 54, 35, 93),
        (57, 58, 65, 59, 60, 38, 95, 61, 62, 96),
        (),
        (66, 68),
        (),
    ),
)
FIRST_PARTS = (0, 2)
SUM_ORDERS = ('yxz', 'zy', 'yz')
EMBED_ORDERS = ('xz', 'zx')
IMAGE_ORDERS = ('zx', 'zx')
ORDERS = ('zxy', 'zy', 'zy')


def place(known_z=None):
    band = lax.axis_index("band")
    z = band // 4 if known_z is None else known_z
    return (z, (band // 2) % 2, band % 2, lax.axis_index("dp"))


def device(z, x, core, y):
    return (z * 4 + x * 2 + core, y)


def slot(z, x, core, y):
    return (z * 4 + x * 2 + core) * 2 + y


def when(cond, run):
    if isinstance(cond, bool):
        if cond:
            run()
    else:
        pl.when(cond)(run)


def both(first, second):
    return second if first is True else first & second


def aligned(rows):
    return pl.multiple_of(rows, 16)


def tell_peers(barrier):
    band, y = lax.axis_index("band"), lax.axis_index("dp")
    bands = lax.axis_size("band")
    for step in range(bands):
        for plane in (y, 1 - y) if step else (1 - y,):
            pl.semaphore_signal(
                barrier, inc=1, device_id=((band + step) % bands, plane), device_id_type=MESH
            )


def tell_near(semaphore):
    z, x, core, y = place()
    near = [
        (device(z, x, 1 - core, y), True),
        (device(z, 1 - x, core, y), True),
        (device(z, x, core, 1 - y), True),
        (device(z + 1, x, core, y), z < 3),
        (device(z - 1, x, core, y), z > 0),
    ]
    for target, cond in near:
        when(
            cond,
            functools.partial(
                pl.semaphore_signal, semaphore, inc=1, device_id=target, device_id_type=MESH
            ),
        )


def hear_near(semaphore):
    z = place()[0]
    pl.semaphore_wait(semaphore, 5 - z // 3 - (3 - z) // 3)


def bulk_copy(ref, send_sem, recv_sem):
    band, y = lax.axis_index("band"), lax.axis_index("dp")
    return pltpu.make_async_remote_copy(
        src_ref=ref,
        dst_ref=ref,
        send_sem=send_sem,
        recv_sem=recv_sem,
        device_id=(band, 1 - y),
        device_id_type=MESH,
    )


def in_order(events):
    return [work for _, _, work in sorted(events, key=lambda event: event[:2])]


class Plan:
    def __init__(self, table, catalogues):
        self.table, self.catalogues = table, catalogues
        self.at = 0

    def run(self):
        z = place()[0]
        for known_z, works in enumerate(self.catalogues):
            chosen = self.table[known_z][self.at]
            if not chosen:
                continue

            @pl.when(z == known_z)
            def _(works=works, chosen=chosen):
                for index in chosen:
                    works[index]()

        self.at += 1


class Gather:
    def __init__(self, known_z, view, orders, bulk, send_sem, recv_sem, pair_send, pair_recv):
        self.view, self.orders, self.bulk = view, orders, bulk
        self.send_sem, self.recv_sem = send_sem, recv_sem
        self.pair_send, self.pair_recv = pair_send, pair_recv
        self.z, self.x, self.core, self.y = place(known_z)

    def place_of(self, chunk, block):
        order = self.orders[chunk]
        place = block[0]
        for dim, at in (("x", block[1]), ("y", block[2])):
            if dim in order:
                place = place * 2 + at
        return sum(self.rails(before) for before in range(chunk)) + place

    def sibling(self):
        return device(self.z, self.x, 1 - self.core, self.y)

    def send(self, chunk, block, dim, cond, direction=0):
        z, x, core, y = self.z, self.x, self.core, self.y
        if dim == "x":
            targets = [(device(z, 1 - x, core, y), cond)]
        elif dim == "y":
            targets = [(device(z, x, core, 1 - y), cond)]
        else:
            targets = []
            if direction >= 0:
                targets.append((device(z + 1, x, core, y), both(cond, z < 3)))
            if direction <= 0:
                targets.append((device(z - 1, x, core, y), both(cond, z > 0)))
        src = self.view(chunk, block, core)
        for target, needed in targets:
            if needed is False:
                continue
            copy = pltpu.make_async_remote_copy(
                src_ref=src,
                dst_ref=src,
                send_sem=self.send_sem.at[chunk, DIMS.index(dim)],
                recv_sem=self.recv_sem.at[self.place_of(chunk, block)],
                device_id=target,
                device_id_type=MESH,
            )
            when(needed, copy.start)

    def pair(self, chunk, block, core):
        src = self.view(chunk, block, core)
        return pltpu.make_async_remote_copy(
            src_ref=src,
            dst_ref=src,
            send_sem=self.pair_send.at[chunk, block[0] // 2],
            recv_sem=self.pair_recv.at[chunk, block[0] // 2],
            device_id=self.sibling(),
            device_id_type=MESH,
        )

    def start(self, chunk):
        own = (self.z, self.x, self.y)
        for dim in self.orders[chunk]:
            self.send(chunk, own, dim, True)
        self.pair(chunk, own, self.core).start()

    def events(self, chunk, start=0.0, pace=1.0):
        held, found = [(0, 0, 0, 0, start)], []
        for dim in self.orders[chunk]:
            clock, new = 0.0, []
            ordered = sorted(held, key=lambda item: item[4])
            if dim == "z":
                for dist in (1, 2, 3):
                    for item in ordered:
                        clock = max(clock, item[4]) + pace
                        new += [(dist, way, item[2], item[3], clock) for way in (1, -1)]
            else:
                for item in ordered:
                    clock = max(clock, item[4]) + pace
                    flip = (1, item[3]) if dim == "x" else (item[2], 1)
                    new.append((item[0], item[1], *flip, clock))
            found += [
                (item[4], chunk, functools.partial(self.arrive, chunk, dim, item)) for item in new
            ]
            held = held + new
        return found

    def arrive(self, chunk, dim, item):
        dist, way, flip_x, flip_y, _ = item
        cond = True
        if way == 1:
            cond = self.z >= dist
        elif way == -1:
            cond = self.z + dist <= 3
        if cond is False:
            return
        block = (
            self.z - dist * way,
            1 - self.x if flip_x else self.x,
            1 - self.y if flip_y else self.y,
        )
        src = self.view(chunk, block, self.core)
        arriving = pltpu.make_async_remote_copy(
            src_ref=src,
            dst_ref=src,
            send_sem=self.send_sem.at[chunk, 0],
            recv_sem=self.recv_sem.at[self.place_of(chunk, block)],
            device_id=self.sibling(),
            device_id_type=MESH,
        )
        when(cond, arriving.wait_recv)
        if dim == "z":
            self.send(chunk, block, "z", cond, way)
        order = self.orders[chunk]
        for later in order[order.index(dim) + 1 :]:
            self.send(chunk, block, later, cond)
        when(cond, self.pair(chunk, block, self.core).start)

    def rails(self, chunk):
        return 4 * (2 if "x" in self.orders[chunk] else 1) * (2 if "y" in self.orders[chunk] else 1)

    def sent(self, chunk, z, over):
        order = self.orders[chunk]
        fresh = (z < 3) + (z > 0) if over == "z" else 1
        total = fresh if over in order else 0
        for _, _, work in self.events(chunk):
            _, dim, (dist, way, *_) = work.args
            if (way == 1 and z < dist) or (way == -1 and z + dist > 3):
                continue
            total += fresh if over in order[order.index(dim) + 1 :] else 0
            if dim == "z" and over == "z":
                total += z < 3 if way == 1 else z > 0
        return total

    def wait_side(self, chunk, side):
        every = self.bulk(chunk, self.rails(chunk) // 2)
        bulk_copy(every, self.pair_send.at[chunk, side], self.pair_recv.at[chunk, side]).wait_recv()

    def wait_pairs(self, chunk):
        for side in (0, 1):
            self.wait_side(chunk, side)

    def finish(self):
        ends = (self.z == 0) | (self.z == 3)
        inner = (self.z == 1) | (self.z == 2)
        for chunk in range(len(self.orders)):
            for dim in self.orders[chunk]:
                send_sem = self.send_sem.at[chunk, DIMS.index(dim)]
                for cond, z in ((ends, 0), (inner, 1)):
                    copy = bulk_copy(self.bulk(chunk, self.sent(chunk, z, dim)), send_sem, self.recv_sem.at[0])
                    when(cond, copy.wait_send)
            every = self.bulk(chunk, self.rails(chunk) // 2)
            for side in (0, 1):
                bulk_copy(every, self.pair_send.at[chunk, side], self.pair_recv.at[chunk, side]).wait_send()


class Reduce:
    def __init__(self, known_z, view, orders, final, buf, bulk, send, recv):
        self.view, self.orders, self.final = view, orders, final
        self.buf, self.bulk = buf, bulk
        self.send_sem, self.recv_sem = send, recv
        self.z, self.x, self.core, self.y = place(known_z)
        self.index = [self.places(chunk) for chunk in range(len(orders))]
        self.first = [sum(len(index) for index in self.index[:chunk]) for chunk in range(len(orders))]

    def coords(self, block):
        zz, flip_x, flip_y = block
        return (zz, 1 - self.x if flip_x else self.x, 1 - self.y if flip_y else self.y)

    def own(self, chunk, block):
        return self.view(chunk, self.coords(block))

    def add(self, target, source):
        target[...] = target[...] + source[...]

    def sibling(self):
        return device(self.z, self.x, 1 - self.core, self.y)

    def blocks(self, chunk):
        return [(zz, fx, fy) for zz in (3, 0, 2, 1) for fx, fy in self.flips(chunk, 0)]

    def places(self, chunk):
        order, keys = self.orders[chunk], []
        for stage, dim in enumerate(order):
            if dim == "z":
                keys += [
                    self.z_key(stage, step, way, flips)
                    for step in range(3)
                    for way in ((1, -1) if step else (1,))
                    for flips in self.flips(chunk, stage)
                ]
                continue
            wheres = range(4) if "z" in order[stage:] else ("own",)
            later = self.flips(chunk, stage + 1)
            keys += [(stage, where, *flips) for where in wheres for flips in later]
        return {key: at for at, key in enumerate(keys)}

    def place_of(self, chunk, key):
        return self.index[chunk][key]

    def send(self, chunk, block, key, target, cond):
        if cond is False:
            return
        where = self.place_of(chunk, key)
        copy = pltpu.make_async_remote_copy(
            src_ref=self.own(chunk, block),
            dst_ref=self.buf(chunk, where),
            send_sem=self.send_sem.at[chunk, key[0]],
            recv_sem=self.recv_sem.at[self.first[chunk] + where],
            device_id=target,
            device_id_type=MESH,
        )
        when(cond, copy.start)

    def landed(self, chunk, key):
        return self.buf(chunk, self.place_of(chunk, key))

    def wait(self, chunk, key):
        landed = self.landed(chunk, key)
        pltpu.make_async_remote_copy(
            src_ref=landed,
            dst_ref=landed,
            send_sem=self.send_sem.at[chunk, 0],
            recv_sem=self.recv_sem.at[self.first[chunk] + self.place_of(chunk, key)],
            device_id=self.sibling(),
            device_id_type=MESH,
        ).wait_recv()

    def flips(self, chunk, stage):
        left = self.orders[chunk][stage:]
        return [
            (fx, fy)
            for fx in ((1, 0) if "x" in left else (0,))
            for fy in ((1, 0) if "y" in left else (0,))
        ]

    def ready(self, chunk, stage, block):
        order = self.orders[chunk]
        zz, fx, fy = block
        where = zz if "z" in order[stage:] else "own"
        if order[stage] == "x" and fx:
            target = device(self.z, 1 - self.x, self.core, self.y)
            self.send(chunk, block, (stage, where, 0, fy), target, True)
        elif order[stage] == "y" and fy:
            target = device(self.z, self.x, self.core, 1 - self.y)
            self.send(chunk, block, (stage, where, fx, 0), target, True)

    def z_key(self, stage, step, way, flips):
        return (stage, step, way if step else 0, *flips)

    def z_start(self, chunk, stage, step, flips):
        up, down = (3 - step, *flips), (step, *flips)
        right = device(self.z + 1, self.x, self.core, self.y)
        left = device(self.z - 1, self.x, self.core, self.y)
        self.send(chunk, up, self.z_key(stage, step, 1, flips), right, self.z == 0)
        self.send(chunk, down, self.z_key(stage, step, -1, flips), left, self.z == 3)

    def z_arrive(self, chunk, stage, step, flips, way):
        z = self.z if way == 1 else 3 - self.z
        cond = (z >= 1) & (z <= step + 1)
        zz = 2 + z - step
        zz = zz if way == 1 else 3 - zz
        block = (zz, *flips)
        key = self.z_key(stage, step, way, flips)
        last = stage + 1 == len(self.orders[chunk]) and step == 2

        def take():
            self.wait(chunk, key)
            if not last:
                self.add(self.own(chunk, block), self.landed(chunk, key))

        when(cond, take)
        if step < 2:
            target = device(self.z + way, self.x, self.core, self.y)
            self.send(chunk, block, self.z_key(stage, step + 1, way, flips), target, cond)

    def z_done(self, chunk, stage, flips):
        block = (self.z, *flips)
        if stage + 1 < len(self.orders[chunk]):
            self.ready(chunk, stage + 1, block)
            return
        final = self.final(chunk)
        final[...] = self.own(chunk, block)[...].astype(F32)
        for way, cond in ((1, self.z >= 1), (-1, self.z <= 2)):
            landed = self.landed(chunk, self.z_key(stage, 2, way, flips))

            def add(landed=landed):
                final[...] += landed[...].astype(F32)

            when(cond, add)

    def xy_arrive(self, chunk, stage, zz, fx, fy):
        key = (stage, zz, fx, fy)
        block = (self.z if zz == "own" else zz, fx, fy)
        self.wait(chunk, key)
        own, landed = self.own(chunk, block), self.landed(chunk, key)
        if stage + 1 < len(self.orders[chunk]):
            self.add(own, landed)
            self.ready(chunk, stage + 1, block)
        else:
            final = self.final(chunk)
            final[...] = own[...].astype(F32) + landed[...].astype(F32)

    def start(self, chunk, block):
        self.ready(chunk, 0, block)

    def events(self, chunks, start=0.0, pace=1.0):
        found = []
        for chunk in chunks:
            times = {block: start for block in self.blocks(chunk)}
            found += [
                (start, chunk, functools.partial(self.start, chunk, block))
                for block in self.blocks(chunk)
                if dict(x=block[1], y=block[2], z=0)[self.orders[chunk][0]]
            ]
            for stage, dim in enumerate(self.orders[chunk]):
                clock, later = 0.0, {}
                if dim == "z":
                    for step in range(3):
                        for flips in self.flips(chunk, stage):
                            needed = (0, 3) if step == 0 else (0, 1, 2, 3)
                            clock = max(clock, *(times[(zz, *flips)] for zz in needed)) + 0.001
                            work = functools.partial(self.z_start, chunk, stage, step, flips)
                            found.append((clock, chunk, work))
                            clock += pace
                            for way in (1, -1):
                                work = functools.partial(self.z_arrive, chunk, stage, step, flips, way)
                                found.append((clock, chunk, work))
                            later[("own", *flips)] = clock + 0.001
                    for flips in self.flips(chunk, stage):
                        work = functools.partial(self.z_done, chunk, stage, flips)
                        found.append((later[("own", *flips)], chunk, work))
                else:
                    pick = 1 if dim == "x" else 2
                    for key in sorted((k for k in times if k[pick]), key=lambda k: times[k]):
                        mine = (key[0], 0, key[2]) if dim == "x" else (key[0], key[1], 0)
                        clock = max(max(clock, times[key]) + pace, times[mine] + 0.001)
                        later[mine] = clock
                        work = functools.partial(self.xy_arrive, chunk, stage, *mine)
                        found.append((clock, chunk, work))
                times = later
        return found

    def finish(self):
        for chunk, order in enumerate(self.orders):
            for stage, dim in enumerate(order):
                after = len(self.flips(chunk, stage + 1)) if stage + 1 < len(order) else 1
                count = 3 * after if dim == "z" else after * (4 if "z" in order[stage + 1 :] else 1)
                every = self.bulk(chunk, count)
                bulk_copy(every, self.send_sem.at[chunk, stage], self.recv_sem.at[0]).wait_send()


class Exchange:
    def __init__(self, source, landing, bulk, send_sem, recv_sem):
        self.source, self.landing, self.bulk = source, landing, bulk
        self.send_sem, self.recv_sem = send_sem, recv_sem
        self.band, self.y = lax.axis_index("band"), lax.axis_index("dp")
        self.bands = lax.axis_size("band")

    def send(self, target):
        pltpu.make_async_remote_copy(
            src_ref=self.source(target),
            dst_ref=self.landing(self.band),
            send_sem=self.send_sem,
            recv_sem=self.recv_sem,
            device_id=(target, self.y),
            device_id_type=MESH,
        ).start()

    def start(self):
        for step in range(1, self.bands):
            self.send((self.band + step) % self.bands)

    def wait(self):
        bulk_copy(self.bulk(self.bands - 1), self.send_sem, self.recv_sem).wait_recv()

    def finish(self):
        bulk_copy(self.bulk(self.bands - 1), self.send_sem, self.recv_sem).wait_send()


def dot_nt(left, right):
    return lax.dot_general(left, right, (((1,), (1,)), ((), ())), preferred_element_type=F32)


def dot_tn(left, right):
    return lax.dot_general(left, right, (((0,), (0,)), ((), ())), preferred_element_type=F32)


def dot_nn(left, right):
    return jnp.dot(left, right, preferred_element_type=F32)


def unit_parts(rows):
    centred = rows - jnp.mean(rows, axis=-1, keepdims=True)
    inverse = lax.rsqrt(jnp.mean(centred * centred, axis=-1, keepdims=True) + EPS_BLOCK)
    return centred * inverse, inverse


class Block:
    def __init__(self, weights, down, refs):
        self.weights, self.down = weights, down
        self.__dict__.update(refs)
        self.width = weights.shape[1]
        self.tokens = self.joint.shape[1]
        self.halves = weights.shape[1] // (2 * HEAD_DIM)

    def weight(self, part):
        return self.weights[pl.ds(aligned(part * self.width), self.width), :]

    def masks(self):
        tokens = self.joint.shape[1]
        lane = lax.broadcasted_iota(jnp.int32, (tokens, 2 * HEAD_DIM), 1)
        low = lane < HEAD_DIM
        return low, low.astype(F32).astype(B16), (~low).astype(F32).astype(B16)

    def pair_rows(self, rows, low, high):
        return jnp.concatenate([rows * low, rows * high], axis=0)

    def own(self, ref):
        return ref[: self.tokens]

    def project(self):
        unit, inverse = unit_parts(self.residual[...])
        self.normed_one[: self.tokens] = (unit * self.gain_one[...]).astype(B16)
        self.unit_one[...] = unit
        self.inverse_one[...] = jnp.broadcast_to(inverse, self.inverse_one.shape)

        @pl.loop(0, 3)
        def _(part):
            self.joint[part] = dot_nn(self.own(self.normed_one), self.weight(part)).astype(B16)

    def attend(self):
        tokens = self.joint.shape[1]
        scale = 1.0 / math.sqrt(HEAD_DIM)

        @pl.loop(0, self.halves)
        def _(pair):
            where, low, high = self.masks()
            lanes = pl.ds(pl.multiple_of(pair * 2 * HEAD_DIM, 2 * HEAD_DIM), 2 * HEAD_DIM)
            query, key, value = (self.joint[part, :, lanes] for part in range(3))
            scores = dot_nt(self.pair_rows(query, low, high), key) * scale
            raised = jnp.exp(scores - jnp.max(scores, axis=-1, keepdims=True))
            probs = raised / jnp.sum(raised, axis=-1, keepdims=True)
            self.probs[pair] = probs
            mixed = dot_nn(probs.astype(B16), value)
            self.mixed[:tokens, lanes] = jnp.where(where, mixed[:tokens], mixed[tokens:]).astype(B16)

    def middle(self):
        middle = self.residual[...] + dot_nn(self.own(self.mixed), self.weight(3))
        unit, inverse = unit_parts(middle)
        self.normed_two[: self.tokens] = (unit * self.gain_two[...]).astype(B16)
        self.unit_two[...] = unit
        self.inverse_two[...] = jnp.broadcast_to(inverse, self.inverse_two.shape)
        self.result[...] = middle

    def both_x(self, ref):
        return ref[: 2 * self.tokens]

    def down_rows(self, part):
        return self.down[pl.ds(aligned(part * self.width), self.width), :]

    def widen(self):
        @pl.loop(0, 2)
        def _(part):
            pre = dot_nn(self.both_x(self.normed_two), self.weight(4 + part))
            self.pre_act[part] = pre
            self.act[part, : 2 * self.tokens] = gelu_tanh(pre).astype(B16)

    def narrow(self):
        parts = [dot_nn(self.act[part, : 2 * self.tokens], self.down_rows(part)) for part in (0, 1)]
        total = parts[0] + parts[1]
        self.result[...] += total[: self.tokens]
        self.result_x[...] = total[self.tokens :].astype(B16)

    def back_narrow(self):
        self.grad_normed[...] = jnp.zeros(self.grad_normed.shape, F32)

        @pl.loop(0, 2)
        def _(part):
            grad_act = dot_nt(self.both_x(self.out_grad), self.down_rows(part))
            grad_pre = (grad_act * gelu_slope(self.pre_act[part])).astype(B16)
            self.grad_pre[part, : 2 * self.tokens] = grad_pre
            self.grad_normed[...] += dot_nt(grad_pre, self.weight(4 + part))

        self.grad_x[...] = self.grad_normed[self.tokens :].astype(B16)

    def turn(self, ref):
        rows = ref.shape[0]
        for at in range(0, self.width, 128):
            self.turned[at : at + 128, :rows] = ref[:, at : at + 128].T

    def down_grad(self, part, core, rail, store):
        self.turn(self.act.at[part])
        for z in (0, 1):
            rail[z * 2 * PART : (z + 1) * 2 * PART, :] = self.turned[
                pl.ds(aligned((z * 2 + core) * 2 * PART), 2 * PART), :
            ]
        for at in range(0, self.width, 256):
            cols = slice(at, at + 256)
            rows = slice(part * 4 * PART, (part + 1) * 4 * PART)
            store[rows, cols] = dot_nn(rail[...], self.out_grad[:, cols]).astype(B16)

    def turn_rail(self, target, ref, core):
        rows = ref.shape[0]
        self.turn(ref)
        for chip in range(8):
            target[chip * CHUNK : (chip + 1) * CHUNK, :] = self.turned[
                pl.ds(aligned((chip * 2 + core) * CHUNK), CHUNK), :rows
            ]

    def pair_grad(self, first, second, first_grad, second_grad, store, where):
        half = CHUNK // 2
        for at in range(0, self.width, 256):
            cols = slice(at, at + 256)
            one = dot_nn(first[...], first_grad(cols))
            two = dot_nn(second[...], second_grad(cols))
            for owner in range(16):
                rows = slice(owner * half, owner * half + half)
                piece = jnp.concatenate([one[rows], two[rows]], axis=0)
                store[pl.ds(where(owner), CHUNK), cols] = piece.astype(B16)

    def back_wide(self):
        grad_normed = self.own(self.grad_normed) + self.grad_from_x[...].astype(F32)
        unit = self.unit_two[...]
        self.small[1:2, :] = jnp.sum(grad_normed * unit, axis=0, keepdims=True)
        scaled = grad_normed * self.gain_two[...]
        back = self.inverse_two[:, :1] * (
            scaled
            - jnp.mean(scaled, axis=-1, keepdims=True)
            - unit * jnp.mean(scaled * unit, axis=-1, keepdims=True)
        )
        grad_middle = self.own(self.out_grad).astype(F32) + back
        self.grad_middle[...] = grad_middle
        branch = grad_middle.astype(B16)
        self.grad_branch[: self.tokens] = branch
        self.grad_mixed[...] = dot_nt(branch, self.weight(3)).astype(B16)

    def back_attend(self):
        tokens = self.joint.shape[1]
        scale = 1.0 / math.sqrt(HEAD_DIM)

        @pl.loop(0, self.halves)
        def _(pair):
            where, low, high = self.masks()
            lanes = pl.ds(pl.multiple_of(pair * 2 * HEAD_DIM, 2 * HEAD_DIM), 2 * HEAD_DIM)
            query, key, value = (self.joint[part, :, lanes] for part in range(3))
            grads = self.pair_rows(self.grad_mixed[:, lanes], low, high)
            probs = self.probs[pair]
            self.grad_joint[2, :tokens, lanes] = dot_tn(probs.astype(B16), grads).astype(B16)
            grad_probs = dot_nt(grads, value)
            total = jnp.sum(grad_probs * probs, axis=-1, keepdims=True)
            grad_scores = (probs * (grad_probs - total)).astype(B16)
            queries = dot_nn(grad_scores, key) * scale
            self.grad_joint[0, :tokens, lanes] = jnp.where(
                where, queries[:tokens], queries[tokens:]
            ).astype(B16)
            keys = dot_tn(grad_scores, self.pair_rows(query, low, high)) * scale
            self.grad_joint[1, :tokens, lanes] = keys.astype(B16)

    def back_project(self):
        parts = [dot_nt(self.grad_joint[part, : self.tokens], self.weight(part)) for part in range(3)]
        grad_normed = parts[0] + parts[1] + parts[2]
        unit = self.unit_one[...]
        self.small[0:1, :] = jnp.sum(grad_normed * unit, axis=0, keepdims=True)
        scaled = grad_normed * self.gain_one[...]
        back = self.inverse_one[:, :1] * (
            scaled
            - jnp.mean(scaled, axis=-1, keepdims=True)
            - unit * jnp.mean(scaled * unit, axis=-1, keepdims=True)
        )
        self.grad_middle[...] += back

    def embed_grad(self):
        return self.grad_middle[...].astype(B16)


def split3(rows):
    first = rows.astype(B16)
    rest = rows - first.astype(F32)
    second = rest.astype(B16)
    return first, second, (rest - second.astype(F32)).astype(B16)


def fold3(stacked):
    rows = stacked.shape[0] // 3
    return stacked[:rows] + (stacked[rows : 2 * rows] + stacked[2 * rows :])


def wide_nn(rows, weight):
    return fold3(dot_nn(jnp.concatenate(split3(rows), axis=0), weight))


def wide_nt(rows, weight):
    return fold3(dot_nt(jnp.concatenate(split3(rows), axis=0), weight))


def wide_tn(left, right):
    one, two = split3(left), split3(right)
    pairs = ((0, 0), (0, 1), (1, 0), (0, 2), (1, 1), (2, 0))
    return dot_tn(
        jnp.concatenate([one[a] for a, _ in pairs], axis=0),
        jnp.concatenate([two[b] for _, b in pairs], axis=0),
    )


def exact_dot(left, right, dims):
    return lax.dot_general(
        left, right, (dims, ((), ())), precision=PRECISE, preferred_element_type=F32
    )


def hyper_unit(rows):
    centred = rows - jnp.mean(rows, axis=-1, keepdims=True)
    inverse = lax.rsqrt(jnp.mean(centred * centred, axis=-1, keepdims=True) + EPS_HYPER)
    return centred * inverse, inverse


def unit_back(scaled, unit, inverse):
    return inverse * (
        scaled
        - jnp.mean(scaled, axis=-1, keepdims=True)
        - unit * jnp.mean(scaled * unit, axis=-1, keepdims=True)
    )


def by_head(rows):
    lane = lax.broadcasted_iota(jnp.int32, rows.shape, 1) // (rows.shape[1] // HHEADS)
    return jnp.concatenate([jnp.where(lane == head, rows, 0.0) for head in range(HHEADS)], axis=0)


def own_lanes(stacked):
    tokens = stacked.shape[0] // HHEADS
    out = jnp.zeros((tokens, stacked.shape[1]), F32)
    for head in range(HHEADS):
        rows = stacked[head * tokens : (head + 1) * tokens]
        lane = lax.broadcasted_iota(jnp.int32, rows.shape, 1) // (rows.shape[1] // HHEADS)
        out = out + jnp.where(lane == head, rows, 0.0)
    return out


def hyper_forward(waves, qkv, out, gain_one, up, down, gain_two):
    width = waves.shape[1]
    joint = wide_nn(waves, qkv)
    query, key, value = (joint[:, at * width : (at + 1) * width] for at in range(3))
    scores = exact_dot(by_head(query), key, ((1,), (1,))) / math.sqrt(width // HHEADS)
    raised = jnp.exp(scores - jnp.max(scores, axis=-1, keepdims=True))
    soft = raised / jnp.sum(raised, axis=-1, keepdims=True)
    mixed = own_lanes(exact_dot(soft, value, ((1,), (0,))))
    unit_one, inverse_one = hyper_unit(waves + wide_nn(mixed, out))
    first = unit_one * gain_one
    inner = wide_nn(first, up)
    unit_two, inverse_two = hyper_unit(first + wide_nn(gelu_tanh(inner), down))
    kept = (joint, soft, mixed, unit_one, inverse_one, inner, unit_two, inverse_two)
    return unit_two * gain_two, kept


def hyper_backward(grad_code, kept, waves, qkv, out, gain_one, up, down, gain_two):
    joint, soft, mixed, unit_one, inverse_one, inner, unit_two, inverse_two = kept
    width = waves.shape[1]
    query, key, value = (joint[:, at * width : (at + 1) * width] for at in range(3))
    first = unit_one * gain_one
    grad_gain_two = jnp.sum(grad_code * unit_two, axis=0, keepdims=True)
    grad_second = unit_back(grad_code * gain_two, unit_two, inverse_two)
    grad_down = wide_tn(gelu_tanh(inner), grad_second)
    grad_inner = wide_nt(grad_second, down) * gelu_slope(inner)
    grad_up = wide_tn(first, grad_inner)
    grad_first = grad_second + wide_nt(grad_inner, up)
    grad_gain_one = jnp.sum(grad_first * unit_one, axis=0, keepdims=True)
    grad_mid = unit_back(grad_first * gain_one, unit_one, inverse_one)
    grad_out = wide_tn(mixed, grad_mid)
    grad_mixed = by_head(wide_nt(grad_mid, out))
    grad_value = exact_dot(soft, grad_mixed, ((0,), (0,)))
    grad_soft = exact_dot(grad_mixed, value, ((1,), (1,)))
    total = jnp.sum(grad_soft * soft, axis=-1, keepdims=True)
    grad_scores = soft * (grad_soft - total) / math.sqrt(width // HHEADS)
    grad_query = own_lanes(exact_dot(grad_scores, key, ((1,), (0,))))
    grad_key = exact_dot(grad_scores, by_head(query), ((0,), (0,)))
    grad_qkv = wide_tn(waves, jnp.concatenate([grad_query, grad_key, grad_value], axis=1))
    return grad_qkv, grad_out, grad_gain_one, grad_up, grad_down, grad_gain_two


def spread(gathered, weights):
    width = weights.shape[1]
    half = CHUNK // 2

    @pl.loop(0, 16)
    def _(two):
        for pair in (0, 1):
            one, other = (
                gathered[pl.ds(aligned((two * 2 + k) * PART + pair * CHUNK), CHUNK), :].astype(F32)
                for k in (0, 1)
            )
            for k, rows in ((0, slice(0, half)), (1, slice(half, CHUNK))):
                target = pl.ds(aligned((2 * pair + k) * width + two * CHUNK), CHUNK)
                weights[target, :] = jnp.concatenate([one[rows], other[rows]], 0).astype(B16)


def spread_up(gathered, weights, x):
    width = weights.shape[1]
    half = CHUNK // 2

    @pl.loop(0, 8)
    def _(chip):
        z, core = chip // 2, chip % 2
        for far in (0, 1):
            one, other = (
                gathered[pl.ds(aligned((chip * 2 + k) * PART + far * CHUNK), CHUNK), :].astype(F32)
                for k in (0, 1)
            )
            row = (z * 4 + (1 - x if far else x) * 2 + core) * CHUNK
            for k, rows in ((0, slice(0, half)), (1, slice(half, CHUNK))):
                target = pl.ds(aligned((4 + k) * width + row), CHUNK)
                weights[target, :] = jnp.concatenate([one[rows], other[rows]], 0).astype(B16)


def swap_rows(rows):
    count = rows.shape[0]
    row = lax.broadcasted_iota(jnp.int32, (count, count), 0)
    col = lax.broadcasted_iota(jnp.int32, (count, count), 1)
    swap = (col == (row % 16) * 16 + row // 16).astype(F32).astype(B16)
    return dot_nn(swap, rows).astype(B16)


def rows16(ref, index):
    return ref.at[pl.ds(aligned(index * 16), 16)]


KEPT = 10
SHARED = ("og", "n1", "mx", "n2", "a0", "a1")
SHARED += ("p0", "p1", "gb", "j0", "j1", "j2")
ACROSS = ("u", "og", "n2", "r", "g", "s")


def layer_kernel(*refs):
    (counts, mask, wavelengths, pixels, kernel_gen, attn_qkv, attn_out, mlp_up, mlp_down, frequency, hyper_qkv, hyper_out, hyper_one, hyper_two,
     hyper_up, hyper_down, bias_gen, out_grad_in, norm_one, norm_two,
     block_out, pixel_out, shares, kernel_grads, code_out, code_grads, vectors, *rest_refs) = refs
    kept_refs, rest_refs = rest_refs[: KEPT], rest_refs[KEPT :]
    (gathered_attn, gathered_up, gathered_down, weights, spare, buf, joint, probs, pre_act, act, grad_pre, out_grad, mixed, normed_one, normed_two,
     unit_one, unit_two, inverse_one, inverse_two, grad_normed, grad_middle, grad_branch, grad_mixed, grad_joint,
     turned, rail_one, rail_mixed, rail_two, up_away, up_share, up_landed, result_x, result_from_x, grad_x, grad_from_x,
     residual, pixel_rows, turned_pixels, pair_pixels, mixing, kernels, pair_kernels, sending,
     landed_grads, summed, small, small_partner, small_all, code_part, code_all, gains, band_scale, pair_scale,
     pix_sem, gen_sem, front_done, narrow_done, *sems) = rest_refs
    z, x, core, y = place()
    band = lax.axis_index("band")
    bands = lax.axis_size("band")
    me = slot(z, x, core, y)
    width = gains.shape[1]
    tokens = out_grad_in.shape[0]
    sibling = (band + 1 - 2 * core, y)
    partner = (band, 1 - y)
    own_rows = pl.ds(aligned(band * 16), 16)
    gather_sems, grads_sems = sems[0:4], sems[4:8]
    (reduce_sems, embed_sems, share_sems, across_sems, front_sems, kernel_sems, cols_sems, summed_sems, vec_half_sems, vec_sems,
     code_sems) = (sems[at : at + 2] for at in range(8, 30, 2))
    gathered = (gathered_attn, gathered_up, gathered_down)

    def to_pair(index, source, target, pair=share_sems):
        return pltpu.make_async_remote_copy(
            src_ref=source,
            dst_ref=target,
            send_sem=pair[0].at[index],
            recv_sem=pair[1].at[index],
            device_id=sibling,
            device_id_type=MESH,
        )

    def shared(name):
        index = SHARED.index(name)
        ref = dict(
            og=out_grad, n1=normed_one, mx=mixed, n2=normed_two, gb=grad_branch
        ).get(name)
        if ref is None:
            ref = dict(a=act, p=grad_pre, j=grad_joint)[name[0]].at[int(name[1])]
        half = ref.shape[0] // 2
        return to_pair(index, ref.at[pl.ds(0, half)], ref.at[pl.ds(half, half)])

    own_block = aligned((z * 4 + core * 2 + y) * PART)

    def across(name):
        own, other = pl.ds(0, tokens), pl.ds(tokens, tokens)
        source, target = dict(
            u=(up_away, gathered_up.at[pl.ds(own_block + CHUNK, CHUNK)]),
            og=(out_grad.at[own], out_grad.at[other]),
            n2=(normed_two.at[own], normed_two.at[other]),
            r=(result_x, result_from_x),
            g=(grad_x, grad_from_x),
            s=(up_share.at[pl.ds(CHUNK, CHUNK)], up_landed),
        )[name]
        return pltpu.make_async_remote_copy(
            src_ref=source,
            dst_ref=target,
            send_sem=across_sems[0].at[ACROSS.index(name)],
            recv_sem=across_sems[1].at[ACROSS.index(name)],
            device_id=device(z, 1 - x, core, y),
            device_id_type=MESH,
        )

    def gen_copy(piece, target):
        return pltpu.make_async_copy(
            kernel_gen.at[:, pl.ds(piece * width, width)], target.at[pl.ds(piece * 128, 128)], gen_sem
        )

    def gen_wait(target):
        every = target.at[pl.ds(0, 16 * 128)]
        pltpu.make_async_copy(every, every, gen_sem).wait()

    barrier = pltpu.get_barrier_semaphore()
    tell_peers(barrier)
    for piece in range(16):
        gen_copy(piece, spare).start()
    load_pixels = pltpu.make_async_copy(pixels, pixel_rows, pix_sem)
    load_pixels.start()

    gains[0:1, :] = norm_one[...].astype(F32).reshape(1, width)
    gains[1:2, :] = norm_two[...].astype(F32).reshape(1, width)
    out_grad[0:tokens, :] = out_grad_in[...]
    for image in range(band_scale.shape[0]):
        used = jnp.where((band < counts[image]) & (mask[image] == 1), 1.0, 0.0)
        bands_here = jnp.full(band_scale.shape[1:], counts[image], jnp.int32).astype(F32)
        band_scale[image] = lax.rsqrt(bands_here) * used

    def rows_of(weight, piece):
        return weight[:, piece * width : (piece + 1) * width].astype(F32)

    pieces = [rows_of(attn_qkv, at) for at in range(3)] + [rows_of(attn_out, 0)]
    for at in (0, 1):
        rows = jnp.concatenate(pieces[2 * at : 2 * at + 2], axis=0).astype(B16)
        gathered_attn[pl.ds(aligned(me * PART + at * CHUNK), CHUNK), :] = rows

    def up_half(of_x):
        group = 4 * PART
        quarters = [
            jnp.concatenate([mlp_up[:, at * group : (at + 1) * group] for at in (first, first + 2)], axis=1)
            for first in (of_x, of_x + 4)
        ]
        return jnp.concatenate([quarter.astype(F32) for quarter in quarters], axis=0).astype(B16)

    for of_x in (0, 1):

        @pl.when(x == of_x)
        def _(of_x=of_x):
            gathered_up[pl.ds(own_block, CHUNK), :] = up_half(of_x)
            up_away[...] = up_half(1 - of_x)

    gathered_down[pl.ds(own_block, PART), :] = mlp_down[...]
    hyper_gains = [gain[...].astype(F32).reshape(1, HW) for gain in (hyper_one, hyper_two)]
    lengths = [jnp.full((1, HW), wavelengths[at], jnp.int32) for at in range(bands)]
    angles = jnp.concatenate(lengths, axis=0).astype(F32) * frequency[...]
    lane = lax.broadcasted_iota(jnp.int32, angles.shape, 1)
    waves = jnp.where(lane < HW // 2, jnp.sin(angles), jnp.cos(angles))
    code, kept = hyper_forward(
        waves, hyper_qkv[...], hyper_out[...], hyper_gains[0], hyper_up[...], hyper_down[...], hyper_gains[1]
    )
    kept = (*kept, jnp.concatenate(hyper_gains, axis=0), waves)
    code_low = code.astype(B16)
    code_out[...] = code_low
    for ref, value in zip(kept_refs, kept):
        ref[...] = value

    def weight_view(part, block, side):
        if part == 0:
            where = slot(block[0], block[1], side, block[2])
        else:
            where = block[0] * 4 + side * 2 + block[2]
        return gathered[part].at[pl.ds(aligned(where * PART), PART)]

    half = tokens // 2

    def image_row(block, side):
        return (block[0] * 4 + block[1] * 2 + side) * tokens

    def rail_row(block):
        return (block[0] * 2 + block[1]) * tokens

    def gather_at(known_z=None):
        return Gather(
            known_z, weight_view, ORDERS, lambda part, count: gathered[part].at[pl.ds(0, count * PART)], *gather_sems
        )

    def embed_at(known_z=None):
        return Reduce(
            known_z,
            lambda chunk, block: spare.at[pl.ds(aligned(rail_row(block) + chunk * half), half)],
            EMBED_ORDERS,
            lambda chunk: residual.at[pl.ds(chunk * half, half)],
            lambda chunk, where: buf.at[pl.ds((chunk * 11 + where) * half, half)],
            lambda chunk, count: buf.at[pl.ds(0, count * half)],
            *embed_sems,
        )

    def front_works(known_z):
        known, sums = gather_at(known_z), embed_at(known_z)
        works = [work for part in range(3) for work in in_order(known.events(part))]
        return works + in_order(sums.events((0, 1)))

    gather, embed = gather_at(), embed_at()
    plan = Plan(FRONT_PLAN, [front_works(known_z) for known_z in range(4)])
    pl.semaphore_wait(barrier, 2 * bands - 1)
    load_pixels.wait()
    for chip in range(8):
        to_pair(0, pixel_rows.at[chip * 2 + 1 - core], pair_pixels.at[chip], front_sems).start()
    to_pair(1, band_scale, pair_scale, front_sems).start()
    plan.run()
    across("u").start()
    for part in FIRST_PARTS:
        gather.start(part)
    plan.run()

    gen_wait(spare)

    @pl.loop(0, 16)
    def _(piece):
        part = dot_nn(code_out[...], spare[pl.ds(aligned(piece * 128), 128), :])
        mixing[pl.ds(aligned(piece * 16), 16), :] = part.astype(B16)

    sending[...] = swap_rows(mixing[...])
    spread_kernels = Exchange(
        lambda target: rows16(sending, target),
        lambda source: rows16(kernels, source),
        lambda count: kernels.at[pl.ds(0, count * 16)],
        *[sem.at[0] for sem in kernel_sems],
    )
    spread_kernels.start()
    plan.run()
    across("u").wait_recv()
    for part in range(3):
        if part not in FIRST_PARTS:
            gather.start(part)
    across("og").start()
    plan.run()
    kernels[own_rows, :] = sending[own_rows, :]
    biases = dot_nn(code_out[...], bias_gen[...])
    row = lax.broadcasted_iota(jnp.int32, biases.shape, 0)
    bias, pair_bias = (
        jnp.sum(jnp.where(row == of, biases, 0.0), axis=0, keepdims=True) for of in (band, sibling[0])
    )
    for group in range(4):
        turned_pixels[group] = pixel_rows[4 * group : 4 * group + 4].reshape(4 * tokens, -1).T
    plan.run()
    spread_kernels.wait()
    to_pair(2, kernels, pair_kernels, front_sems).start()
    plan.run()
    to_pair(0, pair_pixels, pair_pixels, front_sems).wait_recv()
    to_pair(1, band_scale, pair_scale, front_sems).wait_recv()
    to_pair(2, kernels, pair_kernels, front_sems).wait_recv()

    def term(group):
        mine = [group * 4 + x_of * 2 + core for x_of in (0, 1)]
        rows = jnp.concatenate([pixel_rows[image] for image in mine], axis=0)
        pair_rows = pair_pixels[2 * group : 2 * group + 2].reshape(2 * tokens, -1)
        for at in range(0, width, 256):
            cols = slice(at, at + 256)
            one = dot_nn(rows, kernels[:, cols]) + bias[:, cols]
            two = dot_nn(pair_rows, pair_kernels[:, cols]) + pair_bias[:, cols]
            for x_of, image in enumerate(mine):
                own = slice(x_of * tokens, (x_of + 1) * tokens)
                total = one[own] * band_scale[image][:1, :1] + two[own] * pair_scale[image][:1, :1]
                start = (2 * group + x_of) * tokens
                spare[start : start + tokens, cols] = total.astype(B16)

    for group in (3, 0, 2, 1):
        plan.run()
        term(group)
    plan.run()
    gather.wait_pairs(0)
    spread(gathered_attn, weights)

    names = dict(
        residual=residual, out_grad=out_grad, gain_one=gains.at[0:1], gain_two=gains.at[1:2], block_out=block_out,
        joint=joint, probs=probs, pre_act=pre_act, act=act,
        grad_pre=grad_pre, mixed=mixed, normed_one=normed_one, normed_two=normed_two, unit_one=unit_one,
        unit_two=unit_two, inverse_one=inverse_one, inverse_two=inverse_two, result=residual, grad_normed=grad_normed,
        grad_middle=grad_middle, grad_branch=grad_branch, grad_mixed=grad_mixed, grad_joint=grad_joint,
        turned=turned, small=small, result_x=result_x, grad_x=grad_x, grad_from_x=grad_from_x,
    )
    block = Block(weights, gathered_down, names)
    plan.run()
    block.project()
    shared("n1").start()
    plan.run()
    block.attend()
    shared("mx").start()
    plan.run()
    block.middle()
    across("n2").start()
    across("og").wait_recv()
    shared("og").start()
    plan.run()
    gather.wait_pairs(1)
    spread_up(gathered_up, weights, x)
    plan.run()
    across("n2").wait_recv()
    shared("n2").start()
    block.widen()
    for name in ("a0", "a1"):
        shared(name).start()
    plan.run()
    gather.wait_pairs(2)
    gather.finish()
    embed.finish()
    for copy in ((0, pair_pixels, pair_pixels), (1, band_scale, pair_scale), (2, kernels, pair_kernels)):
        to_pair(*copy, front_sems).wait_send()
    tell_near(front_done)

    def part_ref(part):
        return spare.at[pl.ds(8 * tokens, 8 * PART)] if part == 2 else gathered[part]

    def part_view(part, blk):
        where = blk[0] * 4 + blk[1] * 2 + blk[2] if part == 0 else blk[0] * 2 + blk[2]
        return part_ref(part).at[pl.ds(aligned(where * PART), PART)]

    def reduce_at(known_z=None):
        return Reduce(
            known_z,
            part_view,
            SUM_ORDERS,
            lambda part: up_share if part == 1 else shares.at[pl.ds(part * PART, PART)],
            lambda part, where: buf.at[pl.ds(((0, 19, 30)[part] + where) * PART, PART)],
            lambda part, count: part_ref(part).at[pl.ds(0, count * PART)],
            *reduce_sems,
        )

    def up_send():
        shares[pl.ds(aligned(PART + x * CHUNK), CHUNK), :] = up_share[:CHUNK]
        across("s").start()

    def up_take():
        across("s").wait_recv()
        shares[pl.ds(aligned(PART + (1 - x) * CHUNK), CHUNK), :] = up_landed[...]

    image_grads = gathered_down

    def image_view(chunk, blk, side):
        return image_grads.at[pl.ds(aligned(image_row(blk, side) + chunk * half), half)]

    def grads_at(known_z=None):
        return Gather(
            known_z, image_view, IMAGE_ORDERS, lambda chunk, count: image_grads.at[pl.ds(0, count * half)], *grads_sems
        )

    def tail_works(known_z):
        known, images = reduce_at(known_z), grads_at(known_z)
        works = [work for part in (2, 1, 0) for work in in_order(known.events((part,)))]
        works += [work for chunk in (0, 1) for work in in_order(images.events(chunk))]
        return works + [up_send, up_take]

    reduce, grads = reduce_at(), grads_at()
    plan = Plan(TAIL_PLAN, [tail_works(known_z) for known_z in range(4)])
    hear_near(front_done)
    plan.run()
    block.back_narrow()
    for part in (0, 1):
        shared(f"p{part}").start()
    across("g").start()
    plan.run()
    for name in ("og", "a0", "a1"):
        shared(name).wait_recv()
    for part in (0, 1):
        block.down_grad(part, core, rail_two, part_ref(2))
    plan.run()
    block.narrow()
    across("r").start()
    tell_near(narrow_done)
    plan.run()
    across("g").wait_recv()
    block.back_wide()
    shared("gb").start()
    plan.run()
    block.back_attend()
    for part in range(3):
        shared(f"j{part}").start()
    plan.run()
    block.back_project()
    hear_near(narrow_done)
    image_grads[pl.ds(aligned(band * tokens), tokens), :] = block.embed_grad()
    grads.start(0)
    grads.start(1)
    plan.run()
    for name in ("n2", "p0", "p1"):
        shared(name).wait_recv()
    block.turn_rail(rail_two, normed_two, core)

    def up_place(owner):
        zz, xx, yy = owner // 4, owner // 2 % 2, owner % 2
        return aligned((zz * 2 + yy) * PART + ((1 - x) if xx else x) * CHUNK)

    block.pair_grad(
        rail_two, rail_two, lambda cols: grad_pre[0, :, cols], lambda cols: grad_pre[1, :, cols], part_ref(1), up_place
    )
    plan.run()
    for name in ("n1", "mx", "gb", "j0", "j1", "j2"):
        shared(name).wait_recv()
    block.turn_rail(rail_one, normed_one, core)
    block.turn_rail(rail_mixed, mixed, core)
    block.pair_grad(
        rail_one, rail_one, lambda cols: grad_joint[0, :, cols], lambda cols: grad_joint[1, :, cols], part_ref(0),
        lambda owner: owner * PART,
    )
    block.pair_grad(
        rail_one, rail_mixed, lambda cols: grad_joint[2, :, cols], lambda cols: grad_branch[:, cols], part_ref(0),
        lambda owner: owner * PART + CHUNK,
    )
    for name in SHARED:
        shared(name).wait_send()
    for name in ("og", "n2", "g"):
        across(name).wait_send()
    for piece in range(16):
        gen_copy(piece, weights).start()

    kernel_total = pre_act.at[0]
    kernel_total[...] = jnp.zeros(kernel_total.shape, F32)
    small[2:3, :] = jnp.zeros((1, width), F32)
    near_side = z // 2
    for side in (near_side, 1 - near_side):
        plan.run()
        for chunk in (0, 1):
            grads.wait_side(chunk, side)

        @pl.loop(0, 2)
        def _(step, side=side):
            group = 2 * side + step
            for image in range(4):
                half_rows = slice(image % 2 * tokens, (image % 2 + 1) * tokens)
                rows = pl.ds(aligned((group * 4 + image) * tokens), tokens)
                scaled = image_grads[rows, :].astype(F32) * band_scale[group * 4 + image][:1, :1]
                small[2:3, :] += jnp.sum(scaled, axis=0, keepdims=True)
                act[image // 2, half_rows] = scaled.astype(B16)
            scaled = act[:, : 2 * tokens].reshape(4 * tokens, width)
            pixel_rows[pl.ds(group * 4, 4)] = dot_nt(scaled, kernels[...]).astype(B16).reshape(4, tokens, -1)
            kernel_total[...] += dot_nn(turned_pixels[group], scaled)

    store_pixels = pltpu.make_async_copy(pixel_rows, pixel_out, pix_sem)
    store_pixels.start()
    spread_kernels.finish()
    sending[...] = kernel_total[...].astype(B16)
    owner = core == y

    def column_copy(target, plane):
        return pltpu.make_async_remote_copy(
            src_ref=rows16(sending, target),
            dst_ref=rows16(landed_grads, y * bands + band),
            send_sem=cols_sems[0].at[0],
            recv_sem=cols_sems[1].at[0],
            device_id=(target, plane),
            device_id_type=MESH,
        )

    for step in range(1, bands):
        target = (band + step) % bands
        column_copy(target, target % 2).start()

    @pl.when(core != y)
    def _():
        column_copy(band, 1 - y).start()

    @pl.when(owner)
    def _():
        landed_grads[pl.ds(aligned((y * bands + band) * 16), 16), :] = sending[own_rows, :]

    vec_half = pltpu.make_async_remote_copy(
        src_ref=small, dst_ref=small_partner, send_sem=vec_half_sems[0].at[0], recv_sem=vec_half_sems[1].at[0],
        device_id=partner, device_id_type=MESH,
    )
    vec_half.start()
    plan.run()
    vec_half.wait_recv()
    small_all[band] = small[...] + small_partner[...]
    vector_spread = Exchange(
        lambda target: small_all.at[band], lambda source: small_all.at[source], lambda count: small_all.at[pl.ds(0, count)],
        *[sem.at[0] for sem in vec_sems],
    )
    vector_spread.start()
    plan.run()
    pix = summed.shape[0]

    def tell_code(target, plane):
        return pltpu.make_async_remote_copy(
            src_ref=code_all.at[band],
            dst_ref=code_all.at[band],
            send_sem=code_sems[0].at[0],
            recv_sem=code_sems[1].at[0],
            device_id=(target, plane),
            device_id_type=MESH,
        )

    pass_summed = pltpu.make_async_remote_copy(
        src_ref=summed, dst_ref=summed, send_sem=summed_sems[0].at[0], recv_sem=summed_sems[1].at[0],
        device_id=partner, device_id_type=MESH,
    )
    gen_wait(weights)

    @pl.when(owner)
    def _():
        bulk_copy(landed_grads.at[pl.ds(0, (2 * bands - 1) * 16)], cols_sems[0].at[0], cols_sems[1].at[0]).wait_recv()
        summed[...] = landed_grads[0:pix, :] + landed_grads[pix : 2 * pix, :]
        pass_summed.start()
        mixing[...] = swap_rows(summed[...])
        code_part[...] = jnp.zeros(code_part.shape, F32)

        @pl.loop(0, 16)
        def _(piece):
            code_part[...] += dot_nt(
                mixing[pl.ds(aligned(piece * 16), 16), :], weights[pl.ds(aligned(piece * 128), 128), :]
            )

        code_all[band] = code_part[...]
        for step in range(bands):
            for plane in (y, 1 - y) if step else (1 - y,):
                tell_code((band + step) % bands, plane).start()

    @pl.when(core != y)
    def _():
        pass_summed.wait_recv()

    store_columns = pltpu.make_async_copy(summed, kernel_grads, pix_sem)
    store_pixels.wait()
    store_columns.start()
    plan.run()
    across("r").wait_recv()
    block_out[...] = (residual[...] + result_from_x[...].astype(F32)).astype(B16)
    vector_spread.wait()
    store_vectors = pltpu.make_async_copy(small_all, vectors, gen_sem)
    store_vectors.start()
    bulk = code_all.at[pl.ds(0, bands - 1)]
    pl.when(owner)(bulk_copy(bulk, code_sems[0].at[0], code_sems[1].at[0]).wait_recv)
    bulk = code_all.at[pl.ds(0, bands)]
    pl.when(core != y)(bulk_copy(bulk, code_sems[0].at[0], code_sems[1].at[0]).wait_recv)
    total = code_all[0]
    for source in range(1, bands):
        total = total + code_all[source]
    code_grads[...] = total
    plan.run()
    reduce.finish()
    grads.finish()
    for name in ("u", "r", "s"):
        across(name).wait_send()
    vec_half.wait_send()
    vector_spread.finish()

    @pl.when(owner)
    def _():
        sent = landed_grads.at[pl.ds(0, (bands - 1) * 16)]
        bulk_copy(sent, cols_sems[0].at[0], cols_sems[1].at[0]).wait_send()
        sent = code_all.at[pl.ds(0, 2 * bands - 1)]
        bulk_copy(sent, code_sems[0].at[0], code_sems[1].at[0]).wait_send()
        pass_summed.wait_send()

    @pl.when(core != y)
    def _():
        sent = landed_grads.at[pl.ds(0, bands * 16)]
        bulk_copy(sent, cols_sems[0].at[0], cols_sems[1].at[0]).wait_send()

    store_columns.wait()
    store_vectors.wait()


VMEM_BYTES = 63 * 2**20


def layer(counts, mask, wavelengths, pixels, kernel_gen, weights, frequency, hyper, bias_gen, out_grad, gains):
    width = bias_gen.shape[1]
    bands = lax.axis_size("band")
    devices = bands * lax.axis_size("dp")
    images, tokens, pix = pixels.shape
    hidden = hyper[4].shape[1]
    vmem = pl.BlockSpec(memory_space=pltpu.VMEM)
    hbm = pl.BlockSpec(memory_space=pl.ANY)
    smem = pl.BlockSpec(memory_space=pltpu.SMEM)
    shape = jax.ShapeDtypeStruct
    rows = lambda kind, *lead: pltpu.VMEM((*lead, tokens, width), kind)
    pair = lambda *lead: pltpu.VMEM((*lead, 2 * tokens, width), B16)
    four = lambda *lead: pltpu.VMEM((*lead, 4 * tokens, width), B16)
    dma = pltpu.SemaphoreType.DMA
    code = (bands, HW)
    kept = [(bands, 3 * HW), (HHEADS * bands, bands), code, code, (bands, 1), (bands, hidden), code, (bands, 1), (2, HW), code]
    return pl.pallas_call(
        layer_kernel,
        out_shape=[
            shape((tokens, width), B16),
            shape(pixels.shape, B16),
            shape((3 * PART, width), F32),
            shape((pix, width), B16),
            shape(code, B16),
            shape(code, F32),
            shape((bands, 8, width), F32),
            *[shape(dims, F32) for dims in kept],
        ],
        in_specs=[smem] * 3 + [hbm] * 2 + [vmem] * 15,
        out_specs=[vmem, hbm, vmem, hbm, vmem, vmem, hbm] + [vmem] * KEPT,
        scratch_shapes=[
            pltpu.VMEM((devices * PART, width), B16),
            pltpu.VMEM((devices // 2 * PART, width), B16),
            pltpu.VMEM((images * tokens, width), B16),
            pltpu.VMEM((6 * width, width), B16),
            pltpu.VMEM((16 * HW, width), B16),
            pltpu.VMEM(((19 + 11 + 11) * PART, width), B16),
            rows(B16, 3),
            pltpu.VMEM((HEADS // 2, 2 * tokens, tokens), F32),
            pltpu.VMEM((2, 2 * tokens, width), F32),
            four(2),
            four(2),
            four(),
            pair(),
            pair(),
            four(),
            rows(F32),
            rows(F32),
            pltpu.VMEM((tokens, 128), F32),
            pltpu.VMEM((tokens, 128), F32),
            pltpu.VMEM((2 * tokens, width), F32),
            rows(F32),
            pair(),
            rows(B16),
            pair(3),
            pltpu.VMEM((width, 4 * tokens), B16),
            pltpu.VMEM((width // 2, 2 * tokens), B16),
            pltpu.VMEM((width // 2, 2 * tokens), B16),
            pltpu.VMEM((width // 2, 4 * tokens), B16),
            pltpu.VMEM((CHUNK, width), B16),
            pltpu.VMEM((PART, width), F32),
            pltpu.VMEM((CHUNK, width), F32),
            rows(B16),
            rows(B16),
            rows(B16),
            rows(B16),
            rows(F32),
            pltpu.VMEM(pixels.shape, B16),
            pltpu.VMEM((4, pix, 4 * tokens), B16),
            pltpu.VMEM((images // 2, tokens, pix), B16),
            pltpu.VMEM((pix, width), B16),
            pltpu.VMEM((pix, width), B16),
            pltpu.VMEM((pix, width), B16),
            pltpu.VMEM((pix, width), B16),
            pltpu.VMEM((2 * pix, width), B16),
            pltpu.VMEM((pix, width), B16),
            pltpu.VMEM((8, width), F32),
            pltpu.VMEM((8, width), F32),
            pltpu.VMEM((bands, 8, width), F32),
            pltpu.VMEM(code, F32),
            pltpu.VMEM((2 * bands, *code), F32),
            pltpu.VMEM((2, width), F32),
            pltpu.VMEM((images, 8, 128), F32),
            pltpu.VMEM((images, 8, 128), F32),
            dma,
            dma,
            pltpu.SemaphoreType.REGULAR,
            pltpu.SemaphoreType.REGULAR,
            *[dma((3, 3)), dma((32,)), dma((3, 2)), dma((3, 2))],
            *[dma((2, 3)), dma((16,)), dma((2, 2)), dma((2, 2))],
            *[dma((3, 3)), dma((37,))],
            *[dma((2, 2)), dma((20,))],
            *[dma((len(SHARED),))] * 2,
            *[dma((len(ACROSS),))] * 2,
            *[dma((3,))] * 2,
            *[dma((1,))] * 12,
        ],
        compiler_params=pltpu.CompilerParams(
            collective_id=0, has_side_effects=True, vmem_limit_bytes=VMEM_BYTES
        ),
        name="layer",
    )(counts, mask, wavelengths, pixels, kernel_gen, *weights, frequency, *hyper, bias_gen, out_grad, *gains)


def finish_kernel(*refs):
    count = 12 + KEPT
    outside = refs[:count]
    (block_out, pixel_out, grad_qkv, grad_out, grad_gain_one, grad_up, grad_down, grad_gain_two, grad_gen, grad_bias,
     gain_one_sum, gain_two_sum, share_qkv, share_out, share_up, share_down, *scratch) = refs[count:]
    inside, (store, in_sem, copy_sem, gen_sem) = scratch[:count], scratch[count:]
    loads = [pltpu.make_async_copy(*pair, in_sem.at[at]) for at, pair in enumerate(zip(outside, inside))]
    for load in loads:
        load.start()
    (code_low, columns, shares, hyper_qkv, hyper_out, hyper_up, hyper_down, bias_gen, code_grads, vectors,
     *kept_refs, hyper_gains, waves, block_in, pixel_in) = inside
    width = bias_gen.shape[1]
    copies = [
        pltpu.make_async_copy(block_in, block_out, copy_sem.at[0]),
        pltpu.make_async_copy(pixel_in, pixel_out, copy_sem.at[1]),
    ]
    for load in loads[:2]:
        load.wait()
    code = code_low[...]
    swapped = swap_rows(columns[...])
    gen_copies = []
    for piece in range(16):
        store[piece] = dot_tn(code, swapped[piece * 16 : (piece + 1) * 16])
        gen_copies.append(
            pltpu.make_async_copy(
                store.at[piece], grad_gen.at[:, pl.ds(piece * width, width)], gen_sem.at[piece]
            )
        )
        gen_copies[-1].start()
    for load in loads[2:]:
        load.wait()
    for copy in copies:
        copy.start()
    share_qkv[...] = jnp.concatenate([shares[at * 24 : at * 24 + 24, :] for at in range(3)], axis=1)
    share_out[...] = shares[72:96, :]
    group = 4 * PART
    up_pieces = []
    for at in range(8):
        z_of, x_of = at // 2, at % 2
        row = PART + x_of * CHUNK + z_of // 2 * 24
        up_pieces.append(shares[row : row + 24, z_of % 2 * group : (z_of % 2 + 1) * group])
    share_up[...] = jnp.concatenate(up_pieces, axis=1)
    share_down[...] = shares[192:288, :]
    sums = jnp.sum(vectors[...], axis=0)
    gain_one_sum[...] = sums[0]
    gain_two_sum[...] = sums[1]
    bias_grads = vectors[:, 2, :]
    grad_bias[...] = dot_tn(jnp.concatenate([code] * 3, axis=0), jnp.concatenate(split3(bias_grads), axis=0))
    grad_code = code_grads[...] + wide_nt(bias_grads, bias_gen[...])
    grads = hyper_backward(
        grad_code, [ref[...] for ref in kept_refs], waves[...], hyper_qkv[...], hyper_out[...], hyper_gains[0:1, :],
        hyper_up[...], hyper_down[...], hyper_gains[1:2, :],
    )
    for ref, value in zip((grad_qkv, grad_out, grad_gain_one, grad_up, grad_down, grad_gain_two), grads):
        ref[...] = value
    for copy in copies + gen_copies:
        copy.wait()


def finish(hyper, bias_gen, code_low, code_grads, vectors, columns, shares, block_out, pixel_grad, kept, kernel_gen, weights):
    width = bias_gen.shape[1]
    vmem = pl.BlockSpec(memory_space=pltpu.VMEM)
    hbm = pl.BlockSpec(memory_space=pl.ANY)
    shape = lambda array: jax.ShapeDtypeStruct(array.shape, F32)
    line = jax.ShapeDtypeStruct((1, HW), F32)
    weights_in = (hyper[0], hyper[1], hyper[4], hyper[5])
    operands = (code_low, columns, shares, *weights_in, bias_gen, code_grads, vectors, *kept, block_out, pixel_grad)
    return pl.pallas_call(
        finish_kernel,
        out_shape=[
            jax.ShapeDtypeStruct(block_out.shape, B16),
            jax.ShapeDtypeStruct(pixel_grad.shape, B16),
            shape(hyper[0]), shape(hyper[1]), line, shape(hyper[4]), shape(hyper[5]), line,
            shape(kernel_gen), shape(bias_gen), *[jax.ShapeDtypeStruct((width,), F32)] * 2,
            *[shape(weight) for weight in weights],
        ],
        in_specs=[hbm] * len(operands),
        out_specs=[hbm, hbm] + [vmem] * 6 + [hbm] + [vmem] * 7,
        scratch_shapes=[
            *[pltpu.VMEM(operand.shape, operand.dtype) for operand in operands],
            pltpu.VMEM((16, HW, width), F32),
            pltpu.SemaphoreType.DMA((len(operands),)),
            pltpu.SemaphoreType.DMA((2,)),
            pltpu.SemaphoreType.DMA((16,)),
        ],
        compiler_params=pltpu.CompilerParams(vmem_limit_bytes=VMEM_BYTES),
        name="finish",
    )(*operands)


def body(
    pixels,
    wavelengths,
    band_counts,
    band_mask,
    hyper_qkv,
    hyper_out,
    hyper_gain1,
    hyper_up,
    hyper_down,
    hyper_gain2,
    kernel_gen,
    bias_gen,
    norm_gain1,
    attn_qkv,
    attn_out,
    norm_gain2,
    mlp_up,
    mlp_down,
    out_grad,
):
    f32 = jnp.float32
    b16 = jnp.bfloat16
    band_local = pixels.shape[3]
    pixel_local = pixels[0]
    model_width = bias_gen.shape[1]
    hyper_params = tuple(
        (
            weight.astype(f32)
            for weight in (hyper_qkv, hyper_out, hyper_gain1, hyper_up, hyper_down, hyper_gain2)
        )
    )
    wave_tokens = wave_embed(wavelengths, HW)
    band_code, hyper_pull = jax.vjp(lambda *params: hyper_net(wave_tokens, *params), *hyper_params)
    code_low = band_code.astype(b16)
    column_part = jnp.dot(code_low, kernel_gen, preferred_element_type=f32).astype(b16)
    kernel_rows = lax.all_to_all(column_part, "band", split_axis=0, concat_axis=1, tiled=True)
    kernels = kernel_rows.reshape(band_local, -1, model_width)
    first_band = lax.axis_index("band") * band_local
    own_code = lax.dynamic_slice_in_dim(code_low, first_band, band_local, 0)
    count_row = band_counts[0]
    biases = jnp.dot(own_code, bias_gen, preferred_element_type=f32)
    slot_ids = first_band + jnp.arange(band_local, dtype=jnp.int32)
    active = (slot_ids[None, :] < count_row[:, None]) & (band_mask[0] == 1)
    band_weight = jnp.where(active, lax.rsqrt(count_row.astype(f32))[:, None], f32(0.0))
    pixel_rows = pixel_local
    weight_rows = band_weight
    conv_out = jnp.einsum("inbp,bpd->inbd", pixel_rows, kernels, preferred_element_type=f32)
    residual = lax.psum_scatter(
        jnp.sum((conv_out + biases[None, None]) * weight_rows[:, None, :, None], axis=2),
        "band",
        scatter_dimension=0,
        tiled=True,
    )
    gathered = (
        lax.all_gather(attn_qkv, ("band", "dp"), axis=0, tiled=True),
        lax.all_gather(attn_out, ("band", "dp"), axis=0, tiled=True),
        lax.all_gather(mlp_up, ("band", "dp"), axis=0, tiled=True),
        lax.all_gather(mlp_down, ("band", "dp"), axis=0, tiled=True),
    )
    qkv_full, out_full, up_full, down_full = gathered
    gain_one = norm_gain1.astype(f32)
    gain_two = norm_gain2.astype(f32)
    images, tokens = (residual.shape[0], residual.shape[1])
    score_scale = 1.0 / math.sqrt(HEAD_DIM)
    normed_full, unit_one, inverse_one = norm_parts(residual, gain_one)
    normed_one = normed_full.astype(b16)
    joint_rows = jnp.einsum("ind,de->ine", normed_one, qkv_full, preferred_element_type=f32).astype(
        b16
    )
    queries = joint_rows[..., :model_width].reshape(images, tokens, HEADS, HEAD_DIM)
    key_rows = joint_rows[..., model_width : 2 * model_width].reshape(
        images, tokens, HEADS, HEAD_DIM
    )
    value_rows = joint_rows[..., 2 * model_width :].reshape(images, tokens, HEADS, HEAD_DIM)
    scores = (
        jnp.einsum("inhc,imhc->ihnm", queries, key_rows, preferred_element_type=f32) * score_scale
    )
    row_top = jnp.max(scores, axis=-1, keepdims=True)
    log_total = row_top + jnp.log(jnp.sum(jnp.exp(scores - row_top), axis=-1, keepdims=True))
    probs_full = jnp.exp(scores - log_total)
    probs_low = probs_full.astype(b16)
    mixed_low = (
        jnp.einsum("ihnm,imhc->inhc", probs_low, value_rows, preferred_element_type=f32)
        .reshape(images, tokens, model_width)
        .astype(b16)
    )
    middle = residual + jnp.einsum("ind,de->ine", mixed_low, out_full, preferred_element_type=f32)
    normed_two_full, unit_two, inverse_two = norm_parts(middle, gain_two)
    normed_two = normed_two_full.astype(b16)
    pre_act = jnp.einsum("ind,df->inf", normed_two, up_full, preferred_element_type=f32)
    act_low = gelu_tanh(pre_act).astype(b16)
    result = middle + jnp.einsum("inf,fd->ind", act_low, down_full, preferred_element_type=f32)
    block_out = result.astype(b16)[None]
    qkv_back, out_back, up_back, down_back = (
        lax.all_gather(attn_qkv, ("band", "dp"), axis=0, tiled=True),
        lax.all_gather(attn_out, ("band", "dp"), axis=0, tiled=True),
        lax.all_gather(mlp_up, ("band", "dp"), axis=0, tiled=True),
        lax.all_gather(mlp_down, ("band", "dp"), axis=0, tiled=True),
    )
    grad_top = out_grad[0]
    grad_down = jnp.einsum("inf,ind->fd", act_low, grad_top, preferred_element_type=f32)
    grad_act = jnp.einsum("ind,fd->inf", grad_top, down_back, preferred_element_type=f32)
    grad_pre = (grad_act * gelu_slope(pre_act)).astype(b16)
    grad_up = jnp.einsum("ind,inf->df", normed_two, grad_pre, preferred_element_type=f32)
    grad_normed_two = jnp.einsum("inf,df->ind", grad_pre, up_back, preferred_element_type=f32)
    grad_gain_two = jnp.sum(grad_normed_two * unit_two, axis=(0, 1))
    grad_middle = grad_top.astype(f32) + norm_back(grad_normed_two, gain_two, unit_two, inverse_two)
    grad_branch = grad_middle.astype(b16)
    grad_out_proj = jnp.einsum("ind,ine->de", mixed_low, grad_branch, preferred_element_type=f32)
    grad_mixed = (
        jnp.einsum("ine,de->ind", grad_branch, out_back, preferred_element_type=f32)
        .astype(b16)
        .reshape(images, tokens, HEADS, HEAD_DIM)
    )
    grad_values = jnp.einsum("ihnm,inhc->imhc", probs_low, grad_mixed, preferred_element_type=f32)
    grad_probs = jnp.einsum("inhc,imhc->ihnm", grad_mixed, value_rows, preferred_element_type=f32)
    grad_scores = (
        probs_full * (grad_probs - jnp.sum(grad_probs * probs_full, axis=-1, keepdims=True))
    ).astype(b16)
    grad_queries = (
        jnp.einsum("ihnm,imhc->inhc", grad_scores, key_rows, preferred_element_type=f32)
        * score_scale
    )
    grad_keys = (
        jnp.einsum("ihnm,inhc->imhc", grad_scores, queries, preferred_element_type=f32)
        * score_scale
    )
    grad_joint = jnp.concatenate(
        [
            grad_queries.reshape(images, tokens, model_width),
            grad_keys.reshape(images, tokens, model_width),
            grad_values.reshape(images, tokens, model_width),
        ],
        axis=-1,
    ).astype(b16)
    grad_qkv = jnp.einsum("ind,ine->de", normed_one, grad_joint, preferred_element_type=f32)
    grad_normed_one = jnp.einsum("ine,de->ind", grad_joint, qkv_back, preferred_element_type=f32)
    grad_gain_one = jnp.sum(grad_normed_one * unit_one, axis=(0, 1))
    grad_embed = grad_middle + norm_back(grad_normed_one, gain_one, unit_one, inverse_one)
    grad_embed_low = grad_embed.astype(b16)[None]
    grad_rows = lax.all_gather(grad_embed_low, "band", axis=1, tiled=True)[0].astype(f32)
    weight_rows = band_weight
    pixel_rows = pixel_local
    scaled = grad_rows[:, :, None, :] * weight_rows[:, None, :, None]
    bias_total = jnp.sum(scaled, axis=(0, 1))
    scaled_low = scaled.astype(b16)
    kernel_total = jnp.einsum("inbp,inbd->bpd", pixel_rows, scaled_low, preferred_element_type=f32)
    pixel_part = jnp.einsum(
        "inbd,bpd->inbp", scaled_low, kernels, preferred_element_type=f32
    ).astype(b16)
    pixel_total = pixel_part
    kernel_grad, bias_grad, pixel_total = (kernel_total, bias_total, pixel_total)
    pixel_out = pixel_total[None]
    kernel_grad_low = kernel_grad.reshape(band_local, -1).astype(b16)
    grad_columns = lax.all_to_all(kernel_grad_low, "band", split_axis=1, concat_axis=0, tiled=True)
    grad_kernel_part = jnp.einsum("nh,nc->hc", code_low, grad_columns, preferred_element_type=f32)
    grad_code_part = jnp.einsum("nc,hc->nh", grad_columns, kernel_gen, preferred_element_type=f32)
    bias_back = jnp.einsum("bd,hd->bh", bias_grad, bias_gen.astype(f32), precision=PRECISE)
    grad_code_part = grad_code_part + lax.dynamic_update_slice_in_dim(
        jnp.zeros_like(grad_code_part), bias_back, first_band, 0
    )
    grad_bias_part = jnp.einsum("bh,bd->hd", own_code.astype(f32), bias_grad, precision=PRECISE)
    grad_code, grad_bias_gen, grad_norm_gain1, grad_norm_gain2 = lax.psum(
        (grad_code_part, grad_bias_part, grad_gain_one, grad_gain_two), ("band", "dp")
    )
    grad_kernel_gen = lax.psum(grad_kernel_part.astype(jnp.bfloat16), "dp").astype(jnp.float32)
    hyper_grads = hyper_pull(grad_code)
    shares = (
        lax.psum_scatter(grad_qkv, ("band", "dp"), scatter_dimension=0, tiled=True),
        lax.psum_scatter(grad_out_proj, ("band", "dp"), scatter_dimension=0, tiled=True),
        lax.psum_scatter(grad_up, ("band", "dp"), scatter_dimension=0, tiled=True),
        lax.psum_scatter(grad_down, ("band", "dp"), scatter_dimension=0, tiled=True),
    )
    return (
        block_out,
        pixel_out,
        hyper_grads[0],
        hyper_grads[1],
        hyper_grads[2],
        hyper_grads[3],
        hyper_grads[4],
        hyper_grads[5],
        grad_kernel_gen,
        grad_bias_gen,
        grad_norm_gain1,
        shares[0],
        shares[1],
        grad_norm_gain2,
        shares[2],
        shares[3],
    )


def fast_body(
    pixels,
    wavelengths,
    band_counts,
    band_mask,
    hyper_qkv,
    hyper_out,
    hyper_gain1,
    hyper_up,
    hyper_down,
    hyper_gain2,
    kernel_gen,
    bias_gen,
    norm_gain1,
    attn_qkv,
    attn_out,
    norm_gain2,
    mlp_up,
    mlp_down,
    out_grad,
):
    half = np.arange(HW) % (HW // 2)
    frequency = jnp.power(10000.0, jnp.asarray(-half / (HW // 2), F32))[None]
    weights = (attn_qkv, attn_out, mlp_up, mlp_down)
    hyper = (hyper_qkv, hyper_out, hyper_gain1, hyper_gain2, hyper_up, hyper_down)
    block_out, pixel_grad, shares, columns, code_low, code_grads, vectors, *kept = layer(
        band_counts[0],
        band_mask[0, :, 0],
        wavelengths,
        pixels[0, :, :, 0],
        kernel_gen,
        weights,
        frequency,
        hyper,
        bias_gen,
        out_grad[0, 0],
        (norm_gain1, norm_gain2),
    )
    outs = finish(
        hyper,
        bias_gen,
        code_low,
        code_grads,
        vectors,
        columns,
        shares,
        block_out,
        pixel_grad,
        kept,
        kernel_gen,
        weights,
    )
    block_out, pixel_grad, *hyper_grads, grad_gen, grad_bias, gain_one, gain_two = outs[:12]
    hyper_grads[2], hyper_grads[5] = hyper_grads[2][0], hyper_grads[5][0]
    return (
        block_out[None, None],
        pixel_grad[None, :, :, None],
        *hyper_grads,
        grad_gen,
        grad_bias,
        gain_one,
        outs[12],
        outs[13],
        gain_two,
        outs[14],
        outs[15],
    )


def solution(mesh):
    placed = (
        P("dp", None, None, "band", None),
        P(),
        P("dp", None),
        P("dp", None, "band"),
        P(),
        P(),
        P(),
        P(),
        P(),
        P(),
        P(None, "band"),
        P(),
        P(),
        P(("band", "dp"), None),
        P(("band", "dp"), None),
        P(),
        P(("band", "dp"), None),
        P(("band", "dp"), None),
        P("dp", "band", None, None),
    )
    one_slot = (mesh.shape["band"], mesh.shape["dp"]) == (16, 2)
    return jax.shard_map(
        fast_body if one_slot else body,
        mesh=mesh,
        in_specs=placed,
        out_specs=(
            P("dp", "band", None, None),
            P("dp", None, None, "band", None),
            P(),
            P(),
            P(),
            P(),
            P(),
            P(),
            P(None, "band"),
            P(),
            P(),
            P(("band", "dp"), None),
            P(("band", "dp"), None),
            P(),
            P(("band", "dp"), None),
            P(("band", "dp"), None),
        ),
        check_vma=False,
    )
```

```python
import functools
import math

import jax
import jax.numpy as jnp
from jax import lax
from jax.experimental import pallas as pl
from jax.experimental.pallas import tpu as pltpu
from jax.sharding import PartitionSpec as P
import numpy as np

HEADS = 12
HEAD_DIM = 64
HW = 128
HHEADS = 4


PRECISE = lax.Precision.HIGHEST
EPS_BLOCK = 1e-06
EPS_HYPER = 1e-05
GELU_COEF = 0.7978845608028654


def gelu_tanh(tensor):
    return (
        0.5 * tensor * (1.0 + jnp.tanh(GELU_COEF * (tensor + 0.044715 * tensor * tensor * tensor)))
    )


def gelu_slope(tensor):
    tanh_val = jnp.tanh(GELU_COEF * (tensor + 0.044715 * tensor * tensor * tensor))
    return 0.5 * (1.0 + tanh_val) + 0.5 * tensor * (1.0 - tanh_val * tanh_val) * GELU_COEF * (
        1.0 + 3.0 * 0.044715 * tensor * tensor
    )


def layer_norm(tensor, gain_vec, epsilon):
    centred = tensor - jnp.mean(tensor, axis=-1, keepdims=True)
    return (
        centred
        * lax.rsqrt(jnp.mean(centred * centred, axis=-1, keepdims=True) + epsilon)
        * gain_vec
    )


def norm_parts(tensor, gain_vec):
    centred = tensor - jnp.mean(tensor, axis=-1, keepdims=True)
    inverse = lax.rsqrt(jnp.mean(centred * centred, axis=-1, keepdims=True) + EPS_BLOCK)
    unit_rows = centred * inverse
    return (unit_rows * gain_vec, unit_rows, inverse)


def norm_back(grad_rows, gain_vec, unit_rows, inverse):
    scaled = grad_rows * gain_vec
    return inverse * (
        scaled
        - jnp.mean(scaled, axis=-1, keepdims=True)
        - unit_rows * jnp.mean(scaled * unit_rows, axis=-1, keepdims=True)
    )


def wave_embed(wave_ints, token_width):
    half_width = token_width // 2
    frequency = jnp.power(10000.0, -jnp.arange(half_width, dtype=jnp.float32) / half_width)
    angles = wave_ints.astype(jnp.float32)[:, None] * frequency[None, :]
    return jnp.concatenate([jnp.sin(angles), jnp.cos(angles)], axis=1)


def hyper_net(wave_tokens, qkv_weight, out_weight, gain_one, up_weight, down_weight, gain_two):
    tokens, token_width = wave_tokens.shape
    head_size = token_width // HHEADS
    qkv_rows = jnp.dot(wave_tokens, qkv_weight, precision=PRECISE)
    queries = qkv_rows[:, :token_width].reshape(tokens, HHEADS, head_size)
    key_rows = qkv_rows[:, token_width : 2 * token_width].reshape(tokens, HHEADS, head_size)
    value_rows = qkv_rows[:, 2 * token_width :].reshape(tokens, HHEADS, head_size)
    scores = jnp.einsum("nhc,mhc->hnm", queries, key_rows, precision=PRECISE) / math.sqrt(head_size)
    weights_soft = jax.nn.softmax(scores, axis=-1)
    mixed_rows = jnp.einsum("hnm,mhc->nhc", weights_soft, value_rows, precision=PRECISE).reshape(
        tokens, token_width
    )
    first_norm = layer_norm(
        wave_tokens + jnp.dot(mixed_rows, out_weight, precision=PRECISE), gain_one, EPS_HYPER
    )
    inner_act = gelu_tanh(jnp.dot(first_norm, up_weight, precision=PRECISE))
    return layer_norm(
        first_norm + jnp.dot(inner_act, down_weight, precision=PRECISE), gain_two, EPS_HYPER
    )


MESH = pl.DeviceIdType.MESH
B16 = jnp.bfloat16
F32 = jnp.float32
CHUNK = 48
DIMS = "xyz"
PART = 96
FRONT_PLAN = (
    (
        (),
        (),
        (),
        (),
        (1, 3, 2, 42, 41, 29, 11),
        (),
        (),
        (53, 57, 61, 10, 13, 28),
        (54,),
        (55, 66, 72, 5, 58, 63, 48),
        (56, 77, 83, 62, 22, 44, 67, 74, 35, 9, 14, 17, 73, 80, 82, 84, 50, 18, 89, 21, 91, 24, 31, 26, 34),
        (86, 87, 37),
        (39, 47),
        (),
        (),
        (52,),
        (),
        (),
    ),
    (
        (),
        (),
        (),
        (0, 1, 3, 2),
        (42, 29, 41, 7, 40),
        (6, 11),
        (),
        (53,),
        (54, 10, 13),
        (55, 59, 5),
        (56, 58, 64, 48, 62, 70, 45, 67, 75, 71, 27, 19, 68, 76, 14, 81, 73, 22, 88, 28, 17, 78, 82, 84, 31, 85, 89, 32, 91, 79, 44, 24),
        (86, 87, 35),
        (37,),
        (),
        (),
        (50,),
        (),
        (),
    ),
    (
        (),
        (),
        (),
        (0, 1, 3, 2),
        (42, 29, 40, 7),
        (41,),
        (),
        (53, 6, 11),
        (54,),
        (55, 10, 13),
        (56, 58, 4, 45, 62, 60, 67, 48, 65, 70, 73, 28, 82, 75, 19, 89, 12, 81, 84, 22, 71, 88, 27, 76, 91, 15, 69, 30, 78, 35, 86, 85, 87, 79, 43, 23),
        (32,),
        (),
        (36,),
        (49,),
        (),
        (),
        (),
    ),
    (
        (),
        (),
        (),
        (),
        (0, 3, 2, 42, 40, 29, 7),
        (6, 13, 27),
        (),
        (53,),
        (54, 57, 61, 4, 45),
        (55, 77, 83),
        (56, 66, 72, 58, 19, 43, 62, 63, 32, 8, 12, 15, 67, 80, 81, 84, 49, 73, 74, 88, 20, 16, 91, 23, 30, 25, 33),
        (85, 87, 36),
        (38, 46),
        (),
        (),
        (51,),
        (),
        (),
    ),
)
TAIL_PLAN = (
    (
        (),
        (),
        (0, 1, 2, 3),
        (),
        (4, 6),
        (),
        (5,),
        (18, 21, 24, 70, 71, 27, 30, 33, 7, 83, 84, 11, 10, 14, 73, 77),
        (90, 86, 39, 40, 41, 79, 42, 43, 44, 76, 45, 46),
        (92, 89, 81, 47, 48, 94, 50),
        (49, 53, 16, 17, 51, 32, 34, 52, 54, 57, 36, 58, 62, 59, 60, 61, 65),
        (),
        (38, 95, 96, 67, 68),
        (),
    ),
    (
        (),
        (),
        (0, 1, 2, 3),
        (),
        (4,),
        (),
        (5,),
        (8, 7, 70, 71, 69),
        (83, 84, 82, 77, 39, 40, 41, 73, 74, 42, 43, 44, 45, 86, 90, 46, 10, 19, 22, 87, 47, 25, 79),
        (92, 48, 13, 28, 50, 26, 49, 31),
        (51, 29, 35, 52, 54, 32, 34, 12, 57, 36, 15, 59, 58, 60, 61),
        (55, 16, 17, 38, 95, 63),
        (66, 96, 64),
        (67, 68),
    ),
    (
        (),
        (),
        (0, 1, 2, 3),
        (),
        (4,),
        (),
        (5,),
        (7,),
        (69, 70, 71, 82, 83, 84, 39, 40, 41, 42, 43, 74, 44, 45, 46, 10, 72, 77, 9, 12, 85, 87, 20, 47, 23, 90, 48),
        (78, 91, 26, 25, 50, 29, 28, 51, 49),
        (32, 31, 34, 54, 52, 36, 35, 57, 16, 59, 13, 60, 58, 61, 15, 17),
        (38, 95, 56),
        (67, 63, 64, 96, 66, 68),
        (),
    ),
    (
        (),
        (),
        (0, 1, 2, 3),
        (),
        (4,),
        (),
        (5, 6),
        (18, 21, 69, 71, 24, 27, 30, 33, 7, 82, 84, 14, 10, 11, 74),
        (72, 87, 39, 85, 40, 41, 42, 43, 44, 45, 46),
        (78, 75, 91, 47, 15, 17, 48, 80, 88, 50, 49, 51, 93, 31, 34),
        (54, 52, 53, 35, 57, 59, 60, 58, 65, 38, 95, 61, 62, 96),
        (),
        (66, 68),
        (),
    ),
)
FIRST_PARTS = (0, 2)
SUM_ORDERS = ('yxz', 'zy', 'yz')
EMBED_ORDERS = ('xz', 'zx')
IMAGE_ORDERS = ('zx', 'zx')
ORDERS = ('zxy', 'zy', 'zy')


def place(known_z=None):
    band = lax.axis_index("band")
    z = band // 4 if known_z is None else known_z
    return (z, (band // 2) % 2, band % 2, lax.axis_index("dp"))


def device(z, x, core, y):
    return (z * 4 + x * 2 + core, y)


def slot(z, x, core, y):
    return (z * 4 + x * 2 + core) * 2 + y


def when(cond, run):
    if isinstance(cond, bool):
        if cond:
            run()
    else:
        pl.when(cond)(run)


def both(first, second):
    return second if first is True else first & second


def aligned(rows):
    return pl.multiple_of(rows, 16)


def tell_peers(barrier):
    band, y = lax.axis_index("band"), lax.axis_index("dp")
    bands = lax.axis_size("band")
    for step in range(bands):
        for plane in (y, 1 - y) if step else (1 - y,):
            pl.semaphore_signal(
                barrier, inc=1, device_id=((band + step) % bands, plane), device_id_type=MESH
            )


def tell_near(semaphore):
    z, x, core, y = place()
    near = [
        (device(z, x, 1 - core, y), True),
        (device(z, 1 - x, core, y), True),
        (device(z, x, core, 1 - y), True),
        (device(z + 1, x, core, y), z < 3),
        (device(z - 1, x, core, y), z > 0),
    ]
    for target, cond in near:
        when(
            cond,
            functools.partial(
                pl.semaphore_signal, semaphore, inc=1, device_id=target, device_id_type=MESH
            ),
        )


def hear_near(semaphore):
    z = place()[0]
    pl.semaphore_wait(semaphore, 5 - z // 3 - (3 - z) // 3)


def bulk_copy(ref, send_sem, recv_sem):
    band, y = lax.axis_index("band"), lax.axis_index("dp")
    return pltpu.make_async_remote_copy(
        src_ref=ref,
        dst_ref=ref,
        send_sem=send_sem,
        recv_sem=recv_sem,
        device_id=(band, 1 - y),
        device_id_type=MESH,
    )


def in_order(events):
    return [work for _, _, work in sorted(events, key=lambda event: event[:2])]


class Plan:
    def __init__(self, table, catalogues):
        self.table, self.catalogues = table, catalogues
        self.at = 0

    def run(self):
        z = place()[0]
        for known_z, works in enumerate(self.catalogues):
            chosen = self.table[known_z][self.at]
            if not chosen:
                continue

            @pl.when(z == known_z)
            def _(works=works, chosen=chosen):
                for index in chosen:
                    works[index]()

        self.at += 1


class Gather:
    def __init__(self, known_z, view, orders, bulk, send_sem, recv_sem, pair_send, pair_recv):
        self.view, self.orders, self.bulk = view, orders, bulk
        self.send_sem, self.recv_sem = send_sem, recv_sem
        self.pair_send, self.pair_recv = pair_send, pair_recv
        self.z, self.x, self.core, self.y = place(known_z)

    def place_of(self, chunk, block):
        order = self.orders[chunk]
        place = block[0]
        for dim, at in (("x", block[1]), ("y", block[2])):
            if dim in order:
                place = place * 2 + at
        return sum(self.rails(before) for before in range(chunk)) + place

    def sibling(self):
        return device(self.z, self.x, 1 - self.core, self.y)

    def send(self, chunk, block, dim, cond, direction=0):
        z, x, core, y = self.z, self.x, self.core, self.y
        if dim == "x":
            targets = [(device(z, 1 - x, core, y), cond)]
        elif dim == "y":
            targets = [(device(z, x, core, 1 - y), cond)]
        else:
            targets = []
            if direction >= 0:
                targets.append((device(z + 1, x, core, y), both(cond, z < 3)))
            if direction <= 0:
                targets.append((device(z - 1, x, core, y), both(cond, z > 0)))
        src = self.view(chunk, block, core)
        for target, needed in targets:
            if needed is False:
                continue
            copy = pltpu.make_async_remote_copy(
                src_ref=src,
                dst_ref=src,
                send_sem=self.send_sem.at[chunk, DIMS.index(dim)],
                recv_sem=self.recv_sem.at[self.place_of(chunk, block)],
                device_id=target,
                device_id_type=MESH,
            )
            when(needed, copy.start)

    def pair(self, chunk, block, core):
        src = self.view(chunk, block, core)
        return pltpu.make_async_remote_copy(
            src_ref=src,
            dst_ref=src,
            send_sem=self.pair_send.at[chunk, block[0] // 2],
            recv_sem=self.pair_recv.at[chunk, block[0] // 2],
            device_id=self.sibling(),
            device_id_type=MESH,
        )

    def start(self, chunk):
        own = (self.z, self.x, self.y)
        for dim in self.orders[chunk]:
            self.send(chunk, own, dim, True)
        self.pair(chunk, own, self.core).start()

    def events(self, chunk, start=0.0, pace=1.0):
        held, found = [(0, 0, 0, 0, start)], []
        for dim in self.orders[chunk]:
            clock, new = 0.0, []
            ordered = sorted(held, key=lambda item: item[4])
            if dim == "z":
                for dist in (1, 2, 3):
                    for item in ordered:
                        clock = max(clock, item[4]) + pace
                        new += [(dist, way, item[2], item[3], clock) for way in (1, -1)]
            else:
                for item in ordered:
                    clock = max(clock, item[4]) + pace
                    flip = (1, item[3]) if dim == "x" else (item[2], 1)
                    new.append((item[0], item[1], *flip, clock))
            found += [
                (item[4], chunk, functools.partial(self.arrive, chunk, dim, item)) for item in new
            ]
            held = held + new
        return found

    def arrive(self, chunk, dim, item):
        dist, way, flip_x, flip_y, _ = item
        cond = True
        if way == 1:
            cond = self.z >= dist
        elif way == -1:
            cond = self.z + dist <= 3
        if cond is False:
            return
        block = (
            self.z - dist * way,
            1 - self.x if flip_x else self.x,
            1 - self.y if flip_y else self.y,
        )
        src = self.view(chunk, block, self.core)
        arriving = pltpu.make_async_remote_copy(
            src_ref=src,
            dst_ref=src,
            send_sem=self.send_sem.at[chunk, 0],
            recv_sem=self.recv_sem.at[self.place_of(chunk, block)],
            device_id=self.sibling(),
            device_id_type=MESH,
        )
        when(cond, arriving.wait_recv)
        if dim == "z":
            self.send(chunk, block, "z", cond, way)
        order = self.orders[chunk]
        for later in order[order.index(dim) + 1 :]:
            self.send(chunk, block, later, cond)
        when(cond, self.pair(chunk, block, self.core).start)

    def rails(self, chunk):
        return 4 * (2 if "x" in self.orders[chunk] else 1) * (2 if "y" in self.orders[chunk] else 1)

    def sent(self, chunk, z, over):
        order = self.orders[chunk]
        fresh = (z < 3) + (z > 0) if over == "z" else 1
        total = fresh if over in order else 0
        for _, _, work in self.events(chunk):
            _, dim, (dist, way, *_) = work.args
            if (way == 1 and z < dist) or (way == -1 and z + dist > 3):
                continue
            total += fresh if over in order[order.index(dim) + 1 :] else 0
            if dim == "z" and over == "z":
                total += z < 3 if way == 1 else z > 0
        return total

    def wait_side(self, chunk, side):
        every = self.bulk(chunk, self.rails(chunk) // 2)
        bulk_copy(every, self.pair_send.at[chunk, side], self.pair_recv.at[chunk, side]).wait_recv()

    def wait_pairs(self, chunk):
        for side in (0, 1):
            self.wait_side(chunk, side)

    def finish(self):
        ends = (self.z == 0) | (self.z == 3)
        inner = (self.z == 1) | (self.z == 2)
        for chunk in range(len(self.orders)):
            for dim in self.orders[chunk]:
                send_sem = self.send_sem.at[chunk, DIMS.index(dim)]
                for cond, z in ((ends, 0), (inner, 1)):
                    copy = bulk_copy(self.bulk(chunk, self.sent(chunk, z, dim)), send_sem, self.recv_sem.at[0])
                    when(cond, copy.wait_send)
            every = self.bulk(chunk, self.rails(chunk) // 2)
            for side in (0, 1):
                bulk_copy(every, self.pair_send.at[chunk, side], self.pair_recv.at[chunk, side]).wait_send()


class Reduce:
    def __init__(self, known_z, view, orders, final, buf, bulk, send, recv):
        self.view, self.orders, self.final = view, orders, final
        self.buf, self.bulk = buf, bulk
        self.send_sem, self.recv_sem = send, recv
        self.z, self.x, self.core, self.y = place(known_z)
        self.index = [self.places(chunk) for chunk in range(len(orders))]
        self.first = [sum(len(index) for index in self.index[:chunk]) for chunk in range(len(orders))]

    def coords(self, block):
        zz, flip_x, flip_y = block
        return (zz, 1 - self.x if flip_x else self.x, 1 - self.y if flip_y else self.y)

    def own(self, chunk, block):
        return self.view(chunk, self.coords(block))

    def add(self, target, source):
        target[...] = target[...] + source[...]

    def sibling(self):
        return device(self.z, self.x, 1 - self.core, self.y)

    def blocks(self, chunk):
        return [(zz, fx, fy) for zz in (3, 0, 2, 1) for fx, fy in self.flips(chunk, 0)]

    def places(self, chunk):
        order, keys = self.orders[chunk], []
        for stage, dim in enumerate(order):
            if dim == "z":
                keys += [
                    self.z_key(stage, step, way, flips)
                    for step in range(3)
                    for way in ((1, -1) if step else (1,))
                    for flips in self.flips(chunk, stage)
                ]
                continue
            wheres = range(4) if "z" in order[stage:] else ("own",)
            later = self.flips(chunk, stage + 1)
            keys += [(stage, where, *flips) for where in wheres for flips in later]
        return {key: at for at, key in enumerate(keys)}

    def place_of(self, chunk, key):
        return self.index[chunk][key]

    def send(self, chunk, block, key, target, cond):
        if cond is False:
            return
        where = self.place_of(chunk, key)
        copy = pltpu.make_async_remote_copy(
            src_ref=self.own(chunk, block),
            dst_ref=self.buf(chunk, where),
            send_sem=self.send_sem.at[chunk, key[0]],
            recv_sem=self.recv_sem.at[self.first[chunk] + where],
            device_id=target,
            device_id_type=MESH,
        )
        when(cond, copy.start)

    def landed(self, chunk, key):
        return self.buf(chunk, self.place_of(chunk, key))

    def wait(self, chunk, key):
        landed = self.landed(chunk, key)
        pltpu.make_async_remote_copy(
            src_ref=landed,
            dst_ref=landed,
            send_sem=self.send_sem.at[chunk, 0],
            recv_sem=self.recv_sem.at[self.first[chunk] + self.place_of(chunk, key)],
            device_id=self.sibling(),
            device_id_type=MESH,
        ).wait_recv()

    def flips(self, chunk, stage):
        left = self.orders[chunk][stage:]
        return [
            (fx, fy)
            for fx in ((1, 0) if "x" in left else (0,))
            for fy in ((1, 0) if "y" in left else (0,))
        ]

    def ready(self, chunk, stage, block):
        order = self.orders[chunk]
        zz, fx, fy = block
        where = zz if "z" in order[stage:] else "own"
        if order[stage] == "x" and fx:
            target = device(self.z, 1 - self.x, self.core, self.y)
            self.send(chunk, block, (stage, where, 0, fy), target, True)
        elif order[stage] == "y" and fy:
            target = device(self.z, self.x, self.core, 1 - self.y)
            self.send(chunk, block, (stage, where, fx, 0), target, True)

    def z_key(self, stage, step, way, flips):
        return (stage, step, way if step else 0, *flips)

    def z_start(self, chunk, stage, step, flips):
        up, down = (3 - step, *flips), (step, *flips)
        right = device(self.z + 1, self.x, self.core, self.y)
        left = device(self.z - 1, self.x, self.core, self.y)
        self.send(chunk, up, self.z_key(stage, step, 1, flips), right, self.z == 0)
        self.send(chunk, down, self.z_key(stage, step, -1, flips), left, self.z == 3)

    def z_arrive(self, chunk, stage, step, flips, way):
        z = self.z if way == 1 else 3 - self.z
        cond = (z >= 1) & (z <= step + 1)
        zz = 2 + z - step
        zz = zz if way == 1 else 3 - zz
        block = (zz, *flips)
        key = self.z_key(stage, step, way, flips)
        last = stage + 1 == len(self.orders[chunk]) and step == 2

        def take():
            self.wait(chunk, key)
            if not last:
                self.add(self.own(chunk, block), self.landed(chunk, key))

        when(cond, take)
        if step < 2:
            target = device(self.z + way, self.x, self.core, self.y)
            self.send(chunk, block, self.z_key(stage, step + 1, way, flips), target, cond)

    def z_done(self, chunk, stage, flips):
        block = (self.z, *flips)
        if stage + 1 < len(self.orders[chunk]):
            self.ready(chunk, stage + 1, block)
            return
        final = self.final(chunk)
        final[...] = self.own(chunk, block)[...].astype(F32)
        for way, cond in ((1, self.z >= 1), (-1, self.z <= 2)):
            landed = self.landed(chunk, self.z_key(stage, 2, way, flips))

            def add(landed=landed):
                final[...] += landed[...].astype(F32)

            when(cond, add)

    def xy_arrive(self, chunk, stage, zz, fx, fy):
        key = (stage, zz, fx, fy)
        block = (self.z if zz == "own" else zz, fx, fy)
        self.wait(chunk, key)
        own, landed = self.own(chunk, block), self.landed(chunk, key)
        if stage + 1 < len(self.orders[chunk]):
            self.add(own, landed)
            self.ready(chunk, stage + 1, block)
        else:
            final = self.final(chunk)
            final[...] = own[...].astype(F32) + landed[...].astype(F32)

    def start(self, chunk, block):
        self.ready(chunk, 0, block)

    def events(self, chunks, start=0.0, pace=1.0):
        found = []
        for chunk in chunks:
            times = {block: start for block in self.blocks(chunk)}
            found += [
                (start, chunk, functools.partial(self.start, chunk, block))
                for block in self.blocks(chunk)
                if dict(x=block[1], y=block[2], z=0)[self.orders[chunk][0]]
            ]
            for stage, dim in enumerate(self.orders[chunk]):
                clock, later = 0.0, {}
                if dim == "z":
                    for step in range(3):
                        for flips in self.flips(chunk, stage):
                            needed = (0, 3) if step == 0 else (0, 1, 2, 3)
                            clock = max(clock, *(times[(zz, *flips)] for zz in needed)) + 0.001
                            work = functools.partial(self.z_start, chunk, stage, step, flips)
                            found.append((clock, chunk, work))
                            clock += pace
                            for way in (1, -1):
                                work = functools.partial(self.z_arrive, chunk, stage, step, flips, way)
                                found.append((clock, chunk, work))
                            later[("own", *flips)] = clock + 0.001
                    for flips in self.flips(chunk, stage):
                        work = functools.partial(self.z_done, chunk, stage, flips)
                        found.append((later[("own", *flips)], chunk, work))
                else:
                    pick = 1 if dim == "x" else 2
                    for key in sorted((k for k in times if k[pick]), key=lambda k: times[k]):
                        mine = (key[0], 0, key[2]) if dim == "x" else (key[0], key[1], 0)
                        clock = max(max(clock, times[key]) + pace, times[mine] + 0.001)
                        later[mine] = clock
                        work = functools.partial(self.xy_arrive, chunk, stage, *mine)
                        found.append((clock, chunk, work))
                times = later
        return found

    def finish(self):
        for chunk, order in enumerate(self.orders):
            for stage, dim in enumerate(order):
                after = len(self.flips(chunk, stage + 1)) if stage + 1 < len(order) else 1
                count = 3 * after if dim == "z" else after * (4 if "z" in order[stage + 1 :] else 1)
                every = self.bulk(chunk, count)
                bulk_copy(every, self.send_sem.at[chunk, stage], self.recv_sem.at[0]).wait_send()


class Exchange:
    def __init__(self, source, landing, bulk, send_sem, recv_sem):
        self.source, self.landing, self.bulk = source, landing, bulk
        self.send_sem, self.recv_sem = send_sem, recv_sem
        self.band, self.y = lax.axis_index("band"), lax.axis_index("dp")
        self.bands = lax.axis_size("band")

    def send(self, target):
        pltpu.make_async_remote_copy(
            src_ref=self.source(target),
            dst_ref=self.landing(self.band),
            send_sem=self.send_sem,
            recv_sem=self.recv_sem,
            device_id=(target, self.y),
            device_id_type=MESH,
        ).start()

    def start(self):
        for step in range(1, self.bands):
            self.send((self.band + step) % self.bands)

    def wait(self):
        bulk_copy(self.bulk(self.bands - 1), self.send_sem, self.recv_sem).wait_recv()

    def finish(self):
        bulk_copy(self.bulk(self.bands - 1), self.send_sem, self.recv_sem).wait_send()


def dot_nt(left, right):
    return lax.dot_general(left, right, (((1,), (1,)), ((), ())), preferred_element_type=F32)


def dot_tn(left, right):
    return lax.dot_general(left, right, (((0,), (0,)), ((), ())), preferred_element_type=F32)


def dot_nn(left, right):
    return jnp.dot(left, right, preferred_element_type=F32)


def unit_parts(rows):
    centred = rows - jnp.mean(rows, axis=-1, keepdims=True)
    inverse = lax.rsqrt(jnp.mean(centred * centred, axis=-1, keepdims=True) + EPS_BLOCK)
    return centred * inverse, inverse


class Block:
    def __init__(self, weights, down, refs):
        self.weights, self.down = weights, down
        self.__dict__.update(refs)
        self.width = weights.shape[1]
        self.tokens = self.joint.shape[1]
        self.halves = weights.shape[1] // (2 * HEAD_DIM)

    def weight(self, part):
        return self.weights[pl.ds(aligned(part * self.width), self.width), :]

    def masks(self):
        tokens = self.joint.shape[1]
        lane = lax.broadcasted_iota(jnp.int32, (tokens, 2 * HEAD_DIM), 1)
        low = lane < HEAD_DIM
        return low, low.astype(F32).astype(B16), (~low).astype(F32).astype(B16)

    def pair_rows(self, rows, low, high):
        return jnp.concatenate([rows * low, rows * high], axis=0)

    def own(self, ref):
        return ref[: self.tokens]

    def project(self):
        unit, inverse = unit_parts(self.residual[...])
        self.normed_one[: self.tokens] = (unit * self.gain_one[...]).astype(B16)
        self.unit_one[...] = unit
        self.inverse_one[...] = jnp.broadcast_to(inverse, self.inverse_one.shape)

        @pl.loop(0, 3)
        def _(part):
            self.joint[part] = dot_nn(self.own(self.normed_one), self.weight(part)).astype(B16)

    def attend(self):
        tokens = self.joint.shape[1]
        scale = 1.0 / math.sqrt(HEAD_DIM)

        @pl.loop(0, self.halves)
        def _(pair):
            where, low, high = self.masks()
            lanes = pl.ds(pl.multiple_of(pair * 2 * HEAD_DIM, 2 * HEAD_DIM), 2 * HEAD_DIM)
            query, key, value = (self.joint[part, :, lanes] for part in range(3))
            scores = dot_nt(self.pair_rows(query, low, high), key) * scale
            raised = jnp.exp(scores - jnp.max(scores, axis=-1, keepdims=True))
            probs = raised / jnp.sum(raised, axis=-1, keepdims=True)
            self.probs[pair] = probs
            mixed = dot_nn(probs.astype(B16), value)
            self.mixed[:tokens, lanes] = jnp.where(where, mixed[:tokens], mixed[tokens:]).astype(B16)

    def middle(self):
        middle = self.residual[...] + dot_nn(self.own(self.mixed), self.weight(3))
        unit, inverse = unit_parts(middle)
        self.normed_two[: self.tokens] = (unit * self.gain_two[...]).astype(B16)
        self.unit_two[...] = unit
        self.inverse_two[...] = jnp.broadcast_to(inverse, self.inverse_two.shape)
        self.result[...] = middle

    def both_x(self, ref):
        return ref[: 2 * self.tokens]

    def down_rows(self, part):
        return self.down[pl.ds(aligned(part * self.width), self.width), :]

    def widen(self):
        @pl.loop(0, 2)
        def _(part):
            pre = dot_nn(self.both_x(self.normed_two), self.weight(4 + part))
            self.pre_act[part] = pre
            self.act[part, : 2 * self.tokens] = gelu_tanh(pre).astype(B16)

    def narrow(self):
        parts = [dot_nn(self.act[part, : 2 * self.tokens], self.down_rows(part)) for part in (0, 1)]
        total = parts[0] + parts[1]
        self.result[...] += total[: self.tokens]
        self.result_x[...] = total[self.tokens :].astype(B16)

    def back_narrow(self):
        self.grad_normed[...] = jnp.zeros(self.grad_normed.shape, F32)

        @pl.loop(0, 2)
        def _(part):
            grad_act = dot_nt(self.both_x(self.out_grad), self.down_rows(part))
            grad_pre = (grad_act * gelu_slope(self.pre_act[part])).astype(B16)
            self.grad_pre[part, : 2 * self.tokens] = grad_pre
            self.grad_normed[...] += dot_nt(grad_pre, self.weight(4 + part))

        self.grad_x[...] = self.grad_normed[self.tokens :].astype(B16)

    def turn(self, ref):
        rows = ref.shape[0]
        for at in range(0, self.width, 128):
            self.turned[at : at + 128, :rows] = ref[:, at : at + 128].T

    def down_grad(self, part, core, rail, store):
        self.turn(self.act.at[part])
        for z in (0, 1):
            rail[z * 2 * PART : (z + 1) * 2 * PART, :] = self.turned[
                pl.ds(aligned((z * 2 + core) * 2 * PART), 2 * PART), :
            ]
        for at in range(0, self.width, 256):
            cols = slice(at, at + 256)
            rows = slice(part * 4 * PART, (part + 1) * 4 * PART)
            store[rows, cols] = dot_nn(rail[...], self.out_grad[:, cols]).astype(B16)

    def turn_rail(self, target, ref, core):
        rows = ref.shape[0]
        self.turn(ref)
        for chip in range(8):
            target[chip * CHUNK : (chip + 1) * CHUNK, :] = self.turned[
                pl.ds(aligned((chip * 2 + core) * CHUNK), CHUNK), :rows
            ]

    def pair_grad(self, first, second, first_grad, second_grad, store, where):
        half = CHUNK // 2
        for at in range(0, self.width, 256):
            cols = slice(at, at + 256)
            one = dot_nn(first[...], first_grad(cols))
            two = dot_nn(second[...], second_grad(cols))
            for owner in range(16):
                rows = slice(owner * half, owner * half + half)
                piece = jnp.concatenate([one[rows], two[rows]], axis=0)
                store[pl.ds(where(owner), CHUNK), cols] = piece.astype(B16)

    def back_wide(self):
        grad_normed = self.own(self.grad_normed) + self.grad_from_x[...].astype(F32)
        unit = self.unit_two[...]
        self.small[1:2, :] = jnp.sum(grad_normed * unit, axis=0, keepdims=True)
        scaled = grad_normed * self.gain_two[...]
        back = self.inverse_two[:, :1] * (
            scaled
            - jnp.mean(scaled, axis=-1, keepdims=True)
            - unit * jnp.mean(scaled * unit, axis=-1, keepdims=True)
        )
        grad_middle = self.own(self.out_grad).astype(F32) + back
        self.grad_middle[...] = grad_middle
        branch = grad_middle.astype(B16)
        self.grad_branch[: self.tokens] = branch
        self.grad_mixed[...] = dot_nt(branch, self.weight(3)).astype(B16)

    def back_attend(self):
        tokens = self.joint.shape[1]
        scale = 1.0 / math.sqrt(HEAD_DIM)

        @pl.loop(0, self.halves)
        def _(pair):
            where, low, high = self.masks()
            lanes = pl.ds(pl.multiple_of(pair * 2 * HEAD_DIM, 2 * HEAD_DIM), 2 * HEAD_DIM)
            query, key, value = (self.joint[part, :, lanes] for part in range(3))
            grads = self.pair_rows(self.grad_mixed[:, lanes], low, high)
            probs = self.probs[pair]
            self.grad_joint[2, :tokens, lanes] = dot_tn(probs.astype(B16), grads).astype(B16)
            grad_probs = dot_nt(grads, value)
            total = jnp.sum(grad_probs * probs, axis=-1, keepdims=True)
            grad_scores = (probs * (grad_probs - total)).astype(B16)
            queries = dot_nn(grad_scores, key) * scale
            self.grad_joint[0, :tokens, lanes] = jnp.where(
                where, queries[:tokens], queries[tokens:]
            ).astype(B16)
            keys = dot_tn(grad_scores, self.pair_rows(query, low, high)) * scale
            self.grad_joint[1, :tokens, lanes] = keys.astype(B16)

    def back_project(self):
        parts = [dot_nt(self.grad_joint[part, : self.tokens], self.weight(part)) for part in range(3)]
        grad_normed = parts[0] + parts[1] + parts[2]
        unit = self.unit_one[...]
        self.small[0:1, :] = jnp.sum(grad_normed * unit, axis=0, keepdims=True)
        scaled = grad_normed * self.gain_one[...]
        back = self.inverse_one[:, :1] * (
            scaled
            - jnp.mean(scaled, axis=-1, keepdims=True)
            - unit * jnp.mean(scaled * unit, axis=-1, keepdims=True)
        )
        self.grad_middle[...] += back

    def embed_grad(self):
        return self.grad_middle[...].astype(B16)


def split3(rows):
    first = rows.astype(B16)
    rest = rows - first.astype(F32)
    second = rest.astype(B16)
    return first, second, (rest - second.astype(F32)).astype(B16)


def fold3(stacked):
    rows = stacked.shape[0] // 3
    return stacked[:rows] + (stacked[rows : 2 * rows] + stacked[2 * rows :])


def wide_nn(rows, weight):
    return fold3(dot_nn(jnp.concatenate(split3(rows), axis=0), weight))


def wide_nt(rows, weight):
    return fold3(dot_nt(jnp.concatenate(split3(rows), axis=0), weight))


def wide_tn(left, right):
    one, two = split3(left), split3(right)
    pairs = ((0, 0), (0, 1), (1, 0), (0, 2), (1, 1), (2, 0))
    return dot_tn(
        jnp.concatenate([one[a] for a, _ in pairs], axis=0),
        jnp.concatenate([two[b] for _, b in pairs], axis=0),
    )


def exact_dot(left, right, dims):
    return lax.dot_general(
        left, right, (dims, ((), ())), precision=PRECISE, preferred_element_type=F32
    )


def hyper_unit(rows):
    centred = rows - jnp.mean(rows, axis=-1, keepdims=True)
    inverse = lax.rsqrt(jnp.mean(centred * centred, axis=-1, keepdims=True) + EPS_HYPER)
    return centred * inverse, inverse


def unit_back(scaled, unit, inverse):
    return inverse * (
        scaled
        - jnp.mean(scaled, axis=-1, keepdims=True)
        - unit * jnp.mean(scaled * unit, axis=-1, keepdims=True)
    )


def by_head(rows):
    lane = lax.broadcasted_iota(jnp.int32, rows.shape, 1) // (rows.shape[1] // HHEADS)
    return jnp.concatenate([jnp.where(lane == head, rows, 0.0) for head in range(HHEADS)], axis=0)


def own_lanes(stacked):
    tokens = stacked.shape[0] // HHEADS
    out = jnp.zeros((tokens, stacked.shape[1]), F32)
    for head in range(HHEADS):
        rows = stacked[head * tokens : (head + 1) * tokens]
        lane = lax.broadcasted_iota(jnp.int32, rows.shape, 1) // (rows.shape[1] // HHEADS)
        out = out + jnp.where(lane == head, rows, 0.0)
    return out


def hyper_forward(waves, qkv, out, gain_one, up, down, gain_two):
    width = waves.shape[1]
    joint = wide_nn(waves, qkv)
    query, key, value = (joint[:, at * width : (at + 1) * width] for at in range(3))
    scores = exact_dot(by_head(query), key, ((1,), (1,))) / math.sqrt(width // HHEADS)
    raised = jnp.exp(scores - jnp.max(scores, axis=-1, keepdims=True))
    soft = raised / jnp.sum(raised, axis=-1, keepdims=True)
    mixed = own_lanes(exact_dot(soft, value, ((1,), (0,))))
    unit_one, inverse_one = hyper_unit(waves + wide_nn(mixed, out))
    first = unit_one * gain_one
    inner = wide_nn(first, up)
    unit_two, inverse_two = hyper_unit(first + wide_nn(gelu_tanh(inner), down))
    kept = (joint, soft, mixed, unit_one, inverse_one, inner, unit_two, inverse_two)
    return unit_two * gain_two, kept


def hyper_backward(grad_code, kept, waves, qkv, out, gain_one, up, down, gain_two):
    joint, soft, mixed, unit_one, inverse_one, inner, unit_two, inverse_two = kept
    width = waves.shape[1]
    query, key, value = (joint[:, at * width : (at + 1) * width] for at in range(3))
    first = unit_one * gain_one
    grad_gain_two = jnp.sum(grad_code * unit_two, axis=0, keepdims=True)
    grad_second = unit_back(grad_code * gain_two, unit_two, inverse_two)
    grad_down = wide_tn(gelu_tanh(inner), grad_second)
    grad_inner = wide_nt(grad_second, down) * gelu_slope(inner)
    grad_up = wide_tn(first, grad_inner)
    grad_first = grad_second + wide_nt(grad_inner, up)
    grad_gain_one = jnp.sum(grad_first * unit_one, axis=0, keepdims=True)
    grad_mid = unit_back(grad_first * gain_one, unit_one, inverse_one)
    grad_out = wide_tn(mixed, grad_mid)
    grad_mixed = by_head(wide_nt(grad_mid, out))
    grad_value = exact_dot(soft, grad_mixed, ((0,), (0,)))
    grad_soft = exact_dot(grad_mixed, value, ((1,), (1,)))
    total = jnp.sum(grad_soft * soft, axis=-1, keepdims=True)
    grad_scores = soft * (grad_soft - total) / math.sqrt(width // HHEADS)
    grad_query = own_lanes(exact_dot(grad_scores, key, ((1,), (0,))))
    grad_key = exact_dot(grad_scores, by_head(query), ((0,), (0,)))
    grad_qkv = wide_tn(waves, jnp.concatenate([grad_query, grad_key, grad_value], axis=1))
    return grad_qkv, grad_out, grad_gain_one, grad_up, grad_down, grad_gain_two


def spread(gathered, weights):
    width = weights.shape[1]
    half = CHUNK // 2

    @pl.loop(0, 16)
    def _(two):
        for pair in (0, 1):
            one, other = (
                gathered[pl.ds(aligned((two * 2 + k) * PART + pair * CHUNK), CHUNK), :].astype(F32)
                for k in (0, 1)
            )
            for k, rows in ((0, slice(0, half)), (1, slice(half, CHUNK))):
                target = pl.ds(aligned((2 * pair + k) * width + two * CHUNK), CHUNK)
                weights[target, :] = jnp.concatenate([one[rows], other[rows]], 0).astype(B16)


def spread_up(gathered, weights, x):
    width = weights.shape[1]
    half = CHUNK // 2

    @pl.loop(0, 8)
    def _(chip):
        z, core = chip // 2, chip % 2
        for far in (0, 1):
            one, other = (
                gathered[pl.ds(aligned((chip * 2 + k) * PART + far * CHUNK), CHUNK), :].astype(F32)
                for k in (0, 1)
            )
            row = (z * 4 + (1 - x if far else x) * 2 + core) * CHUNK
            for k, rows in ((0, slice(0, half)), (1, slice(half, CHUNK))):
                target = pl.ds(aligned((4 + k) * width + row), CHUNK)
                weights[target, :] = jnp.concatenate([one[rows], other[rows]], 0).astype(B16)


def swap_rows(rows):
    count = rows.shape[0]
    row = lax.broadcasted_iota(jnp.int32, (count, count), 0)
    col = lax.broadcasted_iota(jnp.int32, (count, count), 1)
    swap = (col == (row % 16) * 16 + row // 16).astype(F32).astype(B16)
    return dot_nn(swap, rows).astype(B16)


def rows16(ref, index):
    return ref.at[pl.ds(aligned(index * 16), 16)]


KEPT = 10
SHARED = ("og", "n1", "mx", "n2", "a0", "a1")
SHARED += ("p0", "p1", "gb", "j0", "j1", "j2")
ACROSS = ("u", "og", "n2", "r", "g", "s")


def layer_kernel(*refs):
    (counts, mask, wavelengths, pixels, kernel_gen, attn_qkv, attn_out, mlp_up, mlp_down, frequency, hyper_qkv, hyper_out, hyper_one, hyper_two,
     hyper_up, hyper_down, bias_gen, out_grad_in, norm_one, norm_two,
     block_out, pixel_out, shares, kernel_grads, code_out, code_grads, vectors, *rest_refs) = refs
    kept_refs, rest_refs = rest_refs[: KEPT], rest_refs[KEPT :]
    (gathered_attn, gathered_up, gathered_down, weights, spare, buf, joint, probs, pre_act, act, grad_pre, out_grad, mixed, normed_one, normed_two,
     unit_one, unit_two, inverse_one, inverse_two, grad_normed, grad_middle, grad_branch, grad_mixed, grad_joint,
     turned, rail_one, rail_mixed, rail_two, up_away, up_share, up_landed, result_x, result_from_x, grad_x, grad_from_x,
     residual, pixel_rows, turned_pixels, pair_pixels, mixing, kernels, pair_kernels, sending,
     landed_grads, summed, small, small_partner, small_all, code_part, code_all, gains, band_scale, pair_scale,
     pix_sem, gen_sem, front_done, narrow_done, *sems) = rest_refs
    z, x, core, y = place()
    band = lax.axis_index("band")
    bands = lax.axis_size("band")
    me = slot(z, x, core, y)
    width = gains.shape[1]
    tokens = out_grad_in.shape[0]
    sibling = (band + 1 - 2 * core, y)
    partner = (band, 1 - y)
    own_rows = pl.ds(aligned(band * 16), 16)
    gather_sems, grads_sems = sems[0:4], sems[4:8]
    (reduce_sems, embed_sems, share_sems, across_sems, front_sems, kernel_sems, cols_sems, summed_sems, vec_half_sems, vec_sems,
     code_sems) = (sems[at : at + 2] for at in range(8, 30, 2))
    gathered = (gathered_attn, gathered_up, gathered_down)

    def to_pair(index, source, target, pair=share_sems):
        return pltpu.make_async_remote_copy(
            src_ref=source,
            dst_ref=target,
            send_sem=pair[0].at[index],
            recv_sem=pair[1].at[index],
            device_id=sibling,
            device_id_type=MESH,
        )

    def shared(name):
        index = SHARED.index(name)
        ref = dict(
            og=out_grad, n1=normed_one, mx=mixed, n2=normed_two, gb=grad_branch
        ).get(name)
        if ref is None:
            ref = dict(a=act, p=grad_pre, j=grad_joint)[name[0]].at[int(name[1])]
        half = ref.shape[0] // 2
        return to_pair(index, ref.at[pl.ds(0, half)], ref.at[pl.ds(half, half)])

    own_block = aligned((z * 4 + core * 2 + y) * PART)

    def across(name):
        own, other = pl.ds(0, tokens), pl.ds(tokens, tokens)
        source, target = dict(
            u=(up_away, gathered_up.at[pl.ds(own_block + CHUNK, CHUNK)]),
            og=(out_grad.at[own], out_grad.at[other]),
            n2=(normed_two.at[own], normed_two.at[other]),
            r=(result_x, result_from_x),
            g=(grad_x, grad_from_x),
            s=(up_share.at[pl.ds(CHUNK, CHUNK)], up_landed),
        )[name]
        return pltpu.make_async_remote_copy(
            src_ref=source,
            dst_ref=target,
            send_sem=across_sems[0].at[ACROSS.index(name)],
            recv_sem=across_sems[1].at[ACROSS.index(name)],
            device_id=device(z, 1 - x, core, y),
            device_id_type=MESH,
        )

    def gen_copy(piece, target):
        return pltpu.make_async_copy(
            kernel_gen.at[:, pl.ds(piece * width, width)], target.at[pl.ds(piece * 128, 128)], gen_sem
        )

    def gen_wait(target):
        every = target.at[pl.ds(0, 16 * 128)]
        pltpu.make_async_copy(every, every, gen_sem).wait()

    barrier = pltpu.get_barrier_semaphore()
    tell_peers(barrier)
    for piece in range(16):
        gen_copy(piece, spare).start()
    load_pixels = pltpu.make_async_copy(pixels, pixel_rows, pix_sem)
    load_pixels.start()

    gains[0:1, :] = norm_one[...].astype(F32).reshape(1, width)
    gains[1:2, :] = norm_two[...].astype(F32).reshape(1, width)
    out_grad[0:tokens, :] = out_grad_in[...]
    for image in range(band_scale.shape[0]):
        used = jnp.where((band < counts[image]) & (mask[image] == 1), 1.0, 0.0)
        bands_here = jnp.full(band_scale.shape[1:], counts[image], jnp.int32).astype(F32)
        band_scale[image] = lax.rsqrt(bands_here) * used

    def rows_of(weight, piece):
        return weight[:, piece * width : (piece + 1) * width].astype(F32)

    pieces = [rows_of(attn_qkv, at) for at in range(3)] + [rows_of(attn_out, 0)]
    for at in (0, 1):
        rows = jnp.concatenate(pieces[2 * at : 2 * at + 2], axis=0).astype(B16)
        gathered_attn[pl.ds(aligned(me * PART + at * CHUNK), CHUNK), :] = rows

    def up_half(of_x):
        group = 4 * PART
        quarters = [
            jnp.concatenate([mlp_up[:, at * group : (at + 1) * group] for at in (first, first + 2)], axis=1)
            for first in (of_x, of_x + 4)
        ]
        return jnp.concatenate([quarter.astype(F32) for quarter in quarters], axis=0).astype(B16)

    for of_x in (0, 1):

        @pl.when(x == of_x)
        def _(of_x=of_x):
            gathered_up[pl.ds(own_block, CHUNK), :] = up_half(of_x)
            up_away[...] = up_half(1 - of_x)

    gathered_down[pl.ds(own_block, PART), :] = mlp_down[...]
    hyper_gains = [gain[...].astype(F32).reshape(1, HW) for gain in (hyper_one, hyper_two)]
    lengths = [jnp.full((1, HW), wavelengths[at], jnp.int32) for at in range(bands)]
    angles = jnp.concatenate(lengths, axis=0).astype(F32) * frequency[...]
    lane = lax.broadcasted_iota(jnp.int32, angles.shape, 1)
    waves = jnp.where(lane < HW // 2, jnp.sin(angles), jnp.cos(angles))
    code, kept = hyper_forward(
        waves, hyper_qkv[...], hyper_out[...], hyper_gains[0], hyper_up[...], hyper_down[...], hyper_gains[1]
    )
    kept = (*kept, jnp.concatenate(hyper_gains, axis=0), waves)
    code_low = code.astype(B16)
    code_out[...] = code_low
    for ref, value in zip(kept_refs, kept):
        ref[...] = value

    def weight_view(part, block, side):
        if part == 0:
            where = slot(block[0], block[1], side, block[2])
        else:
            where = block[0] * 4 + side * 2 + block[2]
        return gathered[part].at[pl.ds(aligned(where * PART), PART)]

    half = tokens // 2

    def image_row(block, side):
        return (block[0] * 4 + block[1] * 2 + side) * tokens

    def rail_row(block):
        return (block[0] * 2 + block[1]) * tokens

    def gather_at(known_z=None):
        return Gather(
            known_z, weight_view, ORDERS, lambda part, count: gathered[part].at[pl.ds(0, count * PART)], *gather_sems
        )

    def embed_at(known_z=None):
        return Reduce(
            known_z,
            lambda chunk, block: spare.at[pl.ds(aligned(rail_row(block) + chunk * half), half)],
            EMBED_ORDERS,
            lambda chunk: residual.at[pl.ds(chunk * half, half)],
            lambda chunk, where: buf.at[pl.ds((chunk * 11 + where) * half, half)],
            lambda chunk, count: buf.at[pl.ds(0, count * half)],
            *embed_sems,
        )

    def front_works(known_z):
        known, sums = gather_at(known_z), embed_at(known_z)
        works = [work for part in range(3) for work in in_order(known.events(part))]
        return works + in_order(sums.events((0, 1)))

    gather, embed = gather_at(), embed_at()
    plan = Plan(FRONT_PLAN, [front_works(known_z) for known_z in range(4)])
    pl.semaphore_wait(barrier, 2 * bands - 1)
    load_pixels.wait()
    for chip in range(8):
        to_pair(0, pixel_rows.at[chip * 2 + 1 - core], pair_pixels.at[chip], front_sems).start()
    to_pair(1, band_scale, pair_scale, front_sems).start()
    plan.run()
    across("u").start()
    for part in FIRST_PARTS:
        gather.start(part)
    plan.run()

    gen_wait(spare)

    @pl.loop(0, 16)
    def _(piece):
        part = dot_nn(code_out[...], spare[pl.ds(aligned(piece * 128), 128), :])
        mixing[pl.ds(aligned(piece * 16), 16), :] = part.astype(B16)

    sending[...] = swap_rows(mixing[...])
    spread_kernels = Exchange(
        lambda target: rows16(sending, target),
        lambda source: rows16(kernels, source),
        lambda count: kernels.at[pl.ds(0, count * 16)],
        *[sem.at[0] for sem in kernel_sems],
    )
    spread_kernels.start()
    plan.run()
    across("u").wait_recv()
    for part in range(3):
        if part not in FIRST_PARTS:
            gather.start(part)
    across("og").start()
    plan.run()
    kernels[own_rows, :] = sending[own_rows, :]
    biases = dot_nn(code_out[...], bias_gen[...])
    row = lax.broadcasted_iota(jnp.int32, biases.shape, 0)
    bias, pair_bias = (
        jnp.sum(jnp.where(row == of, biases, 0.0), axis=0, keepdims=True) for of in (band, sibling[0])
    )
    for group in range(4):
        turned_pixels[group] = pixel_rows[4 * group : 4 * group + 4].reshape(4 * tokens, -1).T
    plan.run()
    spread_kernels.wait()
    to_pair(2, kernels, pair_kernels, front_sems).start()
    plan.run()
    to_pair(0, pair_pixels, pair_pixels, front_sems).wait_recv()
    to_pair(1, band_scale, pair_scale, front_sems).wait_recv()
    to_pair(2, kernels, pair_kernels, front_sems).wait_recv()

    def term(group):
        mine = [group * 4 + x_of * 2 + core for x_of in (0, 1)]
        rows = jnp.concatenate([pixel_rows[image] for image in mine], axis=0)
        pair_rows = pair_pixels[2 * group : 2 * group + 2].reshape(2 * tokens, -1)
        for at in range(0, width, 256):
            cols = slice(at, at + 256)
            one = dot_nn(rows, kernels[:, cols]) + bias[:, cols]
            two = dot_nn(pair_rows, pair_kernels[:, cols]) + pair_bias[:, cols]
            for x_of, image in enumerate(mine):
                own = slice(x_of * tokens, (x_of + 1) * tokens)
                total = one[own] * band_scale[image][:1, :1] + two[own] * pair_scale[image][:1, :1]
                start = (2 * group + x_of) * tokens
                spare[start : start + tokens, cols] = total.astype(B16)

    for group in (3, 0, 2, 1):
        plan.run()
        term(group)
    plan.run()
    gather.wait_pairs(0)
    spread(gathered_attn, weights)

    names = dict(
        residual=residual, out_grad=out_grad, gain_one=gains.at[0:1], gain_two=gains.at[1:2], block_out=block_out,
        joint=joint, probs=probs, pre_act=pre_act, act=act,
        grad_pre=grad_pre, mixed=mixed, normed_one=normed_one, normed_two=normed_two, unit_one=unit_one,
        unit_two=unit_two, inverse_one=inverse_one, inverse_two=inverse_two, result=residual, grad_normed=grad_normed,
        grad_middle=grad_middle, grad_branch=grad_branch, grad_mixed=grad_mixed, grad_joint=grad_joint,
        turned=turned, small=small, result_x=result_x, grad_x=grad_x, grad_from_x=grad_from_x,
    )
    block = Block(weights, gathered_down, names)
    plan.run()
    block.project()
    shared("n1").start()
    plan.run()
    block.attend()
    shared("mx").start()
    plan.run()
    block.middle()
    across("n2").start()
    across("og").wait_recv()
    shared("og").start()
    plan.run()
    gather.wait_pairs(1)
    spread_up(gathered_up, weights, x)
    plan.run()
    across("n2").wait_recv()
    shared("n2").start()
    block.widen()
    for name in ("a0", "a1"):
        shared(name).start()
    plan.run()
    gather.wait_pairs(2)
    gather.finish()
    embed.finish()
    for copy in ((0, pair_pixels, pair_pixels), (1, band_scale, pair_scale), (2, kernels, pair_kernels)):
        to_pair(*copy, front_sems).wait_send()
    tell_near(front_done)

    def part_ref(part):
        return spare.at[pl.ds(8 * tokens, 8 * PART)] if part == 2 else gathered[part]

    def part_view(part, blk):
        where = blk[0] * 4 + blk[1] * 2 + blk[2] if part == 0 else blk[0] * 2 + blk[2]
        return part_ref(part).at[pl.ds(aligned(where * PART), PART)]

    def reduce_at(known_z=None):
        return Reduce(
            known_z,
            part_view,
            SUM_ORDERS,
            lambda part: up_share if part == 1 else shares.at[pl.ds(part * PART, PART)],
            lambda part, where: buf.at[pl.ds(((0, 19, 30)[part] + where) * PART, PART)],
            lambda part, count: part_ref(part).at[pl.ds(0, count * PART)],
            *reduce_sems,
        )

    def up_send():
        shares[pl.ds(aligned(PART + x * CHUNK), CHUNK), :] = up_share[:CHUNK]
        across("s").start()

    def up_take():
        across("s").wait_recv()
        shares[pl.ds(aligned(PART + (1 - x) * CHUNK), CHUNK), :] = up_landed[...]

    image_grads = gathered_down

    def image_view(chunk, blk, side):
        return image_grads.at[pl.ds(aligned(image_row(blk, side) + chunk * half), half)]

    def grads_at(known_z=None):
        return Gather(
            known_z, image_view, IMAGE_ORDERS, lambda chunk, count: image_grads.at[pl.ds(0, count * half)], *grads_sems
        )

    def tail_works(known_z):
        known, images = reduce_at(known_z), grads_at(known_z)
        works = [work for part in (2, 1, 0) for work in in_order(known.events((part,)))]
        works += [work for chunk in (0, 1) for work in in_order(images.events(chunk))]
        return works + [up_send, up_take]

    reduce, grads = reduce_at(), grads_at()
    plan = Plan(TAIL_PLAN, [tail_works(known_z) for known_z in range(4)])
    hear_near(front_done)
    plan.run()
    block.back_narrow()
    for part in (0, 1):
        shared(f"p{part}").start()
    across("g").start()
    plan.run()
    for name in ("og", "a0", "a1"):
        shared(name).wait_recv()
    for part in (0, 1):
        block.down_grad(part, core, rail_two, part_ref(2))
    plan.run()
    block.narrow()
    across("r").start()
    tell_near(narrow_done)
    plan.run()
    across("g").wait_recv()
    block.back_wide()
    shared("gb").start()
    plan.run()
    block.back_attend()
    for part in range(3):
        shared(f"j{part}").start()
    plan.run()
    block.back_project()
    hear_near(narrow_done)
    image_grads[pl.ds(aligned(band * tokens), tokens), :] = block.embed_grad()
    grads.start(0)
    grads.start(1)
    plan.run()
    for name in ("n2", "p0", "p1"):
        shared(name).wait_recv()
    block.turn_rail(rail_two, normed_two, core)

    def up_place(owner):
        zz, xx, yy = owner // 4, owner // 2 % 2, owner % 2
        return aligned((zz * 2 + yy) * PART + ((1 - x) if xx else x) * CHUNK)

    block.pair_grad(
        rail_two, rail_two, lambda cols: grad_pre[0, :, cols], lambda cols: grad_pre[1, :, cols], part_ref(1), up_place
    )
    plan.run()
    for name in ("n1", "mx", "gb", "j0", "j1", "j2"):
        shared(name).wait_recv()
    block.turn_rail(rail_one, normed_one, core)
    block.turn_rail(rail_mixed, mixed, core)
    block.pair_grad(
        rail_one, rail_one, lambda cols: grad_joint[0, :, cols], lambda cols: grad_joint[1, :, cols], part_ref(0),
        lambda owner: owner * PART,
    )
    block.pair_grad(
        rail_one, rail_mixed, lambda cols: grad_joint[2, :, cols], lambda cols: grad_branch[:, cols], part_ref(0),
        lambda owner: owner * PART + CHUNK,
    )
    for name in SHARED:
        shared(name).wait_send()
    for name in ("og", "n2", "g"):
        across(name).wait_send()
    for piece in range(16):
        gen_copy(piece, weights).start()

    kernel_total = pre_act.at[0]
    kernel_total[...] = jnp.zeros(kernel_total.shape, F32)
    small[2:3, :] = jnp.zeros((1, width), F32)
    near_side = z // 2
    for side in (near_side, 1 - near_side):
        plan.run()
        for chunk in (0, 1):
            grads.wait_side(chunk, side)

        @pl.loop(0, 2)
        def _(step, side=side):
            group = 2 * side + step
            for image in range(4):
                half_rows = slice(image % 2 * tokens, (image % 2 + 1) * tokens)
                rows = pl.ds(aligned((group * 4 + image) * tokens), tokens)
                scaled = image_grads[rows, :].astype(F32) * band_scale[group * 4 + image][:1, :1]
                small[2:3, :] += jnp.sum(scaled, axis=0, keepdims=True)
                act[image // 2, half_rows] = scaled.astype(B16)
            scaled = act[:, : 2 * tokens].reshape(4 * tokens, width)
            pixel_rows[pl.ds(group * 4, 4)] = dot_nt(scaled, kernels[...]).astype(B16).reshape(4, tokens, -1)
            kernel_total[...] += dot_nn(turned_pixels[group], scaled)

    store_pixels = pltpu.make_async_copy(pixel_rows, pixel_out, pix_sem)
    store_pixels.start()
    spread_kernels.finish()
    sending[...] = kernel_total[...].astype(B16)
    owner = core == y

    def column_copy(target, plane):
        return pltpu.make_async_remote_copy(
            src_ref=rows16(sending, target),
            dst_ref=rows16(landed_grads, y * bands + band),
            send_sem=cols_sems[0].at[0],
            recv_sem=cols_sems[1].at[0],
            device_id=(target, plane),
            device_id_type=MESH,
        )

    for step in range(1, bands):
        target = (band + step) % bands
        column_copy(target, target % 2).start()

    @pl.when(core != y)
    def _():
        column_copy(band, 1 - y).start()

    @pl.when(owner)
    def _():
        landed_grads[pl.ds(aligned((y * bands + band) * 16), 16), :] = sending[own_rows, :]

    vec_half = pltpu.make_async_remote_copy(
        src_ref=small, dst_ref=small_partner, send_sem=vec_half_sems[0].at[0], recv_sem=vec_half_sems[1].at[0],
        device_id=partner, device_id_type=MESH,
    )
    vec_half.start()
    plan.run()
    vec_half.wait_recv()
    small_all[band] = small[...] + small_partner[...]
    vector_spread = Exchange(
        lambda target: small_all.at[band], lambda source: small_all.at[source], lambda count: small_all.at[pl.ds(0, count)],
        *[sem.at[0] for sem in vec_sems],
    )
    vector_spread.start()
    plan.run()
    pix = summed.shape[0]

    def tell_code(target, plane):
        return pltpu.make_async_remote_copy(
            src_ref=code_all.at[band],
            dst_ref=code_all.at[band],
            send_sem=code_sems[0].at[0],
            recv_sem=code_sems[1].at[0],
            device_id=(target, plane),
            device_id_type=MESH,
        )

    pass_summed = pltpu.make_async_remote_copy(
        src_ref=summed, dst_ref=summed, send_sem=summed_sems[0].at[0], recv_sem=summed_sems[1].at[0],
        device_id=partner, device_id_type=MESH,
    )
    gen_wait(weights)

    @pl.when(owner)
    def _():
        bulk_copy(landed_grads.at[pl.ds(0, (2 * bands - 1) * 16)], cols_sems[0].at[0], cols_sems[1].at[0]).wait_recv()
        summed[...] = landed_grads[0:pix, :] + landed_grads[pix : 2 * pix, :]
        pass_summed.start()
        mixing[...] = swap_rows(summed[...])
        code_part[...] = jnp.zeros(code_part.shape, F32)

        @pl.loop(0, 16)
        def _(piece):
            code_part[...] += dot_nt(
                mixing[pl.ds(aligned(piece * 16), 16), :], weights[pl.ds(aligned(piece * 128), 128), :]
            )

        code_all[band] = code_part[...]
        for step in range(bands):
            for plane in (y, 1 - y) if step else (1 - y,):
                tell_code((band + step) % bands, plane).start()

    @pl.when(core != y)
    def _():
        pass_summed.wait_recv()

    store_columns = pltpu.make_async_copy(summed, kernel_grads, pix_sem)
    store_pixels.wait()
    store_columns.start()
    plan.run()
    across("r").wait_recv()
    block_out[...] = (residual[...] + result_from_x[...].astype(F32)).astype(B16)
    vector_spread.wait()
    store_vectors = pltpu.make_async_copy(small_all, vectors, gen_sem)
    store_vectors.start()
    bulk = code_all.at[pl.ds(0, bands - 1)]
    pl.when(owner)(bulk_copy(bulk, code_sems[0].at[0], code_sems[1].at[0]).wait_recv)
    bulk = code_all.at[pl.ds(0, bands)]
    pl.when(core != y)(bulk_copy(bulk, code_sems[0].at[0], code_sems[1].at[0]).wait_recv)
    total = code_all[0]
    for source in range(1, bands):
        total = total + code_all[source]
    code_grads[...] = total
    plan.run()
    reduce.finish()
    grads.finish()
    for name in ("u", "r", "s"):
        across(name).wait_send()
    vec_half.wait_send()
    vector_spread.finish()

    @pl.when(owner)
    def _():
        sent = landed_grads.at[pl.ds(0, (bands - 1) * 16)]
        bulk_copy(sent, cols_sems[0].at[0], cols_sems[1].at[0]).wait_send()
        sent = code_all.at[pl.ds(0, 2 * bands - 1)]
        bulk_copy(sent, code_sems[0].at[0], code_sems[1].at[0]).wait_send()
        pass_summed.wait_send()

    @pl.when(core != y)
    def _():
        sent = landed_grads.at[pl.ds(0, bands * 16)]
        bulk_copy(sent, cols_sems[0].at[0], cols_sems[1].at[0]).wait_send()

    store_columns.wait()
    store_vectors.wait()


VMEM_BYTES = 63 * 2**20


def layer(counts, mask, wavelengths, pixels, kernel_gen, weights, frequency, hyper, bias_gen, out_grad, gains):
    width = bias_gen.shape[1]
    bands = lax.axis_size("band")
    devices = bands * lax.axis_size("dp")
    images, tokens, pix = pixels.shape
    hidden = hyper[4].shape[1]
    vmem = pl.BlockSpec(memory_space=pltpu.VMEM)
    hbm = pl.BlockSpec(memory_space=pl.ANY)
    smem = pl.BlockSpec(memory_space=pltpu.SMEM)
    shape = jax.ShapeDtypeStruct
    rows = lambda kind, *lead: pltpu.VMEM((*lead, tokens, width), kind)
    pair = lambda *lead: pltpu.VMEM((*lead, 2 * tokens, width), B16)
    four = lambda *lead: pltpu.VMEM((*lead, 4 * tokens, width), B16)
    dma = pltpu.SemaphoreType.DMA
    code = (bands, HW)
    kept = [(bands, 3 * HW), (HHEADS * bands, bands), code, code, (bands, 1), (bands, hidden), code, (bands, 1), (2, HW), code]
    return pl.pallas_call(
        layer_kernel,
        out_shape=[
            shape((tokens, width), B16),
            shape(pixels.shape, B16),
            shape((3 * PART, width), F32),
            shape((pix, width), B16),
            shape(code, B16),
            shape(code, F32),
            shape((bands, 8, width), F32),
            *[shape(dims, F32) for dims in kept],
        ],
        in_specs=[smem] * 3 + [hbm] * 2 + [vmem] * 15,
        out_specs=[vmem, hbm, vmem, hbm, vmem, vmem, hbm] + [vmem] * KEPT,
        scratch_shapes=[
            pltpu.VMEM((devices * PART, width), B16),
            pltpu.VMEM((devices // 2 * PART, width), B16),
            pltpu.VMEM((images * tokens, width), B16),
            pltpu.VMEM((6 * width, width), B16),
            pltpu.VMEM((16 * HW, width), B16),
            pltpu.VMEM(((19 + 11 + 11) * PART, width), B16),
            rows(B16, 3),
            pltpu.VMEM((HEADS // 2, 2 * tokens, tokens), F32),
            pltpu.VMEM((2, 2 * tokens, width), F32),
            four(2),
            four(2),
            four(),
            pair(),
            pair(),
            four(),
            rows(F32),
            rows(F32),
            pltpu.VMEM((tokens, 128), F32),
            pltpu.VMEM((tokens, 128), F32),
            pltpu.VMEM((2 * tokens, width), F32),
            rows(F32),
            pair(),
            rows(B16),
            pair(3),
            pltpu.VMEM((width, 4 * tokens), B16),
            pltpu.VMEM((width // 2, 2 * tokens), B16),
            pltpu.VMEM((width // 2, 2 * tokens), B16),
            pltpu.VMEM((width // 2, 4 * tokens), B16),
            pltpu.VMEM((CHUNK, width), B16),
            pltpu.VMEM((PART, width), F32),
            pltpu.VMEM((CHUNK, width), F32),
            rows(B16),
            rows(B16),
            rows(B16),
            rows(B16),
            rows(F32),
            pltpu.VMEM(pixels.shape, B16),
            pltpu.VMEM((4, pix, 4 * tokens), B16),
            pltpu.VMEM((images // 2, tokens, pix), B16),
            pltpu.VMEM((pix, width), B16),
            pltpu.VMEM((pix, width), B16),
            pltpu.VMEM((pix, width), B16),
            pltpu.VMEM((pix, width), B16),
            pltpu.VMEM((2 * pix, width), B16),
            pltpu.VMEM((pix, width), B16),
            pltpu.VMEM((8, width), F32),
            pltpu.VMEM((8, width), F32),
            pltpu.VMEM((bands, 8, width), F32),
            pltpu.VMEM(code, F32),
            pltpu.VMEM((2 * bands, *code), F32),
            pltpu.VMEM((2, width), F32),
            pltpu.VMEM((images, 8, 128), F32),
            pltpu.VMEM((images, 8, 128), F32),
            dma,
            dma,
            pltpu.SemaphoreType.REGULAR,
            pltpu.SemaphoreType.REGULAR,
            *[dma((3, 3)), dma((32,)), dma((3, 2)), dma((3, 2))],
            *[dma((2, 3)), dma((16,)), dma((2, 2)), dma((2, 2))],
            *[dma((3, 3)), dma((37,))],
            *[dma((2, 2)), dma((20,))],
            *[dma((len(SHARED),))] * 2,
            *[dma((len(ACROSS),))] * 2,
            *[dma((3,))] * 2,
            *[dma((1,))] * 12,
        ],
        compiler_params=pltpu.CompilerParams(
            collective_id=0, has_side_effects=True, vmem_limit_bytes=VMEM_BYTES
        ),
        name="layer",
    )(counts, mask, wavelengths, pixels, kernel_gen, *weights, frequency, *hyper, bias_gen, out_grad, *gains)


def finish_kernel(*refs):
    count = 12 + KEPT
    outside = refs[:count]
    (block_out, pixel_out, grad_qkv, grad_out, grad_gain_one, grad_up, grad_down, grad_gain_two, grad_gen, grad_bias,
     gain_one_sum, gain_two_sum, share_qkv, share_out, share_up, share_down, *scratch) = refs[count:]
    inside, (store, in_sem, copy_sem, gen_sem) = scratch[:count], scratch[count:]
    loads = [pltpu.make_async_copy(*pair, in_sem.at[at]) for at, pair in enumerate(zip(outside, inside))]
    for load in loads:
        load.start()
    (code_low, columns, shares, hyper_qkv, hyper_out, hyper_up, hyper_down, bias_gen, code_grads, vectors,
     *kept_refs, hyper_gains, waves, block_in, pixel_in) = inside
    width = bias_gen.shape[1]
    copies = [
        pltpu.make_async_copy(block_in, block_out, copy_sem.at[0]),
        pltpu.make_async_copy(pixel_in, pixel_out, copy_sem.at[1]),
    ]
    for load in loads[:2]:
        load.wait()
    code = code_low[...]
    swapped = swap_rows(columns[...])
    gen_copies = []
    for piece in range(16):
        store[piece] = dot_tn(code, swapped[piece * 16 : (piece + 1) * 16])
        gen_copies.append(
            pltpu.make_async_copy(
                store.at[piece], grad_gen.at[:, pl.ds(piece * width, width)], gen_sem.at[piece]
            )
        )
        gen_copies[-1].start()
    for load in loads[2:]:
        load.wait()
    for copy in copies:
        copy.start()
    share_qkv[...] = jnp.concatenate([shares[at * 24 : at * 24 + 24, :] for at in range(3)], axis=1)
    share_out[...] = shares[72:96, :]
    group = 4 * PART
    up_pieces = []
    for at in range(8):
        z_of, x_of = at // 2, at % 2
        row = PART + x_of * CHUNK + z_of // 2 * 24
        up_pieces.append(shares[row : row + 24, z_of % 2 * group : (z_of % 2 + 1) * group])
    share_up[...] = jnp.concatenate(up_pieces, axis=1)
    share_down[...] = shares[192:288, :]
    sums = jnp.sum(vectors[...], axis=0)
    gain_one_sum[...] = sums[0]
    gain_two_sum[...] = sums[1]
    bias_grads = vectors[:, 2, :]
    grad_bias[...] = dot_tn(jnp.concatenate([code] * 3, axis=0), jnp.concatenate(split3(bias_grads), axis=0))
    grad_code = code_grads[...] + wide_nt(bias_grads, bias_gen[...])
    grads = hyper_backward(
        grad_code, [ref[...] for ref in kept_refs], waves[...], hyper_qkv[...], hyper_out[...], hyper_gains[0:1, :],
        hyper_up[...], hyper_down[...], hyper_gains[1:2, :],
    )
    for ref, value in zip((grad_qkv, grad_out, grad_gain_one, grad_up, grad_down, grad_gain_two), grads):
        ref[...] = value
    for copy in copies + gen_copies:
        copy.wait()


def finish(hyper, bias_gen, code_low, code_grads, vectors, columns, shares, block_out, pixel_grad, kept, kernel_gen, weights):
    width = bias_gen.shape[1]
    vmem = pl.BlockSpec(memory_space=pltpu.VMEM)
    hbm = pl.BlockSpec(memory_space=pl.ANY)
    shape = lambda array: jax.ShapeDtypeStruct(array.shape, F32)
    line = jax.ShapeDtypeStruct((1, HW), F32)
    weights_in = (hyper[0], hyper[1], hyper[4], hyper[5])
    operands = (code_low, columns, shares, *weights_in, bias_gen, code_grads, vectors, *kept, block_out, pixel_grad)
    return pl.pallas_call(
        finish_kernel,
        out_shape=[
            jax.ShapeDtypeStruct(block_out.shape, B16),
            jax.ShapeDtypeStruct(pixel_grad.shape, B16),
            shape(hyper[0]), shape(hyper[1]), line, shape(hyper[4]), shape(hyper[5]), line,
            shape(kernel_gen), shape(bias_gen), *[jax.ShapeDtypeStruct((width,), F32)] * 2,
            *[shape(weight) for weight in weights],
        ],
        in_specs=[hbm] * len(operands),
        out_specs=[hbm, hbm] + [vmem] * 6 + [hbm] + [vmem] * 7,
        scratch_shapes=[
            *[pltpu.VMEM(operand.shape, operand.dtype) for operand in operands],
            pltpu.VMEM((16, HW, width), F32),
            pltpu.SemaphoreType.DMA((len(operands),)),
            pltpu.SemaphoreType.DMA((2,)),
            pltpu.SemaphoreType.DMA((16,)),
        ],
        compiler_params=pltpu.CompilerParams(vmem_limit_bytes=VMEM_BYTES),
        name="finish",
    )(*operands)


def body(
    pixels,
    wavelengths,
    band_counts,
    band_mask,
    hyper_qkv,
    hyper_out,
    hyper_gain1,
    hyper_up,
    hyper_down,
    hyper_gain2,
    kernel_gen,
    bias_gen,
    norm_gain1,
    attn_qkv,
    attn_out,
    norm_gain2,
    mlp_up,
    mlp_down,
    out_grad,
):
    f32 = jnp.float32
    b16 = jnp.bfloat16
    band_local = pixels.shape[3]
    pixel_local = pixels[0]
    model_width = bias_gen.shape[1]
    hyper_params = tuple(
        (
            weight.astype(f32)
            for weight in (hyper_qkv, hyper_out, hyper_gain1, hyper_up, hyper_down, hyper_gain2)
        )
    )
    wave_tokens = wave_embed(wavelengths, HW)
    band_code, hyper_pull = jax.vjp(lambda *params: hyper_net(wave_tokens, *params), *hyper_params)
    code_low = band_code.astype(b16)
    column_part = jnp.dot(code_low, kernel_gen, preferred_element_type=f32).astype(b16)
    kernel_rows = lax.all_to_all(column_part, "band", split_axis=0, concat_axis=1, tiled=True)
    kernels = kernel_rows.reshape(band_local, -1, model_width)
    first_band = lax.axis_index("band") * band_local
    own_code = lax.dynamic_slice_in_dim(code_low, first_band, band_local, 0)
    count_row = band_counts[0]
    biases = jnp.dot(own_code, bias_gen, preferred_element_type=f32)
    slot_ids = first_band + jnp.arange(band_local, dtype=jnp.int32)
    active = (slot_ids[None, :] < count_row[:, None]) & (band_mask[0] == 1)
    band_weight = jnp.where(active, lax.rsqrt(count_row.astype(f32))[:, None], f32(0.0))
    pixel_rows = pixel_local
    weight_rows = band_weight
    conv_out = jnp.einsum("inbp,bpd->inbd", pixel_rows, kernels, preferred_element_type=f32)
    residual = lax.psum_scatter(
        jnp.sum((conv_out + biases[None, None]) * weight_rows[:, None, :, None], axis=2),
        "band",
        scatter_dimension=0,
        tiled=True,
    )
    gathered = (
        lax.all_gather(attn_qkv, ("band", "dp"), axis=0, tiled=True),
        lax.all_gather(attn_out, ("band", "dp"), axis=0, tiled=True),
        lax.all_gather(mlp_up, ("band", "dp"), axis=0, tiled=True),
        lax.all_gather(mlp_down, ("band", "dp"), axis=0, tiled=True),
    )
    qkv_full, out_full, up_full, down_full = gathered
    gain_one = norm_gain1.astype(f32)
    gain_two = norm_gain2.astype(f32)
    images, tokens = (residual.shape[0], residual.shape[1])
    score_scale = 1.0 / math.sqrt(HEAD_DIM)
    normed_full, unit_one, inverse_one = norm_parts(residual, gain_one)
    normed_one = normed_full.astype(b16)
    joint_rows = jnp.einsum("ind,de->ine", normed_one, qkv_full, preferred_element_type=f32).astype(
        b16
    )
    queries = joint_rows[..., :model_width].reshape(images, tokens, HEADS, HEAD_DIM)
    key_rows = joint_rows[..., model_width : 2 * model_width].reshape(
        images, tokens, HEADS, HEAD_DIM
    )
    value_rows = joint_rows[..., 2 * model_width :].reshape(images, tokens, HEADS, HEAD_DIM)
    scores = (
        jnp.einsum("inhc,imhc->ihnm", queries, key_rows, preferred_element_type=f32) * score_scale
    )
    row_top = jnp.max(scores, axis=-1, keepdims=True)
    log_total = row_top + jnp.log(jnp.sum(jnp.exp(scores - row_top), axis=-1, keepdims=True))
    probs_full = jnp.exp(scores - log_total)
    probs_low = probs_full.astype(b16)
    mixed_low = (
        jnp.einsum("ihnm,imhc->inhc", probs_low, value_rows, preferred_element_type=f32)
        .reshape(images, tokens, model_width)
        .astype(b16)
    )
    middle = residual + jnp.einsum("ind,de->ine", mixed_low, out_full, preferred_element_type=f32)
    normed_two_full, unit_two, inverse_two = norm_parts(middle, gain_two)
    normed_two = normed_two_full.astype(b16)
    pre_act = jnp.einsum("ind,df->inf", normed_two, up_full, preferred_element_type=f32)
    act_low = gelu_tanh(pre_act).astype(b16)
    result = middle + jnp.einsum("inf,fd->ind", act_low, down_full, preferred_element_type=f32)
    block_out = result.astype(b16)[None]
    qkv_back, out_back, up_back, down_back = (
        lax.all_gather(attn_qkv, ("band", "dp"), axis=0, tiled=True),
        lax.all_gather(attn_out, ("band", "dp"), axis=0, tiled=True),
        lax.all_gather(mlp_up, ("band", "dp"), axis=0, tiled=True),
        lax.all_gather(mlp_down, ("band", "dp"), axis=0, tiled=True),
    )
    grad_top = out_grad[0]
    grad_down = jnp.einsum("inf,ind->fd", act_low, grad_top, preferred_element_type=f32)
    grad_act = jnp.einsum("ind,fd->inf", grad_top, down_back, preferred_element_type=f32)
    grad_pre = (grad_act * gelu_slope(pre_act)).astype(b16)
    grad_up = jnp.einsum("ind,inf->df", normed_two, grad_pre, preferred_element_type=f32)
    grad_normed_two = jnp.einsum("inf,df->ind", grad_pre, up_back, preferred_element_type=f32)
    grad_gain_two = jnp.sum(grad_normed_two * unit_two, axis=(0, 1))
    grad_middle = grad_top.astype(f32) + norm_back(grad_normed_two, gain_two, unit_two, inverse_two)
    grad_branch = grad_middle.astype(b16)
    grad_out_proj = jnp.einsum("ind,ine->de", mixed_low, grad_branch, preferred_element_type=f32)
    grad_mixed = (
        jnp.einsum("ine,de->ind", grad_branch, out_back, preferred_element_type=f32)
        .astype(b16)
        .reshape(images, tokens, HEADS, HEAD_DIM)
    )
    grad_values = jnp.einsum("ihnm,inhc->imhc", probs_low, grad_mixed, preferred_element_type=f32)
    grad_probs = jnp.einsum("inhc,imhc->ihnm", grad_mixed, value_rows, preferred_element_type=f32)
    grad_scores = (
        probs_full * (grad_probs - jnp.sum(grad_probs * probs_full, axis=-1, keepdims=True))
    ).astype(b16)
    grad_queries = (
        jnp.einsum("ihnm,imhc->inhc", grad_scores, key_rows, preferred_element_type=f32)
        * score_scale
    )
    grad_keys = (
        jnp.einsum("ihnm,inhc->imhc", grad_scores, queries, preferred_element_type=f32)
        * score_scale
    )
    grad_joint = jnp.concatenate(
        [
            grad_queries.reshape(images, tokens, model_width),
            grad_keys.reshape(images, tokens, model_width),
            grad_values.reshape(images, tokens, model_width),
        ],
        axis=-1,
    ).astype(b16)
    grad_qkv = jnp.einsum("ind,ine->de", normed_one, grad_joint, preferred_element_type=f32)
    grad_normed_one = jnp.einsum("ine,de->ind", grad_joint, qkv_back, preferred_element_type=f32)
    grad_gain_one = jnp.sum(grad_normed_one * unit_one, axis=(0, 1))
    grad_embed = grad_middle + norm_back(grad_normed_one, gain_one, unit_one, inverse_one)
    grad_embed_low = grad_embed.astype(b16)[None]
    grad_rows = lax.all_gather(grad_embed_low, "band", axis=1, tiled=True)[0].astype(f32)
    weight_rows = band_weight
    pixel_rows = pixel_local
    scaled = grad_rows[:, :, None, :] * weight_rows[:, None, :, None]
    bias_total = jnp.sum(scaled, axis=(0, 1))
    scaled_low = scaled.astype(b16)
    kernel_total = jnp.einsum("inbp,inbd->bpd", pixel_rows, scaled_low, preferred_element_type=f32)
    pixel_part = jnp.einsum(
        "inbd,bpd->inbp", scaled_low, kernels, preferred_element_type=f32
    ).astype(b16)
    pixel_total = pixel_part
    kernel_grad, bias_grad, pixel_total = (kernel_total, bias_total, pixel_total)
    pixel_out = pixel_total[None]
    kernel_grad_low = kernel_grad.reshape(band_local, -1).astype(b16)
    grad_columns = lax.all_to_all(kernel_grad_low, "band", split_axis=1, concat_axis=0, tiled=True)
    grad_kernel_part = jnp.einsum("nh,nc->hc", code_low, grad_columns, preferred_element_type=f32)
    grad_code_part = jnp.einsum("nc,hc->nh", grad_columns, kernel_gen, preferred_element_type=f32)
    bias_back = jnp.einsum("bd,hd->bh", bias_grad, bias_gen.astype(f32), precision=PRECISE)
    grad_code_part = grad_code_part + lax.dynamic_update_slice_in_dim(
        jnp.zeros_like(grad_code_part), bias_back, first_band, 0
    )
    grad_bias_part = jnp.einsum("bh,bd->hd", own_code.astype(f32), bias_grad, precision=PRECISE)
    grad_code, grad_bias_gen, grad_norm_gain1, grad_norm_gain2 = lax.psum(
        (grad_code_part, grad_bias_part, grad_gain_one, grad_gain_two), ("band", "dp")
    )
    grad_kernel_gen = lax.psum(grad_kernel_part.astype(jnp.bfloat16), "dp").astype(jnp.float32)
    hyper_grads = hyper_pull(grad_code)
    shares = (
        lax.psum_scatter(grad_qkv, ("band", "dp"), scatter_dimension=0, tiled=True),
        lax.psum_scatter(grad_out_proj, ("band", "dp"), scatter_dimension=0, tiled=True),
        lax.psum_scatter(grad_up, ("band", "dp"), scatter_dimension=0, tiled=True),
        lax.psum_scatter(grad_down, ("band", "dp"), scatter_dimension=0, tiled=True),
    )
    return (
        block_out,
        pixel_out,
        hyper_grads[0],
        hyper_grads[1],
        hyper_grads[2],
        hyper_grads[3],
        hyper_grads[4],
        hyper_grads[5],
        grad_kernel_gen,
        grad_bias_gen,
        grad_norm_gain1,
        shares[0],
        shares[1],
        grad_norm_gain2,
        shares[2],
        shares[3],
    )


def fast_body(
    pixels,
    wavelengths,
    band_counts,
    band_mask,
    hyper_qkv,
    hyper_out,
    hyper_gain1,
    hyper_up,
    hyper_down,
    hyper_gain2,
    kernel_gen,
    bias_gen,
    norm_gain1,
    attn_qkv,
    attn_out,
    norm_gain2,
    mlp_up,
    mlp_down,
    out_grad,
):
    half = np.arange(HW) % (HW // 2)
    frequency = jnp.power(10000.0, jnp.asarray(-half / (HW // 2), F32))[None]
    weights = (attn_qkv, attn_out, mlp_up, mlp_down)
    hyper = (hyper_qkv, hyper_out, hyper_gain1, hyper_gain2, hyper_up, hyper_down)
    block_out, pixel_grad, shares, columns, code_low, code_grads, vectors, *kept = layer(
        band_counts[0],
        band_mask[0, :, 0],
        wavelengths,
        pixels[0, :, :, 0],
        kernel_gen,
        weights,
        frequency,
        hyper,
        bias_gen,
        out_grad[0, 0],
        (norm_gain1, norm_gain2),
    )
    outs = finish(
        hyper,
        bias_gen,
        code_low,
        code_grads,
        vectors,
        columns,
        shares,
        block_out,
        pixel_grad,
        kept,
        kernel_gen,
        weights,
    )
    block_out, pixel_grad, *hyper_grads, grad_gen, grad_bias, gain_one, gain_two = outs[:12]
    hyper_grads[2], hyper_grads[5] = hyper_grads[2][0], hyper_grads[5][0]
    return (
        block_out[None, None],
        pixel_grad[None, :, :, None],
        *hyper_grads,
        grad_gen,
        grad_bias,
        gain_one,
        outs[12],
        outs[13],
        gain_two,
        outs[14],
        outs[15],
    )


def solution(mesh):
    placed = (
        P("dp", None, None, "band", None),
        P(),
        P("dp", None),
        P("dp", None, "band"),
        P(),
        P(),
        P(),
        P(),
        P(),
        P(),
        P(None, "band"),
        P(),
        P(),
        P(("band", "dp"), None),
        P(("band", "dp"), None),
        P(),
        P(("band", "dp"), None),
        P(("band", "dp"), None),
        P("dp", "band", None, None),
    )
    one_slot = (mesh.shape["band"], mesh.shape["dp"]) == (16, 2)
    return jax.shard_map(
        fast_body if one_slot else body,
        mesh=mesh,
        in_specs=placed,
        out_specs=(
            P("dp", "band", None, None),
            P("dp", None, None, "band", None),
            P(),
            P(),
            P(),
            P(),
            P(),
            P(),
            P(None, "band"),
            P(),
            P(),
            P(("band", "dp"), None),
            P(("band", "dp"), None),
            P(),
            P(("band", "dp"), None),
            P(("band", "dp"), None),
        ),
        check_vma=False,
    )
```
